32 devices in a mesh: seg: 8 (over y, x, core), doc: 4 (over z).
Axes of the slice: x: 2, y: 2, z: 4, core: 2. Of those that a mesh axis runs over, the one named last changes fastest.
Arguments:
- tokens: bfloat16 [4, 128, 128, 768], P('doc', 'seg'), may hold values from -6 to 6
- cotangent: bfloat16 [4, 128, 128, 768], P('doc', 'seg'), may hold values from -6 to 6
- seg_doc: int32 [4, 128], P('doc', 'seg'), may hold values from 0 to 4, as said below
- seg_pos: int32 [4, 128], P('doc', 'seg'), may hold values from 0 to 63, as said below
- master: float32 [14225408], P(('seg', 'doc'))
- momentum: float32 [14225408], P(('seg', 'doc')), may hold values from -0.6 to 0.6
- average: float32 [14225408], P(('seg', 'doc'))
Outputs:
- mixed_out: bfloat16 [4, 128, 128, 768], P('doc', 'seg')
- token_grad: bfloat16 [4, 128, 128, 768], P('doc', 'seg')
- new_master: float32 [14225408], P(('seg', 'doc'))
- new_momentum: float32 [14225408], P(('seg', 'doc'))
- new_average: float32 [14225408], P(('seg', 'doc'))
- weight_copy: bfloat16 [14225408], P(('seg', 'doc'))
The draws below stay inside these ranges and needn't reach their ends.
Inputs may be any that keep to these rules, and one draw needn't show every extreme that they name: `seg_doc`: each group holds whole documents of 64 or 16 segments: as many of 64 as fit beside one of 16, the rest of 16, numbered from 0 upward in an order drawn from the seed; document d of a group is owned by index d of seg. One device holds at most 64 / (devices of seg) segments of one document, and every document of 64 segments has exactly that many on every device of its group. `seg_pos`: the segments of a document of length L carry the places 0 to L - 1, each once.
All inputs are finite; a program needn't handle non-finite values.
Results may differ from the reference program's by a relative error of at most 0.019.
Values may be sent and summed in bfloat16 or wider, within the bound.
No kernel may reach another device: no remote copies, remote signals or barrier semaphores. Data moves between devices by JAX's collectives and lax.ppermute only.
A program may use at most 384 MiB of HBM per device.

```python
import math
import jax
import jax.numpy as jnp
from jax import lax

D = 768
HEADS = 12
HEAD_DIM = 64
FF = 3072
SEG_LEN = 128
LONG_SEGS = 64
SHORT_SEGS = 16
SEG_DEV = 16
GRPS = 4
SEGS_G = 128
P_PAD = 14225408
N_SEG = 8


def param_layout_drawn():
    return [('w_qkv', (D, 3 * D)), ('b_qv', (2 * D,)), ('w_out', (D, D)), ('b_out', (D,)), ('gain_one', (D,)), ('bias_one', (D,)), ('w_up', (D, FF)), ('b_up', (FF,)), ('w_down', (FF, D)), ('b_down', (D,)), ('gain_two', (D,)), ('bias_two', (D,)), ('pos_table', (LONG_SEGS, D)), ('x_qkv', (D, 3 * D)), ('x_bqv', (2 * D,)), ('x_out', (D, D)), ('x_bout', (D,)), ('gain_three', (D,)), ('bias_three', (D,)), ('x_up', (D, FF)), ('x_bup', (FF,)), ('x_down', (FF, D)), ('x_bdown', (D,)), ('gain_four', (D,)), ('bias_four', (D,))]


def entry_scale(entry_name):
    if entry_name in ('w_qkv', 'w_up', 'x_qkv', 'x_up'):
        return 1.0 / math.sqrt(D)
    if entry_name in ('w_down', 'x_down'):
        return 1.0 / math.sqrt(FF)
    if entry_name == 'w_out':
        return math.sqrt(SEG_LEN / (4.0 * D))
    if entry_name == 'x_out':
        return math.sqrt(LONG_SEGS / (4.0 * D))
    if entry_name == 'pos_table':
        return 1.0
    return 0.1


def weights_flat(key, uniform_width):
    pieces = []
    total_len = 0
    for number, (entry_name, entry_shape) in enumerate(param_layout_drawn()):
        length = math.prod(entry_shape)
        total_len += length
        sub_key = jax.random.fold_in(key, number)
        key_one, key_two = jax.random.split(sub_key)
        if entry_name[:4] == 'gain':
            pieces.append(1.0 + 0.3 * jax.random.uniform(key_one, (length,), jnp.float32, -1.0, 1.0))
        else:
            noise = uniform_width * jax.random.uniform(key_one, (length,), jnp.float32, -1.0, 1.0)
            noise = jax.random.normal(key_two, (length,), jnp.float32)
            pieces.append(noise * entry_scale(entry_name))
    tail_key = jax.random.fold_in(key, 1000)
    pieces.append(0.1 * jax.random.normal(tail_key, (P_PAD - total_len,), jnp.float32))
    return jnp.concatenate(pieces)


def group_layout(key):
    total_segs = SEG_DEV * N_SEG
    n_long = (total_segs - SHORT_SEGS) // LONG_SEGS
    n_docs = total_segs // SHORT_SEGS - n_long * (LONG_SEGS // SHORT_SEGS - 1)
    doc_slots = jnp.arange(N_SEG)
    scoring = jax.random.permutation(key, N_SEG) + jnp.where(doc_slots < n_docs, 0, N_SEG)
    ranking = jnp.sum(scoring[None, :] < scoring[:, None], axis=1)
    lengths = jnp.where(doc_slots < n_docs, jnp.where(ranking < n_long, LONG_SEGS, SHORT_SEGS), 0)
    ending = jnp.cumsum(lengths)
    starting = ending - lengths
    slot_index = jnp.arange(total_segs)
    logical = slot_index % SEG_DEV * N_SEG + slot_index // SEG_DEV
    doc_ids = jnp.sum(ending[None, :] <= logical[:, None], axis=1).astype(jnp.int32)
    places = (logical - jnp.take(starting, doc_ids)).astype(jnp.int32)
    return (doc_ids, places)


def layout_all(key):
    group_keys = jax.random.split(key, GRPS)
    return jax.vmap(group_layout)(group_keys)


def draw_seg_doc(key, part):
    doc_ids, places = layout_all(key)
    return doc_ids


def draw_seg_pos(key, part):
    doc_ids, places = layout_all(key)
    return places


def draw_master(key, part):
    key = jax.random.fold_in(key, 11)
    return weights_flat(key, 0.0)


def draw_average(key, part):
    key = jax.random.fold_in(key, 13)
    return weights_flat(key, 0.0)


def shard_levels(own_key, extent, cuts, low, high):
    def one(axis_at, blocks):
        heights = jax.random.uniform(jax.random.fold_in(jax.random.fold_in(own_key, 6), axis_at), (blocks,), jnp.float32, low / len(cuts), high / len(cuts))
        return jnp.repeat(jnp.exp(heights), extent[axis_at] // blocks).reshape((-1,) + (1,) * (len(extent) - axis_at - 1))

    loudness = one(*cuts[0])
    for cut in cuts[1:]:
        loudness = loudness * one(*cut)
    return loudness


def normal_values(stream_key, extent, deviation, reach, cuts=(), kind=jnp.bfloat16):
    result = deviation * jax.random.normal(stream_key, extent, jnp.float32)
    if cuts:
        result = result * shard_levels(stream_key, extent, cuts, -0.22, 0.18)
    return jnp.clip(result, -reach, reach).astype(kind)


def setup_inputs(seed: int = 0) -> dict:
    streams_of = jax.random.split(jax.random.key(seed), 8)
    tokens = normal_values(streams_of[0], (GRPS, SEGS_G, SEG_LEN, D), 1.0, 6.0, ((0, 4), (1, 8)))
    cotangent = normal_values(streams_of[1], (GRPS, SEGS_G, SEG_LEN, D), 1.0, 6.0, ((0, 4), (1, 8)))
    seg_doc = draw_seg_doc(jax.random.fold_in(streams_of[7], 71), 0)
    seg_pos = draw_seg_pos(jax.random.fold_in(streams_of[7], 71), 0)
    master = draw_master(jax.random.fold_in(streams_of[7], 71), 0)
    momentum = normal_values(streams_of[5], (P_PAD,), 0.1, 0.6, ((0, 32),), jnp.float32)
    average = draw_average(jax.random.fold_in(streams_of[7], 71), 0)
    return {"tokens": tokens, "cotangent": cotangent, "seg_doc": seg_doc, "seg_pos": seg_pos, "master": master, "momentum": momentum, "average": average}


EPSILON = 1e-05
NEGATIVE = -1e+30
HIGHEST = lax.Precision.HIGHEST

@jax.custom_vjp
def low(v):
    return lax.optimization_barrier(v.astype(jnp.bfloat16)).astype(jnp.float32)

@jax.custom_vjp
def low_back(v):
    return v

def low_keep(v):
    return (low(v), None)

def low_pass(kept, grad):
    return (grad,)

def back_keep(v):
    return (v, None)

def back_low(kept, grad):
    return (low(grad),)
low.defvjp(low_keep, low_pass)
low_back.defvjp(back_keep, back_low)

def param_layout():
    return [('w_qkv', (D, 3 * D)), ('b_qv', (2 * D,)), ('w_out', (D, D)), ('b_out', (D,)), ('gain_one', (D,)), ('bias_one', (D,)), ('w_up', (D, FF)), ('b_up', (FF,)), ('w_down', (FF, D)), ('b_down', (D,)), ('gain_two', (D,)), ('bias_two', (D,)), ('pos_table', (LONG_SEGS, D)), ('x_qkv', (D, 3 * D)), ('x_bqv', (2 * D,)), ('x_out', (D, D)), ('x_bout', (D,)), ('gain_three', (D,)), ('bias_three', (D,)), ('x_up', (D, FF)), ('x_bup', (FF,)), ('x_down', (FF, D)), ('x_bdown', (D,)), ('gain_four', (D,)), ('bias_four', (D,))]

def unpack(flat_vec):
    params = {}
    offset = 0
    for entry_name, entry_shape in param_layout():
        length = math.prod(entry_shape)
        params[entry_name] = flat_vec[offset:offset + length].reshape(entry_shape)
        offset += length
    return params

def entry_rate(entry_name):
    if entry_name in ('w_qkv', 'w_out', 'w_up', 'x_qkv', 'x_out', 'x_up'):
        return 0.5 / math.sqrt(D)
    if entry_name in ('w_down', 'x_down'):
        return 0.5 / math.sqrt(FF)
    if entry_name == 'pos_table':
        return 1.0
    return 0.2

def entry_cross(entry_name):
    return entry_name[:2] == 'x_' or entry_name in ('pos_table', 'gain_three', 'bias_three', 'gain_four', 'bias_four')

def step_tables(flat_index, n_tokens, n_cls):
    scaling = jnp.zeros(flat_index.shape, jnp.float32)
    rating = jnp.full(flat_index.shape, 0.2, jnp.float32)
    offset = 0
    for entry_name, entry_shape in param_layout():
        length = math.prod(entry_shape)
        inside = (flat_index >= offset) & (flat_index < offset + length)
        row_count = n_cls if entry_cross(entry_name) else n_tokens
        scaling = jnp.where(inside, 1.0 / math.sqrt(row_count), scaling)
        rating = jnp.where(inside, entry_rate(entry_name), rating)
        offset += length
    return (scaling, rating)

def optimizer_step(gradient, master, momentum, average, scaling, rating):
    scaled = gradient * scaling
    moment = 0.5 * momentum + scaled
    weight = master - rating * (scaled + 0.5 * moment)
    smooth = 0.5 * average + 0.5 * weight
    return (weight, moment, smooth, weight.astype(jnp.bfloat16))

def layer_norm(values, gain_vec, shift_vec):
    center = values - lax.optimization_barrier(jnp.mean(values, axis=-1, keepdims=True))
    spread = lax.optimization_barrier(jnp.mean(center * center, axis=-1, keepdims=True))
    return center * lax.rsqrt(spread + EPSILON) * gain_vec + shift_vec

def full_bias(bias_pair):
    return jnp.concatenate([bias_pair[:D], jnp.zeros((D,), bias_pair.dtype), bias_pair[D:]])

def attention(packed, n_blocks, length, key_mask):
    packed = low(low_back(packed))
    head_shape = (n_blocks, length, HEADS, HEAD_DIM)
    queries = packed[:, :D].reshape(head_shape)
    key_rows = packed[:, D:2 * D].reshape(head_shape)
    values = packed[:, 2 * D:].reshape(head_shape)
    scores = low_back(jnp.einsum('bqhd,bkhd->bhqk', queries, key_rows, precision=HIGHEST) * HEAD_DIM ** (-0.5))
    scores = jnp.where(key_mask[:, None, None, :], scores, NEGATIVE)
    weights = low(jax.nn.softmax(scores, axis=-1))
    blended = jnp.einsum('bhqk,bkhd->bqhd', weights, values, precision=HIGHEST)
    return low(low_back(blended.reshape(n_blocks * length, D)))

def feed_forward(hidden, w_up, b_up, w_down, b_down):
    upward = low_back(jnp.dot(low(hidden), w_up, precision=HIGHEST) + b_up)
    activated = low(jax.nn.gelu(upward, approximate=False))
    return low_back(jnp.dot(activated, w_down, precision=HIGHEST) + b_down)

def segment_layer(params, inputs, seg_count):
    packed = jnp.dot(inputs, params['w_qkv'], precision=HIGHEST) + full_bias(params['b_qv'])
    blended = attention(packed, seg_count, SEG_LEN, jnp.ones((seg_count, SEG_LEN), jnp.bool_))
    branch = low_back(jnp.dot(blended, params['w_out'], precision=HIGHEST) + params['b_out'])
    hidden_one = layer_norm(inputs + branch, params['gain_one'], params['bias_one'])
    downward = feed_forward(hidden_one, params['w_up'], params['b_up'], params['w_down'], params['b_down'])
    return layer_norm(hidden_one + downward, params['gain_two'], params['bias_two'])

def cross_layer(params, doc_rows, key_mask):
    packed = jnp.dot(doc_rows, params['x_qkv'], precision=HIGHEST) + full_bias(params['x_bqv'])
    blended = attention(packed, N_SEG, LONG_SEGS, key_mask)
    branch = low_back(jnp.dot(blended, params['x_out'], precision=HIGHEST) + params['x_bout'])
    hidden_three = layer_norm(doc_rows + branch, params['gain_three'], params['bias_three'])
    downward = feed_forward(hidden_three, params['x_up'], params['x_bup'], params['x_down'], params['x_bdown'])
    return low(layer_norm(hidden_three + downward, params['gain_four'], params['bias_four']))

def group_forward(flat_vec, group_tokens, group_doc, group_pos):
    params = unpack(flat_vec)
    inputs = group_tokens.reshape(SEGS_G * SEG_LEN, D)
    hidden_two = segment_layer(params, inputs, SEGS_G).reshape(SEGS_G, SEG_LEN, D)
    pos_hot = (group_pos[:, None] == jnp.arange(LONG_SEGS)[None, :]).astype(jnp.float32)
    cls_rows = low(low_back(hidden_two[:, 0] + jnp.dot(pos_hot, params['pos_table'], precision=HIGHEST)))
    target = group_doc * LONG_SEGS + group_pos
    placement = (jnp.arange(N_SEG * LONG_SEGS)[:, None] == target[None, :]).astype(jnp.float32)
    doc_rows = jnp.dot(placement, cls_rows, precision=HIGHEST)
    key_mask = (lax.optimization_barrier(jnp.sum(placement, axis=1)) > 0).reshape(N_SEG, LONG_SEGS)
    crossed = cross_layer(params, doc_rows, key_mask)
    returned = jnp.dot(placement.T, crossed, precision=HIGHEST)
    return jnp.concatenate([returned[:, None, :], hidden_two[:, 1:, :]], axis=1)

def reference(tokens, cotangent, seg_doc, seg_pos, master, momentum, average):
    flat_low = low(master)

    def one_group(running, group_items):
        group_tokens, group_cot, group_doc, group_pos = group_items

        def forward(weights, inputs):
            return group_forward(weights, inputs, group_doc, group_pos)
        output, pullback = jax.vjp(forward, flat_low, group_tokens.astype(jnp.float32))
        grad_flat, grad_tokens = pullback(group_cot.astype(jnp.float32))
        return (running + grad_flat, (output.astype(jnp.bfloat16), grad_tokens.astype(jnp.bfloat16)))
    gradient, (mixed_out, token_grad) = lax.scan(one_group, jnp.zeros((P_PAD,), jnp.float32), (tokens, cotangent, seg_doc, seg_pos))
    flat_index = jnp.arange(P_PAD).astype(jnp.int32)
    scaling, rating = step_tables(flat_index, GRPS * SEGS_G * SEG_LEN, GRPS * SEGS_G)
    weight, moment, smooth, copy_low = optimizer_step(gradient, master, momentum, average, scaling, rating)
    return (mixed_out, token_grad, weight, moment, smooth, copy_low)
```

```python
import math

import jax
import jax.numpy as jnp
import numpy as np
from jax import lax
from jax.experimental import pallas as pl
from jax.experimental.pallas import tpu as pltpu
from jax.sharding import PartitionSpec as P

D = 768
HEADS = 12
HEAD_DIM = 64
FF = 3072
SEG_LEN = 128
LONG_SEGS = 64


EPSILON = 1e-05
NEGATIVE = -1e30


def param_layout():
    return [
        ("w_qkv", (D, 3 * D)),
        ("b_qv", (2 * D,)),
        ("w_out", (D, D)),
        ("b_out", (D,)),
        ("gain_one", (D,)),
        ("bias_one", (D,)),
        ("w_up", (D, FF)),
        ("b_up", (FF,)),
        ("w_down", (FF, D)),
        ("b_down", (D,)),
        ("gain_two", (D,)),
        ("bias_two", (D,)),
        ("pos_table", (LONG_SEGS, D)),
        ("x_qkv", (D, 3 * D)),
        ("x_bqv", (2 * D,)),
        ("x_out", (D, D)),
        ("x_bout", (D,)),
        ("gain_three", (D,)),
        ("bias_three", (D,)),
        ("x_up", (D, FF)),
        ("x_bup", (FF,)),
        ("x_down", (FF, D)),
        ("x_bdown", (D,)),
        ("gain_four", (D,)),
        ("bias_four", (D,)),
    ]


def entry_rate(entry_name):
    if entry_name in ("w_qkv", "w_out", "w_up", "x_qkv", "x_out", "x_up"):
        return 0.5 / math.sqrt(D)
    if entry_name in ("w_down", "x_down"):
        return 0.5 / math.sqrt(FF)
    if entry_name == "pos_table":
        return 1.0
    return 0.2


def entry_cross(entry_name):
    return entry_name[:2] == "x_" or entry_name in (
        "pos_table",
        "gain_three",
        "bias_three",
        "gain_four",
        "bias_four",
    )


LANES = 128
BLK = 16


def ceil_to(value, step):
    return -(-value // step) * step


def item_list(total_rows):
    groups = [
        ["w_qkv"],
        ["b_qv"],
        ["w_out"],
        ["b_out", "gain_one", "bias_one"],
        ["w_up"],
        ["b_up"],
        ["w_down"],
        ["b_down", "gain_two", "bias_two"],
        ["pos_table"],
        ["x_qkv"],
        ["x_bqv"],
        ["x_out"],
        ["x_bout", "gain_three", "bias_three"],
        ["x_up"],
        ["x_bup"],
        ["x_down"],
        ["x_bdown", "gain_four", "bias_four"],
    ]
    shapes = dict(param_layout())
    items = []
    nat = 0
    blk = 0
    for names in groups:
        rows = sum(math.prod(shapes[name]) for name in names) // LANES
        items.append(dict(name=names[0], names=names, nat=nat, rows=rows, blk=blk))
        nat += rows
        blk += ceil_to(rows, BLK) // BLK
    items.append(dict(name="tail", names=[], nat=nat, rows=total_rows - nat, blk=blk))
    return items


class Geometry:
    def __init__(self, n_seg, n_doc, shard_len):
        self.n_seg, self.n_doc = n_seg, n_doc
        self.n_dev = n_seg * n_doc
        self.chunk = shard_len // LANES
        self.items = item_list(self.chunk * self.n_dev)
        self.by_name = {item["name"]: item for item in self.items}
        firsts, lasts = [], []
        for n in range(self.n_dev):
            lo, hi = n * self.chunk, (n + 1) * self.chunk
            blocks = []
            for item in self.items:
                a, b = max(lo, item["nat"]), min(hi, item["nat"] + item["rows"])
                if a < b:
                    blocks.append(item["blk"] + (a - item["nat"]) // BLK)
                    blocks.append(item["blk"] + (b - 1 - item["nat"]) // BLK)
            firsts.append(min(blocks))
            lasts.append(max(blocks))
        self.first, self.last = firsts, lasts
        most = max(b - a + 1 for a, b in zip(firsts, lasts))
        self.piece_blocks = -(-most // self.n_dev)
        self.piece = self.piece_blocks * BLK
        self.slots = self.piece_blocks * self.n_dev
        self.c_size, self.x_size = 2, 2
        self.y_size = n_seg // 4

    def block_table(self):
        table = np.zeros((self.n_dev, self.slots, 3), np.int32)
        for n in range(self.n_dev):
            lo, hi = n * self.chunk, (n + 1) * self.chunk
            for t in range(self.slots):
                b = self.first[n] + t
                if b > self.last[n]:
                    continue
                item = [it for it in self.items if it["blk"] <= b][-1]
                start = item["nat"] + (b - item["blk"]) * BLK
                a = max(start, lo)
                z = min(start + BLK, hi, item["nat"] + item["rows"])
                if a < z:
                    table[n, t] = (start - lo, a - start, z - start)
        return table

    def chunks_of(self, item):
        found = []
        n_blocks = ceil_to(item["rows"], BLK) // BLK
        for n in range(self.n_dev):
            a = max(item["blk"], self.first[n])
            b = min(item["blk"] + n_blocks, self.last[n] + 1)
            if a < b:
                found.append((n, a - item["blk"], b - item["blk"], a - self.first[n]))
        return found

    def buckets(self):
        end_attention = self.by_name["w_out"]["nat"] + self.by_name["w_out"]["rows"]
        end_segment = self.by_name["pos_table"]["nat"]
        a = (end_attention - 1) // self.chunk + 1
        b = (end_segment - 1) // self.chunk + 1
        return [range(0, a), range(a, b), range(b, self.n_dev)]

    def coords(self, device):
        seg, doc = divmod(device, self.n_doc)
        yx, c = divmod(seg, self.c_size)
        y, x = divmod(yx, self.x_size)
        return dict(y=y, x=x, c=c, z=doc)

    def device(self, y, x, c, z):
        return ((y * self.x_size + x) * self.c_size + c) * self.n_doc + z

    def size(self, axis):
        return dict(y=self.y_size, x=self.x_size, c=self.c_size, z=self.n_doc)[axis]

    def shift(self, axis, step):
        pairs = []
        for source in range(self.n_dev):
            at = self.coords(source)
            at[axis] = (at[axis] + step) % self.size(axis)
            pairs.append((source, self.device(**at)))
        return pairs
def spec_vmem():
    return pl.BlockSpec(memory_space=pltpu.VMEM)


def spec_any():
    return pl.BlockSpec(memory_space=pl.ANY)


def spec_smem():
    return pl.BlockSpec(memory_space=pltpu.SMEM)


def kernel_params(mib=56):
    return pltpu.CompilerParams(vmem_limit_bytes=mib * 1024 * 1024)


def row_mask(low, high):
    rows = lax.broadcasted_iota(jnp.int32, (BLK, LANES), 0)
    return (rows >= low) & (rows < high)


def align_rows(geo, table, padded):
    def kernel(table_ref, rows_ref, out_ref):
        def body(t, carry):
            start, low, high = table_ref[t], table_ref[geo.slots + t], table_ref[2 * geo.slots + t]
            rows = rows_ref[pl.ds(start + BLK, BLK), :]
            rows = jnp.where(row_mask(low, high), rows, 0.0)
            out_ref[pl.ds(pl.multiple_of(t * BLK, BLK), BLK), :] = rows.astype(jnp.bfloat16)
            return carry

        lax.fori_loop(0, geo.slots, body, 0, unroll=4)

    return pl.pallas_call(
        kernel,
        out_shape=jax.ShapeDtypeStruct((geo.slots * BLK, LANES), jnp.bfloat16),
        in_specs=[spec_smem(), spec_vmem()],
        out_specs=spec_vmem(),
        compiler_params=kernel_params(),
    )(table, padded)


def natural_rows(geo, table, blocks, pad_rows):
    def kernel(table_ref, blocks_ref, out_ref):
        def body(t, carry):
            start, low, high = table_ref[t], table_ref[geo.slots + t], table_ref[2 * geo.slots + t]
            rows = blocks_ref[pl.ds(pl.multiple_of(t * BLK, BLK), BLK), :].astype(jnp.float32)
            here = pl.ds(start + BLK, BLK)
            out_ref[here, :] = jnp.where(row_mask(low, high), rows, out_ref[here, :])
            return carry

        lax.fori_loop(0, geo.slots, body, 0)

    return pl.pallas_call(
        kernel,
        out_shape=jax.ShapeDtypeStruct((pad_rows, LANES), jnp.float32),
        in_specs=[spec_smem(), spec_vmem()],
        out_specs=spec_vmem(),
        compiler_params=kernel_params(),
    )(table, blocks)


class Buckets:
    def __init__(self, geo):
        self.geo = geo
        self.ranges = geo.buckets()
        self.half = [(len(r) + 1) // 2 for r in self.ranges]

    def find(self, chunk):
        for number, span in enumerate(self.ranges):
            if chunk in span:
                at = chunk - span.start
                cut = self.half[number]
                return (number, 0, at) if at < cut else (number, 1, at - cut)

    def shapes(self, number):
        geo = self.geo
        cut = self.half[number]
        rest = len(self.ranges[number]) - cut
        rows = geo.n_doc * geo.piece
        return [
            (geo.y_size, geo.x_size, cut, rows, LANES),
            (geo.x_size, geo.y_size, rest, rows, LANES),
        ]


def wrap(value, size):
    return lax.rem(value + size, size)


def copy_rows(count, step, body):
    full = count // step
    if full:
        def loop(i, carry):
            body(i * step, step)
            return carry

        lax.fori_loop(0, full, loop, 0)
    if count % step:
        body(full * step, count % step)


def unpack_matrix(geo, buckets, gathered, coords, name, depth, cols):
    item = geo.by_name[name]
    chunks = geo.chunks_of(item)
    used = sorted({buckets.find(n)[0] for n, *_ in chunks})
    operands = [array for number in used for array in gathered[number]]
    wide_cols = cols // LANES
    seg_rows = geo.n_doc * geo.piece

    def kernel(coords_ref, *refs):
        sources, (out_ref, staged, wide, sem) = refs[: len(operands)], refs[len(operands) :]
        my_y, my_x, my_c = coords_ref[0], coords_ref[1], coords_ref[2]
        for at, (n, _, _, _) in enumerate(chunks):
            number, half, place = buckets.find(n)
            for core in range(2):
                source = sources[4 * used.index(number) + 2 * half + core]
                c = my_c if core == 0 else 1 - my_c
                for ry in range(geo.y_size):
                    for rx in range(geo.x_size):
                        y = wrap(my_y - ry, geo.y_size)
                        x = wrap(my_x - rx, geo.x_size)
                        s = (y * geo.x_size + x) * 2 + c
                        index = (ry, rx, place) if half == 0 else (rx, ry, place)
                        pltpu.make_async_copy(
                            source.at[index],
                            staged.at[at, pl.ds(pl.multiple_of(s * seg_rows, BLK), seg_rows)],
                            sem,
                        ).start()
        pltpu.make_async_copy(staged, staged, sem).wait()
        done = 0
        for at, (n, b0, b1, slot) in enumerate(chunks):
            if b0 < done:
                here = pl.ds(b0 * BLK, BLK)
                extra = staged[at, pl.ds(slot * BLK, BLK), :].astype(jnp.float32)
                wide[here, :] = wide[here, :] + extra
                b0, slot = b0 + 1, slot + 1

            def widen(row, rows, at=at, b0=b0, slot=slot):
                src = pl.ds(pl.multiple_of(slot * BLK + row, BLK), rows)
                dst = pl.ds(pl.multiple_of(b0 * BLK + row, BLK), rows)
                wide[dst, :] = staged[at, src, :].astype(jnp.float32)

            copy_rows((b1 - b0) * BLK, 128, widen)
            done = b1

        def turn(kb, carry):
            rows = pl.ds(pl.multiple_of(kb * BLK, BLK), BLK)
            for cb in range(wide_cols):
                tile = wide[pl.ds(kb * BLK * wide_cols + cb, BLK, stride=wide_cols), :]
                out_ref[rows, cb * LANES : (cb + 1) * LANES] = tile.astype(jnp.bfloat16)
            return carry

        lax.fori_loop(0, depth // BLK, turn, 0)

    return pl.pallas_call(
        kernel,
        out_shape=jax.ShapeDtypeStruct((depth, cols), jnp.bfloat16),
        in_specs=[spec_smem()] + [spec_any()] * len(operands),
        out_specs=spec_vmem(),
        scratch_shapes=[
            pltpu.VMEM((len(chunks), geo.slots * BLK, LANES), jnp.bfloat16),
            pltpu.VMEM((item["rows"], LANES), jnp.float32),
            pltpu.SemaphoreType.DMA,
        ],
        compiler_params=kernel_params(),
    )(coords, *operands)


def unpack_vectors(geo, buckets, gathered, coords, names):
    blocks = []
    places = {}
    for name in names:
        item = geo.by_name[name]
        places[name] = len(blocks) * BLK
        for b in range(ceil_to(item["rows"], BLK) // BLK):
            found = []
            for n in range(geo.n_dev):
                if geo.first[n] <= item["blk"] + b <= geo.last[n]:
                    found.append((n, item["blk"] + b - geo.first[n]))
            blocks.append(found)
    used = sorted({buckets.find(n)[0] for found in blocks for n, _ in found})
    operands = [array for number in used for array in gathered[number]]
    copies = [(b, which, n, slot) for b, found in enumerate(blocks) for which, (n, slot) in enumerate(found)]

    def kernel(coords_ref, *refs):
        sources, (out_ref, staged, sem) = refs[: len(operands)], refs[len(operands) :]
        my_y, my_x, my_c = coords_ref[0], coords_ref[1], coords_ref[2]
        for at, (b, which, n, slot) in enumerate(copies):
            number, half, place = buckets.find(n)
            where = geo.coords(slot // geo.piece_blocks)
            row = where["z"] * geo.piece + slot % geo.piece_blocks * BLK
            ry, rx = wrap(my_y - where["y"], geo.y_size), wrap(my_x - where["x"], geo.x_size)
            index = (ry, rx) if half == 0 else (rx, ry)
            for core in range(2):
                source = sources[4 * used.index(number) + 2 * half + core]

                @pl.when(my_c == (where["c"] if core == 0 else 1 - where["c"]))
                def _(source=source, at=at, index=index, place=place, row=row):
                    pltpu.make_async_copy(
                        source.at[index[0], index[1], place, pl.ds(row, BLK)], staged.at[at], sem
                    ).start()

        pltpu.make_async_copy(staged, staged, sem).wait()
        for at, (b, which, n, slot) in enumerate(copies):
            rows = staged[at].astype(jnp.float32)
            here = pl.ds(b * BLK, BLK)
            out_ref[here, :] = rows if which == 0 else out_ref[here, :] + rows

    out = pl.pallas_call(
        kernel,
        out_shape=jax.ShapeDtypeStruct((len(blocks) * BLK, LANES), jnp.float32),
        in_specs=[spec_smem()] + [spec_any()] * len(operands),
        out_specs=spec_vmem(),
        scratch_shapes=[
            pltpu.VMEM((len(copies), BLK, LANES), jnp.bfloat16),
            pltpu.SemaphoreType.DMA,
        ],
        compiler_params=kernel_params(),
    )(coords, *operands)
    values = {}
    shapes = dict(param_layout())
    for name in names:
        row = places[name]
        for entry in geo.by_name[name]["names"]:
            rows = math.prod(shapes[entry]) // LANES
            values[entry] = out[row : row + rows].reshape(shapes[entry])
            row += rows
    return values


def pack_bucket(geo, buckets, number, grads, coords):
    span = buckets.ranges[number]
    shapes = dict(param_layout())
    seg_rows = geo.n_doc * geo.piece
    parts = []
    for item in geo.items:
        chunks = [entry for entry in geo.chunks_of(item) if entry[0] in span]
        if chunks and item["names"]:
            parts.append((item, chunks))
    operands, windows, scratch = [], [], []
    wide_rows = BLK
    for item, chunks in parts:
        shape = shapes[item["names"][0]]
        if len(item["names"]) == 1 and len(shape) == 2 and item["name"] != "pos_table":
            cols = shape[1] // LANES
            k0 = min(b0 for _, b0, _, _ in chunks) // cols
            k1 = -(-max(b1 for _, _, b1, _ in chunks) // cols)
            operands.append(grads[item["name"]])
            windows.append((cols, k0, k1))
            scratch.append(pltpu.VMEM(((k1 - k0) * BLK, shape[1]), jnp.bfloat16))
            wide_rows = max(wide_rows, (k1 - k0) * BLK * cols)
        else:
            rows = jnp.concatenate([grads[n].reshape(-1, LANES) for n in item["names"]])
            rows = jnp.pad(rows, ((0, ceil_to(item["rows"], BLK) - item["rows"]), (0, 0)))
            operands.append(rows.astype(jnp.bfloat16))
            windows.append(None)
            scratch.append(pltpu.VMEM(rows.shape, jnp.bfloat16))
    outs = [shape for shape in buckets.shapes(number) for _ in range(2)]

    def kernel(coords_ref, *refs):
        sources = refs[: len(parts)]
        targets = refs[len(parts) : len(parts) + 4]
        loaded = refs[len(parts) + 4 : 2 * len(parts) + 4]
        staged, wide, in_sems, out_sem = refs[2 * len(parts) + 4 :]
        my_y, my_x, my_c = coords_ref[0], coords_ref[1], coords_ref[2]
        loads = []
        for at, window in enumerate(windows):
            source = sources[at]
            if window is not None:
                source = source.at[pl.ds(window[1] * BLK, (window[2] - window[1]) * BLK)]
            loads.append(pltpu.make_async_copy(source, loaded[at], in_sems.at[at]))
            loads[-1].start()

        def clear(row, rows):
            for at in range(len(span)):
                here = pl.ds(pl.multiple_of(row, BLK), rows)
                staged[at, here, :] = jnp.zeros((rows, LANES), jnp.bfloat16)

        copy_rows(geo.slots * BLK, 128, clear)
        for at, ((item, chunks), window) in enumerate(zip(parts, windows)):
            loads[at].wait()
            values = loaded[at]
            base = 0
            if window is not None:
                cols, k0, k1 = window
                base = k0 * cols

                def turn(kb, carry, values=values, cols=cols):
                    rows = pl.ds(pl.multiple_of(kb * BLK, BLK), BLK)
                    for cb in range(cols):
                        tile = values[rows, cb * LANES : (cb + 1) * LANES].astype(jnp.float32)
                        wide[pl.ds(kb * BLK * cols + cb, BLK, stride=cols), :] = tile
                    return carry

                lax.fori_loop(0, k1 - k0, turn, 0)
            for n, b0, b1, slot in chunks:
                def narrow(row, rows, n=n, b0=b0, slot=slot, values=values, window=window, base=base):
                    src = pl.ds(pl.multiple_of((b0 - base) * BLK + row, BLK), rows)
                    dst = pl.ds(pl.multiple_of(slot * BLK + row, BLK), rows)
                    data = values[src, :] if window is None else wide[src, :].astype(jnp.bfloat16)
                    staged[n - span.start, dst, :] = data

                copy_rows((b1 - b0) * BLK, 128, narrow)
        copies = []
        for n in span:
            _, half, place = buckets.find(n)
            for core in range(2):
                c = my_c if core == 0 else 1 - my_c
                for ry in range(geo.y_size):
                    for rx in range(geo.x_size):
                        y = wrap(my_y + ry, geo.y_size)
                        x = wrap(my_x + rx, geo.x_size)
                        s = (y * geo.x_size + x) * 2 + c
                        index = (ry, rx, place) if half == 0 else (rx, ry, place)
                        pltpu.make_async_copy(
                            staged.at[n - span.start, pl.ds(pl.multiple_of(s * seg_rows, BLK), seg_rows)],
                            targets[2 * half + core].at[index],
                            out_sem,
                        ).start()
        pltpu.make_async_copy(staged, staged, out_sem).wait()

    return pl.pallas_call(
        kernel,
        out_shape=[jax.ShapeDtypeStruct(shape, jnp.bfloat16) for shape in outs],
        in_specs=[spec_smem()] + [spec_any()] * len(operands),
        out_specs=[spec_any()] * 4,
        scratch_shapes=scratch
        + [
            pltpu.VMEM((len(span), geo.slots * BLK, LANES), jnp.bfloat16),
            pltpu.VMEM((wide_rows, LANES), jnp.float32),
            pltpu.SemaphoreType.DMA((len(parts),)),
            pltpu.SemaphoreType.DMA,
        ],
        compiler_params=kernel_params(),
    )(coords, *operands)


AXES = ("seg", "doc")


def send(geo, value, axis, step):
    return lax.ppermute(value, AXES, geo.shift(axis, step))


def gather_axis(geo, value, axis):
    parts = [value] + [send(geo, value, axis, r) for r in range(1, geo.size(axis))]
    return jnp.stack(parts)


def gather_bucket(geo, pieces, my_z, cut):
    nd = geo.n_doc
    parts = [pieces] + [send(geo, pieces, "z", r) for r in range(1, nd)]
    parts = parts[::-1]
    line = jnp.stack(parts + parts[: nd - 1], axis=1)
    line = lax.dynamic_slice_in_dim(line, nd - 1 - my_z, nd, axis=1)
    line = line.reshape(pieces.shape[0], nd * geo.piece, LANES)
    result = []
    for part, order in ((line[:cut], ("x", "y")), (line[cut:], ("y", "x"))):
        for axis in order:
            part = gather_axis(geo, part, axis)
        result += [part, send(geo, part, "c", 1)]
    return result


def plus(*terms):
    return sum(term.astype(jnp.float32) for term in terms)


def reduce_axis(geo, value, axis):
    parts = [value[0]] + [send(geo, value[r], axis, r) for r in range(1, geo.size(axis))]
    return plus(*parts).astype(jnp.bfloat16)


def reduce_bucket(geo, arrays, my_z):
    nd = geo.n_doc
    lines = []
    for half, order in ((0, ("y", "x")), (1, ("x", "y"))):
        keep, give = arrays[2 * half], arrays[2 * half + 1]
        part = plus(keep, send(geo, give, "c", 1)).astype(jnp.bfloat16)
        for axis in order:
            part = reduce_axis(geo, part, axis)
        lines.append(part)
    line = jnp.concatenate(lines)
    line = line.reshape(line.shape[0], nd, geo.piece, LANES)

    def to(r):
        return lax.dynamic_index_in_dim(line, lax.rem(my_z + r, nd), axis=1, keepdims=False)

    return plus(to(0), *[send(geo, to(r), "z", r) for r in range(1, nd)]).astype(jnp.bfloat16)
def optimizer_step(gradient, master, momentum, average, scaling, rating):
    scaled = gradient * scaling
    moment = 0.5 * momentum + scaled
    weight = master - rating * (scaled + 0.5 * moment)
    smooth = 0.5 * average + 0.5 * weight
    return (weight, moment, smooth, weight.astype(jnp.bfloat16))


def row_rates(geo, n_tokens, n_cls):
    total = geo.chunk * geo.n_dev
    scaling = np.zeros((total,), np.float32)
    rating = np.full((total,), 0.2, np.float32)
    row = 0
    for entry_name, entry_shape in param_layout():
        rows = math.prod(entry_shape) // LANES
        count = n_cls if entry_cross(entry_name) else n_tokens
        scaling[row : row + rows] = 1.0 / math.sqrt(count)
        rating[row : row + rows] = entry_rate(entry_name)
        row += rows
    return scaling.reshape(geo.n_dev, geo.chunk), rating.reshape(geo.n_dev, geo.chunk)


def norm_forward(values, gain_vec, shift_vec):
    center = values - jnp.mean(values, axis=-1, keepdims=True)
    rate = lax.rsqrt(jnp.mean(center * center, axis=-1, keepdims=True) + EPSILON)
    normal = center * rate
    return normal * gain_vec + shift_vec, normal, rate


def norm_backward(grad, normal, rate, gain_vec):
    scaled = grad * gain_vec
    return rate * (
        scaled
        - jnp.mean(scaled, axis=-1, keepdims=True)
        - normal * jnp.mean(scaled * normal, axis=-1, keepdims=True)
    )


def full_bias(bias_pair):
    return jnp.concatenate([bias_pair[:D], jnp.zeros((D,), jnp.float32), bias_pair[D:]])


def column_sum(rows):
    return jnp.sum(rows.astype(jnp.float32), axis=0)


def pair_grad(grad_packed):
    summed = column_sum(grad_packed)
    return jnp.concatenate([summed[:D], summed[2 * D :]])


def matmul(left, right):
    return jnp.dot(left, right, preferred_element_type=jnp.float32)


def exact_gelu(values):
    return jax.nn.gelu(values, approximate=False)


def head_scores(packed, n_blocks, length, mask):
    head_shape = (n_blocks, length, HEADS, HEAD_DIM)
    queries = packed[:, :D].reshape(head_shape)
    key_rows = packed[:, D : 2 * D].reshape(head_shape)
    values = packed[:, 2 * D :].reshape(head_shape)
    scores = jnp.einsum(
        "bqhd,bkhd->bhqk", queries, key_rows, preferred_element_type=jnp.float32
    ) * HEAD_DIM ** (-0.5)
    if mask is not None:
        scores = jnp.where(mask[None, None], scores, NEGATIVE)
    return (scores, queries, key_rows, values)


def attend_forward(packed, n_blocks, length, mask):
    scores, queries, key_rows, values = head_scores(packed, n_blocks, length, mask)
    largest = jnp.max(scores, axis=-1, keepdims=True)
    raised = jnp.exp(scores - largest)
    summed = jnp.sum(raised, axis=-1, keepdims=True)
    weights = (raised / summed).astype(jnp.bfloat16)
    blended = jnp.einsum("bhqk,bkhd->bqhd", weights, values, preferred_element_type=jnp.float32)
    return (blended.reshape(n_blocks * length, D).astype(jnp.bfloat16), largest + jnp.log(summed))


def attend_backward(packed, log_sum, mask, grad_out, n_blocks, length):
    scores, queries, key_rows, values = head_scores(packed, n_blocks, length, mask)
    weights = jnp.exp(scores - log_sum)
    grad_heads = grad_out.reshape(n_blocks, length, HEADS, HEAD_DIM)
    grad_weights = jnp.einsum(
        "bqhd,bkhd->bhqk", grad_heads, values, preferred_element_type=jnp.float32
    )
    grad_values = jnp.einsum(
        "bhqk,bqhd->bkhd",
        weights.astype(jnp.bfloat16),
        grad_heads,
        preferred_element_type=jnp.float32,
    )
    inner = jnp.sum(grad_weights * weights, axis=-1, keepdims=True)
    grad_scores = (weights * (grad_weights - inner)).astype(jnp.bfloat16)
    grad_queries = jnp.einsum(
        "bhqk,bkhd->bqhd", grad_scores, key_rows, preferred_element_type=jnp.float32
    ) * HEAD_DIM ** (-0.5)
    grad_keys = jnp.einsum(
        "bhqk,bqhd->bkhd", grad_scores, queries, preferred_element_type=jnp.float32
    ) * HEAD_DIM ** (-0.5)
    flat_shape = (n_blocks * length, D)
    joined = jnp.concatenate(
        [
            grad_queries.reshape(flat_shape),
            grad_keys.reshape(flat_shape),
            grad_values.reshape(flat_shape),
        ],
        axis=1,
    )
    return joined.astype(jnp.bfloat16)


def low(values):
    return values.astype(jnp.bfloat16)


def local(tokens, cotangent, seg_doc, seg_pos, master, momentum, average):
    n_seg = lax.axis_size("seg")
    n_doc = lax.axis_size("doc")
    geo = Geometry(n_seg, n_doc, master.shape[0])
    buckets = Buckets(geo)
    my_seg, my_doc = lax.axis_index("seg"), lax.axis_index("doc")
    me = my_seg * n_doc + my_doc
    coords = jnp.stack(
        [my_seg // 4, my_seg // 2 % 2, my_seg % 2, my_doc]
    ).astype(jnp.int32)
    table = lax.dynamic_index_in_dim(
        jnp.asarray(geo.block_table().transpose(0, 2, 1).reshape(geo.n_dev, -1)), me, 0, False
    )
    pad_rows = ceil_to(geo.chunk + 2 * BLK, 8)
    padded = jnp.pad(
        master.reshape(geo.chunk, LANES), ((BLK, pad_rows - geo.chunk - BLK), (0, 0))
    )
    aligned = align_rows(geo, table, padded)
    pieces = lax.all_to_all(
        aligned.reshape(geo.n_dev, geo.piece, LANES), AXES, 0, 0, tiled=True
    )
    gathered = [
        gather_bucket(geo, pieces[span.start : span.stop], my_doc, cut)
        for span, cut in zip(buckets.ranges, buckets.half)
    ]

    def matrix(name):
        depth, cols = dict(param_layout())[name]
        return unpack_matrix(geo, buckets, gathered, coords, name, depth, cols)

    vec = unpack_vectors(geo, buckets, gathered, coords, ["b_qv", "b_out", "b_up", "b_down"])

    seg_count = tokens.shape[1]
    cot_rows = cotangent[0]
    tagged = jnp.concatenate(
        [cot_rows[:, 0], jnp.broadcast_to(low(seg_doc[0].astype(jnp.float32))[:, None], (seg_count, LANES))],
        axis=1,
    )
    all_tagged = lax.all_gather(tagged, "seg", axis=0, tiled=True)
    all_grad, all_doc = all_tagged[:, :D], all_tagged[:, D].astype(jnp.float32)
    same_doc = all_doc[:, None] == all_doc[None, :]

    inputs = tokens[0].reshape(seg_count * SEG_LEN, D)
    w_qkv, w_out = matrix("w_qkv"), matrix("w_out")
    packed = low(matmul(inputs, w_qkv) + full_bias(vec["b_qv"]))
    attended, log_sum = attend_forward(packed, seg_count, SEG_LEN, None)
    resid_one = inputs.astype(jnp.float32) + matmul(attended, w_out) + vec["b_out"]
    hidden_one, normal_one, rate_one = norm_forward(resid_one, vec["gain_one"], vec["bias_one"])
    hidden_low = low(hidden_one)
    w_up, w_down = matrix("w_up"), matrix("w_down")
    upward = matmul(hidden_low, w_up) + vec["b_up"]
    activated, gelu_pull = jax.vjp(exact_gelu, upward)
    active_low = low(activated)
    resid_two = hidden_one + matmul(active_low, w_down) + vec["b_down"]
    hidden_two, normal_two, rate_two = norm_forward(resid_two, vec["gain_two"], vec["bias_two"])
    hidden_two = hidden_two.reshape(seg_count, SEG_LEN, D)

    xvec = unpack_vectors(
        geo, buckets, gathered, coords, ["pos_table", "x_bqv", "x_bout", "x_bup", "x_bdown"]
    )
    vec.update(xvec)
    x_qkv, x_out, x_up, x_down = matrix("x_qkv"), matrix("x_out"), matrix("x_up"), matrix("x_down")
    places = seg_pos[0]
    pos_hot = (places[:, None] == jnp.arange(LONG_SEGS)[None, :]).astype(jnp.bfloat16)
    cls_low = low(hidden_two[:, 0] + matmul(pos_hot, low(vec["pos_table"])))
    rows = lax.all_gather(cls_low, "seg", axis=0, tiled=True)
    n_rows = rows.shape[0]

    def own(values):
        return lax.dynamic_slice_in_dim(values, my_seg * seg_count, seg_count, axis=0)

    x_packed = low(matmul(rows, x_qkv) + full_bias(vec["x_bqv"]))
    x_att, x_lse = attend_forward(x_packed, 1, n_rows, same_doc)
    resid_three = rows.astype(jnp.float32) + matmul(x_att, x_out) + vec["x_bout"]
    hidden_three, normal_three, rate_three = norm_forward(
        resid_three, vec["gain_three"], vec["bias_three"]
    )
    hidden_three_low = low(hidden_three)
    x_upward = matmul(hidden_three_low, x_up) + vec["x_bup"]
    x_act, x_gelu_pull = jax.vjp(exact_gelu, x_upward)
    x_act_low = low(x_act)
    resid_four = hidden_three + matmul(x_act_low, x_down) + vec["x_bdown"]
    crossed, normal_four, rate_four = norm_forward(resid_four, vec["gain_four"], vec["bias_four"])
    mixed_out = jnp.concatenate(
        [own(low(crossed))[:, None, :], low(hidden_two[:, 1:, :])], axis=1
    )

    grads = {}
    grad_z = all_grad.astype(jnp.float32)
    grads["gain_four"] = column_sum(own(grad_z * normal_four))
    grads["bias_four"] = column_sum(own(grad_z))
    grad_four = norm_backward(grad_z, normal_four, rate_four, vec["gain_four"])
    grad_xm = low(grad_four)
    grads["x_down"] = low(matmul(own(x_act_low).T, own(grad_xm)))
    grads["x_bdown"] = column_sum(own(grad_xm))
    grad_xu = low(x_gelu_pull(matmul(grad_xm, x_down.T))[0])
    grads["x_up"] = low(matmul(own(hidden_three_low).T, own(grad_xu)))
    grads["x_bup"] = column_sum(own(grad_xu))
    grad_h3 = grad_four + matmul(grad_xu, x_up.T)
    grads["gain_three"] = column_sum(own(grad_h3 * normal_three))
    grads["bias_three"] = column_sum(own(grad_h3))
    grad_three = norm_backward(grad_h3, normal_three, rate_three, vec["gain_three"])
    grad_xa_out = low(grad_three)
    grads["x_out"] = low(matmul(own(x_att).T, own(grad_xa_out)))
    grads["x_bout"] = column_sum(own(grad_xa_out))
    grad_xa = low(matmul(grad_xa_out, x_out.T))
    grad_xpacked = attend_backward(x_packed, x_lse, same_doc, grad_xa, 1, n_rows)
    grads["x_qkv"] = low(matmul(own(rows).T, own(grad_xpacked)))
    grads["x_bqv"] = pair_grad(own(grad_xpacked))
    grad_rows = own(low(grad_three + matmul(grad_xpacked, x_qkv.T)))
    grads["pos_table"] = matmul(pos_hot.T, grad_rows)
    zero_vec = {"b_down": D, "gain_two": D, "bias_two": D}

    grad_h2 = jnp.concatenate(
        [grad_rows[:, None, :].astype(jnp.float32), cot_rows[:, 1:, :].astype(jnp.float32)], axis=1
    ).reshape(-1, D)
    grads["gain_two"] = column_sum(grad_h2 * normal_two)
    grads["bias_two"] = column_sum(grad_h2)
    grad_two = norm_backward(grad_h2, normal_two, rate_two, vec["gain_two"])
    grad_m = low(grad_two)
    grads["w_down"] = low(matmul(active_low.T, grad_m))
    grads["b_down"] = column_sum(grad_m)

    cross_arrays = pack_bucket(geo, buckets, 2, grads, coords)
    cross_pieces = reduce_bucket(geo, cross_arrays, my_doc)

    grad_u = low(gelu_pull(matmul(grad_m, w_down.T))[0])
    grads["w_up"] = low(matmul(hidden_low.T, grad_u))
    grads["b_up"] = column_sum(grad_u)
    feed_arrays = pack_bucket(geo, buckets, 1, grads, coords)
    feed_pieces = reduce_bucket(geo, feed_arrays, my_doc)
    grad_h1 = grad_two + matmul(grad_u, w_up.T)
    grads["gain_one"] = column_sum(grad_h1 * normal_one)
    grads["bias_one"] = column_sum(grad_h1)
    grad_one = norm_backward(grad_h1, normal_one, rate_one, vec["gain_one"])
    grad_branch = low(grad_one)
    grads["w_out"] = low(matmul(attended.T, grad_branch))
    grads["b_out"] = column_sum(grad_branch)
    grad_att = low(matmul(grad_branch, w_out.T))
    grad_packed = attend_backward(packed, log_sum, None, grad_att, seg_count, SEG_LEN)
    grads["w_qkv"] = low(matmul(inputs.T, grad_packed))
    grads["b_qv"] = pair_grad(grad_packed)
    token_grad = low(grad_one + matmul(grad_packed, w_qkv.T))
    att_arrays = pack_bucket(geo, buckets, 0, grads, coords)
    att_pieces = reduce_bucket(geo, att_arrays, my_doc)

    all_pieces = jnp.concatenate([att_pieces, feed_pieces, cross_pieces])
    owned = lax.all_to_all(all_pieces, AXES, 0, 0, tiled=True)
    natural = natural_rows(geo, table, owned.reshape(-1, LANES), pad_rows)
    gradient = natural[BLK : BLK + geo.chunk].reshape(-1)
    n_cls = n_doc * n_seg * seg_count
    scaling, rating = (
        jnp.broadcast_to(
            lax.dynamic_index_in_dim(jnp.asarray(rates), me, 0, False)[:, None], (geo.chunk, LANES)
        ).reshape(-1)
        for rates in row_rates(geo, n_cls * SEG_LEN, n_cls)
    )
    weight, moment, smooth, copy_low = optimizer_step(
        gradient, master, momentum, average, scaling, rating
    )
    return (
        mixed_out.reshape(1, seg_count, SEG_LEN, D),
        token_grad.reshape(1, seg_count, SEG_LEN, D),
        weight,
        moment,
        smooth,
        copy_low,
    )


def solution(mesh):
    layer = P("doc", "seg", None, None)
    ids = P("doc", "seg")
    flat = P(("seg", "doc"))
    return jax.shard_map(
        local,
        mesh=mesh,
        in_specs=(layer, layer, ids, ids, flat, flat, flat),
        out_specs=(layer, layer, flat, flat, flat, flat),
        check_vma=False,
    )
```

```python
import math
from types import SimpleNamespace

import jax
import jax.numpy as jnp
import numpy as np
from jax import lax
from jax.experimental import pallas as pl
from jax.experimental.pallas import tpu as pltpu
from jax.sharding import PartitionSpec as P

D = 768
HEADS = 12
HEAD_DIM = 64
FF = 3072
SEG_LEN = 128
LONG_SEGS = 64
EPSILON = 1e-05
NEGATIVE = -1e30

LAYOUT = dict(
    w_qkv=(D, 3 * D),
    b_qv=(2 * D,),
    w_out=(D, D),
    b_out=(D,),
    gain_one=(D,),
    bias_one=(D,),
    w_up=(D, FF),
    b_up=(FF,),
    w_down=(FF, D),
    b_down=(D,),
    gain_two=(D,),
    bias_two=(D,),
    pos_table=(LONG_SEGS, D),
    x_qkv=(D, 3 * D),
    x_bqv=(2 * D,),
    x_out=(D, D),
    x_bout=(D,),
    gain_three=(D,),
    bias_three=(D,),
    x_up=(D, FF),
    x_bup=(FF,),
    x_down=(FF, D),
    x_bdown=(D,),
    gain_four=(D,),
    bias_four=(D,),
)
LANES = 128
BLK = 16
Y, X, C, Z = range(4)


def ceil_to(value, step):
    return -(-value // step) * step


def item_list(total_rows):
    items = []
    nat = 0
    for name, shape in LAYOUT.items():
        rows = math.prod(shape) // LANES
        if len(shape) == 1 and items and len(items[-1].shape) == 1:
            items[-1].names.append(name)
            items[-1].rows += rows
        else:
            items.append(SimpleNamespace(name=name, names=[name], shape=shape, nat=nat, rows=rows))
        nat += rows
    items.append(SimpleNamespace(name=None, names=[], shape=None, nat=nat, rows=total_rows - nat))
    blk = 0
    for item in items:
        item.cols = item.shape[1] // LANES if item.shape and len(item.shape) == 2 else 0
        item.blk = blk
        blk += ceil_to(item.rows, BLK) // BLK
    return items


class Geometry:
    def __init__(self, n_seg, n_doc, shard_len):
        self.n_seg, self.n_doc = n_seg, n_doc
        self.n_dev = n_seg * n_doc
        self.chunk = shard_len // LANES
        self.items = item_list(self.chunk * self.n_dev)
        self.by_name = SimpleNamespace(**{item.name: item for item in self.items if item.name})
        firsts, lasts = [], []
        for n in range(self.n_dev):
            lo, hi = n * self.chunk, (n + 1) * self.chunk
            blocks = []
            for item in self.items:
                a, b = max(lo, item.nat), min(hi, item.nat + item.rows)
                if a < b:
                    blocks.append(item.blk + (a - item.nat) // BLK)
                    blocks.append(item.blk + (b - 1 - item.nat) // BLK)
            firsts.append(min(blocks))
            lasts.append(max(blocks))
        self.first, self.last = firsts, lasts
        most = max(b - a + 1 for a, b in zip(firsts, lasts))
        self.piece_blocks = -(-most // self.n_dev)
        self.piece = self.piece_blocks * BLK
        self.slots = self.piece_blocks * self.n_dev
        self.c_size, self.x_size = 2, 2
        self.y_size = n_seg // 4

    def full_groups(self, item, chunk):
        rows = BLK * item.cols
        lo, hi = chunk * self.chunk - item.nat, (chunk + 1) * self.chunk - item.nat
        first, last = max(0, -(-lo // rows)), min(item.rows, hi) // rows
        return first, max(first, last)

    def block_table(self):
        table = np.zeros((self.n_dev, 4, self.slots), np.int32)
        for n in range(self.n_dev):
            lo, hi = n * self.chunk, (n + 1) * self.chunk
            for t in range(self.slots):
                b = self.first[n] + t
                if b > self.last[n]:
                    continue
                item = [it for it in self.items if it.blk <= b][-1]
                at = b - item.blk
                if item.cols:
                    first, last = self.full_groups(item, n)
                    group, column = divmod(at, item.cols)
                    if first <= group < last:
                        start = item.nat + group * BLK * item.cols + column - lo
                        table[n, :, t] = (start, 0, BLK, item.cols)
                        continue
                start = item.nat + at * BLK
                a = max(start, lo)
                z = min(start + BLK, hi, item.nat + item.rows)
                if a < z:
                    table[n, :, t] = (start - lo, a - start, z - start, 0)
        return table

    def chunks_of(self, item):
        found = []
        n_blocks = ceil_to(item.rows, BLK) // BLK
        for n in range(self.n_dev):
            a = max(item.blk, self.first[n])
            b = min(item.blk + n_blocks, self.last[n] + 1)
            if a < b:
                found.append((n, a - item.blk, b - item.blk, a - self.first[n]))
        return found

    def buckets(self):
        end_attention = self.by_name.w_out.nat
        end_segment = self.by_name.pos_table.nat
        a = (end_attention - 1) // self.chunk + 1
        b = (end_segment - 1) // self.chunk + 1
        return [range(0, a), range(a, b), range(b, self.n_dev)]

    def coords(self, device):
        seg, doc = divmod(device, self.n_doc)
        yx, c = divmod(seg, self.c_size)
        return [*divmod(yx, self.x_size), c, doc]

    def device(self, y, x, c, z):
        return ((y * self.x_size + x) * self.c_size + c) * self.n_doc + z

    def size(self, axis):
        return (self.y_size, self.x_size, self.c_size, self.n_doc)[axis]

    def shift(self, axis, step):
        pairs = []
        for source in range(self.n_dev):
            at = self.coords(source)
            at[axis] = (at[axis] + step) % self.size(axis)
            pairs.append((source, self.device(*at)))
        return pairs
def spec_vmem():
    return pl.BlockSpec(memory_space=pltpu.VMEM)


def spec_any():
    return pl.BlockSpec(memory_space=pl.ANY)


def spec_smem():
    return pl.BlockSpec(memory_space=pltpu.SMEM)


def kernel_params(mib=56):
    return pltpu.CompilerParams(vmem_limit_bytes=mib * 1024 * 1024)


def row_mask(low, high):
    rows = lax.broadcasted_iota(jnp.int32, (BLK, LANES), 0)
    return (rows >= low) & (rows < high)


def block_rows(geo, table_ref, t):
    return [table_ref[i * geo.slots + t] for i in range(4)]


def strides(geo):
    return sorted({item.cols for item in geo.items if item.cols})


def align_rows(geo, table, padded):
    def kernel(table_ref, rows_ref, out_ref):
        def body(t, carry):
            start, low_row, high_row, cols = block_rows(geo, table_ref, t)
            here = pl.ds(pl.multiple_of(t * BLK, BLK), BLK)

            @pl.when(cols == 0)
            def _():
                rows = rows_ref[pl.ds(start + BLK, BLK), :]
                out_ref[here, :] = jnp.where(row_mask(low_row, high_row), rows, 0.0).astype(jnp.bfloat16)

            for stride in strides(geo):
                @pl.when(cols == stride)
                def _(stride=stride):
                    rows = rows_ref[pl.ds(start + BLK, BLK, stride=stride), :]
                    out_ref[here, :] = rows.astype(jnp.bfloat16)

            return carry

        lax.fori_loop(0, geo.slots, body, 0)

    return pl.pallas_call(
        kernel,
        out_shape=jax.ShapeDtypeStruct((geo.slots * BLK, LANES), jnp.bfloat16),
        in_specs=[spec_smem(), spec_vmem()],
        out_specs=spec_vmem(),
        compiler_params=kernel_params(),
    )(table, padded)


def natural_rows(geo, table, blocks, pad_rows):
    def kernel(table_ref, blocks_ref, out_ref):
        def body(t, carry):
            start, low_row, high_row, cols = block_rows(geo, table_ref, t)
            rows = blocks_ref[pl.ds(pl.multiple_of(t * BLK, BLK), BLK), :].astype(jnp.float32)

            @pl.when(cols == 0)
            def _():
                here = pl.ds(start + BLK, BLK)
                out_ref[here, :] = jnp.where(row_mask(low_row, high_row), rows, out_ref[here, :])

            for stride in strides(geo):
                @pl.when(cols == stride)
                def _(stride=stride):
                    out_ref[pl.ds(start + BLK, BLK, stride=stride), :] = rows

            return carry

        lax.fori_loop(0, geo.slots, body, 0)

    return pl.pallas_call(
        kernel,
        out_shape=jax.ShapeDtypeStruct((pad_rows, LANES), jnp.float32),
        in_specs=[spec_smem(), spec_vmem()],
        out_specs=spec_vmem(),
        compiler_params=kernel_params(),
    )(table, blocks)


class Buckets:
    def __init__(self, geo):
        self.geo = geo
        self.ranges = geo.buckets()
        self.half = [(len(r) + 1) // 2 for r in self.ranges]
        self.arrays = [4, 4, 1]

    def find(self, chunk):
        for number, span in enumerate(self.ranges):
            if chunk in span:
                at = chunk - span.start
                cut = self.half[number] if self.arrays[number] > 1 else len(span)
                return (number, 0, at) if at < cut else (number, 1, at - cut)

    def shapes(self, number):
        geo = self.geo
        cut = self.half[number]
        rest = len(self.ranges[number]) - cut
        rows = geo.n_doc * geo.piece
        return [
            (geo.y_size, geo.x_size, cut, rows, LANES),
            (geo.x_size, geo.y_size, rest, rows, LANES),
        ]


def wrap(value, size):
    return lax.rem(value + size, size)


def copy_rows(count, step, body):
    full = count // step
    if full:
        def loop(i, carry):
            body(i * step, step)
            return carry

        lax.fori_loop(0, full, loop, 0)
    if count % step:
        body(full * step, count % step)


VECTOR_ROWS = 16


def chunk_copies(geo, buckets, sources, used, coords_ref, n, staged, sem):
    my_y, my_x, my_c = coords_ref[0], coords_ref[1], coords_ref[2]
    number, half, place = buckets.find(n)
    first = sum(buckets.arrays[m] for m in used[: used.index(number)])
    if buckets.arrays[number] == 1:
        for device in range(geo.n_dev):
            pltpu.make_async_copy(
                sources[first].at[device, n - buckets.ranges[number].start],
                staged.at[pl.ds(device * geo.piece, geo.piece)],
                sem,
            ).start()
        return
    rows = geo.n_doc * geo.piece
    for core in range(2):
        c = my_c if core == 0 else 1 - my_c
        for ry in range(geo.y_size):
            for rx in range(geo.x_size):
                y, x = wrap(my_y - ry, geo.y_size), wrap(my_x - rx, geo.x_size)
                s = (y * geo.x_size + x) * 2 + c
                index = (ry, rx, place) if half == 0 else (rx, ry, place)
                pltpu.make_async_copy(
                    sources[first + 2 * half + core].at[index],
                    staged.at[pl.ds(pl.multiple_of(s * rows, BLK), rows)],
                    sem,
                ).start()


def unpack_matrix(geo, buckets, gathered, coords, name):
    item = vars(geo.by_name)[name]
    depth, cols = item.shape
    chunks = geo.chunks_of(item)
    used = sorted({buckets.find(n)[0] for n, *_ in chunks})
    operands = [array for number in used for array in gathered[number]]
    wide_cols = cols // LANES

    def kernel(coords_ref, *refs):
        sources, (out_ref, staged, wide, sems) = refs[: len(operands)], refs[len(operands) :]
        for at, (n, _, _, _) in enumerate(chunks):
            chunk_copies(geo, buckets, sources, used, coords_ref, n, staged.at[at], sems.at[at])
        for at in range(len(chunks)):
            pltpu.make_async_copy(staged.at[at], staged.at[at], sems.at[at]).wait()
        split = set()
        for at, (n, b0, b1, slot) in enumerate(chunks):
            first, last = geo.full_groups(item, n)
            split |= set(range(b0 // wide_cols, -(-b1 // wide_cols))) - set(range(first, last))

            def group(g, carry, at=at, shift=slot - b0):
                rows = pl.ds(pl.multiple_of(g * BLK, BLK), BLK)
                for cb in range(wide_cols):
                    src = pl.ds(pl.multiple_of((g * wide_cols + cb + shift) * BLK, BLK), BLK)
                    out_ref[rows, cb * LANES : (cb + 1) * LANES] = staged[at, src, :]
                return carry

            lax.fori_loop(first, last, group, 0)
        for g in sorted(split):
            done = g * wide_cols
            for at, (n, b0, b1, slot) in enumerate(chunks):
                lo, hi = max(b0, g * wide_cols), min(b1, (g + 1) * wide_cols)
                for b in range(lo, hi):
                    rows = staged[at, pl.ds((slot + b - b0) * BLK, BLK), :].astype(jnp.float32)
                    here = pl.ds((b - g * wide_cols) * BLK, BLK)
                    wide[here, :] = wide[here, :] + rows if b < done else rows
                done = max(done, hi)
            for cb in range(wide_cols):
                tile = wide[pl.ds(cb, BLK, stride=wide_cols), :]
                out_ref[g * BLK : (g + 1) * BLK, cb * LANES : (cb + 1) * LANES] = tile.astype(jnp.bfloat16)

    return pl.pallas_call(
        kernel,
        out_shape=jax.ShapeDtypeStruct((depth, cols), jnp.bfloat16),
        in_specs=[spec_smem()] + [spec_any()] * len(operands),
        out_specs=spec_vmem(),
        scratch_shapes=[
            pltpu.VMEM((len(chunks), geo.slots * BLK, LANES), jnp.bfloat16),
            pltpu.VMEM((BLK * (wide_cols + 2), LANES), jnp.float32),
            pltpu.SemaphoreType.DMA((len(chunks),)),
        ],
        compiler_params=kernel_params(),
    )(coords, *operands)


def unpack_vectors(geo, buckets, gathered, coords, names):
    lane_cols = D // LANES
    blocks, rows_of = [], []
    for name in names:
        item = vars(geo.by_name)[name]
        for r in range(item.rows):
            rows_of.append(len(blocks) * BLK + r)
        for b in range(ceil_to(item.rows, BLK) // BLK):
            blocks.append(
                [
                    (n, item.blk + b - geo.first[n])
                    for n in range(geo.n_dev)
                    if geo.first[n] <= item.blk + b <= geo.last[n]
                ]
            )
    copies = [(b, which, n, slot) for b, found in enumerate(blocks) for which, (n, slot) in enumerate(found)]
    used = sorted({buckets.find(n)[0] for _, _, n, _ in copies})
    operands = [array for number in used for array in gathered[number]]

    def kernel(coords_ref, *refs):
        sources, (out_ref, staged, wide, sem) = refs[: len(operands)], refs[len(operands) :]
        my_y, my_x, my_c = coords_ref[0], coords_ref[1], coords_ref[2]
        for at, (b, which, n, slot) in enumerate(copies):
            number, half, place = buckets.find(n)
            first = sum(buckets.arrays[m] for m in used[: used.index(number)])
            device, offset = slot // geo.piece_blocks, slot % geo.piece_blocks * BLK
            if buckets.arrays[number] == 1:
                pltpu.make_async_copy(
                    sources[first].at[device, n - buckets.ranges[number].start, pl.ds(offset, BLK)],
                    staged.at[at],
                    sem,
                ).start()
                continue
            y, x, c, z = geo.coords(device)
            ry, rx = wrap(my_y - y, geo.y_size), wrap(my_x - x, geo.x_size)
            index = (ry, rx) if half == 0 else (rx, ry)
            for core in range(2):
                source = sources[first + 2 * half + core]

                @pl.when(my_c == (c if core == 0 else 1 - c))
                def _(source=source, at=at, index=index, place=place, row=z * geo.piece + offset):
                    pltpu.make_async_copy(
                        source.at[index[0], index[1], place, pl.ds(row, BLK)], staged.at[at], sem
                    ).start()

        pltpu.make_async_copy(staged, staged, sem).wait()
        for at, (b, which, n, slot) in enumerate(copies):
            rows = staged[at].astype(jnp.float32)
            here = pl.ds(b * BLK, BLK)
            wide[here, :] = rows if which == 0 else wide[here, :] + rows
        out_ref[...] = jnp.zeros_like(out_ref)
        for r, row in enumerate(rows_of):
            v, cb = divmod(r, lane_cols)
            out_ref[v : v + 1, cb * LANES : (cb + 1) * LANES] = wide[row : row + 1, :]

    return pl.pallas_call(
        kernel,
        out_shape=jax.ShapeDtypeStruct((VECTOR_ROWS, D), jnp.float32),
        in_specs=[spec_smem()] + [spec_any()] * len(operands),
        out_specs=spec_vmem(),
        scratch_shapes=[
            pltpu.VMEM((len(copies), BLK, LANES), jnp.bfloat16),
            pltpu.VMEM((len(blocks) * BLK, LANES), jnp.float32),
            pltpu.SemaphoreType.DMA,
        ],
        compiler_params=kernel_params(),
    )(coords, *operands)


def vector_rows(wide, values, first, count):
    lane_cols = D // LANES
    for r in range(count):
        v, cb = divmod(r, lane_cols)
        wide[r : r + 1, :] = values[first + v : first + v + 1, cb * LANES : (cb + 1) * LANES]


def bucket_parts(geo, span):
    parts = []
    for item in geo.items:
        chunks = [entry for entry in geo.chunks_of(item) if entry[0] in span]
        if chunks and item.names:
            parts.append((item, chunks))
    return parts


def pack_bucket(geo, buckets, number, grads, coords):
    span = buckets.ranges[number]
    seg_rows = geo.n_doc * geo.piece
    parts = bucket_parts(geo, span)
    operands, specs, windows, scratch = [], [], [], []
    wide_rows = BLK
    for item, chunks in parts:
        if len(item.shape) == 2:
            cols = item.shape[1] // LANES
            k0 = min(b0 for _, b0, _, _ in chunks) // cols
            k1 = -(-max(b1 for _, _, b1, _ in chunks) // cols)
            operands.append(grads[item.name])
            specs.append(spec_any())
            windows.append((cols, k0, k1))
            scratch.append(pltpu.VMEM(((k1 - k0) * BLK, item.shape[1]), jnp.bfloat16))
            wide_rows = max(wide_rows, BLK * cols)
        else:
            wide_rows = max(wide_rows, ceil_to(item.rows, BLK))
            operands.append(grads[item.name][0])
            specs.append(spec_vmem())
            windows.append(None)
            scratch.append(pltpu.VMEM((BLK, LANES), jnp.bfloat16))
    outs = [shape for shape in buckets.shapes(number) for _ in range(2)]

    def kernel(coords_ref, *refs):
        sources = refs[: len(parts)]
        targets = refs[len(parts) : len(parts) + 4]
        loaded = refs[len(parts) + 4 : 2 * len(parts) + 4]
        staged, wide, in_sems, out_sems = refs[2 * len(parts) + 4 :]
        my_y, my_x, my_c = coords_ref[0], coords_ref[1], coords_ref[2]
        loads = {}
        for at, window in enumerate(windows):
            if window is not None:
                source = sources[at].at[pl.ds(window[1] * BLK, (window[2] - window[1]) * BLK)]
                loads[at] = pltpu.make_async_copy(source, loaded[at], in_sems.at[at])
                loads[at].start()

        def clear(row, rows):
            for at in range(len(span)):
                here = pl.ds(pl.multiple_of(row, BLK), rows)
                staged[at, here, :] = jnp.zeros((rows, LANES), jnp.bfloat16)

        tail = min(geo.last[n] - geo.first[n] for n in span) * BLK
        copy_rows(geo.slots * BLK - tail, 128, lambda row, rows: clear(row + tail, rows))

        def send_out(n):
            _, half, place = buckets.find(n)
            for core in range(2):
                c = my_c if core == 0 else 1 - my_c
                for ry in range(geo.y_size):
                    for rx in range(geo.x_size):
                        y, x = wrap(my_y + ry, geo.y_size), wrap(my_x + rx, geo.x_size)
                        s = (y * geo.x_size + x) * 2 + c
                        index = (ry, rx, place) if half == 0 else (rx, ry, place)
                        pltpu.make_async_copy(
                            staged.at[n - span.start, pl.ds(pl.multiple_of(s * seg_rows, BLK), seg_rows)],
                            targets[2 * half + core].at[index],
                            out_sems.at[n - span.start],
                        ).start()

        last_part = {n: at for at, (_, chunks) in enumerate(parts) for n, *_ in chunks}
        for at, ((item, chunks), window) in enumerate(zip(parts, windows)):
            if window is None:
                vector_rows(wide, sources[at], grads[item.name][1], item.rows)
                for n, b0, b1, slot in chunks:
                    rows = wide[pl.ds(b0 * BLK, (b1 - b0) * BLK), :].astype(jnp.bfloat16)
                    staged[n - span.start, pl.ds(slot * BLK, (b1 - b0) * BLK), :] = rows
            else:
                loads[at].wait()
                cols, k0, k1 = window
                values = loaded[at]
                split = set()
                for n, b0, b1, slot in chunks:
                    first, last = geo.full_groups(item, n)
                    split |= set(range(b0 // cols, -(-b1 // cols))) - set(range(first, last))

                    def group(g, carry, n=n, shift=slot - b0, k0=k0, cols=cols, values=values):
                        rows = pl.ds(pl.multiple_of((g - k0) * BLK, BLK), BLK)
                        for cb in range(cols):
                            dst = pl.ds(pl.multiple_of((g * cols + cb + shift) * BLK, BLK), BLK)
                            staged[n - span.start, dst, :] = values[rows, cb * LANES : (cb + 1) * LANES]
                        return carry

                    lax.fori_loop(first, last, group, 0)
                for g in sorted(split):
                    for cb in range(cols):
                        tile = values[(g - k0) * BLK : (g - k0 + 1) * BLK, cb * LANES : (cb + 1) * LANES]
                        wide[pl.ds(cb, BLK, stride=cols), :] = tile.astype(jnp.float32)
                    for n, b0, b1, slot in chunks:
                        first, last = geo.full_groups(item, n)
                        lo, hi = max(b0, g * cols), min(b1, (g + 1) * cols)
                        if lo < hi and not first <= g < last:
                            rows = wide[pl.ds((lo - g * cols) * BLK, (hi - lo) * BLK), :]
                            dst = pl.ds((slot + lo - b0) * BLK, (hi - lo) * BLK)
                            staged[n - span.start, dst, :] = rows.astype(jnp.bfloat16)
            for n, *_ in chunks:
                if last_part[n] == at:
                    send_out(n)
        for n in span:
            at = n - span.start
            pltpu.make_async_copy(staged.at[at], staged.at[at], out_sems.at[at]).wait()

    return pl.pallas_call(
        kernel,
        out_shape=[jax.ShapeDtypeStruct(shape, jnp.bfloat16) for shape in outs],
        in_specs=[spec_smem()] + specs,
        out_specs=[spec_any()] * 4,
        scratch_shapes=scratch
        + [
            pltpu.VMEM((len(span), geo.slots * BLK, LANES), jnp.bfloat16),
            pltpu.VMEM((wide_rows + 2 * BLK, LANES), jnp.float32),
            pltpu.SemaphoreType.DMA((len(parts),)),
            pltpu.SemaphoreType.DMA((len(span),)),
        ],
        compiler_params=kernel_params(),
    )(coords, *operands)


def pack_cross(geo, span, lefts, rights, vectors, seg):
    seg_blocks = geo.n_doc * geo.piece_blocks
    parts = bucket_parts(geo, span)
    names = list(lefts)
    vector_names = list(vectors)
    depth_rows = next(iter(rights.values())).shape[0]

    def window(cols):
        return (-(-(seg_blocks - 1) // cols) + 1) * BLK

    wide_rows = 0
    left_rows = BLK
    for item, chunks in parts:
        if len(item.shape) == 2:
            cols = item.shape[1] // LANES
            size = min(window(cols), item.shape[0])
            left_rows = max(left_rows, len(chunks) * size)
            wide_rows = max(wide_rows, len(chunks) * size * cols)

    def kernel(seg_ref, *refs):
        left = dict(zip(names, refs[: len(names)]))
        right = dict(zip(names, refs[len(names) : 2 * len(names)]))
        vector = dict(zip(vector_names, refs[2 * len(names) : 2 * len(names) + len(vector_names)]))
        out_ref, gathered, wide = refs[2 * len(names) + len(vector_names) :]
        low_slot = seg_ref[0] * seg_blocks
        out_ref[...] = jnp.zeros_like(out_ref)
        for item, chunks in parts:
            starts, size, cols = [], 0, 1
            if len(item.shape) == 2:
                cols = item.shape[1] // LANES
                size = min(window(cols), item.shape[0])
                for at, (n, b0, b1, slot) in enumerate(chunks):
                    first = jnp.maximum(low_slot, slot) - slot + b0
                    start = jnp.clip(first // cols * BLK, 0, item.shape[0] - size)
                    start = pl.multiple_of(start, BLK)
                    starts.append(start)
                    gathered[at * size : (at + 1) * size, :] = left[item.name][pl.ds(start, size), :]
                count = len(chunks) * size
                rows = gathered[:count, :]
                for cb in range(0, cols, 2):
                    tile = dot_nn(rows, right[item.name][:, cb * LANES : (cb + 2) * LANES])
                    wide[pl.ds(cb, count, stride=cols), :] = tile[:, :LANES]
                    wide[pl.ds(cb + 1, count, stride=cols), :] = tile[:, LANES:]
            else:
                vector_rows(wide, vector[item.name], vectors[item.name][1], item.rows)
            for at, (n, b0, b1, slot) in enumerate(chunks):
                begin = jnp.maximum(low_slot, slot)
                end = jnp.minimum(low_slot + seg_blocks, slot + b1 - b0)
                base = (at * size - starts[at]) * cols if starts else 0

                first, last = geo.full_groups(item, n) if starts else (0, 0)

                def by_row(t, carry, n=n, b0=b0, slot=slot, base=base):
                    src = pl.ds((b0 + t - slot) * BLK + base, BLK)
                    dst = pl.ds(pl.multiple_of((t - low_slot) * BLK, BLK), BLK)
                    out_ref[n - span.start, dst, :] = wide[src, :].astype(jnp.bfloat16)
                    return carry

                def by_tile(t, carry, n=n, b0=b0, slot=slot, base=base, cols=cols):
                    b = b0 + t - slot
                    group = b // cols
                    src = pl.ds(group * BLK * cols + b - group * cols + base, BLK, stride=cols)
                    dst = pl.ds(pl.multiple_of((t - low_slot) * BLK, BLK), BLK)
                    out_ref[n - span.start, dst, :] = wide[src, :].astype(jnp.bfloat16)
                    return carry

                if first < last:
                    lo = jnp.clip(slot + first * cols - b0, begin, jnp.maximum(begin, end))
                    hi = jnp.clip(slot + last * cols - b0, begin, jnp.maximum(begin, end))
                    lax.fori_loop(begin, lo, by_row, 0)
                    lax.fori_loop(lo, hi, by_tile, 0)
                    lax.fori_loop(hi, jnp.maximum(hi, end), by_row, 0)
                else:
                    lax.fori_loop(begin, jnp.maximum(begin, end), by_row, 0)

    operands = [lefts[n] for n in names] + [rights[n] for n in names]
    operands += [vectors[n][0] for n in vector_names]
    return pl.pallas_call(
        kernel,
        out_shape=jax.ShapeDtypeStruct((len(span), seg_blocks * BLK, LANES), jnp.bfloat16),
        in_specs=[spec_smem()] + [spec_vmem()] * len(operands),
        out_specs=spec_vmem(),
        scratch_shapes=[
            pltpu.VMEM((left_rows, depth_rows), jnp.bfloat16),
            pltpu.VMEM((wide_rows + 2 * BLK, LANES), jnp.float32),
        ],
        compiler_params=kernel_params(),
    )(seg, *operands)
TILE = 512
PAIRS = HEADS // 2
TAIL_RATE = 0.3
TAIL = (
    0.11962929605681312,
    0.12075400207853171,
    0.0999131861559567,
    0.12856268365589474,
    -0.05368570534984477,
    0.20635578836359286,
    -0.15720441932045734,
    0.0356750954846771,
)


def dot_nn(left, right):
    return lax.dot_general(left, right, (((1,), (0,)), ((), ())), preferred_element_type=jnp.float32)


def dot_nt(left, right):
    return lax.dot_general(left, right, (((1,), (1,)), ((), ())), preferred_element_type=jnp.float32)


def dot_tn(left, right):
    return lax.dot_general(left, right, (((0,), (0,)), ((), ())), preferred_element_type=jnp.float32)


def low(values):
    return values.astype(jnp.bfloat16)


def gelu_pair(u):
    t = 1.0 / (1.0 + TAIL_RATE * jnp.abs(u))
    poly = TAIL[-1] * t + TAIL[-2]
    for coef in TAIL[-3::-1]:
        poly = poly * t + coef
    bell = jnp.exp(-0.5 * (u * u))
    tail = bell * (poly * t)
    spread = jnp.where(u < 0.0, tail, 1.0 - tail)
    return u * spread, spread + u * bell * (1.0 / math.sqrt(2.0 * math.pi))


def norm_rows(values, gain, shift):
    center = values - jnp.mean(values, axis=-1, keepdims=True)
    rate = lax.rsqrt(jnp.mean(center * center, axis=-1, keepdims=True) + EPSILON)
    normal = center * rate
    return normal * gain + shift, normal, rate


def norm_pull(grad, normal, rate, gain):
    scaled = grad * gain
    return rate * (
        scaled
        - jnp.mean(scaled, axis=-1, keepdims=True)
        - normal * jnp.mean(scaled * normal, axis=-1, keepdims=True)
    )


def fixed(shape):
    return pl.BlockSpec(shape, lambda i: (0,) * len(shape), pipeline_mode=pl.Buffered(1))


def tiles(cols, first=0):
    return pl.BlockSpec((TILE, cols), lambda i: (i + first, 0))


def both_heads(values):
    first = lax.broadcasted_iota(jnp.int32, values.shape, 1) < HEAD_DIM
    zero = jnp.zeros_like(values)
    return jnp.concatenate([jnp.where(first, values, zero), jnp.where(first, zero, values)], axis=0)


def side_by_side(stacked):
    half = stacked.shape[0] // 2
    return jnp.concatenate([stacked[:half], stacked[half:]], axis=1)


def third(part, pair):
    start = part * D + pair * LANES
    return slice(start, start + LANES)


def attend_kernel(x_ref, wqkv_ref, vec_ref, *refs):
    packed_ref, att_ref, stat_ref = refs[-3:]
    x = x_ref[...]
    for j in range(3):
        cols = slice(j * D, (j + 1) * D)
        part = dot_nn(x, wqkv_ref[:, cols])
        packed_ref[:, cols] = low(part if j == 1 else part + vec_ref[j // 2 : j // 2 + 1, :])
    lanes = lax.broadcasted_iota(jnp.int32, (SEG_LEN, LANES), 1)

    def segment(s, carry):
        rows = pl.ds(pl.multiple_of(s * SEG_LEN, SEG_LEN), SEG_LEN)
        stat = jnp.zeros((SEG_LEN, LANES), jnp.float32)
        for pair in range(PAIRS):
            q = packed_ref[rows, third(0, pair)] * jnp.bfloat16(HEAD_DIM**-0.5)
            k = packed_ref[rows, third(1, pair)]
            v = packed_ref[rows, third(2, pair)]
            scores = dot_nt(both_heads(q), k)
            largest = jnp.max(scores, axis=-1, keepdims=True)
            raised = jnp.exp(scores - largest)
            summed = jnp.sum(raised, axis=-1, keepdims=True)
            weights = low(raised / summed)
            att_ref[rows, pair * LANES : (pair + 1) * LANES] = low(
                dot_nn(side_by_side(weights), both_heads(v))
            )
            log_sum = largest + jnp.log(summed)
            stat = jnp.where(lanes == 2 * pair, log_sum[:SEG_LEN], stat)
            stat = jnp.where(lanes == 2 * pair + 1, log_sum[SEG_LEN:], stat)
        stat_ref[rows, :] = stat
        return carry

    lax.fori_loop(0, TILE // SEG_LEN, segment, 0)


def in_parts(kernel, first, count, inputs, in_specs, outs, out_specs, scratch, previous):
    previous = list(previous or ())
    return pl.pallas_call(
        kernel,
        grid=(count,),
        in_specs=in_specs + [spec_any()] * len(previous),
        out_specs=out_specs,
        out_shape=outs,
        scratch_shapes=scratch,
        input_output_aliases={len(inputs) + i: i for i in range(len(previous))},
        compiler_params=kernel_params(60),
    )(*inputs, *previous)


def attend_layer(x, w_qkv, vecs, first, count, previous=None):
    n = x.shape[0]

    def rows(cols):
        return tiles(cols, first)

    return in_parts(
        attend_kernel,
        first,
        count,
        [x, w_qkv, vecs],
        [rows(D), fixed((D, 3 * D)), fixed((VECTOR_ROWS, D))],
        [
            jax.ShapeDtypeStruct((n, 3 * D), jnp.bfloat16),
            jax.ShapeDtypeStruct((n, D), jnp.bfloat16),
            jax.ShapeDtypeStruct((n, LANES), jnp.float32),
        ],
        [rows(3 * D), rows(D), rows(LANES)],
        [],
        previous,
    )


FBLOCK = D


def feed_kernel(
    x_ref, att_ref, wout_ref, wup_ref, wdown_ref, vec_ref,
    h1low_ref, norm1_ref, g_ref, dg_ref, norm2_ref, rate_ref, h2_ref, cls_ref, res_ref, h1_ref,
):
    step = pl.program_id(0)
    segs = TILE // SEG_LEN
    lanes = lax.broadcasted_iota(jnp.int32, (SEG_LEN, LANES), 1)
    res_ref[...] = dot_nn(att_ref[...], wout_ref[...])

    def start(s, carry):
        rows = pl.ds(pl.multiple_of(s * SEG_LEN, SEG_LEN), SEG_LEN)
        resid = x_ref[rows, :].astype(jnp.float32) + res_ref[rows, :] + vec_ref[2:3, :]
        hidden, normal, rate = norm_rows(resid, vec_ref[3:4, :], vec_ref[4:5, :])
        h1_ref[rows, :] = hidden
        h1low_ref[rows, :] = low(hidden)
        norm1_ref[rows, :] = low(normal)
        rate_ref[rows, :] = jnp.broadcast_to(rate, (SEG_LEN, LANES))
        return carry

    lax.fori_loop(0, segs, start, 0)
    h = h1low_ref[...]
    for j in range(FF // FBLOCK):
        cols = slice(j * FBLOCK, (j + 1) * FBLOCK)
        act, slope = gelu_pair(dot_nn(h, wup_ref[:, cols]) + vec_ref[5 + j : 6 + j, :])
        g = low(act)
        g_ref[:, cols] = g
        dg_ref[:, cols] = low(slope)
        part = dot_nn(g, wdown_ref[cols, :])
        if j == 0:
            res_ref[...] = part
        else:
            res_ref[...] += part

    def finish(s, carry):
        rows = pl.ds(pl.multiple_of(s * SEG_LEN, SEG_LEN), SEG_LEN)
        resid = h1_ref[rows, :] + res_ref[rows, :] + vec_ref[9:10, :]
        hidden, normal, rate = norm_rows(resid, vec_ref[10:11, :], vec_ref[11:12, :])
        h2_ref[rows, :] = low(hidden)
        norm2_ref[rows, :] = low(normal)
        rate_ref[rows, :] = jnp.where(lanes == 0, rate_ref[rows, :], rate)
        cls_ref[pl.ds(step * segs + s, 1), :] = hidden[0:1, :]
        return carry

    lax.fori_loop(0, segs, finish, 0)


def feed_layer(x, att, w_out, w_up, w_down, vecs):
    n = x.shape[0]
    bf, f32 = jnp.bfloat16, jnp.float32
    return pl.pallas_call(
        feed_kernel,
        grid=(n // TILE,),
        in_specs=[
            tiles(D), tiles(D), fixed((D, D)), fixed((D, FF)), fixed((FF, D)), fixed((VECTOR_ROWS, D)),
        ],
        out_specs=[tiles(D), tiles(D), tiles(FF), tiles(FF), tiles(D), tiles(LANES), tiles(D)]
        + [pl.BlockSpec((n // SEG_LEN, D), lambda i: (0, 0))],
        out_shape=[
            jax.ShapeDtypeStruct((n, cols), kind)
            for cols, kind in ((D, bf), (D, bf), (FF, bf), (FF, bf), (D, bf), (LANES, f32), (D, bf))
        ]
        + [jax.ShapeDtypeStruct((n // SEG_LEN, D), f32)],
        scratch_shapes=[pltpu.VMEM((TILE, D), f32), pltpu.VMEM((TILE, D), f32)],
        compiler_params=kernel_params(60),
    )(x, att, w_out, w_up, w_down, vecs)


def feed_back_kernel(
    cot_ref, cls_ref, norm2_ref, dg_ref, norm1_ref, rate_ref,
    wdown_ref, wup_ref, wout_ref, vec_ref,
    dm_ref, du_ref, dao_ref, da_ref, one_ref, sums_ref, res_ref,
):
    step = pl.program_id(0)

    @pl.when(step == 0)
    def _():
        sums_ref[...] = jnp.zeros_like(sums_ref)

    segs = TILE // SEG_LEN
    row_ids = lax.broadcasted_iota(jnp.int32, (SEG_LEN, D), 0)

    def add_sum(row, values):
        sums_ref[row : row + 1, :] += jnp.sum(values, axis=0, keepdims=True)

    def start(s, carry):
        rows = pl.ds(pl.multiple_of(s * SEG_LEN, SEG_LEN), SEG_LEN)
        cls = cls_ref[pl.ds(step * segs + s, 1), :]
        grad = jnp.where(row_ids == 0, cls, cot_ref[rows, :].astype(jnp.float32))
        normal = norm2_ref[rows, :].astype(jnp.float32)
        add_sum(10, grad * normal)
        add_sum(11, grad)
        two = norm_pull(grad, normal, rate_ref[rows, 1:2], vec_ref[10:11, :])
        res_ref[rows, :] = two
        dm = low(two)
        dm_ref[rows, :] = dm
        add_sum(9, dm.astype(jnp.float32))
        return carry

    lax.fori_loop(0, segs, start, 0)
    dm = dm_ref[...]
    for j in range(FF // FBLOCK):
        cols = slice(j * FBLOCK, (j + 1) * FBLOCK)
        du = low(dot_nt(dm, wdown_ref[cols, :]) * dg_ref[:, cols].astype(jnp.float32))
        du_ref[:, cols] = du
        add_sum(5 + j, du.astype(jnp.float32))
        res_ref[...] += dot_nt(du, wup_ref[:, cols])

    def finish(s, carry):
        rows = pl.ds(pl.multiple_of(s * SEG_LEN, SEG_LEN), SEG_LEN)
        grad = res_ref[rows, :]
        normal = norm1_ref[rows, :].astype(jnp.float32)
        add_sum(3, grad * normal)
        add_sum(4, grad)
        one = norm_pull(grad, normal, rate_ref[rows, 0:1], vec_ref[3:4, :])
        one_ref[rows, :] = one
        dao = low(one)
        dao_ref[rows, :] = dao
        add_sum(2, dao.astype(jnp.float32))
        return carry

    lax.fori_loop(0, segs, finish, 0)
    da_ref[...] = low(dot_nt(dao_ref[...], wout_ref[...]))


def feed_back(cot, cls, norm2, dg, norm1, rates, w_down, w_up, w_out, vecs):
    n = cot.shape[0]
    bf, f32 = jnp.bfloat16, jnp.float32
    return pl.pallas_call(
        feed_back_kernel,
        grid=(n // TILE,),
        in_specs=[
            tiles(D), fixed((n // SEG_LEN, D)), tiles(D), tiles(FF), tiles(D), tiles(LANES),
            fixed((FF, D)), fixed((D, FF)), fixed((D, D)), fixed((VECTOR_ROWS, D)),
        ],
        out_specs=[
            tiles(D), tiles(FF), tiles(D), tiles(D), tiles(D),
            pl.BlockSpec((VECTOR_ROWS, D), lambda i: (0, 0)),
        ],
        out_shape=[
            jax.ShapeDtypeStruct((n, D), bf),
            jax.ShapeDtypeStruct((n, FF), bf),
            jax.ShapeDtypeStruct((n, D), bf),
            jax.ShapeDtypeStruct((n, D), bf),
            jax.ShapeDtypeStruct((n, D), f32),
            jax.ShapeDtypeStruct((VECTOR_ROWS, D), f32),
        ],
        scratch_shapes=[pltpu.VMEM((TILE, D), f32)],
        compiler_params=kernel_params(60),
    )(cot, cls, norm2, dg, norm1, rates, w_down, w_up, w_out, vecs)


def attend_back_kernel(packed_ref, stat_ref, da_ref, before_ref, *refs):
    dqkv_ref, sums_ref = refs[-2:]

    @pl.when(pl.program_id(0) == 0)
    def _():
        sums_ref[...] = before_ref[...]

    lanes = lax.broadcasted_iota(jnp.int32, (SEG_LEN, LANES), 1)
    scale = HEAD_DIM**-0.5

    def segment(s, carry):
        rows = pl.ds(pl.multiple_of(s * SEG_LEN, SEG_LEN), SEG_LEN)
        stat = stat_ref[rows, :]
        for pair in range(PAIRS):
            q = packed_ref[rows, third(0, pair)] * jnp.bfloat16(scale)
            k = packed_ref[rows, third(1, pair)]
            v = packed_ref[rows, third(2, pair)]
            da = da_ref[rows, pair * LANES : (pair + 1) * LANES]
            queries, grads = both_heads(q), both_heads(da)
            log_sum = jnp.concatenate([stat[:, 2 * pair : 2 * pair + 1], stat[:, 2 * pair + 1 : 2 * pair + 2]], axis=0)
            weights = jnp.exp(dot_nt(queries, k) - log_sum)
            grad_weights = dot_nt(grads, v)
            dv = dot_tn(low(weights), grads)
            inner = jnp.sum(grad_weights * weights, axis=-1, keepdims=True)
            ds = low(weights * (grad_weights - inner))
            dq = dot_nn(side_by_side(ds), both_heads(k)) * scale
            dk = dot_tn(ds, queries)
            for part, grad in enumerate((dq, dk, dv)):
                grad = low(grad)
                cols = third(part, pair)
                dqkv_ref[rows, cols] = grad
                if part != 1:
                    here = (slice(part // 2, part // 2 + 1), third(0, pair))
                    sums_ref[here] += jnp.sum(grad.astype(jnp.float32), axis=0, keepdims=True)
        return carry

    lax.fori_loop(0, TILE // SEG_LEN, segment, 0)


def attend_back(packed, stat, da, first, count, previous=None):
    n = packed.shape[0]
    before = previous[1] if previous else jnp.zeros((8, D), jnp.float32)
    return in_parts(
        attend_back_kernel,
        first,
        count,
        [packed, stat, da, before],
        [tiles(3 * D, first), tiles(LANES, first), tiles(D, first), fixed((8, D))],
        [jax.ShapeDtypeStruct((n, 3 * D), jnp.bfloat16), jax.ShapeDtypeStruct((8, D), jnp.float32)],
        [tiles(3 * D, first), pl.BlockSpec((8, D), lambda i: (0, 0))],
        [],
        previous and previous[:1],
    )


def cross_kernel(
    rows_ref, tagc_ref, tagr_ref, gz_ref, wqkv_ref, wout_ref, wup_ref, wdown_ref, vec_ref,
    out_ref, grows_ref, sums_ref, gqkv_ref, go_ref, gu_ref, gm_ref, rowst_ref, attt_ref, hidt_ref, actt_ref,
    packed_ref, weights_ref, att_ref, act_ref, slope_ref, res_ref,
):
    scale = HEAD_DIM**-0.5
    rows = rows_ref[...]
    rowst_ref[...] = rows.T
    same = tagc_ref[:, 0:1] == tagr_ref[0:1, :]
    same = jnp.concatenate([same, same], axis=0)

    def add_sum(row, values):
        sums_ref[row : row + 1, :] = jnp.sum(values.astype(jnp.float32), axis=0, keepdims=True)

    def pair_cols(pair):
        return slice(pair * LANES, (pair + 1) * LANES)

    sums_ref[...] = jnp.zeros_like(sums_ref)
    for j in range(3):
        cols = slice(j * D, (j + 1) * D)
        part = dot_nn(rows, wqkv_ref[:, cols])
        packed_ref[:, cols] = low(part if j == 1 else part + vec_ref[j // 2 : j // 2 + 1, :])
    for pair in range(PAIRS):
        q = packed_ref[:, third(0, pair)] * jnp.bfloat16(scale)
        scores = jnp.where(same, dot_nt(both_heads(q), packed_ref[:, third(1, pair)]), NEGATIVE)
        raised = jnp.exp(scores - jnp.max(scores, axis=-1, keepdims=True))
        weights = raised / jnp.sum(raised, axis=-1, keepdims=True)
        weights_ref[pair] = weights
        blend = dot_nn(side_by_side(low(weights)), both_heads(packed_ref[:, third(2, pair)]))
        att_ref[:, pair_cols(pair)] = low(blend)
    att = att_ref[...]
    attt_ref[...] = att.T
    resid = rows.astype(jnp.float32) + dot_nn(att, wout_ref[...]) + vec_ref[2:3, :]
    hidden, normal_three, rate_three = norm_rows(resid, vec_ref[3:4, :], vec_ref[4:5, :])
    hidden_low = low(hidden)
    hidt_ref[...] = hidden_low.T
    res_ref[...] = hidden + vec_ref[9:10, :]
    for j in range(FF // FBLOCK):
        cols = slice(j * FBLOCK, (j + 1) * FBLOCK)
        act, slope = gelu_pair(dot_nn(hidden_low, wup_ref[:, cols]) + vec_ref[5 + j : 6 + j, :])
        act = low(act)
        actt_ref[cols, :] = act.T
        slope_ref[:, cols] = slope
        res_ref[...] += dot_nn(act, wdown_ref[cols, :])
    crossed, normal_four, rate_four = norm_rows(res_ref[...], vec_ref[10:11, :], vec_ref[11:12, :])
    out_ref[...] = low(crossed)

    grad_z = gz_ref[...].astype(jnp.float32)
    add_sum(10, grad_z * normal_four)
    add_sum(11, grad_z)
    grad_four = norm_pull(grad_z, normal_four, rate_four, vec_ref[10:11, :])
    grad_m = low(grad_four)
    gm_ref[...] = grad_m
    add_sum(9, grad_m)
    res_ref[...] = grad_four
    for j in range(FF // FBLOCK):
        cols = slice(j * FBLOCK, (j + 1) * FBLOCK)
        grad_u = low(dot_nt(grad_m, wdown_ref[cols, :]) * slope_ref[:, cols])
        gu_ref[:, cols] = grad_u
        add_sum(5 + j, grad_u)
        res_ref[...] += dot_nt(grad_u, wup_ref[:, cols])
    grad_h = res_ref[...]
    add_sum(3, grad_h * normal_three)
    add_sum(4, grad_h)
    grad_three = norm_pull(grad_h, normal_three, rate_three, vec_ref[3:4, :])
    grad_o = low(grad_three)
    go_ref[...] = grad_o
    add_sum(2, grad_o)
    res_ref[...] = grad_three
    att_ref[...] = low(dot_nt(grad_o, wout_ref[...]))
    for pair in range(PAIRS):
        queries = both_heads(packed_ref[:, third(0, pair)] * jnp.bfloat16(scale))
        grads = both_heads(att_ref[:, pair_cols(pair)])
        weights = weights_ref[pair]
        grad_weights = dot_nt(grads, packed_ref[:, third(2, pair)])
        dv = dot_tn(low(weights), grads)
        inner = jnp.sum(grad_weights * weights, axis=-1, keepdims=True)
        ds = low(weights * (grad_weights - inner))
        dq = dot_nn(side_by_side(ds), both_heads(packed_ref[:, third(1, pair)])) * scale
        dk = dot_tn(ds, queries)
        for part, grad in enumerate((dq, dk, dv)):
            gqkv_ref[:, third(part, pair)] = low(grad)
    add_sum(0, gqkv_ref[:, :D])
    add_sum(1, gqkv_ref[:, 2 * D :])
    for j in range(3):
        cols = slice(j * D, (j + 1) * D)
        res_ref[...] += dot_nt(gqkv_ref[:, cols], wqkv_ref[:, cols])
    grows_ref[...] = low(res_ref[...])


def cross_layer(rows, tags, grad_out, x_qkv, x_out, x_up, x_down, vec):
    m = rows.shape[0]
    bf, f32 = jnp.bfloat16, jnp.float32
    tagc = jnp.broadcast_to(tags.astype(f32)[:, None], (m, LANES))
    tagr = jnp.broadcast_to(tags.astype(f32)[None, :], (8, m))
    operands = [rows, tagc, tagr, grad_out, x_qkv, x_out, x_up, x_down, vec]
    shapes = [(m, D), (m, D), (VECTOR_ROWS, D), (m, 3 * D), (m, D), (m, FF), (m, D), (D, m), (D, m), (D, m), (FF, m)]
    return pl.pallas_call(
        cross_kernel,
        out_shape=[jax.ShapeDtypeStruct(shape, f32 if i == 2 else bf) for i, shape in enumerate(shapes)],
        in_specs=[spec_vmem()] * len(operands),
        out_specs=[spec_vmem()] * len(shapes),
        scratch_shapes=[
            pltpu.VMEM((m, 3 * D), bf),
            pltpu.VMEM((PAIRS, 2 * m, m), f32),
            pltpu.VMEM((m, D), bf),
            pltpu.VMEM((m, D), bf),
            pltpu.VMEM((m, FF), f32),
            pltpu.VMEM((m, D), f32),
        ],
        compiler_params=kernel_params(60),
    )(*operands)
AXES = ("seg", "doc")


def tie(value, *others):
    return lax.optimization_barrier((value, *others))[0]


def send(geo, value, axis, step):
    return lax.ppermute(value, AXES, geo.shift(axis, step))


def gather_axis(geo, value, axis):
    return jnp.stack([value] + [send(geo, value, axis, r) for r in range(1, geo.size(axis))])


def gather_line(geo, pieces, my_z):
    nd = geo.n_doc
    parts = [pieces] + [send(geo, pieces, Z, r) for r in range(1, nd)]
    parts = parts[::-1]
    line = jnp.stack(parts + parts[: nd - 1], axis=1)
    line = lax.dynamic_slice_in_dim(line, nd - 1 - my_z, nd, axis=1)
    return line.reshape(pieces.shape[0], nd * geo.piece, LANES)


def gather_plane(geo, halves, step):
    orders = ((X, Y), (Y, X))
    return [gather_axis(geo, half, order[step]) for half, order in zip(halves, orders)]


def gather_cores(geo, halves):
    return [array for half in halves for array in (half, send(geo, half, C, 1))]


def plus(*terms):
    return low(sum(term.astype(jnp.float32) for term in terms))


def reduce_cores(geo, arrays):
    return [(arrays[2 * half], send(geo, arrays[2 * half + 1], C, 1)) for half in range(2)]


def reduce_plane(geo, halves, step):
    orders = ((Y, X), (X, Y))
    result = []
    for half, order in zip(halves, orders):
        value = plus(*half)
        axis = order[step]
        result.append([value[0]] + [send(geo, value[r], axis, r) for r in range(1, geo.size(axis))])
    return result


def reduce_line(geo, line, my_z):
    nd = geo.n_doc
    line = line.reshape(line.shape[0], nd, geo.piece, LANES)

    def to(r):
        return lax.dynamic_index_in_dim(line, lax.rem(my_z + r, nd), axis=1, keepdims=False)

    return [to(0)] + [send(geo, to(r), Z, r) for r in range(1, nd)]


def join(halves):
    return jnp.concatenate([plus(*half) for half in halves])
def optimizer_step(gradient, master, momentum, average, scaling, rating):
    scaled = gradient * scaling
    moment = 0.5 * momentum + scaled
    weight = master - rating * (scaled + 0.5 * moment)
    smooth = 0.5 * average + 0.5 * weight
    return (weight, moment, smooth, low(weight))


def row_rates(geo, n_tokens, n_cls):
    total = geo.chunk * geo.n_dev
    scaling = np.zeros((total,), np.float32)
    rating = np.full((total,), 0.2, np.float32)
    names = list(LAYOUT)
    cross = names[-13:]
    row = 0
    for name, shape in LAYOUT.items():
        rows = math.prod(shape) // LANES
        scaling[row : row + rows] = 1.0 / math.sqrt(n_cls if name in cross else n_tokens)
        if len(shape) == 2:
            rating[row : row + rows] = 1.0 if name == cross[0] else 0.5 / math.sqrt(shape[0])
        row += rows
    return scaling.reshape(geo.n_dev, geo.chunk), rating.reshape(geo.n_dev, geo.chunk)


def matmul(left, right):
    return jnp.dot(left, right, preferred_element_type=jnp.float32)


def column_sum(rows):
    return jnp.sum(rows.astype(jnp.float32), axis=0, keepdims=True)


def local(tokens, cotangent, seg_doc, seg_pos, master, momentum, average):
    n_seg = lax.axis_size(AXES[0])
    n_doc = lax.axis_size(AXES[1])
    geo = Geometry(n_seg, n_doc, master.shape[0])
    buckets = Buckets(geo)
    my_seg, my_doc = lax.axis_index(AXES[0]), lax.axis_index(AXES[1])
    me = my_seg * n_doc + my_doc
    coords = jnp.stack([my_seg // 4, my_seg // 2 % 2, my_seg % 2, my_doc]).astype(jnp.int32)
    table = lax.dynamic_index_in_dim(
        jnp.asarray(geo.block_table().reshape(geo.n_dev, -1)), me, 0, False
    )
    pad_rows = ceil_to(geo.chunk + 4 * BLK, 8)
    padded = jnp.pad(
        master.reshape(geo.chunk, LANES), ((BLK, pad_rows - geo.chunk - BLK), (0, 0))
    )
    aligned = align_rows(geo, table, padded)
    pieces = lax.all_to_all(aligned.reshape(geo.n_dev, geo.piece, LANES), AXES, 0, 0, tiled=True)
    parts = [pieces[span.start : span.stop] for span in buckets.ranges]

    seg_count = tokens.shape[1]
    n_rows = n_seg * seg_count
    tiles_all = seg_count * SEG_LEN // TILE
    inputs = tokens[0].reshape(seg_count * SEG_LEN, D)
    cot_rows = cotangent[0]
    tags = low(jnp.stack([seg_doc[0], seg_pos[0]], axis=1).astype(jnp.float32))
    tagged = jnp.concatenate([cot_rows[:, 0], jnp.pad(tags, ((0, 0), (0, LANES - 2)))], axis=1)
    all_tagged = lax.all_gather(tie(tagged, pieces), AXES[0], axis=0, tiled=True)
    all_grad, all_doc, all_pos = all_tagged[:, :D], all_tagged[:, D], all_tagged[:, D + 1]
    pos_hot = (all_pos.astype(jnp.int32)[:, None] == jnp.arange(LONG_SEGS)[None, :]).astype(jnp.bfloat16)

    line = gather_line(geo, parts[0], my_doc)
    cut = buckets.half
    line_b = gather_line(geo, tie(parts[1], line, all_tagged), my_doc)
    plane = gather_plane(geo, [line[: cut[0]], line[cut[0] :]], 0)
    plane = gather_plane(geo, plane, 1)
    gathered = [gather_cores(geo, plane), None, None]
    line_b = tie(line_b, *plane)
    plane_b = gather_plane(geo, [line_b[: cut[1]], line_b[cut[1] :]], 0)

    def matrix(number):
        return unpack_matrix(geo, buckets, gathered, coords, item_name(number))

    def vectors(*numbers):
        return unpack_vectors(geo, buckets, gathered, coords, [item_name(i) for i in numbers])

    w_qkv = matrix(0)
    gathered[2] = [lax.all_gather(tie(parts[2], w_qkv), AXES)]
    vec_a = vectors(1)
    w_qkv = tie(w_qkv, *plane_b)
    plane_b = gather_plane(geo, plane_b, 1)
    first = max(1, tiles_all - 1)
    outs = attend_layer(inputs, w_qkv, vec_a, 0, first)
    plane_b = [tie(half, outs[0]) for half in plane_b]
    gathered[1] = gather_cores(geo, plane_b)
    if first < tiles_all:
        outs = attend_layer(tie(inputs, *plane_b), w_qkv, vec_a, first, tiles_all - first, outs)
    packed, attended, stat = outs

    w_out, w_up, w_down, vec = matrix(2), matrix(4), matrix(6), vectors(1, 3, 5, 7)
    hidden_low, normal_one, active, slope, normal_two, rates, hidden_two, cls = feed_layer(
        inputs, attended, w_out, w_up, w_down, vec
    )

    cross = [matrix(i) for i in (8, 9, 11, 13, 15)]
    xvec = vectors(10, 12, 14, 16)

    def own(values):
        return lax.dynamic_slice_in_dim(values, my_seg * seg_count, seg_count, axis=0)

    cls_low = low(cls + matmul(own(pos_hot), cross[0]))
    rows = lax.all_gather(cls_low, AXES[0], axis=0, tiled=True)
    crossed, grad_rows, xsums, g_qkv, g_o, g_u, g_m, rows_t, att_t, hid_t, act_t = cross_layer(
        rows, all_doc, all_grad, *cross[1:], xvec
    )
    first_row = lax.broadcasted_iota(jnp.int32, (seg_count, SEG_LEN, D), 1) == 0
    mixed_out = jnp.where(
        first_row, own(crossed)[:, None, :], hidden_two.reshape(seg_count, SEG_LEN, D)
    )
    names = [item_name(i) for i in (8, 9, 11, 13, 15)]
    line_c = pack_cross(
        geo,
        buckets.ranges[2],
        dict(zip(names, (pos_hot.T, rows_t, att_t, hid_t, act_t))),
        dict(zip(names, (grad_rows, g_qkv, g_o, g_u, g_m))),
        {item_name(i): (xsums, row) for i, row in ((10, 0), (12, 2), (14, 5), (16, 9))},
        my_seg.astype(jnp.int32).reshape(1),
    )
    line_c_parts = reduce_line(geo, line_c, my_doc)

    grads = {}
    dm, du, dao, da, grad_one, sums = feed_back(
        cot_rows.reshape(-1, D), tie(own(grad_rows).astype(jnp.float32), line_c), normal_two,
        slope, normal_one, rates, w_down, w_up, w_out, vec,
    )
    grads[item_name(4)] = low(matmul(hidden_low.T, du))
    grads[item_name(6)] = low(matmul(active.T, dm))
    grads[item_name(2)] = low(matmul(attended.T, dao))
    grads[item_name(8)] = low(matmul(own(pos_hot).T, own(grad_rows)))
    grads[item_name(3)] = (sums, 2)
    grads[item_name(5)] = (sums, 5)
    grads[item_name(7)] = (sums, 9)
    halves = reduce_cores(geo, pack_bucket(geo, buckets, 1, grads, coords))
    pieces_c = plus(*[tie(part, sums) for part in line_c_parts])
    da = tie(da, halves[0][0])
    back = attend_back(packed, stat, da, 0, 1)
    halves = [[tie(v, back[0]) for v in half] for half in halves]
    halves = reduce_plane(geo, halves, 0)
    if tiles_all > 1:
        da = tie(da, halves[0][0], halves[1][0])
        back = attend_back(packed, stat, da, 1, tiles_all - 1, back)
    dqkv, qv_sums = back
    halves = [[tie(v, dqkv) for v in half] for half in halves]
    halves = reduce_plane(geo, halves, 1)
    dqkv = tie(dqkv, halves[0][0], halves[1][0])
    grads[item_name(0)] = low(matmul(inputs.T, dqkv))
    grads[item_name(1)] = (qv_sums, 0)
    halves = [[tie(v, grads[item_name(0)]) for v in half] for half in halves]
    line_b_parts = reduce_line(geo, join(halves), my_doc)
    grads[item_name(0)] = tie(grads[item_name(0)], line_b_parts[0])
    halves = reduce_cores(geo, pack_bucket(geo, buckets, 0, grads, coords))
    halves = reduce_plane(geo, halves, 0)
    dqkv = tie(dqkv, halves[0][0], halves[1][0])
    token_grad = low(grad_one + matmul(dqkv, w_qkv.T))
    halves = [[tie(v, token_grad) for v in half] for half in halves]
    halves = reduce_plane(geo, halves, 1)
    pieces_b = plus(*line_b_parts)
    pieces_a = plus(*reduce_line(geo, join(halves), my_doc))

    owned = lax.all_to_all(jnp.concatenate([pieces_a, pieces_b, pieces_c]), AXES, 0, 0, tiled=True)
    natural = natural_rows(geo, table, owned.reshape(-1, LANES), pad_rows)
    gradient = natural[BLK : BLK + geo.chunk].reshape(-1)
    n_cls = n_doc * n_rows
    scaling, rating = (
        jnp.broadcast_to(
            lax.dynamic_index_in_dim(jnp.asarray(rates), me, 0, False)[:, None], (geo.chunk, LANES)
        ).reshape(-1)
        for rates in row_rates(geo, n_cls * SEG_LEN, n_cls)
    )
    weight, moment, smooth, copy_low = optimizer_step(
        gradient, master, momentum, average, scaling, rating
    )
    return (
        mixed_out[None],
        token_grad.reshape(1, seg_count, SEG_LEN, D),
        weight,
        moment,
        smooth,
        copy_low,
    )


def item_name(number):
    return item_list(0)[number].name


def solution(mesh):
    layer = P(AXES[1], AXES[0], None, None)
    ids = P(AXES[1], AXES[0])
    flat = P(AXES)
    return jax.shard_map(
        local,
        mesh=mesh,
        in_specs=(layer, layer, ids, ids, flat, flat, flat),
        out_specs=(layer, layer, flat, flat, flat, flat),
        check_vma=False,
    )
```

```python
import math
from types import SimpleNamespace

import jax
import jax.numpy as jnp
import numpy as np
from jax import lax
from jax.experimental import pallas as pl
from jax.experimental.pallas import tpu as pltpu
from jax.sharding import PartitionSpec as P

D = 768
HEADS = 12
HEAD_DIM = 64
FF = 3072
SEG_LEN = 128
LONG_SEGS = 64
EPSILON = 1e-05
NEGATIVE = -1e30

LAYOUT = dict(
    w_qkv=(D, 3 * D),
    b_qv=(2 * D,),
    w_out=(D, D),
    b_out=(D,),
    gain_one=(D,),
    bias_one=(D,),
    w_up=(D, FF),
    b_up=(FF,),
    w_down=(FF, D),
    b_down=(D,),
    gain_two=(D,),
    bias_two=(D,),
    pos_table=(LONG_SEGS, D),
    x_qkv=(D, 3 * D),
    x_bqv=(2 * D,),
    x_out=(D, D),
    x_bout=(D,),
    gain_three=(D,),
    bias_three=(D,),
    x_up=(D, FF),
    x_bup=(FF,),
    x_down=(FF, D),
    x_bdown=(D,),
    gain_four=(D,),
    bias_four=(D,),
)
LANES = 128
BLK = 16
Y, X, C, Z = range(4)


def ceil_to(value, step):
    return -(-value // step) * step


def item_list(total_rows):
    items = []
    nat = 0
    for name, shape in LAYOUT.items():
        rows = math.prod(shape) // LANES
        if len(shape) == 1 and items and len(items[-1].shape) == 1:
            items[-1].names.append(name)
            items[-1].rows += rows
        else:
            items.append(SimpleNamespace(name=name, names=[name], shape=shape, nat=nat, rows=rows))
        nat += rows
    items.append(SimpleNamespace(name=None, names=[], shape=None, nat=nat, rows=total_rows - nat))
    blk = 0
    for item in items:
        item.cols = item.shape[1] // LANES if item.shape and len(item.shape) == 2 else 0
        item.blk = blk
        blk += ceil_to(item.rows, BLK) // BLK
    return items


class Geometry:
    def __init__(self, n_seg, n_doc, shard_len):
        self.n_seg, self.n_doc = n_seg, n_doc
        self.n_dev = n_seg * n_doc
        self.chunk = shard_len // LANES
        self.items = item_list(self.chunk * self.n_dev)
        self.by_name = SimpleNamespace(**{item.name: item for item in self.items if item.name})
        firsts, lasts = [], []
        for n in range(self.n_dev):
            lo, hi = n * self.chunk, (n + 1) * self.chunk
            blocks = []
            for item in self.items:
                a, b = max(lo, item.nat), min(hi, item.nat + item.rows)
                if a < b:
                    blocks.append(item.blk + (a - item.nat) // BLK)
                    blocks.append(item.blk + (b - 1 - item.nat) // BLK)
            firsts.append(min(blocks))
            lasts.append(max(blocks))
        self.first, self.last = firsts, lasts
        most = max(b - a + 1 for a, b in zip(firsts, lasts))
        self.piece_blocks = -(-most // self.n_dev)
        self.piece = self.piece_blocks * BLK
        self.slots = self.piece_blocks * self.n_dev
        self.groups = -(-most // (self.piece_blocks * n_doc))
        self.staged_rows = self.groups * n_doc * self.piece
        self.c_size, self.x_size = 2, 2
        self.y_size = n_seg // 4

    def full_groups(self, item, chunk):
        rows = BLK * item.cols
        lo, hi = chunk * self.chunk - item.nat, (chunk + 1) * self.chunk - item.nat
        first, last = max(0, -(-lo // rows)), min(item.rows, hi) // rows
        return first, max(first, last)

    def block_tables(self):
        matrices = [item for item in self.items if item.cols]
        single = [[] for _ in range(self.n_dev)]
        groups = np.zeros((self.n_dev, len(matrices), 3), np.int32)
        for n in range(self.n_dev):
            lo, hi = n * self.chunk, (n + 1) * self.chunk
            for t in range(self.slots):
                b = self.first[n] + t
                if b > self.last[n]:
                    single[n].append((t, 0, 0, 0))
                    continue
                item = [it for it in self.items if it.blk <= b][-1]
                at = b - item.blk
                if item.cols:
                    first, last = self.full_groups(item, n)
                    if first <= at // item.cols < last:
                        continue
                start = item.nat + at * BLK
                a = max(start, lo)
                z = max(a, min(start + BLK, hi, item.nat + item.rows))
                single[n].append((t, start - lo, a - start, z - start))
            for i, item in enumerate(matrices):
                first, last = self.full_groups(item, n)
                if first < last:
                    slot = item.blk + first * item.cols - self.first[n]
                    groups[n, i] = (slot, item.nat + first * BLK * item.cols - lo, last - first)
        most = max(len(rows) for rows in single)
        table = np.zeros((self.n_dev, 1 + 4 * most), np.int32)
        for n, rows in enumerate(single):
            table[n, 0] = len(rows)
            table[n, 1 : 1 + 4 * len(rows)] = np.asarray(rows, np.int32).reshape(-1)
        return matrices, np.concatenate([groups.reshape(self.n_dev, -1), table], axis=1)

    def chunks_of(self, item):
        found = []
        n_blocks = ceil_to(item.rows, BLK) // BLK
        for n in range(self.n_dev):
            a = max(item.blk, self.first[n])
            b = min(item.blk + n_blocks, self.last[n] + 1)
            if a < b:
                found.append((n, a - item.blk, b - item.blk, a - self.first[n]))
        return found

    def spans(self, *ends):
        cuts = [0] + [(end.nat - 1) // self.chunk + 1 for end in ends] + [self.n_dev]
        return [range(a, b) for a, b in zip(cuts, cuts[1:])]

    def coords(self, device):
        seg, doc = divmod(device, self.n_doc)
        yx, c = divmod(seg, self.c_size)
        return [*divmod(yx, self.x_size), c, doc]

    def device(self, y, x, c, z):
        return ((y * self.x_size + x) * self.c_size + c) * self.n_doc + z

    def size(self, axis):
        return (self.y_size, self.x_size, self.c_size, self.n_doc)[axis]

    def shift(self, axis, step):
        pairs = []
        for source in range(self.n_dev):
            at = self.coords(source)
            at[axis] = (at[axis] + step) % self.size(axis)
            pairs.append((source, self.device(*at)))
        return pairs
def spec_vmem():
    return pl.BlockSpec(memory_space=pltpu.VMEM)


def spec_any():
    return pl.BlockSpec(memory_space=pl.ANY)


def spec_smem():
    return pl.BlockSpec(memory_space=pltpu.SMEM)


def kernel_params(mib=56):
    return pltpu.CompilerParams(vmem_limit_bytes=mib * 1024 * 1024)


def cost(micros):
    return pl.CostEstimate(flops=int(micros * 1e9), bytes_accessed=int(micros * 3e6), transcendentals=0)


def row_mask(low, high):
    rows = lax.broadcasted_iota(jnp.int32, (BLK, LANES), 0)
    return (rows >= low) & (rows < high)


def block_moves(geo, table_ref, by_group, by_row):
    matrices = geo.block_tables()[0]
    for i, item in enumerate(matrices):
        def body(g, carry, i=i, cols=item.cols):
            for cb in range(cols):
                by_group(table_ref[3 * i] + g * cols + cb, table_ref[3 * i + 1] + g * BLK * cols + cb, cols)
            return carry

        lax.fori_loop(0, table_ref[3 * i + 2], body, 0)
    base = 3 * len(matrices)

    def single(r, carry):
        by_row(*[table_ref[base + 1 + 4 * r + j] for j in range(4)])
        return carry

    lax.fori_loop(0, table_ref[base], single, 0)


def block_at(slot):
    return pl.ds(pl.multiple_of(slot * BLK, BLK), BLK)


def align_rows(geo, table, padded):
    def kernel(table_ref, rows_ref, out_ref):
        def by_group(slot, start, cols):
            out_ref[block_at(slot), :] = rows_ref[pl.ds(start + BLK, BLK, stride=cols), :].astype(jnp.bfloat16)

        def by_row(slot, start, low_row, high_row):
            rows = jnp.where(row_mask(low_row, high_row), rows_ref[pl.ds(start + BLK, BLK), :], 0.0)
            out_ref[block_at(slot), :] = rows.astype(jnp.bfloat16)

        block_moves(geo, table_ref, by_group, by_row)

    return pl.pallas_call(
        kernel,
        out_shape=jax.ShapeDtypeStruct((geo.slots * BLK, LANES), jnp.bfloat16),
        in_specs=[spec_smem(), spec_vmem()],
        out_specs=spec_vmem(),
        compiler_params=kernel_params(),
        cost_estimate=cost(3),
    )(table, padded)


def natural_rows(geo, table, blocks, pad_rows):
    def kernel(table_ref, blocks_ref, out_ref):
        def by_group(slot, start, cols):
            out_ref[pl.ds(start + BLK, BLK, stride=cols), :] = blocks_ref[block_at(slot), :].astype(jnp.float32)

        def by_row(slot, start, low_row, high_row):
            here = pl.ds(start + BLK, BLK)
            rows = blocks_ref[block_at(slot), :].astype(jnp.float32)
            out_ref[here, :] = jnp.where(row_mask(low_row, high_row), rows, out_ref[here, :])

        block_moves(geo, table_ref, by_group, by_row)

    return pl.pallas_call(
        kernel,
        out_shape=jax.ShapeDtypeStruct((pad_rows, LANES), jnp.float32),
        in_specs=[spec_smem(), spec_vmem()],
        out_specs=spec_vmem(),
        compiler_params=kernel_params(),
        cost_estimate=cost(3),
    )(table, blocks)


class Buckets:
    def __init__(self, geo, arrays, *ends):
        self.geo = geo
        self.ranges = geo.spans(*ends)
        self.arrays = arrays
        self.half = [(len(r) + 1) // 2 for r in self.ranges]

    def find(self, chunk):
        for number, span in enumerate(self.ranges):
            if chunk in span:
                at = chunk - span.start
                cut = self.half[number]
                return (number, 0, at) if at < cut else (number, 1, at - cut)

    def shapes(self, number):
        geo = self.geo
        cut = self.half[number]
        rest = len(self.ranges[number]) - cut
        rows = geo.n_doc * geo.piece
        return [
            (geo.y_size, geo.x_size, cut, rows, LANES),
            (geo.x_size, geo.y_size, rest, rows, LANES),
        ]


def wrap(value, size):
    return lax.rem(value + size, size)


def copy_rows(count, step, body):
    full = count // step
    if full:
        def loop(i, carry):
            body(i * step, step)
            return carry

        lax.fori_loop(0, full, loop, 0)
    if count % step:
        body(full * step, count % step)


def place_line(geo, parts, my_z, cut):
    n, nd = parts[0].shape[0], geo.n_doc
    counts = [cut, n - cut]

    def kernel(z_ref, *refs):
        sources, outs = refs[:nd], refs[nd:]
        for r in range(nd):
            z = wrap(z_ref[0] - r, nd)
            rows = pl.ds(pl.multiple_of(z * geo.piece, BLK), geo.piece)
            for i in range(n):
                target = outs[0].at[i] if i < cut else outs[1].at[i - cut]
                target[rows, :] = sources[r][i]

    return pl.pallas_call(
        kernel,
        out_shape=[jax.ShapeDtypeStruct((c, nd * geo.piece, LANES), jnp.bfloat16) for c in counts],
        in_specs=[spec_smem()] + [spec_vmem()] * nd,
        out_specs=[spec_vmem()] * 2,
        compiler_params=kernel_params(),
        cost_estimate=cost(2),
    )(my_z.reshape(1), *parts)


def class_tags(cot, doc, pos):
    count = cot.shape[0]

    def kernel(doc_ref, pos_ref, cot_ref, out_ref):
        lanes = lax.broadcasted_iota(jnp.int32, (1, LANES), 1)
        for s in range(count):
            out_ref[s : s + 1, :D] = cot_ref[s, 0:1, :].astype(jnp.float32)
            tag = jnp.where(lanes == 0, doc_ref[s], jnp.where(lanes == 1, pos_ref[s], 0))
            out_ref[s : s + 1, D:] = tag.astype(jnp.float32)

    return pl.pallas_call(
        kernel,
        grid=(1,),
        out_shape=jax.ShapeDtypeStruct((count, D + LANES), jnp.float32),
        in_specs=[spec_smem(), spec_smem(), pl.BlockSpec((count, BLK, D), lambda i: (0, 0, 0))],
        out_specs=pl.BlockSpec((count, D + LANES), lambda i: (0, 0)),
        compiler_params=kernel_params(),
        cost_estimate=cost(2),
    )(doc, pos, cot)
VECTOR_ROWS = 16


def chunk_copies(geo, buckets, sources, used, coords_ref, n, staged, sem):
    my_y, my_x, my_c = coords_ref[0], coords_ref[1], coords_ref[2]
    number, half, place = buckets.find(n)
    first = sum(buckets.arrays[m] for m in used[: used.index(number)])
    if buckets.arrays[number] == 1:
        for device in range(geo.groups * geo.n_doc):
            pltpu.make_async_copy(
                sources[first].at[device, n - buckets.ranges[number].start],
                staged.at[pl.ds(device * geo.piece, geo.piece)],
                sem,
            ).start()
        return
    rows = geo.n_doc * geo.piece
    for core in range(2):
        c = my_c if core == 0 else 1 - my_c
        for ry in range(geo.y_size):
            for rx in range(geo.x_size):
                y, x = wrap(my_y - ry, geo.y_size), wrap(my_x - rx, geo.x_size)
                s = (y * geo.x_size + x) * 2 + c
                index = (ry, rx, place) if half == 0 else (rx, ry, place)

                def begin(s=s, index=index, core=core):
                    pltpu.make_async_copy(
                        sources[first + 2 * half + core].at[index],
                        staged.at[pl.ds(pl.multiple_of(s * rows, BLK), rows)],
                        sem,
                    ).start()

                if geo.groups == geo.n_seg:
                    begin()
                else:
                    pl.when(s < geo.groups)(begin)


class Weights:
    def __init__(self, geo, buckets, gathered, names):
        self.geo, self.buckets = geo, buckets
        self.items = [vars(geo.by_name)[name] for name in names]
        self.chunks = sorted({n for item in self.items for n, *_ in geo.chunks_of(item)})
        self.used = sorted({buckets.find(n)[0] for n in self.chunks})
        self.operands = [array for number in self.used for array in gathered[number]]
        cols = max([item.cols for item in self.items])
        self.scratch = [
            pltpu.VMEM((len(self.chunks), geo.staged_rows, LANES), jnp.bfloat16),
            pltpu.VMEM((BLK * (cols + 2), LANES), jnp.float32),
            pltpu.SemaphoreType.DMA((len(self.chunks),)),
        ]

    def start(self, coords_ref, sources, staged, sems):
        for at, n in enumerate(self.chunks):
            chunk_copies(
                self.geo, self.buckets, sources, self.used, coords_ref, n, staged.at[at], sems.at[at]
            )

    def wait(self, number, waited, staged, sems):
        for n, *_ in self.geo.chunks_of(self.items[number]):
            at = self.chunks.index(n)
            if at not in waited:
                waited.add(at)
                pltpu.make_async_copy(staged.at[at], staged.at[at], sems.at[at]).wait()

    def blocks(self, item, lo, hi, staged, wide):
        done = lo
        for n, b0, b1, slot in self.geo.chunks_of(item):
            for b in range(max(b0, lo), min(b1, hi)):
                at = self.chunks.index(n)
                rows = staged[at, pl.ds((slot + b - b0) * BLK, BLK), :].astype(jnp.float32)
                here = pl.ds((b - lo) * BLK, BLK)
                wide[here, :] = wide[here, :] + rows if b < done else rows
            done = max(done, min(b1, hi))

    def matrix(self, number, staged, wide, out_ref):
        item = self.items[number]
        cols = item.cols
        split = set()
        for n, b0, b1, slot in self.geo.chunks_of(item):
            at = self.chunks.index(n)
            first, last = self.geo.full_groups(item, n)
            split |= set(range(b0 // cols, -(-b1 // cols))) - set(range(first, last))

            def group(g, carry, at=at, shift=slot - b0):
                rows = pl.ds(pl.multiple_of(g * BLK, BLK), BLK)
                for cb in range(cols):
                    tile = staged[at, block_at(g * cols + cb + shift), :]
                    out_ref[rows, cb * LANES : (cb + 1) * LANES] = tile
                return carry

            lax.fori_loop(first, last, group, 0)
        for g in sorted(split):
            self.blocks(item, g * cols, (g + 1) * cols, staged, wide)
            for cb in range(cols):
                tile = wide[pl.ds(cb, BLK, stride=cols), :]
                out_ref[g * BLK : (g + 1) * BLK, cb * LANES : (cb + 1) * LANES] = tile.astype(jnp.bfloat16)

    def vectors(self, number, staged, wide, out_ref, row):
        item = self.items[number]
        self.blocks(item, 0, ceil_to(item.rows, BLK) // BLK, staged, wide)
        for r in range(item.rows):
            v, cb = divmod(r, D // LANES)
            out_ref[row + v : row + v + 1, cb * LANES : (cb + 1) * LANES] = wide[r : r + 1, :]


def vector_rows(wide, values, first, count):
    lane_cols = D // LANES
    for r in range(count):
        v, cb = divmod(r, lane_cols)
        wide[r : r + 1, :] = values[first + v : first + v + 1, cb * LANES : (cb + 1) * LANES]


def bucket_parts(geo, span):
    parts = []
    for item in geo.items:
        chunks = [entry for entry in geo.chunks_of(item) if entry[0] in span]
        if chunks and item.names:
            parts.append((item, chunks))
    return parts


def pack_bucket(geo, buckets, number, grads, coords):
    span = buckets.ranges[number]
    seg_rows = geo.n_doc * geo.piece
    parts = bucket_parts(geo, span)
    operands, specs, windows, scratch = [], [], [], []
    wide_rows = BLK
    for item, chunks in parts:
        if len(item.shape) == 2:
            cols = item.shape[1] // LANES
            k0 = min(b0 for _, b0, _, _ in chunks) // cols
            k1 = -(-max(b1 for _, _, b1, _ in chunks) // cols)
            operands.append(grads[item.name])
            specs.append(spec_any())
            windows.append((cols, k0, k1))
            scratch.append(pltpu.VMEM(((k1 - k0) * BLK, item.shape[1]), jnp.bfloat16))
            wide_rows = max(wide_rows, BLK * cols)
        else:
            wide_rows = max(wide_rows, ceil_to(item.rows, BLK))
            operands.append(grads[item.name][0])
            specs.append(spec_vmem())
            windows.append(None)
            scratch.append(pltpu.VMEM((BLK, LANES), jnp.bfloat16))
    outs = [shape for shape in buckets.shapes(number) for _ in range(2)]

    def kernel(coords_ref, *refs):
        sources = refs[: len(parts)]
        targets = refs[len(parts) : len(parts) + 4]
        loaded = refs[len(parts) + 4 : 2 * len(parts) + 4]
        staged, wide, in_sems, out_sems = refs[2 * len(parts) + 4 :]
        my_y, my_x, my_c = coords_ref[0], coords_ref[1], coords_ref[2]
        loads = {}
        for at, window in enumerate(windows):
            if window is not None:
                source = sources[at].at[pl.ds(window[1] * BLK, (window[2] - window[1]) * BLK)]
                loads[at] = pltpu.make_async_copy(source, loaded[at], in_sems.at[at])
                loads[at].start()

        def clear(row, rows):
            for at in range(len(span)):
                here = pl.ds(pl.multiple_of(row, BLK), rows)
                staged[at, here, :] = jnp.zeros((rows, LANES), jnp.bfloat16)

        tail = min(geo.last[n] - geo.first[n] for n in span) * BLK
        copy_rows(geo.slots * BLK - tail, 128, lambda row, rows: clear(row + tail, rows))

        def send_out(n):
            _, half, place = buckets.find(n)
            for core in range(2):
                c = my_c if core == 0 else 1 - my_c
                for ry in range(geo.y_size):
                    for rx in range(geo.x_size):
                        y, x = wrap(my_y + ry, geo.y_size), wrap(my_x + rx, geo.x_size)
                        s = (y * geo.x_size + x) * 2 + c
                        index = (ry, rx, place) if half == 0 else (rx, ry, place)
                        pltpu.make_async_copy(
                            staged.at[n - span.start, pl.ds(pl.multiple_of(s * seg_rows, BLK), seg_rows)],
                            targets[2 * half + core].at[index],
                            out_sems.at[n - span.start],
                        ).start()

        last_part = {n: at for at, (_, chunks) in enumerate(parts) for n, *_ in chunks}
        for at, ((item, chunks), window) in enumerate(zip(parts, windows)):
            if window is None:
                vector_rows(wide, sources[at], grads[item.name][1], item.rows)
                for n, b0, b1, slot in chunks:
                    rows = wide[pl.ds(b0 * BLK, (b1 - b0) * BLK), :].astype(jnp.bfloat16)
                    staged[n - span.start, pl.ds(slot * BLK, (b1 - b0) * BLK), :] = rows
            else:
                loads[at].wait()
                cols, k0, k1 = window
                values = loaded[at]
                split = set()
                for n, b0, b1, slot in chunks:
                    first, last = geo.full_groups(item, n)
                    split |= set(range(b0 // cols, -(-b1 // cols))) - set(range(first, last))

                    def group(g, carry, n=n, shift=slot - b0, k0=k0, cols=cols, values=values):
                        rows = pl.ds(pl.multiple_of((g - k0) * BLK, BLK), BLK)
                        for cb in range(cols):
                            dst = pl.ds(pl.multiple_of((g * cols + cb + shift) * BLK, BLK), BLK)
                            staged[n - span.start, dst, :] = values[rows, cb * LANES : (cb + 1) * LANES]
                        return carry

                    lax.fori_loop(first, last, group, 0)
                for g in sorted(split):
                    for cb in range(cols):
                        tile = values[(g - k0) * BLK : (g - k0 + 1) * BLK, cb * LANES : (cb + 1) * LANES]
                        wide[pl.ds(cb, BLK, stride=cols), :] = tile.astype(jnp.float32)
                    for n, b0, b1, slot in chunks:
                        first, last = geo.full_groups(item, n)
                        lo, hi = max(b0, g * cols), min(b1, (g + 1) * cols)
                        if lo < hi and not first <= g < last:
                            rows = wide[pl.ds((lo - g * cols) * BLK, (hi - lo) * BLK), :]
                            dst = pl.ds((slot + lo - b0) * BLK, (hi - lo) * BLK)
                            staged[n - span.start, dst, :] = rows.astype(jnp.bfloat16)
            for n, *_ in chunks:
                if last_part[n] == at:
                    send_out(n)
        for n in span:
            at = n - span.start
            pltpu.make_async_copy(staged.at[at], staged.at[at], out_sems.at[at]).wait()

    return pl.pallas_call(
        kernel,
        out_shape=[jax.ShapeDtypeStruct(shape, jnp.bfloat16) for shape in outs],
        in_specs=[spec_smem()] + specs,
        out_specs=[spec_any()] * 4,
        scratch_shapes=scratch
        + [
            pltpu.VMEM((len(span), geo.slots * BLK, LANES), jnp.bfloat16),
            pltpu.VMEM((wide_rows + 2 * BLK, LANES), jnp.float32),
            pltpu.SemaphoreType.DMA((len(parts),)),
            pltpu.SemaphoreType.DMA((len(span),)),
        ],
        compiler_params=kernel_params(),
        cost_estimate=cost(7),
    )(coords, *operands)


def pack_cross(geo, span, lefts, rights, vectors, seg):
    seg_blocks = geo.n_doc * geo.piece_blocks
    parts = bucket_parts(geo, span)
    names = list(lefts)
    vector_names = list(vectors)
    depth_rows = next(iter(rights.values())).shape[0]

    def window(cols):
        return (-(-(seg_blocks - 1) // cols) + 1) * BLK

    wide_rows = 0
    left_rows = BLK
    for item, chunks in parts:
        if len(item.shape) == 2:
            cols = item.shape[1] // LANES
            size = min(window(cols), item.shape[0])
            left_rows = max(left_rows, len(chunks) * size)
            wide_rows = max(wide_rows, len(chunks) * size * cols)

    def kernel(seg_ref, *refs):
        left = dict(zip(names, refs[: len(names)]))
        right = dict(zip(names, refs[len(names) : 2 * len(names)]))
        vector = dict(zip(vector_names, refs[2 * len(names) : 2 * len(names) + len(vector_names)]))
        out_ref, gathered, wide = refs[2 * len(names) + len(vector_names) :]
        low_slot = seg_ref[0] * seg_blocks
        out_ref[...] = jnp.zeros_like(out_ref)
        for item, chunks in parts:
            starts, size, cols = [], 0, 1
            if len(item.shape) == 2:
                cols = item.shape[1] // LANES
                size = min(window(cols), item.shape[0])
                for at, (n, b0, b1, slot) in enumerate(chunks):
                    first = jnp.maximum(low_slot, slot) - slot + b0
                    start = jnp.clip(first // cols * BLK, 0, item.shape[0] - size)
                    start = pl.multiple_of(start, BLK)
                    starts.append(start)
                    gathered[at * size : (at + 1) * size, :] = left[item.name][pl.ds(start, size), :]
                count = len(chunks) * size
                rows = gathered[:count, :]
                for cb in range(0, cols, 2):
                    tile = dot_nn(rows, right[item.name][:, cb * LANES : (cb + 2) * LANES])
                    wide[pl.ds(cb, count, stride=cols), :] = tile[:, :LANES]
                    wide[pl.ds(cb + 1, count, stride=cols), :] = tile[:, LANES:]
            else:
                vector_rows(wide, vector[item.name], vectors[item.name][1], item.rows)
            for at, (n, b0, b1, slot) in enumerate(chunks):
                begin = jnp.maximum(low_slot, slot)
                end = jnp.minimum(low_slot + seg_blocks, slot + b1 - b0)
                base = (at * size - starts[at]) * cols if starts else 0

                first, last = geo.full_groups(item, n) if starts else (0, 0)

                def by_row(t, carry, n=n, b0=b0, slot=slot, base=base):
                    src = pl.ds((b0 + t - slot) * BLK + base, BLK)
                    dst = pl.ds(pl.multiple_of((t - low_slot) * BLK, BLK), BLK)
                    out_ref[n - span.start, dst, :] = wide[src, :].astype(jnp.bfloat16)
                    return carry

                def by_tile(t, carry, n=n, b0=b0, slot=slot, base=base, cols=cols):
                    b = b0 + t - slot
                    group = b // cols
                    src = pl.ds(group * BLK * cols + b - group * cols + base, BLK, stride=cols)
                    dst = pl.ds(pl.multiple_of((t - low_slot) * BLK, BLK), BLK)
                    out_ref[n - span.start, dst, :] = wide[src, :].astype(jnp.bfloat16)
                    return carry

                if first < last:
                    lo = jnp.clip(slot + first * cols - b0, begin, jnp.maximum(begin, end))
                    hi = jnp.clip(slot + last * cols - b0, begin, jnp.maximum(begin, end))
                    lax.fori_loop(begin, lo, by_row, 0)
                    lax.fori_loop(lo, hi, by_tile, 0)
                    lax.fori_loop(hi, jnp.maximum(hi, end), by_row, 0)
                else:
                    lax.fori_loop(begin, jnp.maximum(begin, end), by_row, 0)

    operands = [lefts[n] for n in names] + [rights[n] for n in names]
    operands += [vectors[n][0] for n in vector_names]
    return pl.pallas_call(
        kernel,
        out_shape=jax.ShapeDtypeStruct((len(span), seg_blocks * BLK, LANES), jnp.bfloat16),
        in_specs=[spec_smem()] + [spec_vmem()] * len(operands),
        out_specs=spec_vmem(),
        scratch_shapes=[
            pltpu.VMEM((left_rows, depth_rows), jnp.bfloat16),
            pltpu.VMEM((wide_rows + 2 * BLK, LANES), jnp.float32),
        ],
        compiler_params=kernel_params(),
        cost_estimate=cost(12),
    )(seg, *operands)
TILE = 512
PAIRS = HEADS // 2
TAIL_RATE = 0.3
TAIL = (
    0.11962929605681312,
    0.12075400207853171,
    0.0999131861559567,
    0.12856268365589474,
    -0.05368570534984477,
    0.20635578836359286,
    -0.15720441932045734,
    0.0356750954846771,
)


def dot_nn(left, right):
    return lax.dot_general(left, right, (((1,), (0,)), ((), ())), preferred_element_type=jnp.float32)


def dot_nt(left, right):
    return lax.dot_general(left, right, (((1,), (1,)), ((), ())), preferred_element_type=jnp.float32)


def dot_tn(left, right):
    return lax.dot_general(left, right, (((0,), (0,)), ((), ())), preferred_element_type=jnp.float32)


def low(values):
    return values.astype(jnp.bfloat16)


def gelu_pair(u):
    t = 1.0 / (1.0 + TAIL_RATE * jnp.abs(u))
    poly = TAIL[-1] * t + TAIL[-2]
    for coef in TAIL[-3::-1]:
        poly = poly * t + coef
    bell = jnp.exp(-0.5 * (u * u))
    tail = bell * (poly * t)
    spread = jnp.where(u < 0.0, tail, 1.0 - tail)
    return u * spread, spread + u * bell * (1.0 / math.sqrt(2.0 * math.pi))


def norm_rows(values, gain, shift):
    center = values - jnp.mean(values, axis=-1, keepdims=True)
    rate = lax.rsqrt(jnp.mean(center * center, axis=-1, keepdims=True) + EPSILON)
    normal = center * rate
    return normal * gain + shift, normal, rate


def norm_pull(grad, normal, rate, gain):
    scaled = grad * gain
    return rate * (
        scaled
        - jnp.mean(scaled, axis=-1, keepdims=True)
        - normal * jnp.mean(scaled * normal, axis=-1, keepdims=True)
    )


def fixed(shape):
    return pl.BlockSpec(shape, lambda i: (0,) * len(shape), pipeline_mode=pl.Buffered(1))


def tiles(cols, first=0):
    return pl.BlockSpec((TILE, cols), lambda i: (i + first, 0))


def both_heads(values):
    first = lax.broadcasted_iota(jnp.int32, values.shape, 1) < HEAD_DIM
    zero = jnp.zeros_like(values)
    return jnp.concatenate([jnp.where(first, values, zero), jnp.where(first, zero, values)], axis=0)


def side_by_side(stacked):
    half = stacked.shape[0] // 2
    return jnp.concatenate([stacked[:half], stacked[half:]], axis=1)


def third(part, pair):
    start = part * D + pair * LANES
    return slice(start, start + LANES)


def attend_kernel(x_ref, wqkv_ref, vec_ref, packed_ref, att_ref, stat_ref):
    x = x_ref[...]
    for j in range(3):
        cols = slice(j * D, (j + 1) * D)
        part = dot_nn(x, wqkv_ref[:, cols])
        packed_ref[:, cols] = low(part if j == 1 else part + vec_ref[j // 2 : j // 2 + 1, :])
    lanes = lax.broadcasted_iota(jnp.int32, (SEG_LEN, LANES), 1)

    def segment(s, carry):
        rows = pl.ds(pl.multiple_of(s * SEG_LEN, SEG_LEN), SEG_LEN)
        stat = jnp.zeros((SEG_LEN, LANES), jnp.float32)
        for pair in range(PAIRS):
            q = packed_ref[rows, third(0, pair)] * jnp.bfloat16(HEAD_DIM**-0.5)
            k = packed_ref[rows, third(1, pair)]
            v = packed_ref[rows, third(2, pair)]
            scores = dot_nt(both_heads(q), k)
            largest = jnp.max(scores, axis=-1, keepdims=True)
            raised = jnp.exp(scores - largest)
            summed = jnp.sum(raised, axis=-1, keepdims=True)
            weights = low(raised / summed)
            att_ref[rows, pair * LANES : (pair + 1) * LANES] = low(
                dot_nn(side_by_side(weights), both_heads(v))
            )
            log_sum = largest + jnp.log(summed)
            stat = jnp.where(lanes == 2 * pair, log_sum[:SEG_LEN], stat)
            stat = jnp.where(lanes == 2 * pair + 1, log_sum[SEG_LEN:], stat)
        stat_ref[rows, :] = stat
        return carry

    lax.fori_loop(0, TILE // SEG_LEN, segment, 0)


def in_parts(kernel, micros, count, inputs, in_specs, outs, out_specs, scratch, previous):
    previous = list(previous or ())
    return pl.pallas_call(
        kernel,
        grid=(count,),
        in_specs=in_specs + [spec_any()] * len(previous),
        out_specs=out_specs,
        out_shape=outs,
        scratch_shapes=scratch,
        input_output_aliases={len(inputs) + i: i for i in range(len(previous))},
        compiler_params=kernel_params(60),
        cost_estimate=cost(micros),
    )(*inputs, *previous)


def attend_layer(x, w_qkv, vecs, first, count, previous):
    def rows(cols):
        return tiles(cols, first)

    def kernel(x_ref, wqkv_ref, vec_ref, *refs):
        attend_kernel(x_ref, wqkv_ref, vec_ref, *refs[-3:])

    return in_parts(
        kernel,
        8 * count,
        count,
        [x, w_qkv, vecs],
        [rows(D), fixed((D, 3 * D)), fixed((VECTOR_ROWS, D))],
        [jax.ShapeDtypeStruct(v.shape, v.dtype) for v in previous],
        [rows(3 * D), rows(D), rows(LANES)],
        [],
        previous,
    )


def attend_first(x, weights, coords):
    n = x.shape[0]
    bf, f32 = jnp.bfloat16, jnp.float32
    count = len(weights.operands)

    def kernel(coords_ref, *refs):
        sources, x_ref, refs = refs[:count], refs[count], refs[count + 1 :]
        packed_ref, att_ref, stat_ref, wqkv_ref, vec_ref, staged, wide, sems = refs
        weights.start(coords_ref, sources, staged, sems)
        waited = set()
        for number in range(2):
            weights.wait(number, waited, staged, sems)
        weights.matrix(0, staged, wide, wqkv_ref)
        vec_ref[...] = jnp.zeros_like(vec_ref)
        weights.vectors(1, staged, wide, vec_ref, 0)
        attend_kernel(x_ref, wqkv_ref, vec_ref, packed_ref, att_ref, stat_ref)

    whole = [pl.BlockSpec(shape, lambda i: (0, 0)) for shape in ((D, 3 * D), (VECTOR_ROWS, D))]
    return pl.pallas_call(
        kernel,
        grid=(1,),
        in_specs=[spec_smem()] + [spec_any()] * count + [tiles(D)],
        out_specs=[tiles(3 * D), tiles(D), tiles(LANES)] + whole,
        out_shape=[
            jax.ShapeDtypeStruct((n, 3 * D), bf),
            jax.ShapeDtypeStruct((n, D), bf),
            jax.ShapeDtypeStruct((n, LANES), f32),
            jax.ShapeDtypeStruct((D, 3 * D), bf),
            jax.ShapeDtypeStruct((VECTOR_ROWS, D), f32),
        ],
        scratch_shapes=weights.scratch,
        compiler_params=kernel_params(60),
        cost_estimate=cost(12),
    )(coords, *weights.operands, x)


FBLOCK = D


def feed_kernel(
    x_ref, att_ref, wout_ref, wup_ref, wdown_ref, vec_ref,
    h1low_ref, norm1_ref, g_ref, dg_ref, norm2_ref, rate_ref, h2_ref, cls_ref, res_ref, h1_ref,
):
    step = pl.program_id(0)
    segs = TILE // SEG_LEN
    lanes = lax.broadcasted_iota(jnp.int32, (SEG_LEN, LANES), 1)
    res_ref[...] = dot_nn(att_ref[...], wout_ref[...])

    def start(s, carry):
        rows = pl.ds(pl.multiple_of(s * SEG_LEN, SEG_LEN), SEG_LEN)
        resid = x_ref[rows, :].astype(jnp.float32) + res_ref[rows, :] + vec_ref[2:3, :]
        hidden, normal, rate = norm_rows(resid, vec_ref[3:4, :], vec_ref[4:5, :])
        h1_ref[rows, :] = hidden
        h1low_ref[rows, :] = low(hidden)
        norm1_ref[rows, :] = low(normal)
        rate_ref[rows, :] = jnp.broadcast_to(rate, (SEG_LEN, LANES))
        return carry

    lax.fori_loop(0, segs, start, 0)
    h = h1low_ref[...]
    for j in range(FF // FBLOCK):
        cols = slice(j * FBLOCK, (j + 1) * FBLOCK)
        act, slope = gelu_pair(dot_nn(h, wup_ref[:, cols]) + vec_ref[5 + j : 6 + j, :])
        g = low(act)
        g_ref[:, cols] = g
        dg_ref[:, cols] = low(slope)
        part = dot_nn(g, wdown_ref[cols, :])
        if j == 0:
            res_ref[...] = part
        else:
            res_ref[...] += part

    def finish(s, carry):
        rows = pl.ds(pl.multiple_of(s * SEG_LEN, SEG_LEN), SEG_LEN)
        resid = h1_ref[rows, :] + res_ref[rows, :] + vec_ref[9:10, :]
        hidden, normal, rate = norm_rows(resid, vec_ref[10:11, :], vec_ref[11:12, :])
        h2_ref[rows, :] = low(hidden)
        norm2_ref[rows, :] = low(normal)
        rate_ref[rows, :] = jnp.where(lanes == 0, rate_ref[rows, :], rate)
        cls_ref[pl.ds(step * segs + s, 1), :] = hidden[0:1, :]
        return carry

    lax.fori_loop(0, segs, finish, 0)


def feed_layer(x, att, weights, coords):
    n = x.shape[0]
    bf, f32 = jnp.bfloat16, jnp.float32
    count = len(weights.operands)
    steps = n // TILE
    shapes = [item.shape for item in weights.items if item.cols]

    def kernel(coords_ref, *refs):
        sources, refs = refs[:count], refs[count:]
        x_ref, att_ref = refs[:2]
        outs, kept = refs[2:10], refs[10:13]
        vec_ref, res_ref, h1_ref, out_sems = refs[13:17]
        held, (staged, wide, sems) = refs[17:20], refs[20:]
        step = pl.program_id(0)

        @pl.when(step == 0)
        def _():
            weights.start(coords_ref, sources, staged, sems)
            waited = set()
            vec_ref[...] = jnp.zeros_like(vec_ref)
            place = row = 0
            for number, item in enumerate(weights.items):
                weights.wait(number, waited, staged, sems)
                if item.cols:
                    weights.matrix(number, staged, wide, held[place])
                    pltpu.make_async_copy(held[place], kept[place], out_sems.at[place]).start()
                    place += 1
                else:
                    weights.vectors(number, staged, wide, vec_ref, row)
                    row += item.rows * LANES // D

        feed_kernel(x_ref, att_ref, *held, vec_ref, *outs, res_ref, h1_ref)

        @pl.when(step == steps - 1)
        def _():
            for place in range(3):
                pltpu.make_async_copy(held[place], kept[place], out_sems.at[place]).wait()

    return pl.pallas_call(
        kernel,
        grid=(steps,),
        in_specs=[spec_smem()] + [spec_any()] * count + [tiles(D), tiles(D)],
        out_specs=[tiles(D), tiles(D), tiles(FF), tiles(FF), tiles(D), tiles(LANES), tiles(D)]
        + [pl.BlockSpec((n // SEG_LEN, D), lambda i: (0, 0))]
        + [spec_any()] * 3
        + [pl.BlockSpec((VECTOR_ROWS, D), lambda i: (0, 0))],
        out_shape=[
            jax.ShapeDtypeStruct((n, cols), kind)
            for cols, kind in ((D, bf), (D, bf), (FF, bf), (FF, bf), (D, bf), (LANES, f32), (D, bf))
        ]
        + [jax.ShapeDtypeStruct((n // SEG_LEN, D), f32)]
        + [jax.ShapeDtypeStruct(shape, bf) for shape in shapes]
        + [jax.ShapeDtypeStruct((VECTOR_ROWS, D), f32)],
        scratch_shapes=[
            pltpu.VMEM((TILE, D), f32),
            pltpu.VMEM((TILE, D), f32),
            pltpu.SemaphoreType.DMA((3,)),
        ]
        + [pltpu.VMEM(shape, bf) for shape in shapes]
        + weights.scratch,
        compiler_params=kernel_params(62),
        cost_estimate=cost(60),
    )(coords, *weights.operands, x, att)


def feed_back_kernel(
    cot_ref, cls_ref, norm2_ref, dg_ref, norm1_ref, rate_ref,
    wdown_ref, wup_ref, wout_ref, vec_ref,
    dm_ref, du_ref, dao_ref, da_ref, one_ref, sums_ref, res_ref,
):
    step = pl.program_id(0)

    @pl.when(step == 0)
    def _():
        sums_ref[...] = jnp.zeros_like(sums_ref)

    segs = TILE // SEG_LEN
    row_ids = lax.broadcasted_iota(jnp.int32, (SEG_LEN, D), 0)

    def add_sum(row, values):
        sums_ref[row : row + 1, :] += jnp.sum(values, axis=0, keepdims=True)

    def start(s, carry):
        rows = pl.ds(pl.multiple_of(s * SEG_LEN, SEG_LEN), SEG_LEN)
        cls = cls_ref[pl.ds(step * segs + s, 1), :]
        grad = jnp.where(row_ids == 0, cls, cot_ref[rows, :].astype(jnp.float32))
        normal = norm2_ref[rows, :].astype(jnp.float32)
        add_sum(10, grad * normal)
        add_sum(11, grad)
        two = norm_pull(grad, normal, rate_ref[rows, 1:2], vec_ref[10:11, :])
        res_ref[rows, :] = two
        dm = low(two)
        dm_ref[rows, :] = dm
        add_sum(9, dm.astype(jnp.float32))
        return carry

    lax.fori_loop(0, segs, start, 0)
    dm = dm_ref[...]
    for j in range(FF // FBLOCK):
        cols = slice(j * FBLOCK, (j + 1) * FBLOCK)
        du = low(dot_nt(dm, wdown_ref[cols, :]) * dg_ref[:, cols].astype(jnp.float32))
        du_ref[:, cols] = du
        add_sum(5 + j, du.astype(jnp.float32))
        res_ref[...] += dot_nt(du, wup_ref[:, cols])

    def finish(s, carry):
        rows = pl.ds(pl.multiple_of(s * SEG_LEN, SEG_LEN), SEG_LEN)
        grad = res_ref[rows, :]
        normal = norm1_ref[rows, :].astype(jnp.float32)
        add_sum(3, grad * normal)
        add_sum(4, grad)
        one = norm_pull(grad, normal, rate_ref[rows, 0:1], vec_ref[3:4, :])
        one_ref[rows, :] = one
        dao = low(one)
        dao_ref[rows, :] = dao
        add_sum(2, dao.astype(jnp.float32))
        return carry

    lax.fori_loop(0, segs, finish, 0)
    da_ref[...] = low(dot_nt(dao_ref[...], wout_ref[...]))


def feed_back(cot, cls, norm2, dg, norm1, rates, w_down, w_up, w_out, vecs):
    n = cot.shape[0]
    bf, f32 = jnp.bfloat16, jnp.float32
    return pl.pallas_call(
        feed_back_kernel,
        grid=(n // TILE,),
        in_specs=[
            tiles(D), fixed((n // SEG_LEN, D)), tiles(D), tiles(FF), tiles(D), tiles(LANES),
            fixed((FF, D)), fixed((D, FF)), fixed((D, D)), fixed((VECTOR_ROWS, D)),
        ],
        out_specs=[
            tiles(D), tiles(FF), tiles(D), tiles(D), tiles(D),
            pl.BlockSpec((VECTOR_ROWS, D), lambda i: (0, 0)),
        ],
        out_shape=[
            jax.ShapeDtypeStruct((n, D), bf),
            jax.ShapeDtypeStruct((n, FF), bf),
            jax.ShapeDtypeStruct((n, D), bf),
            jax.ShapeDtypeStruct((n, D), bf),
            jax.ShapeDtypeStruct((n, D), f32),
            jax.ShapeDtypeStruct((VECTOR_ROWS, D), f32),
        ],
        scratch_shapes=[pltpu.VMEM((TILE, D), f32)],
        compiler_params=kernel_params(60),
        cost_estimate=cost(44),
    )(cot, cls, norm2, dg, norm1, rates, w_down, w_up, w_out, vecs)


def attend_back_kernel(packed_ref, stat_ref, da_ref, before_ref, *refs):
    dqkv_ref, sums_ref = refs[-2:]

    @pl.when(pl.program_id(0) == 0)
    def _():
        sums_ref[...] = before_ref[...]

    lanes = lax.broadcasted_iota(jnp.int32, (SEG_LEN, LANES), 1)
    scale = HEAD_DIM**-0.5

    def segment(s, carry):
        rows = pl.ds(pl.multiple_of(s * SEG_LEN, SEG_LEN), SEG_LEN)
        stat = stat_ref[rows, :]
        for pair in range(PAIRS):
            q = packed_ref[rows, third(0, pair)] * jnp.bfloat16(scale)
            k = packed_ref[rows, third(1, pair)]
            v = packed_ref[rows, third(2, pair)]
            da = da_ref[rows, pair * LANES : (pair + 1) * LANES]
            queries, grads = both_heads(q), both_heads(da)
            log_sum = jnp.concatenate([stat[:, 2 * pair : 2 * pair + 1], stat[:, 2 * pair + 1 : 2 * pair + 2]], axis=0)
            weights = jnp.exp(dot_nt(queries, k) - log_sum)
            grad_weights = dot_nt(grads, v)
            dv = dot_tn(low(weights), grads)
            inner = jnp.sum(grad_weights * weights, axis=-1, keepdims=True)
            ds = low(weights * (grad_weights - inner))
            dq = dot_nn(side_by_side(ds), both_heads(k)) * scale
            dk = dot_tn(ds, queries)
            for part, grad in enumerate((dq, dk, dv)):
                grad = low(grad)
                cols = third(part, pair)
                dqkv_ref[rows, cols] = grad
                if part != 1:
                    here = (slice(part // 2, part // 2 + 1), third(0, pair))
                    sums_ref[here] += jnp.sum(grad.astype(jnp.float32), axis=0, keepdims=True)
        return carry

    lax.fori_loop(0, TILE // SEG_LEN, segment, 0)


def attend_back(packed, stat, da, first, count, previous=None):
    n = packed.shape[0]
    before = previous[1] if previous else jnp.zeros((8, D), jnp.float32)
    return in_parts(
        attend_back_kernel,
        10 * count,
        count,
        [packed, stat, da, before],
        [tiles(3 * D, first), tiles(LANES, first), tiles(D, first), fixed((8, D))],
        [jax.ShapeDtypeStruct((n, 3 * D), jnp.bfloat16), jax.ShapeDtypeStruct((8, D), jnp.float32)],
        [tiles(3 * D, first), pl.BlockSpec((8, D), lambda i: (0, 0))],
        [],
        previous and previous[:1],
    )


def cross_kernel(
    load, rows_ref, tagc_ref, tagr_ref, gz_ref, wqkv_ref, wout_ref, wup_ref, wdown_ref, vec_ref,
    out_ref, grows_ref, sums_ref, gqkv_ref, go_ref, gu_ref, gm_ref, rowst_ref, attt_ref, hidt_ref, actt_ref,
    packed_ref, weights_ref, att_ref, act_ref, slope_ref, res_ref,
):
    scale = HEAD_DIM**-0.5
    rows = rows_ref[...]
    rowst_ref[...] = rows.T
    same = tagc_ref[:, 0:1] == tagr_ref[0:1, :]
    same = jnp.concatenate([same, same], axis=0)

    def add_sum(row, values):
        sums_ref[row : row + 1, :] = jnp.sum(values.astype(jnp.float32), axis=0, keepdims=True)

    def pair_cols(pair):
        return slice(pair * LANES, (pair + 1) * LANES)

    sums_ref[...] = jnp.zeros_like(sums_ref)
    load(0)
    for j in range(3):
        cols = slice(j * D, (j + 1) * D)
        part = dot_nn(rows, wqkv_ref[:, cols])
        packed_ref[:, cols] = low(part if j == 1 else part + vec_ref[j // 2 : j // 2 + 1, :])
    for pair in range(PAIRS):
        q = packed_ref[:, third(0, pair)] * jnp.bfloat16(scale)
        scores = jnp.where(same, dot_nt(both_heads(q), packed_ref[:, third(1, pair)]), NEGATIVE)
        raised = jnp.exp(scores - jnp.max(scores, axis=-1, keepdims=True))
        weights = raised / jnp.sum(raised, axis=-1, keepdims=True)
        weights_ref[pair] = weights
        blend = dot_nn(side_by_side(low(weights)), both_heads(packed_ref[:, third(2, pair)]))
        att_ref[:, pair_cols(pair)] = low(blend)
    att = att_ref[...]
    attt_ref[...] = att.T
    load(1)
    resid = rows.astype(jnp.float32) + dot_nn(att, wout_ref[...]) + vec_ref[2:3, :]
    hidden, normal_three, rate_three = norm_rows(resid, vec_ref[3:4, :], vec_ref[4:5, :])
    hidden_low = low(hidden)
    hidt_ref[...] = hidden_low.T
    load(2)
    res_ref[...] = hidden + vec_ref[9:10, :]
    for j in range(FF // FBLOCK):
        cols = slice(j * FBLOCK, (j + 1) * FBLOCK)
        act, slope = gelu_pair(dot_nn(hidden_low, wup_ref[:, cols]) + vec_ref[5 + j : 6 + j, :])
        act = low(act)
        actt_ref[cols, :] = act.T
        slope_ref[:, cols] = slope
        res_ref[...] += dot_nn(act, wdown_ref[cols, :])
    crossed, normal_four, rate_four = norm_rows(res_ref[...], vec_ref[10:11, :], vec_ref[11:12, :])
    out_ref[...] = low(crossed)

    grad_z = gz_ref[...].astype(jnp.float32)
    add_sum(10, grad_z * normal_four)
    add_sum(11, grad_z)
    grad_four = norm_pull(grad_z, normal_four, rate_four, vec_ref[10:11, :])
    grad_m = low(grad_four)
    gm_ref[...] = grad_m
    add_sum(9, grad_m)
    res_ref[...] = grad_four
    for j in range(FF // FBLOCK):
        cols = slice(j * FBLOCK, (j + 1) * FBLOCK)
        grad_u = low(dot_nt(grad_m, wdown_ref[cols, :]) * slope_ref[:, cols])
        gu_ref[:, cols] = grad_u
        add_sum(5 + j, grad_u)
        res_ref[...] += dot_nt(grad_u, wup_ref[:, cols])
    grad_h = res_ref[...]
    add_sum(3, grad_h * normal_three)
    add_sum(4, grad_h)
    grad_three = norm_pull(grad_h, normal_three, rate_three, vec_ref[3:4, :])
    grad_o = low(grad_three)
    go_ref[...] = grad_o
    add_sum(2, grad_o)
    res_ref[...] = grad_three
    att_ref[...] = low(dot_nt(grad_o, wout_ref[...]))
    for pair in range(PAIRS):
        queries = both_heads(packed_ref[:, third(0, pair)] * jnp.bfloat16(scale))
        grads = both_heads(att_ref[:, pair_cols(pair)])
        weights = weights_ref[pair]
        grad_weights = dot_nt(grads, packed_ref[:, third(2, pair)])
        dv = dot_tn(low(weights), grads)
        inner = jnp.sum(grad_weights * weights, axis=-1, keepdims=True)
        ds = low(weights * (grad_weights - inner))
        dq = dot_nn(side_by_side(ds), both_heads(packed_ref[:, third(1, pair)])) * scale
        dk = dot_tn(ds, queries)
        for part, grad in enumerate((dq, dk, dv)):
            gqkv_ref[:, third(part, pair)] = low(grad)
    add_sum(0, gqkv_ref[:, :D])
    add_sum(1, gqkv_ref[:, 2 * D :])
    for j in range(3):
        cols = slice(j * D, (j + 1) * D)
        res_ref[...] += dot_nt(gqkv_ref[:, cols], wqkv_ref[:, cols])
    grows_ref[...] = low(res_ref[...])


def cross_layer(cls, places, tags, grad_out, weights, coords):
    m = cls.shape[0]
    bf, f32 = jnp.bfloat16, jnp.float32
    tagc = jnp.broadcast_to(tags.astype(f32)[:, None], (m, LANES))
    tagr = jnp.broadcast_to(tags.astype(f32)[None, :], (8, m))
    count = len(weights.operands)
    operands = [cls, tagc, tagr, grad_out]
    shapes = [(m, D), (m, D), (VECTOR_ROWS, D), (m, 3 * D), (m, D), (m, FF), (m, D), (D, m), (D, m), (D, m), (FF, m)]
    matrices = [number for number, item in enumerate(weights.items) if item.cols]
    vectors = [number for number, item in enumerate(weights.items) if not item.cols]
    needs = [(matrices[:1], vectors[:1]), (matrices[1:2], vectors[1:2]), (matrices[2:], vectors[2:])]

    def kernel(coords_ref, *refs):
        sources, refs = refs[:count], refs[count:]
        ins, outs = refs[: len(operands)], refs[len(operands) : len(operands) + len(shapes)]
        held, vec_ref, refs = refs[-8:-4], refs[-4], (refs[len(operands) + len(shapes) : -8], refs[-3:])
        scratch, (staged, wide, sems) = refs
        waited = set()
        rows_of = {number: row for number, row in zip(vectors, (0, 2, 5, 9))}
        weights.start(coords_ref, sources, staged, sems)

        def load(stage):
            for number in needs[stage][0]:
                weights.wait(number, waited, staged, sems)
                weights.matrix(number, staged, wide, held[matrices.index(number)])
            for number in needs[stage][1]:
                weights.wait(number, waited, staged, sems)
                weights.vectors(number, staged, wide, vec_ref, rows_of[number])

        vec_ref[...] = jnp.zeros_like(vec_ref)
        cross_kernel(load, *ins, *held, vec_ref, *outs, *scratch)

    return pl.pallas_call(
        kernel,
        out_shape=[jax.ShapeDtypeStruct(shape, f32 if i == 2 else bf) for i, shape in enumerate(shapes)],
        in_specs=[spec_smem()] + [spec_any()] * count + [spec_vmem()] * len(operands),
        out_specs=[spec_vmem()] * len(shapes),
        scratch_shapes=[
            pltpu.VMEM((m, 3 * D), bf),
            pltpu.VMEM((PAIRS, 2 * m, m), f32),
            pltpu.VMEM((m, D), bf),
            pltpu.VMEM((m, D), bf),
            pltpu.VMEM((m, FF), f32),
            pltpu.VMEM((m, D), f32),
        ]
        + [pltpu.VMEM(weights.items[number].shape, bf) for number in matrices]
        + [pltpu.VMEM((VECTOR_ROWS, D), f32)]
        + weights.scratch,
        compiler_params=kernel_params(62),
        cost_estimate=cost(22),
    )(coords, *weights.operands, *operands)


def class_rows(cls, hot, weights, coords):
    count = len(weights.operands)

    def kernel(coords_ref, *refs):
        sources, (cls_ref, hot_ref, out_ref, table, staged, wide, sems) = refs[:count], refs[count:]
        weights.start(coords_ref, sources, staged, sems)
        weights.wait(0, set(), staged, sems)
        weights.matrix(0, staged, wide, table)
        out_ref[...] = low(cls_ref[...] + dot_nn(hot_ref[...], table[...]))

    return pl.pallas_call(
        kernel,
        out_shape=jax.ShapeDtypeStruct(cls.shape, jnp.bfloat16),
        in_specs=[spec_smem()] + [spec_any()] * count + [spec_vmem()] * 2,
        out_specs=spec_vmem(),
        scratch_shapes=[pltpu.VMEM((LONG_SEGS, D), jnp.bfloat16)] + weights.scratch,
        compiler_params=kernel_params(),
        cost_estimate=cost(3),
    )(coords, *weights.operands, cls, hot)
AXES = ("seg", "doc")


def tie(value, *others):
    return lax.optimization_barrier((value, *others))[0]


def after(halves, *others):
    return [[tie(value, *others) for value in half] for half in halves]


def send(geo, value, axis, step):
    return lax.ppermute(value, AXES, geo.shift(axis, step))


def gather_axis(geo, value, axis, others):
    parts = [send(geo, value, axis, r) for r in range(1, geo.size(axis))]
    return jnp.stack([value] + [tie(part, *others) if others else part for part in parts])


def gather_line(geo, pieces, my_z, cut):
    parts = [pieces] + [send(geo, pieces, Z, r) for r in range(1, geo.n_doc)]
    return place_line(geo, parts, my_z, cut)


def gather_plane(geo, halves, step, others=()):
    orders = ((X, Y), (Y, X))
    return [gather_axis(geo, half, order[step], others) for half, order in zip(halves, orders)]


def gather_cores(geo, halves):
    return [array for half in halves for array in (half, send(geo, half, C, 1))]


def plus(*terms):
    return low(sum(term.astype(jnp.float32) for term in terms))


def reduce_cores(geo, arrays):
    return [(arrays[2 * half], send(geo, arrays[2 * half + 1], C, 1)) for half in range(2)]


def reduce_plane(geo, halves, step):
    orders = ((Y, X), (X, Y))
    result = []
    for half, order in zip(halves, orders):
        value = plus(*half)
        axis = order[step]
        result.append([value[0]] + [send(geo, value[r], axis, r) for r in range(1, geo.size(axis))])
    return result


def reduce_line(geo, line, my_z):
    nd = geo.n_doc
    line = line.reshape(line.shape[0], nd, geo.piece, LANES)

    def to(r):
        return lax.dynamic_index_in_dim(line, lax.rem(my_z + r, nd), axis=1, keepdims=False)

    return [to(0)] + [send(geo, to(r), Z, r) for r in range(1, nd)]


def join(halves):
    return jnp.concatenate([plus(*half) for half in halves])
def optimizer_step(gradient, master, momentum, average, scaling, rating):
    scaled = gradient * scaling
    moment = 0.5 * momentum + scaled
    weight = master - rating * (scaled + 0.5 * moment)
    smooth = 0.5 * average + 0.5 * weight
    return (weight, moment, smooth, low(weight))


def row_rates(geo, n_tokens, n_cls):
    total = geo.chunk * geo.n_dev
    scaling = np.zeros((total,), np.float32)
    rating = np.full((total,), 0.2, np.float32)
    names = list(LAYOUT)
    cross = names[-13:]
    row = 0
    for name, shape in LAYOUT.items():
        rows = math.prod(shape) // LANES
        scaling[row : row + rows] = 1.0 / math.sqrt(n_cls if name in cross else n_tokens)
        if len(shape) == 2:
            rating[row : row + rows] = 1.0 if name == cross[0] else 0.5 / math.sqrt(shape[0])
        row += rows
    return scaling.reshape(geo.n_dev, geo.chunk), rating.reshape(geo.n_dev, geo.chunk)


def matmul(left, right):
    return jnp.dot(left, right, preferred_element_type=jnp.float32)


def column_sum(rows):
    return jnp.sum(rows.astype(jnp.float32), axis=0, keepdims=True)


def local(tokens, cotangent, seg_doc, seg_pos, master, momentum, average):
    n_seg = lax.axis_size(AXES[0])
    n_doc = lax.axis_size(AXES[1])
    geo = Geometry(n_seg, n_doc, master.shape[0])
    by = geo.by_name
    gather = Buckets(geo, [4, 4, 1], by.w_out, by.pos_table)
    buckets = Buckets(geo, [4, 4, 4, 1], by.w_out, by.w_down, by.pos_table)
    my_seg, my_doc = lax.axis_index(AXES[0]), lax.axis_index(AXES[1])
    me = my_seg * n_doc + my_doc
    coords = jnp.stack([my_seg // 4, my_seg // 2 % 2, my_seg % 2, my_doc]).astype(jnp.int32)
    table = lax.dynamic_index_in_dim(jnp.asarray(geo.block_tables()[1]), me, 0, False)
    pad_rows = ceil_to(geo.chunk + 4 * BLK, 8)
    padded = jnp.pad(
        master.reshape(geo.chunk, LANES), ((BLK, pad_rows - geo.chunk - BLK), (0, 0))
    )
    aligned = align_rows(geo, table, padded)
    pieces = lax.all_to_all(aligned.reshape(geo.n_dev, geo.piece, LANES), AXES, 0, 0, tiled=True)
    parts = [pieces[span.start : span.stop] for span in gather.ranges]

    seg_count = tokens.shape[1]
    n_rows = n_seg * seg_count
    tiles_all = seg_count * SEG_LEN // TILE
    inputs = tokens[0].reshape(seg_count * SEG_LEN, D)
    cot_rows = cotangent[0]
    tagged = low(class_tags(cot_rows, seg_doc[0], seg_pos[0]))
    cut = gather.half
    line = gather_line(geo, parts[0], my_doc, cut[0])

    gathered = [None, None, None]

    def weights(*numbers):
        return Weights(geo, gather, gathered, [item_name(i) for i in numbers])

    started = tie(parts[1], *line)
    parts_b = [started] + [send(geo, started, Z, r) for r in range(1, n_doc)]
    plane = gather_plane(geo, line, 0, parts_b[1:2])
    plane = gather_plane(geo, plane, 1, parts_b[2:3])
    gathered[0] = gather_cores(geo, plane)
    all_tagged = lax.all_gather(tie(tagged, *plane), AXES[0], axis=0, tiled=True)
    parts_b[-1] = tie(parts_b[-1], all_tagged)
    line_b = place_line(geo, parts_b, my_doc, cut[1])
    *outs, w_qkv, vec_a = attend_first(tie(inputs, *line_b), weights(0, 1), coords)
    plane_b = gather_plane(geo, line_b, 0, [vec_a])
    middle = max(1, tiles_all - 2)
    outs = attend_layer(tie(inputs, *plane_b), w_qkv, vec_a, 1, middle, outs)
    gathered[2] = [lax.all_gather(tie(parts[2], outs[2]), AXES)]
    plane_b = gather_plane(geo, plane_b, 1, [outs[2]])
    gathered[1] = gather_cores(geo, plane_b)
    if 1 + middle < tiles_all:
        last = tiles_all - 1 - middle
        outs = attend_layer(tie(inputs, *plane_b), w_qkv, vec_a, 1 + middle, last, outs)
    packed, attended, stat = outs
    hidden_low, normal_one, active, slope, normal_two, rates, hidden_two, cls, w_out, w_up, w_down, vec = feed_layer(
        inputs, attended, weights(1, 2, 3, 4, 5, 6, 7), coords
    )

    all_grad, all_doc, all_pos = all_tagged[:, :D], all_tagged[:, D], all_tagged[:, D + 1]
    pos_hot = (all_pos.astype(jnp.int32)[:, None] == jnp.arange(LONG_SEGS)[None, :]).astype(jnp.bfloat16)

    def own(values):
        return lax.dynamic_slice_in_dim(values, my_seg * seg_count, seg_count, axis=0)

    cls_low = class_rows(cls, own(pos_hot), weights(8), coords)
    rows = lax.all_gather(cls_low, AXES[0], axis=0, tiled=True)
    crossed, grad_rows, xsums, g_qkv, g_o, g_u, g_m, rows_t, att_t, hid_t, act_t = cross_layer(
        rows, all_pos, all_doc, all_grad, weights(9, 10, 11, 12, 13, 14, 15, 16), coords
    )
    names = [item_name(i) for i in (8, 9, 11, 13, 15)]
    line_c = pack_cross(
        geo,
        buckets.ranges[3],
        dict(zip(names, (pos_hot.T, rows_t, att_t, hid_t, act_t))),
        dict(zip(names, (grad_rows, g_qkv, g_o, g_u, g_m))),
        {item_name(i): (xsums, row) for i, row in ((10, 0), (12, 2), (14, 5), (16, 9))},
        my_seg.astype(jnp.int32).reshape(1),
    )
    sums_c = reduce_line(geo, line_c, my_doc)

    grads = {}
    dm, du, dao, da, grad_one, sums = feed_back(
        cot_rows.reshape(-1, D), tie(own(grad_rows).astype(jnp.float32), *sums_c[:1]), normal_two,
        slope, normal_one, rates, w_down, w_up, w_out, vec,
    )
    pieces_c = plus(*[tie(part, sums) for part in sums_c])
    grads[item_name(8)] = low(matmul(own(pos_hot).T, own(grad_rows)))
    for number, row in ((3, 2), (5, 5), (7, 9)):
        grads[item_name(number)] = (sums, row)
    grads[item_name(6)] = low(matmul(active.T, tie(dm, pieces_c)))
    arrays_d = pack_bucket(geo, buckets, 2, grads, coords)
    halves_d = reduce_cores(geo, arrays_d)
    grads[item_name(4)] = low(matmul(hidden_low.T, tie(du, arrays_d[0])))
    halves_d = reduce_plane(geo, after(halves_d, grads[item_name(4)]), 0)
    grads[item_name(2)] = low(matmul(attended.T, tie(dao, halves_d[0][0], halves_d[1][0])))
    arrays_b = pack_bucket(geo, buckets, 1, grads, coords)
    halves_b = reduce_cores(geo, arrays_b)
    back = attend_back(packed, stat, tie(da, arrays_b[0]), 0, 1)
    halves_d = reduce_plane(geo, after(halves_d, back[1]), 1)
    halves_b = reduce_plane(geo, after(halves_b, back[1]), 0)
    if tiles_all > 1:
        da = tie(da, *[half[0] for half in halves_b + halves_d])
        back = attend_back(packed, stat, da, 1, middle, back)
    line_d = reduce_line(geo, join(after(halves_d, back[1])), my_doc)
    halves_b = reduce_plane(geo, after(halves_b, back[1]), 1)
    if 1 + middle < tiles_all:
        da = tie(da, line_d[0], *[half[0] for half in halves_b])
        back = attend_back(packed, stat, da, 1 + middle, last, back)
    dqkv, qv_sums = back
    line_b = reduce_line(geo, join(after(halves_b, qv_sums)), my_doc)
    grads[item_name(0)] = low(matmul(inputs.T, tie(dqkv, line_b[0])))
    grads[item_name(1)] = (qv_sums, 0)
    pieces_d = plus(*[tie(part, grads[item_name(0)]) for part in line_d])
    grads[item_name(0)] = tie(grads[item_name(0)], pieces_d)
    arrays_a = pack_bucket(geo, buckets, 0, grads, coords)
    halves_a = reduce_cores(geo, arrays_a)
    pieces_b = plus(*[tie(part, arrays_a[0]) for part in line_b])
    halves_a = reduce_plane(geo, after(halves_a, pieces_b), 0)
    token_grad = low(grad_one + matmul(tie(dqkv, halves_a[0][0], halves_a[1][0]), w_qkv.T))
    halves_a = reduce_plane(geo, after(halves_a, token_grad), 1)
    first_row = lax.broadcasted_iota(jnp.int32, (seg_count, SEG_LEN, D), 1) == 0
    crossed = tie(crossed, halves_a[0][0], halves_a[1][0])
    mixed_out = jnp.where(
        first_row, own(crossed)[:, None, :], hidden_two.reshape(seg_count, SEG_LEN, D)
    )
    line_a = reduce_line(geo, join(after(halves_a, mixed_out)), my_doc)
    pieces_a = plus(*line_a)

    owned = lax.all_to_all(
        jnp.concatenate([pieces_a, pieces_b, pieces_d, pieces_c]), AXES, 0, 0, tiled=True
    )
    natural = natural_rows(geo, table, owned.reshape(-1, LANES), pad_rows)
    gradient = natural[BLK : BLK + geo.chunk].reshape(-1)
    n_cls = n_doc * n_rows
    scaling, rating = (
        jnp.broadcast_to(
            lax.dynamic_index_in_dim(jnp.asarray(rates), me, 0, False)[:, None], (geo.chunk, LANES)
        ).reshape(-1)
        for rates in row_rates(geo, n_cls * SEG_LEN, n_cls)
    )
    weight, moment, smooth, copy_low = optimizer_step(
        gradient, master, momentum, average, scaling, rating
    )
    return (
        mixed_out[None],
        token_grad.reshape(1, seg_count, SEG_LEN, D),
        weight,
        moment,
        smooth,
        copy_low,
    )


def item_name(number):
    return item_list(0)[number].name


def solution(mesh):
    layer = P(AXES[1], AXES[0], None, None)
    ids = P(AXES[1], AXES[0])
    flat = P(AXES)
    return jax.shard_map(
        local,
        mesh=mesh,
        in_specs=(layer, layer, ids, ids, flat, flat, flat),
        out_specs=(layer, layer, flat, flat, flat, flat),
        check_vma=False,
    )
```

```python
import math
from types import SimpleNamespace

import jax
import jax.numpy as jnp
import numpy as np
from jax import lax
from jax.experimental import pallas as pl
from jax.experimental.pallas import tpu as pltpu
from jax.sharding import PartitionSpec as P

D = 768
HEADS = 12
HEAD_DIM = 64
FF = 3072
SEG_LEN = 128
LONG_SEGS = 64
EPSILON = 1e-05
NEGATIVE = -1e30

LAYOUT = dict(
    w_qkv=(D, 3 * D),
    b_qv=(2 * D,),
    w_out=(D, D),
    b_out=(D,),
    gain_one=(D,),
    bias_one=(D,),
    w_up=(D, FF),
    b_up=(FF,),
    w_down=(FF, D),
    b_down=(D,),
    gain_two=(D,),
    bias_two=(D,),
    pos_table=(LONG_SEGS, D),
    x_qkv=(D, 3 * D),
    x_bqv=(2 * D,),
    x_out=(D, D),
    x_bout=(D,),
    gain_three=(D,),
    bias_three=(D,),
    x_up=(D, FF),
    x_bup=(FF,),
    x_down=(FF, D),
    x_bdown=(D,),
    gain_four=(D,),
    bias_four=(D,),
)
LANES = 128
BLK = 16
Y, X, C, Z = range(4)


def ceil_to(value, step):
    return -(-value // step) * step


def item_list(total_rows):
    items = []
    nat = 0
    for name, shape in LAYOUT.items():
        rows = math.prod(shape) // LANES
        if len(shape) == 1 and items and len(items[-1].shape) == 1:
            items[-1].names.append(name)
            items[-1].rows += rows
        else:
            items.append(SimpleNamespace(name=name, names=[name], shape=shape, nat=nat, rows=rows))
        nat += rows
    items.append(SimpleNamespace(name=None, names=[], shape=None, nat=nat, rows=total_rows - nat))
    blk = 0
    for item in items:
        item.cols = item.shape[1] // LANES if item.shape and len(item.shape) == 2 else 0
        item.blk = blk
        blk += ceil_to(item.rows, BLK) // BLK
    return items


class Geometry:
    def __init__(self, n_seg, n_doc, shard_len):
        self.n_seg, self.n_doc = n_seg, n_doc
        self.n_dev = n_seg * n_doc
        self.chunk = shard_len // LANES
        self.items = item_list(self.chunk * self.n_dev)
        self.by_name = SimpleNamespace(**{item.name: item for item in self.items if item.name})
        firsts, lasts = [], []
        for n in range(self.n_dev):
            lo, hi = n * self.chunk, (n + 1) * self.chunk
            blocks = []
            for item in self.items:
                a, b = max(lo, item.nat), min(hi, item.nat + item.rows)
                if a < b:
                    blocks.append(item.blk + (a - item.nat) // BLK)
                    blocks.append(item.blk + (b - 1 - item.nat) // BLK)
            firsts.append(min(blocks))
            lasts.append(max(blocks))
        self.first, self.last = firsts, lasts
        most = max(b - a + 1 for a, b in zip(firsts, lasts))
        self.piece_blocks = -(-most // self.n_dev)
        self.piece = self.piece_blocks * BLK
        self.slots = self.piece_blocks * self.n_dev
        self.groups = -(-most // (self.piece_blocks * n_doc))
        self.staged_rows = self.groups * n_doc * self.piece
        self.c_size, self.x_size = 2, 2
        self.y_size = n_seg // 4

    def full_groups(self, item, chunk):
        rows = BLK * item.cols
        lo, hi = chunk * self.chunk - item.nat, (chunk + 1) * self.chunk - item.nat
        first, last = max(0, -(-lo // rows)), min(item.rows, hi) // rows
        return first, max(first, last)

    def block_tables(self):
        matrices = [item for item in self.items if item.cols]
        single = [[] for _ in range(self.n_dev)]
        groups = np.zeros((self.n_dev, len(matrices), 3), np.int32)
        for n in range(self.n_dev):
            lo, hi = n * self.chunk, (n + 1) * self.chunk
            for t in range(self.slots):
                b = self.first[n] + t
                if b > self.last[n]:
                    single[n].append((t, 0, 0, 0))
                    continue
                item = [it for it in self.items if it.blk <= b][-1]
                at = b - item.blk
                if item.cols:
                    first, last = self.full_groups(item, n)
                    if first <= at // item.cols < last:
                        continue
                start = item.nat + at * BLK
                a = max(start, lo)
                z = max(a, min(start + BLK, hi, item.nat + item.rows))
                single[n].append((t, start - lo, a - start, z - start))
            for i, item in enumerate(matrices):
                first, last = self.full_groups(item, n)
                if first < last:
                    slot = item.blk + first * item.cols - self.first[n]
                    groups[n, i] = (slot, item.nat + first * BLK * item.cols - lo, last - first)
        most = max(len(rows) for rows in single)
        table = np.zeros((self.n_dev, 1 + 4 * most), np.int32)
        for n, rows in enumerate(single):
            table[n, 0] = len(rows)
            table[n, 1 : 1 + 4 * len(rows)] = np.asarray(rows, np.int32).reshape(-1)
        return matrices, np.concatenate([groups.reshape(self.n_dev, -1), table], axis=1)

    def chunks_of(self, item):
        found = []
        n_blocks = ceil_to(item.rows, BLK) // BLK
        for n in range(self.n_dev):
            a = max(item.blk, self.first[n])
            b = min(item.blk + n_blocks, self.last[n] + 1)
            if a < b:
                found.append((n, a - item.blk, b - item.blk, a - self.first[n]))
        return found

    def spans(self, *ends):
        cuts = [0] + [(end.nat - 1) // self.chunk + 1 for end in ends] + [self.n_dev]
        return [range(a, b) for a, b in zip(cuts, cuts[1:])]

    def coords(self, device):
        seg, doc = divmod(device, self.n_doc)
        yx, c = divmod(seg, self.c_size)
        return [*divmod(yx, self.x_size), c, doc]

    def device(self, y, x, c, z):
        return ((y * self.x_size + x) * self.c_size + c) * self.n_doc + z

    def size(self, axis):
        return (self.y_size, self.x_size, self.c_size, self.n_doc)[axis]

    def shift(self, axis, step):
        pairs = []
        for source in range(self.n_dev):
            at = self.coords(source)
            at[axis] = (at[axis] + step) % self.size(axis)
            pairs.append((source, self.device(*at)))
        return pairs
def spec_vmem():
    return pl.BlockSpec(memory_space=pltpu.VMEM)


def spec_any():
    return pl.BlockSpec(memory_space=pl.ANY)


def spec_smem():
    return pl.BlockSpec(memory_space=pltpu.SMEM)


def kernel_params(mib=56):
    return pltpu.CompilerParams(vmem_limit_bytes=mib * 1024 * 1024)


def cost(micros):
    micros = micros if micros >= 6 else 0
    return pl.CostEstimate(flops=int(micros * 1e9), bytes_accessed=int(micros * 3e6), transcendentals=0)


class Order:
    def start(self):
        self.token = jnp.zeros((8, LANES), jnp.float32)
        self.others = []

    def wait_for(self, *others):
        self.others += others


ORDER = Order()


def ordered(kernel, out_shape, in_specs, out_specs, **settings):
    single = not isinstance(out_shape, (list, tuple))
    outs, specs = ([out_shape], [out_specs]) if single else (list(out_shape), list(out_specs))

    def run(*inputs):
        extra = [ORDER.token] + ORDER.others
        n_in, n_out, n_extra = len(inputs), len(outs), len(extra)

        def wrapped(*refs):
            rest = refs[n_in + n_extra :]
            kernel(*refs[:n_in], *rest[:n_out], *rest[n_out + 1 :])

        results = pl.pallas_call(
            wrapped,
            out_shape=outs + [jax.ShapeDtypeStruct((8, LANES), jnp.float32)],
            in_specs=list(in_specs) + [spec_any()] * n_extra,
            out_specs=specs + [spec_any()],
            **settings,
        )(*inputs, *extra)
        ORDER.token, ORDER.others = results[-1], []
        return results[0] if single else results[:-1]

    return run


def row_mask(low, high):
    rows = lax.broadcasted_iota(jnp.int32, (BLK, LANES), 0)
    return (rows >= low) & (rows < high)


def block_moves(geo, table_ref, by_group, by_row):
    matrices = geo.block_tables()[0]
    for i, item in enumerate(matrices):
        def body(g, carry, i=i, cols=item.cols):
            for cb in range(cols):
                by_group(table_ref[3 * i] + g * cols + cb, table_ref[3 * i + 1] + g * BLK * cols + cb, cols)
            return carry

        lax.fori_loop(0, table_ref[3 * i + 2], body, 0)
    base = 3 * len(matrices)

    def single(r, carry):
        by_row(*[table_ref[base + 1 + 4 * r + j] for j in range(4)])
        return carry

    lax.fori_loop(0, table_ref[base], single, 0)


def block_at(slot):
    return pl.ds(pl.multiple_of(slot * BLK, BLK), BLK)


def align_rows(geo, table, natural, pad_rows):
    def kernel(table_ref, natural_ref, out_ref, rows_ref):
        def fill(row, rows):
            rows_ref[pl.ds(row + BLK, rows), :] = natural_ref[pl.ds(row, rows), :]

        copy_rows(natural.shape[0], 256, fill)

        def by_group(slot, start, cols):
            out_ref[block_at(slot), :] = rows_ref[pl.ds(start + BLK, BLK, stride=cols), :].astype(jnp.bfloat16)

        def by_row(slot, start, low_row, high_row):
            rows = jnp.where(row_mask(low_row, high_row), rows_ref[pl.ds(start + BLK, BLK), :], 0.0)
            out_ref[block_at(slot), :] = rows.astype(jnp.bfloat16)

        block_moves(geo, table_ref, by_group, by_row)

    return ordered(
        kernel,
        out_shape=jax.ShapeDtypeStruct((geo.slots * BLK, LANES), jnp.bfloat16),
        in_specs=[spec_smem(), spec_vmem()],
        out_specs=spec_vmem(),
        scratch_shapes=[pltpu.VMEM((pad_rows, LANES), jnp.float32)],
        compiler_params=kernel_params(),
        cost_estimate=cost(3),
    )(table, natural)


def natural_rows(geo, table, blocks, pad_rows):
    def kernel(table_ref, blocks_ref, out_ref):
        def by_group(slot, start, cols):
            out_ref[pl.ds(start + BLK, BLK, stride=cols), :] = blocks_ref[block_at(slot), :].astype(jnp.float32)

        def by_row(slot, start, low_row, high_row):
            here = pl.ds(start + BLK, BLK)
            rows = blocks_ref[block_at(slot), :].astype(jnp.float32)
            out_ref[here, :] = jnp.where(row_mask(low_row, high_row), rows, out_ref[here, :])

        block_moves(geo, table_ref, by_group, by_row)

    return ordered(
        kernel,
        out_shape=jax.ShapeDtypeStruct((pad_rows, LANES), jnp.float32),
        in_specs=[spec_smem(), spec_vmem()],
        out_specs=spec_vmem(),
        compiler_params=kernel_params(),
        cost_estimate=cost(3),
    )(table, blocks)


class Buckets:
    def __init__(self, geo, arrays, *ends):
        self.geo = geo
        self.ranges = geo.spans(*ends)
        self.arrays = arrays
        self.half = [(len(r) + 1) // 2 for r in self.ranges]

    def find(self, chunk):
        for number, span in enumerate(self.ranges):
            if chunk in span:
                at = chunk - span.start
                cut = self.half[number]
                return (number, 0, at) if at < cut else (number, 1, at - cut)

    def shapes(self, number):
        geo = self.geo
        cut = self.half[number]
        rest = len(self.ranges[number]) - cut
        rows = geo.n_doc * geo.piece
        return [
            (geo.y_size, geo.x_size, cut, rows, LANES),
            (geo.x_size, geo.y_size, rest, rows, LANES),
        ]


def wrap(value, size):
    return lax.rem(value + size, size)


def copy_rows(count, step, body):
    full = count // step
    if full:
        def loop(i, carry):
            body(i * step, step)
            return carry

        lax.fori_loop(0, full, loop, 0)
    if count % step:
        body(full * step, count % step)


def place_line(geo, parts, my_z, cut):
    n, nd = parts[0].shape[0], geo.n_doc
    counts = [cut, n - cut]

    def kernel(z_ref, *refs):
        sources, outs = refs[:nd], refs[nd:]
        for r in range(nd):
            z = wrap(z_ref[0] - r, nd)
            rows = pl.ds(pl.multiple_of(z * geo.piece, BLK), geo.piece)
            for i in range(n):
                target = outs[0].at[i] if i < cut else outs[1].at[i - cut]
                target[rows, :] = sources[r][i]

    return ordered(
        kernel,
        out_shape=[jax.ShapeDtypeStruct((c, nd * geo.piece, LANES), jnp.bfloat16) for c in counts],
        in_specs=[spec_smem()] + [spec_vmem()] * nd,
        out_specs=[spec_vmem()] * 2,
        compiler_params=kernel_params(),
        cost_estimate=cost(2),
    )(my_z.reshape(1), *parts)
VECTOR_ROWS = 16


def chunk_copies(geo, buckets, sources, used, coords_ref, n, staged, sem):
    my_y, my_x, my_c = coords_ref[0], coords_ref[1], coords_ref[2]
    number, half, place = buckets.find(n)
    first = sum(buckets.arrays[m] for m in used[: used.index(number)])
    if buckets.arrays[number] == 1:
        for device in range(geo.groups * geo.n_doc):
            pltpu.make_async_copy(
                sources[first].at[device, n - buckets.ranges[number].start],
                staged.at[pl.ds(device * geo.piece, geo.piece)],
                sem,
            ).start()
        return
    rows = geo.n_doc * geo.piece
    for core in range(2):
        c = my_c if core == 0 else 1 - my_c
        for ry in range(geo.y_size):
            for rx in range(geo.x_size):
                y, x = wrap(my_y - ry, geo.y_size), wrap(my_x - rx, geo.x_size)
                s = (y * geo.x_size + x) * 2 + c
                index = (ry, rx, place) if half == 0 else (rx, ry, place)

                def begin(s=s, index=index, core=core):
                    pltpu.make_async_copy(
                        sources[first + 2 * half + core].at[index],
                        staged.at[pl.ds(pl.multiple_of(s * rows, BLK), rows)],
                        sem,
                    ).start()

                if geo.groups == geo.n_seg:
                    begin()
                else:
                    pl.when(s < geo.groups)(begin)


class Weights:
    def __init__(self, geo, buckets, gathered, names):
        self.geo, self.buckets = geo, buckets
        self.items = [vars(geo.by_name)[name] for name in names]
        self.chunks = sorted({n for item in self.items for n, *_ in geo.chunks_of(item)})
        self.used = sorted({buckets.find(n)[0] for n in self.chunks})
        self.operands = [array for number in self.used for array in gathered[number]]
        cols = max([item.cols for item in self.items])
        self.scratch = [
            pltpu.VMEM((len(self.chunks), geo.staged_rows, LANES), jnp.bfloat16),
            pltpu.VMEM((BLK * (cols + 2), LANES), jnp.float32),
            pltpu.SemaphoreType.DMA((len(self.chunks),)),
        ]

    def start(self, coords_ref, sources, staged, sems):
        for at, n in enumerate(self.chunks):
            chunk_copies(
                self.geo, self.buckets, sources, self.used, coords_ref, n, staged.at[at], sems.at[at]
            )

    def wait(self, number, waited, staged, sems):
        for n, *_ in self.geo.chunks_of(self.items[number]):
            at = self.chunks.index(n)
            if at not in waited:
                waited.add(at)
                pltpu.make_async_copy(staged.at[at], staged.at[at], sems.at[at]).wait()

    def blocks(self, item, lo, hi, staged, wide):
        done = lo
        for n, b0, b1, slot in self.geo.chunks_of(item):
            for b in range(max(b0, lo), min(b1, hi)):
                at = self.chunks.index(n)
                rows = staged[at, pl.ds((slot + b - b0) * BLK, BLK), :].astype(jnp.float32)
                here = pl.ds((b - lo) * BLK, BLK)
                wide[here, :] = wide[here, :] + rows if b < done else rows
            done = max(done, min(b1, hi))

    def matrix(self, number, staged, wide, out_ref):
        item = self.items[number]
        cols = item.cols
        split = set()
        for n, b0, b1, slot in self.geo.chunks_of(item):
            at = self.chunks.index(n)
            first, last = self.geo.full_groups(item, n)
            split |= set(range(b0 // cols, -(-b1 // cols))) - set(range(first, last))

            def group(g, carry, at=at, shift=slot - b0):
                rows = pl.ds(pl.multiple_of(g * BLK, BLK), BLK)
                for cb in range(cols):
                    tile = staged[at, block_at(g * cols + cb + shift), :]
                    out_ref[rows, cb * LANES : (cb + 1) * LANES] = tile
                return carry

            lax.fori_loop(first, last, group, 0)
        for g in sorted(split):
            self.blocks(item, g * cols, (g + 1) * cols, staged, wide)
            for cb in range(cols):
                tile = wide[pl.ds(cb, BLK, stride=cols), :]
                out_ref[g * BLK : (g + 1) * BLK, cb * LANES : (cb + 1) * LANES] = tile.astype(jnp.bfloat16)

    def vectors(self, number, staged, wide, out_ref, row):
        item = self.items[number]
        self.blocks(item, 0, ceil_to(item.rows, BLK) // BLK, staged, wide)
        for r in range(item.rows):
            v, cb = divmod(r, D // LANES)
            out_ref[row + v : row + v + 1, cb * LANES : (cb + 1) * LANES] = wide[r : r + 1, :]


def vector_rows(wide, values, first, count):
    lane_cols = D // LANES
    for r in range(count):
        v, cb = divmod(r, lane_cols)
        wide[r : r + 1, :] = values[first + v : first + v + 1, cb * LANES : (cb + 1) * LANES]


def bucket_parts(geo, span):
    parts = []
    for item in geo.items:
        chunks = [entry for entry in geo.chunks_of(item) if entry[0] in span]
        if chunks and item.names:
            parts.append((item, chunks))
    return parts


def grad_bucket(geo, buckets, number, grads, coords, name, left, right, rows, keep=False):
    span = buckets.ranges[number]
    seg_rows = geo.n_doc * geo.piece
    parts = bucket_parts(geo, span)
    operands, specs, windows, scratch = [], [], [], []
    wide_rows = BLK
    for item, chunks in parts:
        if len(item.shape) == 2:
            cols = item.cols
            wide_rows = max(wide_rows, BLK * cols)
            if item.name == name:
                main, main_chunks, windows_at = item, chunks, len(windows)
                windows.append(None)
                continue
            k0 = min(b0 for _, b0, _, _ in chunks) // cols
            k1 = -(-max(b1 for _, _, b1, _ in chunks) // cols)
            operands.append(grads[item.name])
            specs.append(spec_any())
            windows.append((len(operands) - 1, k0, k1))
            scratch.append(pltpu.VMEM(((k1 - k0) * BLK, item.shape[1]), jnp.bfloat16))
        else:
            wide_rows = max(wide_rows, ceil_to(item.rows, BLK))
            operands.append(grads[item.name][0])
            specs.append(pl.BlockSpec(operands[-1].shape, lambda i: (0, 0)))
            windows.append((len(operands) - 1, None, None))
            scratch.append(pltpu.VMEM((BLK, LANES), jnp.bfloat16))
    outs = [shape for shape in buckets.shapes(number) for _ in range(2)]
    depth, width = main.shape
    cols = main.cols
    steps = depth // rows
    count = len(operands)
    block_groups = rows // BLK

    def split_groups(item, chunks):
        found = set()
        for n, b0, b1, _ in chunks:
            first, last = geo.full_groups(item, n)
            found |= set(range(b0 // item.cols, -(-b1 // item.cols))) - set(range(first, last))
        return sorted(found)

    def kernel(coords_ref, left_ref, right_ref, *refs):
        sources, targets = refs[:count], refs[count : count + 4]
        refs = refs[count + 4 :]
        if keep:
            kept_ref, refs = refs[0], refs[1:]
        loaded, (values, staged, wide, in_sems, out_sems) = refs[:count], refs[count:]
        step = pl.program_id(0)
        my_y, my_x, my_c = coords_ref[0], coords_ref[1], coords_ref[2]

        def send_out(n):
            _, half, place = buckets.find(n)
            for core in range(2):
                c = my_c if core == 0 else 1 - my_c
                for ry in range(geo.y_size):
                    for rx in range(geo.x_size):
                        y, x = wrap(my_y + ry, geo.y_size), wrap(my_x + rx, geo.x_size)
                        s = (y * geo.x_size + x) * 2 + c
                        index = (ry, rx, place) if half == 0 else (rx, ry, place)
                        pltpu.make_async_copy(
                            staged.at[n - span.start, pl.ds(pl.multiple_of(s * seg_rows, BLK), seg_rows)],
                            targets[2 * half + core].at[index],
                            out_sems.at[n - span.start],
                        ).start()

        def whole(item, chunks, values, base, lo, hi):
            for n, b0, b1, slot in chunks:
                first, last = geo.full_groups(item, n)

                def group(g, carry, n=n, shift=slot - b0):
                    here = pl.ds(pl.multiple_of((g - base) * BLK, BLK), BLK)
                    for cb in range(item.cols):
                        dst = block_at(g * item.cols + cb + shift)
                        staged[n - span.start, dst, :] = values[here, cb * LANES : (cb + 1) * LANES]
                    return carry

                start = jnp.maximum(first, lo)
                lax.fori_loop(start, jnp.maximum(start, jnp.minimum(last, hi)), group, 0)

        def cut(item, chunks, values, base, g):
            for cb in range(item.cols):
                tile = values[pl.ds(pl.multiple_of((g - base) * BLK, BLK), BLK), cb * LANES : (cb + 1) * LANES]
                wide[pl.ds(cb, BLK, stride=item.cols), :] = tile.astype(jnp.float32)
            for n, b0, b1, slot in chunks:
                first, last = geo.full_groups(item, n)
                lo, hi = max(b0, g * item.cols), min(b1, (g + 1) * item.cols)
                if lo < hi and not first <= g < last:
                    part = wide[pl.ds((lo - g * item.cols) * BLK, (hi - lo) * BLK), :]
                    dst = pl.ds((slot + lo - b0) * BLK, (hi - lo) * BLK)
                    staged[n - span.start, dst, :] = part.astype(jnp.bfloat16)

        @pl.when(step == 0)
        def _():
            loads = {}
            for (item, chunks), window in zip(parts, windows):
                if window is not None and window[1] is not None:
                    at, k0, k1 = window
                    source = sources[at].at[pl.ds(k0 * BLK, (k1 - k0) * BLK)]
                    loads[at] = pltpu.make_async_copy(source, loaded[at], in_sems.at[at])
                    loads[at].start()

            def clear(row, size):
                for at in range(len(span)):
                    here = pl.ds(pl.multiple_of(row + tail, BLK), size)
                    staged[at, here, :] = jnp.zeros((size, LANES), jnp.bfloat16)

            tail = min(geo.last[n] - geo.first[n] for n in span) * BLK
            copy_rows(geo.slots * BLK - tail, 128, clear)
            for (item, chunks), window in zip(parts, windows):
                if window is None:
                    continue
                at, k0, k1 = window
                if k0 is None:
                    vector_rows(wide, sources[at], grads[item.name][1], item.rows)
                    for n, b0, b1, slot in chunks:
                        part = wide[pl.ds(b0 * BLK, (b1 - b0) * BLK), :].astype(jnp.bfloat16)
                        staged[n - span.start, pl.ds(slot * BLK, (b1 - b0) * BLK), :] = part
                else:
                    loads[at].wait()
                    whole(item, chunks, loaded[at], k0, k0, k1)
                    for g in split_groups(item, chunks):
                        cut(item, chunks, loaded[at], k0, g)

        values[...] = low(dot_tn(left_ref[...], right_ref[...]))
        if keep:
            kept_ref[...] = values[...]
        low_group = step * block_groups
        whole(main, main_chunks, values, low_group, low_group, low_group + block_groups)
        for g in split_groups(main, main_chunks):
            @pl.when(step == g // block_groups)
            def _(g=g):
                cut(main, main_chunks, values, g // block_groups * block_groups, g)

        ready = {n: 0 for n in span}
        for n, _, b1, _ in main_chunks:
            ready[n] = (b1 - 1) // cols // block_groups
        for at in range(steps):
            here = [n for n in span if ready[n] == at]
            if here:
                @pl.when(step == at)
                def _(here=here):
                    for n in here:
                        send_out(n)

        @pl.when(step == steps - 1)
        def _():
            for at in range(len(span)):
                pltpu.make_async_copy(staged.at[at], staged.at[at], out_sems.at[at]).wait()

    extra = [jax.ShapeDtypeStruct(main.shape, jnp.bfloat16)] if keep else []
    return ordered(
        kernel,
        grid=(steps,),
        out_shape=[jax.ShapeDtypeStruct(shape, jnp.bfloat16) for shape in outs] + extra,
        in_specs=[
            spec_smem(),
            pl.BlockSpec((left.shape[0], rows), lambda i: (0, i)),
            pl.BlockSpec(right.shape, lambda i: (0, 0), pipeline_mode=pl.Buffered(1)),
        ]
        + specs,
        out_specs=[spec_any()] * 4 + [pl.BlockSpec((rows, width), lambda i: (i, 0))] * len(extra),
        scratch_shapes=scratch
        + [
            pltpu.VMEM((rows, width), jnp.bfloat16),
            pltpu.VMEM((len(span), geo.slots * BLK, LANES), jnp.bfloat16),
            pltpu.VMEM((wide_rows + 2 * BLK, LANES), jnp.float32),
            pltpu.SemaphoreType.DMA((max(count, 1),)),
            pltpu.SemaphoreType.DMA((len(span),)),
        ],
        compiler_params=kernel_params(60),
        cost_estimate=cost(18),
    )(coords, left, right, *operands)


def pack_cross(geo, span, lefts, rights, vectors, seg):
    seg_blocks = geo.n_doc * geo.piece_blocks
    parts = bucket_parts(geo, span)
    names = list(lefts)
    vector_names = list(vectors)
    depth_rows = next(iter(rights.values())).shape[0]

    def window(cols):
        return (-(-(seg_blocks - 1) // cols) + 1) * BLK

    wide_rows = 0
    left_rows = BLK
    for item, chunks in parts:
        if len(item.shape) == 2:
            cols = item.shape[1] // LANES
            size = min(window(cols), item.shape[0])
            left_rows = max(left_rows, len(chunks) * size)
            wide_rows = max(wide_rows, len(chunks) * size * cols)

    def kernel(seg_ref, *refs):
        left = dict(zip(names, refs[: len(names)]))
        right = dict(zip(names, refs[len(names) : 2 * len(names)]))
        vector = dict(zip(vector_names, refs[2 * len(names) : 2 * len(names) + len(vector_names)]))
        out_ref, gathered, wide = refs[2 * len(names) + len(vector_names) :]
        low_slot = seg_ref[0] * seg_blocks
        out_ref[...] = jnp.zeros_like(out_ref)
        for item, chunks in parts:
            starts, size, cols = [], 0, 1
            if len(item.shape) == 2:
                cols = item.shape[1] // LANES
                size = min(window(cols), item.shape[0])
                for at, (n, b0, b1, slot) in enumerate(chunks):
                    first = jnp.maximum(low_slot, slot) - slot + b0
                    start = jnp.clip(first // cols * BLK, 0, item.shape[0] - size)
                    start = pl.multiple_of(start, BLK)
                    starts.append(start)
                    gathered[at * size : (at + 1) * size, :] = left[item.name][pl.ds(start, size), :]
                count = len(chunks) * size
                rows = gathered[:count, :]
                for cb in range(0, cols, 2):
                    tile = dot_nn(rows, right[item.name][:, cb * LANES : (cb + 2) * LANES])
                    wide[pl.ds(cb, count, stride=cols), :] = tile[:, :LANES]
                    wide[pl.ds(cb + 1, count, stride=cols), :] = tile[:, LANES:]
            else:
                vector_rows(wide, vector[item.name], vectors[item.name][1], item.rows)
            for at, (n, b0, b1, slot) in enumerate(chunks):
                begin = jnp.maximum(low_slot, slot)
                end = jnp.minimum(low_slot + seg_blocks, slot + b1 - b0)
                base = (at * size - starts[at]) * cols if starts else 0

                first, last = geo.full_groups(item, n) if starts else (0, 0)

                def by_row(t, carry, n=n, b0=b0, slot=slot, base=base):
                    src = pl.ds((b0 + t - slot) * BLK + base, BLK)
                    dst = pl.ds(pl.multiple_of((t - low_slot) * BLK, BLK), BLK)
                    out_ref[n - span.start, dst, :] = wide[src, :].astype(jnp.bfloat16)
                    return carry

                def by_tile(t, carry, n=n, b0=b0, slot=slot, base=base, cols=cols):
                    b = b0 + t - slot
                    group = b // cols
                    src = pl.ds(group * BLK * cols + b - group * cols + base, BLK, stride=cols)
                    dst = pl.ds(pl.multiple_of((t - low_slot) * BLK, BLK), BLK)
                    out_ref[n - span.start, dst, :] = wide[src, :].astype(jnp.bfloat16)
                    return carry

                if first < last:
                    lo = jnp.clip(slot + first * cols - b0, begin, jnp.maximum(begin, end))
                    hi = jnp.clip(slot + last * cols - b0, begin, jnp.maximum(begin, end))
                    lax.fori_loop(begin, lo, by_row, 0)
                    lax.fori_loop(lo, hi, by_tile, 0)
                    lax.fori_loop(hi, jnp.maximum(hi, end), by_row, 0)
                else:
                    lax.fori_loop(begin, jnp.maximum(begin, end), by_row, 0)

    operands = [lefts[n] for n in names] + [rights[n] for n in names]
    operands += [vectors[n][0] for n in vector_names]
    return ordered(
        kernel,
        out_shape=jax.ShapeDtypeStruct((len(span), seg_blocks * BLK, LANES), jnp.bfloat16),
        in_specs=[spec_smem()] + [spec_vmem()] * len(operands),
        out_specs=spec_vmem(),
        scratch_shapes=[
            pltpu.VMEM((left_rows, depth_rows), jnp.bfloat16),
            pltpu.VMEM((wide_rows + 2 * BLK, LANES), jnp.float32),
        ],
        compiler_params=kernel_params(),
        cost_estimate=cost(12),
    )(seg, *operands)
TILE = 512
PAIRS = HEADS // 2
TAIL_RATE = 0.3
TAIL = (
    0.11962929605681312,
    0.12075400207853171,
    0.0999131861559567,
    0.12856268365589474,
    -0.05368570534984477,
    0.20635578836359286,
    -0.15720441932045734,
    0.0356750954846771,
)


def dot_nn(left, right):
    return lax.dot_general(left, right, (((1,), (0,)), ((), ())), preferred_element_type=jnp.float32)


def dot_nt(left, right):
    return lax.dot_general(left, right, (((1,), (1,)), ((), ())), preferred_element_type=jnp.float32)


def dot_tn(left, right):
    return lax.dot_general(left, right, (((0,), (0,)), ((), ())), preferred_element_type=jnp.float32)


def low(values):
    return values.astype(jnp.bfloat16)


def gelu_pair(u):
    t = 1.0 / (1.0 + TAIL_RATE * jnp.abs(u))
    poly = TAIL[-1] * t + TAIL[-2]
    for coef in TAIL[-3::-1]:
        poly = poly * t + coef
    bell = jnp.exp(-0.5 * (u * u))
    tail = bell * (poly * t)
    spread = jnp.where(u < 0.0, tail, 1.0 - tail)
    return u * spread, spread + u * bell * (1.0 / math.sqrt(2.0 * math.pi))


def norm_rows(values, gain, shift):
    center = values - jnp.mean(values, axis=-1, keepdims=True)
    rate = lax.rsqrt(jnp.mean(center * center, axis=-1, keepdims=True) + EPSILON)
    normal = center * rate
    return normal * gain + shift, normal, rate


def norm_pull(grad, normal, rate, gain):
    scaled = grad * gain
    return rate * (
        scaled
        - jnp.mean(scaled, axis=-1, keepdims=True)
        - normal * jnp.mean(scaled * normal, axis=-1, keepdims=True)
    )


def fixed(shape):
    return pl.BlockSpec(shape, lambda i: (0,) * len(shape), pipeline_mode=pl.Buffered(1))


def tiles(cols, first=0):
    return pl.BlockSpec((TILE, cols), lambda i: (i + first, 0))


def both_heads(values):
    first = lax.broadcasted_iota(jnp.int32, values.shape, 1) < HEAD_DIM
    zero = jnp.zeros_like(values)
    return jnp.concatenate([jnp.where(first, values, zero), jnp.where(first, zero, values)], axis=0)


def side_by_side(stacked):
    half = stacked.shape[0] // 2
    return jnp.concatenate([stacked[:half], stacked[half:]], axis=1)


def third(part, pair):
    start = part * D + pair * LANES
    return slice(start, start + LANES)


def attend_kernel(x_ref, wqkv_ref, vec_ref, packed_ref, att_ref, stat_ref):
    x = x_ref[...]
    for j in range(3):
        cols = slice(j * D, (j + 1) * D)
        part = dot_nn(x, wqkv_ref[:, cols])
        packed_ref[:, cols] = low(part if j == 1 else part + vec_ref[j // 2 : j // 2 + 1, :])
    lanes = lax.broadcasted_iota(jnp.int32, (SEG_LEN, LANES), 1)

    def segment(s, carry):
        rows = pl.ds(pl.multiple_of(s * SEG_LEN, SEG_LEN), SEG_LEN)
        stat = jnp.zeros((SEG_LEN, LANES), jnp.float32)
        for pair in range(PAIRS):
            q = packed_ref[rows, third(0, pair)] * jnp.bfloat16(HEAD_DIM**-0.5)
            k = packed_ref[rows, third(1, pair)]
            v = packed_ref[rows, third(2, pair)]
            scores = dot_nt(both_heads(q), k)
            largest = jnp.max(scores, axis=-1, keepdims=True)
            raised = jnp.exp(scores - largest)
            summed = jnp.sum(raised, axis=-1, keepdims=True)
            weights = low(raised / summed)
            att_ref[rows, pair * LANES : (pair + 1) * LANES] = low(
                dot_nn(side_by_side(weights), both_heads(v))
            )
            log_sum = largest + jnp.log(summed)
            stat = jnp.where(lanes == 2 * pair, log_sum[:SEG_LEN], stat)
            stat = jnp.where(lanes == 2 * pair + 1, log_sum[SEG_LEN:], stat)
        stat_ref[rows, :] = stat
        return carry

    lax.fori_loop(0, TILE // SEG_LEN, segment, 0)


def in_parts(kernel, micros, count, inputs, in_specs, outs, out_specs, scratch, previous):
    previous = list(previous or ())
    return ordered(
        kernel,
        grid=(count,),
        in_specs=in_specs + [spec_any()] * len(previous),
        out_specs=out_specs,
        out_shape=outs,
        scratch_shapes=scratch,
        input_output_aliases={len(inputs) + i: i for i in range(len(previous))},
        compiler_params=kernel_params(60),
        cost_estimate=cost(micros),
    )(*inputs, *previous)


def attend_layer(x, w_qkv, vecs, first, count, previous):
    def rows(cols):
        return tiles(cols, first)

    def kernel(x_ref, wqkv_ref, vec_ref, *refs):
        attend_kernel(x_ref, wqkv_ref, vec_ref, *refs[-3:])

    return in_parts(
        kernel,
        8 * count,
        count,
        [x, w_qkv, vecs],
        [rows(D), fixed((D, 3 * D)), fixed((VECTOR_ROWS, D))],
        [jax.ShapeDtypeStruct(v.shape, v.dtype) for v in previous],
        [rows(3 * D), rows(D), rows(LANES)],
        [],
        previous,
    )


def attend_first(x, weights, coords):
    n = x.shape[0]
    bf, f32 = jnp.bfloat16, jnp.float32
    count = len(weights.operands)

    def kernel(coords_ref, *refs):
        sources, x_ref, refs = refs[:count], refs[count], refs[count + 1 :]
        packed_ref, att_ref, stat_ref, wqkv_ref, vec_ref, staged, wide, sems = refs
        weights.start(coords_ref, sources, staged, sems)
        waited = set()
        for number in range(2):
            weights.wait(number, waited, staged, sems)
        weights.matrix(0, staged, wide, wqkv_ref)
        vec_ref[...] = jnp.zeros_like(vec_ref)
        weights.vectors(1, staged, wide, vec_ref, 0)
        attend_kernel(x_ref, wqkv_ref, vec_ref, packed_ref, att_ref, stat_ref)

    whole = [pl.BlockSpec(shape, lambda i: (0, 0)) for shape in ((D, 3 * D), (VECTOR_ROWS, D))]
    return ordered(
        kernel,
        grid=(1,),
        in_specs=[spec_smem()] + [spec_any()] * count + [tiles(D)],
        out_specs=[tiles(3 * D), tiles(D), tiles(LANES)] + whole,
        out_shape=[
            jax.ShapeDtypeStruct((n, 3 * D), bf),
            jax.ShapeDtypeStruct((n, D), bf),
            jax.ShapeDtypeStruct((n, LANES), f32),
            jax.ShapeDtypeStruct((D, 3 * D), bf),
            jax.ShapeDtypeStruct((VECTOR_ROWS, D), f32),
        ],
        scratch_shapes=weights.scratch,
        compiler_params=kernel_params(60),
        cost_estimate=cost(12),
    )(coords, *weights.operands, x)


FBLOCK = D


def feed_kernel(
    x_ref, att_ref, wout_ref, wup_ref, wdown_ref, vec_ref,
    h1low_ref, norm1_ref, g_ref, dg_ref, norm2_ref, rate_ref, h2_ref, cls_ref, res_ref, h1_ref,
):
    step = pl.program_id(0)
    segs = TILE // SEG_LEN
    lanes = lax.broadcasted_iota(jnp.int32, (SEG_LEN, LANES), 1)
    res_ref[...] = dot_nn(att_ref[...], wout_ref[...])

    def start(s, carry):
        rows = pl.ds(pl.multiple_of(s * SEG_LEN, SEG_LEN), SEG_LEN)
        resid = x_ref[rows, :].astype(jnp.float32) + res_ref[rows, :] + vec_ref[2:3, :]
        hidden, normal, rate = norm_rows(resid, vec_ref[3:4, :], vec_ref[4:5, :])
        h1_ref[rows, :] = hidden
        h1low_ref[rows, :] = low(hidden)
        norm1_ref[rows, :] = low(normal)
        rate_ref[rows, :] = jnp.broadcast_to(rate, (SEG_LEN, LANES))
        return carry

    lax.fori_loop(0, segs, start, 0)
    h = h1low_ref[...]
    for j in range(FF // FBLOCK):
        cols = slice(j * FBLOCK, (j + 1) * FBLOCK)
        act, slope = gelu_pair(dot_nn(h, wup_ref[:, cols]) + vec_ref[5 + j : 6 + j, :])
        g = low(act)
        g_ref[:, cols] = g
        dg_ref[:, cols] = low(slope)
        part = dot_nn(g, wdown_ref[cols, :])
        if j == 0:
            res_ref[...] = part
        else:
            res_ref[...] += part

    def finish(s, carry):
        rows = pl.ds(pl.multiple_of(s * SEG_LEN, SEG_LEN), SEG_LEN)
        resid = h1_ref[rows, :] + res_ref[rows, :] + vec_ref[9:10, :]
        hidden, normal, rate = norm_rows(resid, vec_ref[10:11, :], vec_ref[11:12, :])
        h2_ref[rows, :] = low(hidden)
        norm2_ref[rows, :] = low(normal)
        rate_ref[rows, :] = jnp.where(lanes == 0, rate_ref[rows, :], rate)
        cls_ref[pl.ds(step * segs + s, 1), :] = hidden[0:1, :]
        return carry

    lax.fori_loop(0, segs, finish, 0)


def feed_layer(x, att, weights, coords):
    n = x.shape[0]
    bf, f32 = jnp.bfloat16, jnp.float32
    count = len(weights.operands)
    steps = n // TILE
    shapes = [item.shape for item in weights.items if item.cols]

    def kernel(coords_ref, *refs):
        sources, refs = refs[:count], refs[count:]
        x_ref, att_ref = refs[:2]
        outs, kept = refs[2:10], refs[10:13]
        vec_ref, res_ref, h1_ref, out_sems = refs[13:17]
        held, (staged, wide, sems) = refs[17:20], refs[20:]
        step = pl.program_id(0)

        @pl.when(step == 0)
        def _():
            weights.start(coords_ref, sources, staged, sems)
            waited = set()
            vec_ref[...] = jnp.zeros_like(vec_ref)
            place = row = 0
            for number, item in enumerate(weights.items):
                weights.wait(number, waited, staged, sems)
                if item.cols:
                    weights.matrix(number, staged, wide, held[place])
                    pltpu.make_async_copy(held[place], kept[place], out_sems.at[place]).start()
                    place += 1
                else:
                    weights.vectors(number, staged, wide, vec_ref, row)
                    row += item.rows * LANES // D

        feed_kernel(x_ref, att_ref, *held, vec_ref, *outs, res_ref, h1_ref)

        @pl.when(step == steps - 1)
        def _():
            for place in range(3):
                pltpu.make_async_copy(held[place], kept[place], out_sems.at[place]).wait()

    return ordered(
        kernel,
        grid=(steps,),
        in_specs=[spec_smem()] + [spec_any()] * count + [tiles(D), tiles(D)],
        out_specs=[tiles(D), tiles(D), tiles(FF), tiles(FF), tiles(D), tiles(LANES), tiles(D)]
        + [pl.BlockSpec((n // SEG_LEN, D), lambda i: (0, 0))]
        + [spec_any()] * 3
        + [pl.BlockSpec((VECTOR_ROWS, D), lambda i: (0, 0))],
        out_shape=[
            jax.ShapeDtypeStruct((n, cols), kind)
            for cols, kind in ((D, bf), (D, bf), (FF, bf), (FF, bf), (D, bf), (LANES, f32), (D, bf))
        ]
        + [jax.ShapeDtypeStruct((n // SEG_LEN, D), f32)]
        + [jax.ShapeDtypeStruct(shape, bf) for shape in shapes]
        + [jax.ShapeDtypeStruct((VECTOR_ROWS, D), f32)],
        scratch_shapes=[
            pltpu.VMEM((TILE, D), f32),
            pltpu.VMEM((TILE, D), f32),
            pltpu.SemaphoreType.DMA((3,)),
        ]
        + [pltpu.VMEM(shape, bf) for shape in shapes]
        + weights.scratch,
        compiler_params=kernel_params(62),
        cost_estimate=cost(60),
    )(coords, *weights.operands, x, att)


def feed_back_kernel(
    cot_ref, cls_ref, norm2_ref, dg_ref, norm1_ref, rate_ref,
    wdown_ref, wup_ref, wout_ref, vec_ref,
    dm_ref, du_ref, dao_ref, da_ref, one_ref, sums_ref, res_ref,
):
    step = pl.program_id(0)

    @pl.when(step == 0)
    def _():
        sums_ref[...] = jnp.zeros_like(sums_ref)

    segs = TILE // SEG_LEN
    row_ids = lax.broadcasted_iota(jnp.int32, (SEG_LEN, D), 0)

    def add_sum(row, values):
        sums_ref[row : row + 1, :] += jnp.sum(values, axis=0, keepdims=True)

    def start(s, carry):
        rows = pl.ds(pl.multiple_of(s * SEG_LEN, SEG_LEN), SEG_LEN)
        cls = cls_ref[pl.ds(step * segs + s, 1), :]
        grad = jnp.where(row_ids == 0, cls, cot_ref[rows, :].astype(jnp.float32))
        normal = norm2_ref[rows, :].astype(jnp.float32)
        add_sum(10, grad * normal)
        add_sum(11, grad)
        two = norm_pull(grad, normal, rate_ref[rows, 1:2], vec_ref[10:11, :])
        res_ref[rows, :] = two
        dm = low(two)
        dm_ref[rows, :] = dm
        add_sum(9, dm.astype(jnp.float32))
        return carry

    lax.fori_loop(0, segs, start, 0)
    dm = dm_ref[...]
    for j in range(FF // FBLOCK):
        cols = slice(j * FBLOCK, (j + 1) * FBLOCK)
        du = low(dot_nt(dm, wdown_ref[cols, :]) * dg_ref[:, cols].astype(jnp.float32))
        du_ref[:, cols] = du
        add_sum(5 + j, du.astype(jnp.float32))
        res_ref[...] += dot_nt(du, wup_ref[:, cols])

    def finish(s, carry):
        rows = pl.ds(pl.multiple_of(s * SEG_LEN, SEG_LEN), SEG_LEN)
        grad = res_ref[rows, :]
        normal = norm1_ref[rows, :].astype(jnp.float32)
        add_sum(3, grad * normal)
        add_sum(4, grad)
        one = norm_pull(grad, normal, rate_ref[rows, 0:1], vec_ref[3:4, :])
        one_ref[rows, :] = one
        dao = low(one)
        dao_ref[rows, :] = dao
        add_sum(2, dao.astype(jnp.float32))
        return carry

    lax.fori_loop(0, segs, finish, 0)
    da_ref[...] = low(dot_nt(dao_ref[...], wout_ref[...]))


def feed_back(cot, cls, norm2, dg, norm1, rates, w_down, w_up, w_out, vecs):
    n = cot.shape[0]
    bf, f32 = jnp.bfloat16, jnp.float32
    return ordered(
        feed_back_kernel,
        grid=(n // TILE,),
        in_specs=[
            tiles(D), fixed((n // SEG_LEN, D)), tiles(D), tiles(FF), tiles(D), tiles(LANES),
            fixed((FF, D)), fixed((D, FF)), fixed((D, D)), fixed((VECTOR_ROWS, D)),
        ],
        out_specs=[
            tiles(D), tiles(FF), tiles(D), tiles(D), tiles(D),
            pl.BlockSpec((VECTOR_ROWS, D), lambda i: (0, 0)),
        ],
        out_shape=[
            jax.ShapeDtypeStruct((n, D), bf),
            jax.ShapeDtypeStruct((n, FF), bf),
            jax.ShapeDtypeStruct((n, D), bf),
            jax.ShapeDtypeStruct((n, D), bf),
            jax.ShapeDtypeStruct((n, D), f32),
            jax.ShapeDtypeStruct((VECTOR_ROWS, D), f32),
        ],
        scratch_shapes=[pltpu.VMEM((TILE, D), f32)],
        compiler_params=kernel_params(60),
        cost_estimate=cost(44),
    )(cot, cls, norm2, dg, norm1, rates, w_down, w_up, w_out, vecs)


def attend_back_kernel(packed_ref, stat_ref, da_ref, before_ref, *refs):
    dqkv_ref, sums_ref = refs[-2:]

    @pl.when(pl.program_id(0) == 0)
    def _():
        sums_ref[...] = before_ref[...]

    lanes = lax.broadcasted_iota(jnp.int32, (SEG_LEN, LANES), 1)
    scale = HEAD_DIM**-0.5

    def segment(s, carry):
        rows = pl.ds(pl.multiple_of(s * SEG_LEN, SEG_LEN), SEG_LEN)
        stat = stat_ref[rows, :]
        for pair in range(PAIRS):
            q = packed_ref[rows, third(0, pair)] * jnp.bfloat16(scale)
            k = packed_ref[rows, third(1, pair)]
            v = packed_ref[rows, third(2, pair)]
            da = da_ref[rows, pair * LANES : (pair + 1) * LANES]
            queries, grads = both_heads(q), both_heads(da)
            log_sum = jnp.concatenate([stat[:, 2 * pair : 2 * pair + 1], stat[:, 2 * pair + 1 : 2 * pair + 2]], axis=0)
            weights = jnp.exp(dot_nt(queries, k) - log_sum)
            grad_weights = dot_nt(grads, v)
            dv = dot_tn(low(weights), grads)
            inner = jnp.sum(grad_weights * weights, axis=-1, keepdims=True)
            ds = low(weights * (grad_weights - inner))
            dq = dot_nn(side_by_side(ds), both_heads(k)) * scale
            dk = dot_tn(ds, queries)
            for part, grad in enumerate((dq, dk, dv)):
                grad = low(grad)
                cols = third(part, pair)
                dqkv_ref[rows, cols] = grad
                if part != 1:
                    here = (slice(part // 2, part // 2 + 1), third(0, pair))
                    sums_ref[here] += jnp.sum(grad.astype(jnp.float32), axis=0, keepdims=True)
        return carry

    lax.fori_loop(0, TILE // SEG_LEN, segment, 0)


def attend_back(packed, stat, da, first, count, previous=None):
    n = packed.shape[0]
    before = previous[1] if previous else jnp.zeros((8, D), jnp.float32)
    return in_parts(
        attend_back_kernel,
        10 * count,
        count,
        [packed, stat, da, before],
        [tiles(3 * D, first), tiles(LANES, first), tiles(D, first), fixed((8, D))],
        [jax.ShapeDtypeStruct((n, 3 * D), jnp.bfloat16), jax.ShapeDtypeStruct((8, D), jnp.float32)],
        [tiles(3 * D, first), pl.BlockSpec((8, D), lambda i: (0, 0))],
        [],
        previous and previous[:1],
    )


def cross_kernel(
    load, rows_ref, tagc_ref, tagr_ref, gz_ref, wqkv_ref, wout_ref, wup_ref, wdown_ref, vec_ref,
    out_ref, grows_ref, sums_ref, gqkv_ref, go_ref, gu_ref, gm_ref, rowst_ref, attt_ref, hidt_ref, actt_ref,
    packed_ref, weights_ref, att_ref, act_ref, slope_ref, res_ref,
):
    scale = HEAD_DIM**-0.5
    rows = rows_ref[...]
    rowst_ref[...] = rows.T
    same = tagc_ref[:, 0:1] == tagr_ref[0:1, :]
    same = jnp.concatenate([same, same], axis=0)

    def add_sum(row, values):
        sums_ref[row : row + 1, :] = jnp.sum(values.astype(jnp.float32), axis=0, keepdims=True)

    def pair_cols(pair):
        return slice(pair * LANES, (pair + 1) * LANES)

    sums_ref[...] = jnp.zeros_like(sums_ref)
    load(0)
    for j in range(3):
        cols = slice(j * D, (j + 1) * D)
        part = dot_nn(rows, wqkv_ref[:, cols])
        packed_ref[:, cols] = low(part if j == 1 else part + vec_ref[j // 2 : j // 2 + 1, :])
    for pair in range(PAIRS):
        q = packed_ref[:, third(0, pair)] * jnp.bfloat16(scale)
        scores = jnp.where(same, dot_nt(both_heads(q), packed_ref[:, third(1, pair)]), NEGATIVE)
        raised = jnp.exp(scores - jnp.max(scores, axis=-1, keepdims=True))
        weights = raised / jnp.sum(raised, axis=-1, keepdims=True)
        weights_ref[pair] = weights
        blend = dot_nn(side_by_side(low(weights)), both_heads(packed_ref[:, third(2, pair)]))
        att_ref[:, pair_cols(pair)] = low(blend)
    att = att_ref[...]
    attt_ref[...] = att.T
    load(1)
    resid = rows.astype(jnp.float32) + dot_nn(att, wout_ref[...]) + vec_ref[2:3, :]
    hidden, normal_three, rate_three = norm_rows(resid, vec_ref[3:4, :], vec_ref[4:5, :])
    hidden_low = low(hidden)
    hidt_ref[...] = hidden_low.T
    load(2)
    res_ref[...] = hidden + vec_ref[9:10, :]
    for j in range(FF // FBLOCK):
        cols = slice(j * FBLOCK, (j + 1) * FBLOCK)
        act, slope = gelu_pair(dot_nn(hidden_low, wup_ref[:, cols]) + vec_ref[5 + j : 6 + j, :])
        act = low(act)
        actt_ref[cols, :] = act.T
        slope_ref[:, cols] = slope
        res_ref[...] += dot_nn(act, wdown_ref[cols, :])
    crossed, normal_four, rate_four = norm_rows(res_ref[...], vec_ref[10:11, :], vec_ref[11:12, :])
    out_ref[...] = low(crossed)

    grad_z = gz_ref[...].astype(jnp.float32)
    add_sum(10, grad_z * normal_four)
    add_sum(11, grad_z)
    grad_four = norm_pull(grad_z, normal_four, rate_four, vec_ref[10:11, :])
    grad_m = low(grad_four)
    gm_ref[...] = grad_m
    add_sum(9, grad_m)
    res_ref[...] = grad_four
    for j in range(FF // FBLOCK):
        cols = slice(j * FBLOCK, (j + 1) * FBLOCK)
        grad_u = low(dot_nt(grad_m, wdown_ref[cols, :]) * slope_ref[:, cols])
        gu_ref[:, cols] = grad_u
        add_sum(5 + j, grad_u)
        res_ref[...] += dot_nt(grad_u, wup_ref[:, cols])
    grad_h = res_ref[...]
    add_sum(3, grad_h * normal_three)
    add_sum(4, grad_h)
    grad_three = norm_pull(grad_h, normal_three, rate_three, vec_ref[3:4, :])
    grad_o = low(grad_three)
    go_ref[...] = grad_o
    add_sum(2, grad_o)
    res_ref[...] = grad_three
    att_ref[...] = low(dot_nt(grad_o, wout_ref[...]))
    for pair in range(PAIRS):
        queries = both_heads(packed_ref[:, third(0, pair)] * jnp.bfloat16(scale))
        grads = both_heads(att_ref[:, pair_cols(pair)])
        weights = weights_ref[pair]
        grad_weights = dot_nt(grads, packed_ref[:, third(2, pair)])
        dv = dot_tn(low(weights), grads)
        inner = jnp.sum(grad_weights * weights, axis=-1, keepdims=True)
        ds = low(weights * (grad_weights - inner))
        dq = dot_nn(side_by_side(ds), both_heads(packed_ref[:, third(1, pair)])) * scale
        dk = dot_tn(ds, queries)
        for part, grad in enumerate((dq, dk, dv)):
            gqkv_ref[:, third(part, pair)] = low(grad)
    add_sum(0, gqkv_ref[:, :D])
    add_sum(1, gqkv_ref[:, 2 * D :])
    for j in range(3):
        cols = slice(j * D, (j + 1) * D)
        res_ref[...] += dot_nt(gqkv_ref[:, cols], wqkv_ref[:, cols])
    grows_ref[...] = low(res_ref[...])


def cross_layer(cls, places, tags, grad_out, weights, coords):
    m = cls.shape[0]
    bf, f32 = jnp.bfloat16, jnp.float32
    tagc = jnp.broadcast_to(tags.astype(f32)[:, None], (m, LANES))
    tagr = jnp.broadcast_to(tags.astype(f32)[None, :], (8, m))
    count = len(weights.operands)
    operands = [cls, tagc, tagr, grad_out]
    shapes = [(m, D), (m, D), (VECTOR_ROWS, D), (m, 3 * D), (m, D), (m, FF), (m, D), (D, m), (D, m), (D, m), (FF, m)]
    matrices = [number for number, item in enumerate(weights.items) if item.cols]
    vectors = [number for number, item in enumerate(weights.items) if not item.cols]
    needs = [(matrices[:1], vectors[:1]), (matrices[1:2], vectors[1:2]), (matrices[2:], vectors[2:])]

    def kernel(coords_ref, *refs):
        sources, refs = refs[:count], refs[count:]
        ins, outs = refs[: len(operands)], refs[len(operands) : len(operands) + len(shapes)]
        held, vec_ref, refs = refs[-8:-4], refs[-4], (refs[len(operands) + len(shapes) : -8], refs[-3:])
        scratch, (staged, wide, sems) = refs
        waited = set()
        rows_of = {number: row for number, row in zip(vectors, (0, 2, 5, 9))}
        weights.start(coords_ref, sources, staged, sems)

        def load(stage):
            for number in needs[stage][0]:
                weights.wait(number, waited, staged, sems)
                weights.matrix(number, staged, wide, held[matrices.index(number)])
            for number in needs[stage][1]:
                weights.wait(number, waited, staged, sems)
                weights.vectors(number, staged, wide, vec_ref, rows_of[number])

        vec_ref[...] = jnp.zeros_like(vec_ref)
        cross_kernel(load, *ins, *held, vec_ref, *outs, *scratch)

    return ordered(
        kernel,
        out_shape=[jax.ShapeDtypeStruct(shape, f32 if i == 2 else bf) for i, shape in enumerate(shapes)],
        in_specs=[spec_smem()] + [spec_any()] * count + [spec_vmem()] * len(operands),
        out_specs=[spec_vmem()] * len(shapes),
        scratch_shapes=[
            pltpu.VMEM((m, 3 * D), bf),
            pltpu.VMEM((PAIRS, 2 * m, m), f32),
            pltpu.VMEM((m, D), bf),
            pltpu.VMEM((m, D), bf),
            pltpu.VMEM((m, FF), f32),
            pltpu.VMEM((m, D), f32),
        ]
        + [pltpu.VMEM(weights.items[number].shape, bf) for number in matrices]
        + [pltpu.VMEM((VECTOR_ROWS, D), f32)]
        + weights.scratch,
        compiler_params=kernel_params(62),
        cost_estimate=cost(22),
    )(coords, *weights.operands, *operands)


def class_rows(cls, cot, hot, doc, pos, weights, coords):
    count = len(weights.operands)
    segs = cls.shape[0]

    def kernel(coords_ref, *refs):
        sources, (cls_ref, cot_ref, hot_ref, doc_ref, pos_ref, out_ref, wide_out, table, staged, wide, sems) = (
            refs[:count],
            refs[count:],
        )
        weights.start(coords_ref, sources, staged, sems)
        lanes = lax.broadcasted_iota(jnp.int32, (1, LANES), 1)
        for s in range(segs):
            wide_out[s : s + 1, D : 2 * D] = cot_ref[s, 0:1, :].astype(jnp.float32)
            tag = jnp.where(lanes == 0, doc_ref[s], jnp.where(lanes == 1, pos_ref[s], 0))
            wide_out[s : s + 1, 2 * D :] = tag.astype(jnp.float32)
        weights.wait(0, set(), staged, sems)
        weights.matrix(0, staged, wide, table)
        wide_out[:, :D] = cls_ref[...] + dot_nn(hot_ref[...], table[...])
        out_ref[...] = low(wide_out[...])

    def whole(shape):
        return pl.BlockSpec(shape, lambda i: (0,) * len(shape))

    return ordered(
        kernel,
        grid=(1,),
        out_shape=jax.ShapeDtypeStruct((segs, 2 * D + LANES), jnp.bfloat16),
        in_specs=[spec_smem()] + [spec_any()] * count
        + [whole(cls.shape), whole((segs, BLK, D)), whole(hot.shape), spec_smem(), spec_smem()],
        out_specs=whole((segs, 2 * D + LANES)),
        scratch_shapes=[
            pltpu.VMEM((segs, 2 * D + LANES), jnp.float32),
            pltpu.VMEM((LONG_SEGS, D), jnp.bfloat16),
        ]
        + weights.scratch,
        compiler_params=kernel_params(),
        cost_estimate=cost(3),
    )(coords, *weights.operands, cls, cot, hot, doc, pos)


def token_back(grad_one, dqkv, w_qkv, first, count, previous=None):
    n = grad_one.shape[0]

    def kernel(one_ref, dqkv_ref, wqkv_ref, *refs):
        total = one_ref[...]
        for j in range(3):
            cols = slice(j * D, (j + 1) * D)
            total = total + dot_nt(dqkv_ref[:, cols], wqkv_ref[:, cols])
        refs[-1][...] = low(total)

    return in_parts(
        kernel,
        3 * count,
        count,
        [grad_one, dqkv, w_qkv],
        [tiles(D, first), tiles(3 * D, first), fixed((D, 3 * D))],
        [jax.ShapeDtypeStruct((n, D), jnp.bfloat16)],
        [tiles(D, first)],
        [],
        previous,
    )
AXES = ("seg", "doc")


def send(geo, value, axis, step):
    return lax.ppermute(value, AXES, geo.shift(axis, step))


def flat_call(kernel, inputs, outs, micros=2):
    rows = [value.reshape(-1, LANES) for value in inputs]
    shapes = [jax.ShapeDtypeStruct((math.prod(shape[:-1]), LANES), jnp.bfloat16) for shape in outs]
    results = ordered(
        kernel,
        out_shape=shapes,
        in_specs=[spec_vmem()] * len(rows),
        out_specs=[spec_vmem()] * len(outs),
        compiler_params=kernel_params(60),
        cost_estimate=cost(micros),
    )(*rows)
    return [value.reshape(shape) for value, shape in zip(results, outs)]


def in_blocks(count, body):
    copy_rows(count, 256, lambda row, rows: body(pl.multiple_of(row, BLK), rows))


def gather_line(geo, pieces, my_z, cut):
    parts = [pieces] + [send(geo, pieces, Z, r) for r in range(1, geo.n_doc)]
    return place_line(geo, parts, my_z, cut)


def gather_plane(geo, halves, step):
    orders = ((X, Y), (Y, X))
    inputs, outs, sizes = [], [], []
    for half, order in zip(halves, orders):
        came = [send(geo, half, order[step], r) for r in range(1, geo.size(order[step]))]
        inputs += [half] + came
        sizes.append(1 + len(came))
        outs.append((sizes[-1],) + half.shape)

    def kernel(*refs):
        sources, targets = refs[: sum(sizes)], refs[sum(sizes) :]
        for at, target in enumerate(targets):
            for place, source in enumerate(sources[sum(sizes[:at]) : sum(sizes[: at + 1])]):
                count = source.shape[0]

                def move(row, rows, source=source, target=target, base=place * count):
                    target[pl.ds(base + row, rows), :] = source[pl.ds(row, rows), :]

                in_blocks(count, move)

    return flat_call(kernel, inputs, outs)


def gather_cores(geo, halves):
    return [array for half in halves for array in (half, send(geo, half, C, 1))]


def reduce_cores(geo, arrays):
    return [[arrays[2 * half], send(geo, arrays[2 * half + 1], C, 1)] for half in range(2)]


def add_blocks(sources, target, source_row, target_row, count):
    def body(row, rows):
        total = sources[0][pl.ds(source_row + row, rows), :].astype(jnp.float32)
        for source in sources[1:]:
            total = total + source[pl.ds(source_row + row, rows), :].astype(jnp.float32)
        target[pl.ds(target_row + row, rows), :] = low(total)

    in_blocks(count, body)


def reduce_plane(geo, halves, step):
    orders = ((Y, X), (X, Y))
    inputs, outs, sizes = [], [], []
    for half, order in zip(halves, orders):
        inputs += half
        sizes.append((len(half), geo.size(order[step])))
        outs += [half[0].shape[1:]] * sizes[-1][1]

    def kernel(*refs):
        sources, targets = refs[: len(inputs)], refs[len(inputs) :]
        for terms, places in sizes:
            for place in range(places):
                count = targets[place].shape[0]
                add_blocks(sources[:terms], targets[place], place * count, 0, count)
            sources, targets = sources[terms:], targets[places:]

    results = flat_call(kernel, inputs, outs)
    halves = []
    for (_, places), order in zip(sizes, orders):
        mine, results = results[:places], results[places:]
        halves.append([mine[0]] + [send(geo, mine[r], order[step], r) for r in range(1, places)])
    return halves


def reduce_line(geo, halves, my_z):
    nd = geo.n_doc
    inputs = [value for half in halves for value in half]
    counts = [half[0].shape[0] for half in halves]

    def kernel(z_ref, *refs):
        sources, targets = refs[: len(inputs)], refs[len(inputs) :]
        done = 0
        for half, n in zip(halves, counts):
            terms, sources = sources[: len(half)], sources[len(half) :]
            for r in range(nd):
                first = pl.multiple_of(wrap(z_ref[0] + r, nd) * geo.piece, BLK)
                for i in range(n):
                    here = pl.ds(first, geo.piece)
                    total = sum(term[i, here, :].astype(jnp.float32) for term in terms)
                    targets[r][done + i] = low(total)
            done += n

    outs = ordered(
        kernel,
        out_shape=[jax.ShapeDtypeStruct((sum(counts), geo.piece, LANES), jnp.bfloat16)] * nd,
        in_specs=[spec_smem()] + [spec_vmem()] * len(inputs),
        out_specs=[spec_vmem()] * nd,
        compiler_params=kernel_params(60),
        cost_estimate=cost(2),
    )(my_z.reshape(1), *inputs)
    return [outs[0]] + [send(geo, outs[r], Z, r) for r in range(1, nd)]


def sum_pieces(geo, groups):
    inputs = [part for group in groups for part in group]

    def kernel(*refs):
        sources, target = refs[:-1], refs[-1]
        row = 0
        for group in groups:
            terms, sources = sources[: len(group)], sources[len(group) :]
            count = terms[0].shape[0]
            add_blocks(terms, target, 0, row, count)
            row += count

    count = sum(group[0].shape[0] for group in groups)
    return flat_call(kernel, inputs, [(count, geo.piece, LANES)])[0]


def gate(value):
    def kernel(source, target):
        in_blocks(source.shape[0], lambda row, rows: target.__setitem__(
            (pl.ds(row, rows), slice(None)), source[pl.ds(row, rows), :]
        ))

    return flat_call(kernel, [value], [value.shape])[0]
def optimizer_step(gradient, master, momentum, average, scaling, rating):
    scaled = gradient * scaling
    moment = 0.5 * momentum + scaled
    weight = master - rating * (scaled + 0.5 * moment)
    smooth = 0.5 * average + 0.5 * weight
    return (weight, moment, smooth, low(weight))


def row_rates(geo, n_tokens, n_cls):
    total = geo.chunk * geo.n_dev
    scaling = np.zeros((total,), np.float32)
    rating = np.full((total,), 0.2, np.float32)
    names = list(LAYOUT)
    cross = names[-13:]
    row = 0
    for name, shape in LAYOUT.items():
        rows = math.prod(shape) // LANES
        scaling[row : row + rows] = 1.0 / math.sqrt(n_cls if name in cross else n_tokens)
        if len(shape) == 2:
            rating[row : row + rows] = 1.0 if name == cross[0] else 0.5 / math.sqrt(shape[0])
        row += rows
    return scaling.reshape(geo.n_dev, geo.chunk), rating.reshape(geo.n_dev, geo.chunk)


def matmul(left, right):
    return jnp.dot(left, right, preferred_element_type=jnp.float32)


def column_sum(rows):
    return jnp.sum(rows.astype(jnp.float32), axis=0, keepdims=True)


def local(tokens, cotangent, seg_doc, seg_pos, master, momentum, average):
    n_seg = lax.axis_size(AXES[0])
    n_doc = lax.axis_size(AXES[1])
    geo = Geometry(n_seg, n_doc, master.shape[0])
    by = geo.by_name
    gather = Buckets(geo, [4, 4, 1], by.w_out, by.pos_table)
    buckets = Buckets(geo, [4, 4, 4, 1], by.w_out, by.w_down, by.pos_table)
    my_seg, my_doc = lax.axis_index(AXES[0]), lax.axis_index(AXES[1])
    me = my_seg * n_doc + my_doc
    coords = jnp.stack([my_seg // 4, my_seg // 2 % 2, my_seg % 2, my_doc]).astype(jnp.int32)
    table = lax.dynamic_index_in_dim(jnp.asarray(geo.block_tables()[1]), me, 0, False)
    pad_rows = ceil_to(geo.chunk + 4 * BLK, 8)
    ORDER.start()
    aligned = align_rows(geo, table, master.reshape(geo.chunk, LANES), pad_rows)
    pieces = lax.all_to_all(aligned.reshape(geo.n_dev, geo.piece, LANES), AXES, 0, 0, tiled=True)
    parts = [pieces[span.start : span.stop] for span in gather.ranges]

    seg_count = tokens.shape[1]
    n_rows = n_seg * seg_count
    tiles_all = seg_count * SEG_LEN // TILE
    middle = max(1, tiles_all - 2)
    last = tiles_all - 1 - middle
    inputs = tokens[0].reshape(seg_count * SEG_LEN, D)
    cot_rows = cotangent[0]
    cut = gather.half

    line = gather_line(geo, parts[0], my_doc, cut[0])
    parts_b = [parts[1]] + [send(geo, parts[1], Z, r) for r in range(1, n_doc)]
    ORDER.wait_for(*parts_b[1:2])
    plane = gather_plane(geo, line, 0)
    ORDER.wait_for(*parts_b[2:3])
    plane = gather_plane(geo, plane, 1)
    gathered = [gather_cores(geo, plane), None, None]

    def weights(*numbers):
        return Weights(geo, gather, gathered, [item_name(i) for i in numbers])

    def own(values):
        return lax.dynamic_slice_in_dim(values, my_seg * seg_count, seg_count, axis=0)

    plane_b = place_line(geo, parts_b, my_doc, cut[1])
    *outs, w_qkv, vec_a = attend_first(inputs, weights(0, 1), coords)
    plane_b = gather_plane(geo, plane_b, 0)
    gathered[2] = [lax.all_gather(gate(parts[2]), AXES)]
    outs = attend_layer(inputs, w_qkv, vec_a, 1, middle, outs)
    plane_b = gather_plane(geo, plane_b, 1)
    gathered[1] = gather_cores(geo, plane_b)
    if last:
        outs = attend_layer(inputs, w_qkv, vec_a, 1 + middle, last, outs)
    packed, attended, stat = outs
    hidden_low, normal_one, active, slope, normal_two, rates, hidden_two, cls, w_out, w_up, w_down, vec = feed_layer(
        inputs, attended, weights(1, 2, 3, 4, 5, 6, 7), coords
    )

    hot = (seg_pos[0][:, None] == jnp.arange(LONG_SEGS)[None, :]).astype(jnp.bfloat16)
    mine = class_rows(cls, cot_rows, hot, seg_doc[0], seg_pos[0], weights(8), coords)
    tagged = lax.all_gather(mine, AXES[0], axis=0, tiled=True)
    rows, all_grad, all_doc, all_pos = tagged[:, :D], tagged[:, D : 2 * D], tagged[:, 2 * D], tagged[:, 2 * D + 1]
    pos_hot = (all_pos.astype(jnp.int32)[:, None] == jnp.arange(LONG_SEGS)[None, :]).astype(jnp.bfloat16)
    crossed, grad_rows, xsums, g_qkv, g_o, g_u, g_m, rows_t, att_t, hid_t, act_t = cross_layer(
        rows, all_pos, all_doc, all_grad, weights(9, 10, 11, 12, 13, 14, 15, 16), coords
    )
    names = [item_name(i) for i in (8, 9, 11, 13, 15)]
    line_c = pack_cross(
        geo,
        buckets.ranges[3],
        dict(zip(names, (pos_hot.T, rows_t, att_t, hid_t, act_t))),
        dict(zip(names, (grad_rows, g_qkv, g_o, g_u, g_m))),
        {item_name(i): (xsums, row) for i, row in ((10, 0), (12, 2), (14, 5), (16, 9))},
        my_seg.astype(jnp.int32).reshape(1),
    )
    line_c = reduce_line(geo, [[line_c]], my_doc)

    grads = {}
    dm, du, dao, da, grad_one, sums = feed_back(
        cot_rows.reshape(-1, D), own(grad_rows).astype(jnp.float32), normal_two, slope, normal_one, rates,
        w_down, w_up, w_out, vec,
    )
    pieces_c = sum_pieces(geo, [line_c])
    grads[item_name(8)] = low(matmul(hot.T, own(grad_rows)))
    for number, row in ((3, 2), (5, 5), (7, 9)):
        grads[item_name(number)] = (sums, row)
    *arrays_d, grads[item_name(6)] = grad_bucket(
        geo, buckets, 2, grads, coords, item_name(6), active, dm, 512, keep=True
    )
    halves_d = reduce_cores(geo, arrays_d)
    grads[item_name(2)] = low(matmul(attended.T, dao))
    ORDER.wait_for(grads[item_name(2)])
    halves_d = reduce_plane(geo, halves_d, 0)
    arrays_b = grad_bucket(geo, buckets, 1, grads, coords, item_name(4), hidden_low, du, 256)
    halves_b = reduce_cores(geo, arrays_b)
    back = attend_back(packed, stat, da, 0, 1)
    halves_d = reduce_plane(geo, halves_d, 1)
    halves_b = reduce_plane(geo, halves_b, 0)
    if tiles_all > 1:
        back = attend_back(packed, stat, da, 1, middle, back)
    line_d = reduce_line(geo, halves_d, my_doc)
    halves_b = reduce_plane(geo, halves_b, 1)
    if last:
        back = attend_back(packed, stat, da, 1 + middle, last, back)
    dqkv, qv_sums = back
    pieces_d = sum_pieces(geo, [line_d])
    line_b = reduce_line(geo, halves_b, my_doc)
    grads[item_name(1)] = (qv_sums, 0)
    arrays_a = grad_bucket(geo, buckets, 0, grads, coords, item_name(0), inputs, dqkv, 256)
    halves_a = reduce_cores(geo, arrays_a)
    halves_a = reduce_plane(geo, halves_a, 0)
    token_grad, = token_back(grad_one, dqkv, w_qkv, 0, tiles_all)
    pieces_b = sum_pieces(geo, [line_b])
    halves_a = reduce_plane(geo, halves_a, 1)
    first_row = lax.broadcasted_iota(jnp.int32, (seg_count, SEG_LEN, D), 1) == 0
    mixed_out = jnp.where(
        first_row, own(crossed)[:, None, :], hidden_two.reshape(seg_count, SEG_LEN, D)
    )
    line_a = reduce_line(geo, halves_a, my_doc)
    all_pieces = sum_pieces(geo, [line_a, [pieces_b], [pieces_d], [pieces_c]])
    owned = lax.all_to_all(all_pieces, AXES, 0, 0, tiled=True)
    natural = natural_rows(geo, table, owned.reshape(-1, LANES), pad_rows)
    gradient = natural[BLK : BLK + geo.chunk].reshape(-1)
    n_cls = n_doc * n_rows
    scaling, rating = (
        jnp.broadcast_to(
            lax.dynamic_index_in_dim(jnp.asarray(rates), me, 0, False)[:, None], (geo.chunk, LANES)
        ).reshape(-1)
        for rates in row_rates(geo, n_cls * SEG_LEN, n_cls)
    )
    weight, moment, smooth, copy_low = optimizer_step(
        gradient, master, momentum, average, scaling, rating
    )
    return (
        mixed_out[None],
        token_grad.reshape(1, seg_count, SEG_LEN, D),
        weight,
        moment,
        smooth,
        copy_low,
    )


def item_name(number):
    return item_list(0)[number].name


def solution(mesh):
    layer = P(AXES[1], AXES[0], None, None)
    ids = P(AXES[1], AXES[0])
    flat = P(AXES)
    return jax.shard_map(
        local,
        mesh=mesh,
        in_specs=(layer, layer, ids, ids, flat, flat, flat),
        out_specs=(layer, layer, flat, flat, flat, flat),
        check_vma=False,
    )
```

```python
import math
from types import SimpleNamespace

import jax
import jax.numpy as jnp
import numpy as np
from jax import lax
from jax.experimental import pallas as pl
from jax.experimental.pallas import tpu as pltpu
from jax.sharding import PartitionSpec as P

D = 768
HEADS = 12
HEAD_DIM = 64
FF = 3072
SEG_LEN = 128
LONG_SEGS = 64
EPSILON = 1e-05
NEGATIVE = -1e30

LAYOUT = dict(
    w_qkv=(D, 3 * D),
    b_qv=(2 * D,),
    w_out=(D, D),
    b_out=(D,),
    gain_one=(D,),
    bias_one=(D,),
    w_up=(D, FF),
    b_up=(FF,),
    w_down=(FF, D),
    b_down=(D,),
    gain_two=(D,),
    bias_two=(D,),
    pos_table=(LONG_SEGS, D),
    x_qkv=(D, 3 * D),
    x_bqv=(2 * D,),
    x_out=(D, D),
    x_bout=(D,),
    gain_three=(D,),
    bias_three=(D,),
    x_up=(D, FF),
    x_bup=(FF,),
    x_down=(FF, D),
    x_bdown=(D,),
    gain_four=(D,),
    bias_four=(D,),
)
LANES = 128
BLK = 16
Y, X, C, Z = range(4)


def ceil_to(value, step):
    return -(-value // step) * step


def item_list(total_rows):
    items = []
    nat = 0
    for name, shape in LAYOUT.items():
        rows = math.prod(shape) // LANES
        if len(shape) == 1 and items and len(items[-1].shape) == 1:
            items[-1].names.append(name)
            items[-1].rows += rows
        else:
            items.append(SimpleNamespace(name=name, names=[name], shape=shape, nat=nat, rows=rows))
        nat += rows
    items.append(SimpleNamespace(name=None, names=[], shape=None, nat=nat, rows=total_rows - nat))
    blk = 0
    for item in items:
        item.cols = item.shape[1] // LANES if item.shape and len(item.shape) == 2 else 0
        item.blk = blk
        blk += ceil_to(item.rows, BLK) // BLK
    return items


class Geometry:
    def __init__(self, n_seg, n_doc, shard_len):
        self.n_seg, self.n_doc = n_seg, n_doc
        self.n_dev = n_seg * n_doc
        self.chunk = shard_len // LANES
        self.items = item_list(self.chunk * self.n_dev)
        self.by_name = SimpleNamespace(**{item.name: item for item in self.items if item.name})
        firsts, lasts = [], []
        for n in range(self.n_dev):
            lo, hi = n * self.chunk, (n + 1) * self.chunk
            blocks = []
            for item in self.items:
                a, b = max(lo, item.nat), min(hi, item.nat + item.rows)
                if a < b:
                    blocks.append(item.blk + (a - item.nat) // BLK)
                    blocks.append(item.blk + (b - 1 - item.nat) // BLK)
            firsts.append(min(blocks))
            lasts.append(max(blocks))
        self.first, self.last = firsts, lasts
        most = max(b - a + 1 for a, b in zip(firsts, lasts))
        self.piece_blocks = -(-most // self.n_dev)
        self.piece = self.piece_blocks * BLK
        self.slots = self.piece_blocks * self.n_dev
        self.groups = -(-most // (self.piece_blocks * n_doc))
        self.share = n_doc * self.piece
        self.staged_rows = self.groups * self.share
        self.c_size, self.x_size = 2, 2
        self.y_size = n_seg // 4

    def full_groups(self, item, chunk):
        rows = BLK * item.cols
        lo, hi = chunk * self.chunk - item.nat, (chunk + 1) * self.chunk - item.nat
        first, last = max(0, -(-lo // rows)), min(item.rows, hi) // rows
        return first, max(first, last)

    def block_tables(self):
        matrices = [item for item in self.items if item.cols]
        single = [[] for _ in range(self.n_dev)]
        groups = np.zeros((self.n_dev, len(matrices), 3), np.int32)
        for n in range(self.n_dev):
            lo, hi = n * self.chunk, (n + 1) * self.chunk
            for t in range(self.slots):
                b = self.first[n] + t
                if b > self.last[n]:
                    single[n].append((t, 0, 0, 0))
                    continue
                item = [it for it in self.items if it.blk <= b][-1]
                at = b - item.blk
                if item.cols:
                    first, last = self.full_groups(item, n)
                    if first <= at // item.cols < last:
                        continue
                start = item.nat + at * BLK
                a = max(start, lo)
                z = max(a, min(start + BLK, hi, item.nat + item.rows))
                single[n].append((t, start - lo, a - start, z - start))
            for i, item in enumerate(matrices):
                first, last = self.full_groups(item, n)
                if first < last:
                    slot = item.blk + first * item.cols - self.first[n]
                    groups[n, i] = (slot, item.nat + first * BLK * item.cols - lo, last - first)
        most = max(len(rows) for rows in single)
        table = np.zeros((self.n_dev, 1 + 4 * most), np.int32)
        for n, rows in enumerate(single):
            table[n, 0] = len(rows)
            table[n, 1 : 1 + 4 * len(rows)] = np.asarray(rows, np.int32).reshape(-1)
        return matrices, np.concatenate([groups.reshape(self.n_dev, -1), table], axis=1)

    def chunks_of(self, item):
        found = []
        n_blocks = ceil_to(item.rows, BLK) // BLK
        for n in range(self.n_dev):
            a = max(item.blk, self.first[n])
            b = min(item.blk + n_blocks, self.last[n] + 1)
            if a < b:
                found.append((n, a - item.blk, b - item.blk, a - self.first[n]))
        return found

    def spans(self, *ends):
        cuts = [0] + [ceil_to((end.nat - 1) // self.chunk + 1, self.n_doc) for end in ends] + [self.n_dev]
        return [range(a, b) for a, b in zip(cuts, cuts[1:])]

    def coords(self, device):
        seg, doc = divmod(device, self.n_doc)
        yx, c = divmod(seg, self.c_size)
        return [*divmod(yx, self.x_size), c, doc]

    def device(self, y, x, c, z):
        return ((y * self.x_size + x) * self.c_size + c) * self.n_doc + z

    def size(self, axis):
        return (self.y_size, self.x_size, self.c_size, self.n_doc)[axis]

    def shift(self, axis, step):
        pairs = []
        for source in range(self.n_dev):
            at = self.coords(source)
            at[axis] = (at[axis] + step) % self.size(axis)
            pairs.append((source, self.device(*at)))
        return pairs
def spec_vmem():
    return pl.BlockSpec(memory_space=pltpu.VMEM)


def spec_any():
    return pl.BlockSpec(memory_space=pl.ANY)


def spec_smem():
    return pl.BlockSpec(memory_space=pltpu.SMEM)


def kernel_params(mib=56):
    return pltpu.CompilerParams(vmem_limit_bytes=mib * 1024 * 1024)


def cost(micros):
    micros = micros if micros >= 6 else 0
    return pl.CostEstimate(flops=int(micros * 1e9), bytes_accessed=int(micros * 3e6), transcendentals=0)


class Order:
    def start(self):
        self.token = jnp.zeros((8, LANES), jnp.float32)
        self.others = []

    def wait_for(self, *others):
        self.others += others


ORDER = Order()


def ordered(kernel, out_shape, in_specs, out_specs, **settings):
    single = not isinstance(out_shape, (list, tuple))
    outs, specs = ([out_shape], [out_specs]) if single else (list(out_shape), list(out_specs))

    def run(*inputs):
        extra = [ORDER.token] + ORDER.others
        n_in, n_out, n_extra = len(inputs), len(outs), len(extra)

        def wrapped(*refs):
            rest = refs[n_in + n_extra :]
            kernel(*refs[:n_in], *rest[:n_out], *rest[n_out + 1 :])

        results = pl.pallas_call(
            wrapped,
            out_shape=outs + [jax.ShapeDtypeStruct((8, LANES), jnp.float32)],
            in_specs=list(in_specs) + [spec_any()] * n_extra,
            out_specs=specs + [spec_any()],
            **settings,
        )(*inputs, *extra)
        ORDER.token, ORDER.others = results[-1], []
        return results[0] if single else results[:-1]

    return run


def row_mask(low, high):
    rows = lax.broadcasted_iota(jnp.int32, (BLK, LANES), 0)
    return (rows >= low) & (rows < high)


def block_moves(geo, table_ref, by_group, by_row):
    matrices = geo.block_tables()[0]
    for i, item in enumerate(matrices):
        def body(g, carry, i=i, cols=item.cols):
            for cb in range(cols):
                by_group(table_ref[3 * i] + g * cols + cb, table_ref[3 * i + 1] + g * BLK * cols + cb, cols)
            return carry

        lax.fori_loop(0, table_ref[3 * i + 2], body, 0)
    base = 3 * len(matrices)

    def single(r, carry):
        by_row(*[table_ref[base + 1 + 4 * r + j] for j in range(4)])
        return carry

    lax.fori_loop(0, table_ref[base], single, 0)


def block_at(slot):
    return pl.ds(pl.multiple_of(slot * BLK, BLK), BLK)


def align_rows(geo, table, natural, pad_rows):
    def kernel(table_ref, natural_ref, out_ref, rows_ref):
        def fill(row, rows):
            rows_ref[pl.ds(row + BLK, rows), :] = natural_ref[pl.ds(row, rows), :]

        copy_rows(natural.shape[0], 256, fill)

        def by_group(slot, start, cols):
            out_ref[block_at(slot), :] = rows_ref[pl.ds(start + BLK, BLK, stride=cols), :].astype(jnp.bfloat16)

        def by_row(slot, start, low_row, high_row):
            rows = jnp.where(row_mask(low_row, high_row), rows_ref[pl.ds(start + BLK, BLK), :], 0.0)
            out_ref[block_at(slot), :] = rows.astype(jnp.bfloat16)

        block_moves(geo, table_ref, by_group, by_row)

    return ordered(
        kernel,
        out_shape=jax.ShapeDtypeStruct((geo.slots * BLK, LANES), jnp.bfloat16),
        in_specs=[spec_smem(), spec_vmem()],
        out_specs=spec_vmem(),
        scratch_shapes=[pltpu.VMEM((pad_rows, LANES), jnp.float32)],
        compiler_params=kernel_params(),
        cost_estimate=cost(3),
    )(table, natural)


def update_rows(geo, table, blocks, begins, factors, state, pad_rows):
    rows_all = geo.chunk
    runs = begins.shape[0]

    def kernel(table_ref, begins_ref, factors_ref, blocks_ref, *refs):
        inputs, outs, held, (grad_ref, in_sems) = refs[:3], refs[3:7], refs[7:10], refs[10:]
        loads = [
            pltpu.make_async_copy(source, target, in_sems.at[i])
            for i, (source, target) in enumerate(zip(inputs, held))
        ]
        for load in loads:
            load.start()

        def by_group(slot, start, cols):
            grad_ref[pl.ds(start + BLK, BLK, stride=cols), :] = blocks_ref[block_at(slot), :].astype(jnp.float32)

        def by_row(slot, start, low_row, high_row):
            here = pl.ds(start + BLK, BLK)
            rows = blocks_ref[block_at(slot), :].astype(jnp.float32)
            grad_ref[here, :] = jnp.where(row_mask(low_row, high_row), rows, grad_ref[here, :])

        block_moves(geo, table_ref, by_group, by_row)
        for load in loads:
            load.wait()

        def step(row, rows):
            here = pl.ds(row, rows)
            at = lax.broadcasted_iota(jnp.int32, (rows, LANES), 0) + row
            scale = jnp.full((rows, LANES), factors_ref[0], jnp.float32)
            rate = jnp.full((rows, LANES), factors_ref[runs], jnp.float32)
            for run in range(1, runs):
                later = at >= begins_ref[run]
                scale = jnp.where(later, factors_ref[run], scale)
                rate = jnp.where(later, factors_ref[runs + run], rate)
            scaled = grad_ref[pl.ds(row + BLK, rows), :] * scale
            moment = 0.5 * held[1][here, :] + scaled
            weight = held[0][here, :] - rate * (scaled + 0.5 * moment)
            outs[0][here, :] = weight
            outs[1][here, :] = moment
            outs[2][here, :] = 0.5 * held[2][here, :] + 0.5 * weight
            outs[3][here, :] = weight.astype(jnp.bfloat16)

        copy_rows(rows_all, 128, step)

    full = [jax.ShapeDtypeStruct((rows_all, LANES), kind) for kind in (jnp.float32,) * 3 + (jnp.bfloat16,)]
    return ordered(
        kernel,
        out_shape=full,
        in_specs=[spec_smem()] * 3 + [spec_vmem()] + [spec_any()] * 3,
        out_specs=[spec_vmem()] * 4,
        scratch_shapes=[pltpu.VMEM((rows_all, LANES), jnp.float32)] * 3
        + [pltpu.VMEM((pad_rows, LANES), jnp.float32), pltpu.SemaphoreType.DMA((3,))],
        compiler_params=kernel_params(),
        cost_estimate=cost(3),
    )(table, begins, factors, blocks, *state)


class Buckets:
    def __init__(self, geo, arrays, *ends):
        self.geo = geo
        self.ranges = geo.spans(*ends)
        self.arrays = arrays

    def find(self, chunk):
        for number, span in enumerate(self.ranges):
            if chunk in span:
                return number, chunk - span.start

    def shapes(self, number):
        geo = self.geo
        count = len(self.ranges[number])
        return [
            (geo.y_size, geo.x_size, count, geo.share // 2, LANES),
            (geo.x_size, geo.y_size, count, geo.share // 2, LANES),
        ]


def wrap(value, size):
    return lax.rem(value + size, size)


def copy_rows(count, step, body):
    full = count // step
    if full:
        def loop(i, carry):
            body(i * step, step)
            return carry

        lax.fori_loop(0, full, loop, 0)
    if count % step:
        body(full * step, count % step)


def place_line(geo, parts, my_z):
    count, nd = parts[0].shape[0], geo.n_doc
    rows = geo.share // 2

    def kernel(z_ref, *refs):
        sources, outs = refs[:nd], refs[nd:]
        for r in range(nd):
            z = wrap(z_ref[0] - r, nd)
            for s in range(count):
                for half in range(2):
                    outs[half][s * nd + z] = sources[r][s, half * rows : (half + 1) * rows]

    return ordered(
        kernel,
        out_shape=[jax.ShapeDtypeStruct((count * nd, rows, LANES), jnp.bfloat16)] * 2,
        in_specs=[spec_smem()] + [spec_vmem()] * nd,
        out_specs=[spec_vmem()] * 2,
        compiler_params=kernel_params(),
        cost_estimate=cost(2),
    )(my_z.reshape(1), *parts)
VECTOR_ROWS = 16


def chunk_copies(geo, buckets, sources, used, coords_ref, n, staged, sem):
    my_y, my_x, my_c = coords_ref[0], coords_ref[1], coords_ref[2]
    number, place = buckets.find(n)
    first = sum(buckets.arrays[m] for m in used[: used.index(number)])
    if buckets.arrays[number] == 1:
        line, z = divmod(place, geo.n_doc)
        for s in range(geo.groups):
            pltpu.make_async_copy(
                sources[first].at[s * geo.n_doc + z, line],
                staged.at[pl.ds(s * geo.share, geo.share)],
                sem,
            ).start()
        return
    rows = geo.share // 2
    for core in range(2):
        c = my_c if core == 0 else 1 - my_c
        for ry in range(geo.y_size):
            for rx in range(geo.x_size):
                y, x = wrap(my_y - ry, geo.y_size), wrap(my_x - rx, geo.x_size)
                s = (y * geo.x_size + x) * 2 + c

                def begin(s=s, ry=ry, rx=rx, core=core):
                    for half in range(2):
                        index = (ry, rx, place) if half == 0 else (rx, ry, place)
                        pltpu.make_async_copy(
                            sources[first + 2 * half + core].at[index],
                            staged.at[pl.ds(pl.multiple_of(s * geo.share + half * rows, BLK), rows)],
                            sem,
                        ).start()

                if geo.groups == geo.n_seg:
                    begin()
                else:
                    pl.when(s < geo.groups)(begin)


class Weights:
    def __init__(self, geo, buckets, gathered, names):
        self.geo, self.buckets = geo, buckets
        self.items = [vars(geo.by_name)[name] for name in names]
        self.chunks = sorted({n for item in self.items for n, *_ in geo.chunks_of(item)})
        self.used = sorted({buckets.find(n)[0] for n in self.chunks})
        self.operands = [array for number in self.used for array in gathered[number]]
        cols = max([item.cols for item in self.items])
        self.scratch = [
            pltpu.VMEM((len(self.chunks), geo.staged_rows, LANES), jnp.bfloat16),
            pltpu.VMEM((BLK * (cols + 2), LANES), jnp.float32),
            pltpu.SemaphoreType.DMA((len(self.chunks),)),
        ]

    def start(self, coords_ref, sources, staged, sems):
        for at, n in enumerate(self.chunks):
            chunk_copies(
                self.geo, self.buckets, sources, self.used, coords_ref, n, staged.at[at], sems.at[at]
            )

    def wait(self, number, waited, staged, sems):
        for n, *_ in self.geo.chunks_of(self.items[number]):
            at = self.chunks.index(n)
            if at not in waited:
                waited.add(at)
                pltpu.make_async_copy(staged.at[at], staged.at[at], sems.at[at]).wait()

    def blocks(self, item, lo, hi, staged, wide):
        done = lo
        for n, b0, b1, slot in self.geo.chunks_of(item):
            for b in range(max(b0, lo), min(b1, hi)):
                at = self.chunks.index(n)
                rows = staged[at, pl.ds((slot + b - b0) * BLK, BLK), :].astype(jnp.float32)
                here = pl.ds((b - lo) * BLK, BLK)
                wide[here, :] = wide[here, :] + rows if b < done else rows
            done = max(done, min(b1, hi))

    def matrix(self, number, staged, wide, out_ref):
        item = self.items[number]
        cols = item.cols
        split = set()
        for n, b0, b1, slot in self.geo.chunks_of(item):
            at = self.chunks.index(n)
            first, last = self.geo.full_groups(item, n)
            split |= set(range(b0 // cols, -(-b1 // cols))) - set(range(first, last))

            def group(g, carry, at=at, shift=slot - b0):
                rows = pl.ds(pl.multiple_of(g * BLK, BLK), BLK)
                for cb in range(cols):
                    tile = staged[at, block_at(g * cols + cb + shift), :]
                    out_ref[rows, cb * LANES : (cb + 1) * LANES] = tile
                return carry

            lax.fori_loop(first, last, group, 0)
        for g in sorted(split):
            self.blocks(item, g * cols, (g + 1) * cols, staged, wide)
            for cb in range(cols):
                tile = wide[pl.ds(cb, BLK, stride=cols), :]
                out_ref[g * BLK : (g + 1) * BLK, cb * LANES : (cb + 1) * LANES] = tile.astype(jnp.bfloat16)

    def vectors(self, number, staged, wide, out_ref, row):
        item = self.items[number]
        self.blocks(item, 0, ceil_to(item.rows, BLK) // BLK, staged, wide)
        for r in range(item.rows):
            v, cb = divmod(r, D // LANES)
            out_ref[row + v : row + v + 1, cb * LANES : (cb + 1) * LANES] = wide[r : r + 1, :]


def vector_rows(wide, values, first, count):
    lane_cols = D // LANES
    for r in range(count):
        v, cb = divmod(r, lane_cols)
        wide[r : r + 1, :] = values[first + v : first + v + 1, cb * LANES : (cb + 1) * LANES]


def bucket_parts(geo, span):
    parts = []
    for item in geo.items:
        chunks = [entry for entry in geo.chunks_of(item) if entry[0] in span]
        if chunks and item.names:
            parts.append((item, chunks))
    return parts


def grad_bucket(geo, buckets, number, grads, coords, name, left, right, rows, keep=False):
    span = buckets.ranges[number]
    parts = bucket_parts(geo, span)
    operands, specs, windows, scratch = [], [], [], []
    wide_rows = BLK
    for item, chunks in parts:
        if len(item.shape) == 2:
            cols = item.cols
            wide_rows = max(wide_rows, BLK * cols)
            if item.name == name:
                main, main_chunks, windows_at = item, chunks, len(windows)
                windows.append(None)
                continue
            k0 = min(b0 for _, b0, _, _ in chunks) // cols
            k1 = -(-max(b1 for _, _, b1, _ in chunks) // cols)
            operands.append(grads[item.name])
            specs.append(spec_any())
            windows.append((len(operands) - 1, k0, k1))
            scratch.append(pltpu.VMEM(((k1 - k0) * BLK, item.shape[1]), jnp.bfloat16))
        else:
            wide_rows = max(wide_rows, ceil_to(item.rows, BLK))
            operands.append(grads[item.name][0])
            specs.append(pl.BlockSpec(operands[-1].shape, lambda i: (0, 0)))
            windows.append((len(operands) - 1, None, None))
            scratch.append(pltpu.VMEM((BLK, LANES), jnp.bfloat16))
    outs = [shape for shape in buckets.shapes(number) for _ in range(2)]
    depth, width = main.shape
    cols = main.cols
    steps = depth // rows
    count = len(operands)
    block_groups = rows // BLK

    def split_groups(item, chunks):
        found = set()
        for n, b0, b1, _ in chunks:
            first, last = geo.full_groups(item, n)
            found |= set(range(b0 // item.cols, -(-b1 // item.cols))) - set(range(first, last))
        return sorted(found)

    def kernel(coords_ref, left_ref, right_ref, *refs):
        sources, targets = refs[:count], refs[count : count + 4]
        refs = refs[count + 4 :]
        if keep:
            kept_ref, refs = refs[0], refs[1:]
        loaded, (values, staged, wide, in_sems, out_sems) = refs[:count], refs[count:]
        step = pl.program_id(0)
        my_y, my_x, my_c = coords_ref[0], coords_ref[1], coords_ref[2]

        def send_out(n):
            _, place = buckets.find(n)
            half_rows = geo.share // 2
            for core in range(2):
                c = my_c if core == 0 else 1 - my_c
                for ry in range(geo.y_size):
                    for rx in range(geo.x_size):
                        y, x = wrap(my_y + ry, geo.y_size), wrap(my_x + rx, geo.x_size)
                        s = (y * geo.x_size + x) * 2 + c
                        for half in range(2):
                            index = (ry, rx, place) if half == 0 else (rx, ry, place)
                            here = pl.ds(pl.multiple_of(s * geo.share + half * half_rows, BLK), half_rows)
                            pltpu.make_async_copy(
                                staged.at[n - span.start, here],
                                targets[2 * half + core].at[index],
                                out_sems.at[n - span.start],
                            ).start()

        def whole(item, chunks, values, base, lo, hi):
            for n, b0, b1, slot in chunks:
                first, last = geo.full_groups(item, n)

                def group(g, carry, n=n, shift=slot - b0):
                    here = pl.ds(pl.multiple_of((g - base) * BLK, BLK), BLK)
                    for cb in range(item.cols):
                        dst = block_at(g * item.cols + cb + shift)
                        staged[n - span.start, dst, :] = values[here, cb * LANES : (cb + 1) * LANES]
                    return carry

                start = jnp.maximum(first, lo)
                lax.fori_loop(start, jnp.maximum(start, jnp.minimum(last, hi)), group, 0)

        def cut(item, chunks, values, base, g):
            for cb in range(item.cols):
                tile = values[pl.ds(pl.multiple_of((g - base) * BLK, BLK), BLK), cb * LANES : (cb + 1) * LANES]
                wide[pl.ds(cb, BLK, stride=item.cols), :] = tile.astype(jnp.float32)
            for n, b0, b1, slot in chunks:
                first, last = geo.full_groups(item, n)
                lo, hi = max(b0, g * item.cols), min(b1, (g + 1) * item.cols)
                if lo < hi and not first <= g < last:
                    part = wide[pl.ds((lo - g * item.cols) * BLK, (hi - lo) * BLK), :]
                    dst = pl.ds((slot + lo - b0) * BLK, (hi - lo) * BLK)
                    staged[n - span.start, dst, :] = part.astype(jnp.bfloat16)

        @pl.when(step == 0)
        def _():
            loads = {}
            for (item, chunks), window in zip(parts, windows):
                if window is not None and window[1] is not None:
                    at, k0, k1 = window
                    source = sources[at].at[pl.ds(k0 * BLK, (k1 - k0) * BLK)]
                    loads[at] = pltpu.make_async_copy(source, loaded[at], in_sems.at[at])
                    loads[at].start()

            def clear(row, size):
                for at in range(len(span)):
                    here = pl.ds(pl.multiple_of(row + tail, BLK), size)
                    staged[at, here, :] = jnp.zeros((size, LANES), jnp.bfloat16)

            tail = min(geo.last[n] - geo.first[n] for n in span) * BLK
            copy_rows(geo.slots * BLK - tail, 128, clear)
            for (item, chunks), window in zip(parts, windows):
                if window is None:
                    continue
                at, k0, k1 = window
                if k0 is None:
                    vector_rows(wide, sources[at], grads[item.name][1], item.rows)
                    for n, b0, b1, slot in chunks:
                        part = wide[pl.ds(b0 * BLK, (b1 - b0) * BLK), :].astype(jnp.bfloat16)
                        staged[n - span.start, pl.ds(slot * BLK, (b1 - b0) * BLK), :] = part
                else:
                    loads[at].wait()
                    whole(item, chunks, loaded[at], k0, k0, k1)
                    for g in split_groups(item, chunks):
                        cut(item, chunks, loaded[at], k0, g)

        values[...] = low(dot_tn(left_ref[...], right_ref[...]))
        if keep:
            kept_ref[...] = values[...]
        low_group = step * block_groups
        whole(main, main_chunks, values, low_group, low_group, low_group + block_groups)
        for g in split_groups(main, main_chunks):
            @pl.when(step == g // block_groups)
            def _(g=g):
                cut(main, main_chunks, values, g // block_groups * block_groups, g)

        ready = {n: 0 for n in span}
        for n, _, b1, _ in main_chunks:
            ready[n] = (b1 - 1) // cols // block_groups
        for at in range(steps):
            here = [n for n in span if ready[n] == at]
            if here:
                @pl.when(step == at)
                def _(here=here):
                    for n in here:
                        send_out(n)

        @pl.when(step == steps - 1)
        def _():
            for at in range(len(span)):
                pltpu.make_async_copy(staged.at[at], staged.at[at], out_sems.at[at]).wait()

    extra = [jax.ShapeDtypeStruct(main.shape, jnp.bfloat16)] if keep else []
    return ordered(
        kernel,
        grid=(steps,),
        out_shape=[jax.ShapeDtypeStruct(shape, jnp.bfloat16) for shape in outs] + extra,
        in_specs=[
            spec_smem(),
            pl.BlockSpec((left.shape[0], rows), lambda i: (0, i)),
            pl.BlockSpec(right.shape, lambda i: (0, 0), pipeline_mode=pl.Buffered(1)),
        ]
        + specs,
        out_specs=[spec_any()] * 4 + [pl.BlockSpec((rows, width), lambda i: (i, 0))] * len(extra),
        scratch_shapes=scratch
        + [
            pltpu.VMEM((rows, width), jnp.bfloat16),
            pltpu.VMEM((len(span), geo.slots * BLK, LANES), jnp.bfloat16),
            pltpu.VMEM((wide_rows + 2 * BLK, LANES), jnp.float32),
            pltpu.SemaphoreType.DMA((max(count, 1),)),
            pltpu.SemaphoreType.DMA((len(span),)),
        ],
        compiler_params=kernel_params(60),
        cost_estimate=cost(18),
    )(coords, left, right, *operands)


def pack_cross(geo, span, lefts, rights, vectors, seg):
    seg_blocks = geo.n_doc * geo.piece_blocks
    parts = bucket_parts(geo, span)
    names = list(lefts)
    vector_names = list(vectors)
    depth_rows = next(iter(rights.values())).shape[0]

    def window(cols):
        return (-(-(seg_blocks - 1) // cols) + 1) * BLK

    wide_rows = 0
    left_rows = BLK
    for item, chunks in parts:
        if len(item.shape) == 2:
            cols = item.shape[1] // LANES
            size = min(window(cols), item.shape[0])
            left_rows = max(left_rows, len(chunks) * size)
            wide_rows = max(wide_rows, len(chunks) * size * cols)

    def kernel(seg_ref, *refs):
        left = dict(zip(names, refs[: len(names)]))
        right = dict(zip(names, refs[len(names) : 2 * len(names)]))
        vector = dict(zip(vector_names, refs[2 * len(names) : 2 * len(names) + len(vector_names)]))
        out_ref, gathered, wide = refs[2 * len(names) + len(vector_names) :]
        low_slot = seg_ref[0] * seg_blocks
        out_ref[...] = jnp.zeros_like(out_ref)
        for item, chunks in parts:
            starts, size, cols = [], 0, 1
            if len(item.shape) == 2:
                cols = item.shape[1] // LANES
                size = min(window(cols), item.shape[0])
                for at, (n, b0, b1, slot) in enumerate(chunks):
                    first = jnp.maximum(low_slot, slot) - slot + b0
                    start = jnp.clip(first // cols * BLK, 0, item.shape[0] - size)
                    start = pl.multiple_of(start, BLK)
                    starts.append(start)
                    gathered[at * size : (at + 1) * size, :] = left[item.name][pl.ds(start, size), :]
                count = len(chunks) * size
                rows = gathered[:count, :]
                for cb in range(0, cols, 2):
                    tile = dot_nn(rows, right[item.name][:, cb * LANES : (cb + 2) * LANES])
                    wide[pl.ds(cb, count, stride=cols), :] = tile[:, :LANES]
                    wide[pl.ds(cb + 1, count, stride=cols), :] = tile[:, LANES:]
            else:
                vector_rows(wide, vector[item.name], vectors[item.name][1], item.rows)
            for at, (n, b0, b1, slot) in enumerate(chunks):
                begin = jnp.maximum(low_slot, slot)
                end = jnp.minimum(low_slot + seg_blocks, slot + b1 - b0)
                base = (at * size - starts[at]) * cols if starts else 0

                first, last = geo.full_groups(item, n) if starts else (0, 0)

                def by_row(t, carry, n=n, b0=b0, slot=slot, base=base):
                    src = pl.ds((b0 + t - slot) * BLK + base, BLK)
                    dst = pl.ds(pl.multiple_of((t - low_slot) * BLK, BLK), BLK)
                    out_ref[n - span.start, dst, :] = wide[src, :].astype(jnp.bfloat16)
                    return carry

                def by_tile(t, carry, n=n, b0=b0, slot=slot, base=base, cols=cols):
                    b = b0 + t - slot
                    group = b // cols
                    src = pl.ds(group * BLK * cols + b - group * cols + base, BLK, stride=cols)
                    dst = pl.ds(pl.multiple_of((t - low_slot) * BLK, BLK), BLK)
                    out_ref[n - span.start, dst, :] = wide[src, :].astype(jnp.bfloat16)
                    return carry

                if first < last:
                    lo = jnp.clip(slot + first * cols - b0, begin, jnp.maximum(begin, end))
                    hi = jnp.clip(slot + last * cols - b0, begin, jnp.maximum(begin, end))
                    lax.fori_loop(begin, lo, by_row, 0)
                    lax.fori_loop(lo, hi, by_tile, 0)
                    lax.fori_loop(hi, jnp.maximum(hi, end), by_row, 0)
                else:
                    lax.fori_loop(begin, jnp.maximum(begin, end), by_row, 0)

    operands = [lefts[n] for n in names] + [rights[n] for n in names]
    operands += [vectors[n][0] for n in vector_names]
    return ordered(
        kernel,
        out_shape=jax.ShapeDtypeStruct((len(span), seg_blocks * BLK, LANES), jnp.bfloat16),
        in_specs=[spec_smem()] + [spec_vmem()] * len(operands),
        out_specs=spec_vmem(),
        scratch_shapes=[
            pltpu.VMEM((left_rows, depth_rows), jnp.bfloat16),
            pltpu.VMEM((wide_rows + 2 * BLK, LANES), jnp.float32),
        ],
        compiler_params=kernel_params(),
        cost_estimate=cost(12),
    )(seg, *operands)
TILE = 512
PAIRS = HEADS // 2
TAIL_RATE = 0.3
TAIL = (
    0.11962929605681312,
    0.12075400207853171,
    0.0999131861559567,
    0.12856268365589474,
    -0.05368570534984477,
    0.20635578836359286,
    -0.15720441932045734,
    0.0356750954846771,
)


def dot_nn(left, right):
    return lax.dot_general(left, right, (((1,), (0,)), ((), ())), preferred_element_type=jnp.float32)


def dot_nt(left, right):
    return lax.dot_general(left, right, (((1,), (1,)), ((), ())), preferred_element_type=jnp.float32)


def dot_tn(left, right):
    return lax.dot_general(left, right, (((0,), (0,)), ((), ())), preferred_element_type=jnp.float32)


def low(values):
    return values.astype(jnp.bfloat16)


def gelu_pair(u):
    t = 1.0 / (1.0 + TAIL_RATE * jnp.abs(u))
    poly = TAIL[-1] * t + TAIL[-2]
    for coef in TAIL[-3::-1]:
        poly = poly * t + coef
    bell = jnp.exp(-0.5 * (u * u))
    tail = bell * (poly * t)
    spread = jnp.where(u < 0.0, tail, 1.0 - tail)
    return u * spread, spread + u * bell * (1.0 / math.sqrt(2.0 * math.pi))


def norm_rows(values, gain, shift):
    center = values - jnp.mean(values, axis=-1, keepdims=True)
    rate = lax.rsqrt(jnp.mean(center * center, axis=-1, keepdims=True) + EPSILON)
    normal = center * rate
    return normal * gain + shift, normal, rate


def norm_pull(grad, normal, rate, gain):
    scaled = grad * gain
    return rate * (
        scaled
        - jnp.mean(scaled, axis=-1, keepdims=True)
        - normal * jnp.mean(scaled * normal, axis=-1, keepdims=True)
    )


def fixed(shape):
    return pl.BlockSpec(shape, lambda i: (0,) * len(shape), pipeline_mode=pl.Buffered(1))


def tiles(cols, first=0):
    return pl.BlockSpec((TILE, cols), lambda i: (i + first, 0))


def both_heads(values):
    first = lax.broadcasted_iota(jnp.int32, values.shape, 1) < HEAD_DIM
    zero = jnp.zeros_like(values)
    return jnp.concatenate([jnp.where(first, values, zero), jnp.where(first, zero, values)], axis=0)


def side_by_side(stacked):
    half = stacked.shape[0] // 2
    return jnp.concatenate([stacked[:half], stacked[half:]], axis=1)


def third(part, pair):
    start = part * D + pair * LANES
    return slice(start, start + LANES)


def attend_kernel(x_ref, wqkv_ref, vec_ref, packed_ref, att_ref, stat_ref):
    x = x_ref[...]
    for j in range(3):
        cols = slice(j * D, (j + 1) * D)
        part = dot_nn(x, wqkv_ref[:, cols])
        packed_ref[:, cols] = low(part if j == 1 else part + vec_ref[j // 2 : j // 2 + 1, :])
    lanes = lax.broadcasted_iota(jnp.int32, (SEG_LEN, LANES), 1)

    def segment(s, carry):
        rows = pl.ds(pl.multiple_of(s * SEG_LEN, SEG_LEN), SEG_LEN)
        stat = jnp.zeros((SEG_LEN, LANES), jnp.float32)
        for pair in range(PAIRS):
            q = packed_ref[rows, third(0, pair)] * jnp.bfloat16(HEAD_DIM**-0.5)
            k = packed_ref[rows, third(1, pair)]
            v = packed_ref[rows, third(2, pair)]
            scores = dot_nt(both_heads(q), k)
            largest = jnp.max(scores, axis=-1, keepdims=True)
            raised = jnp.exp(scores - largest)
            summed = jnp.sum(raised, axis=-1, keepdims=True)
            weights = low(raised * (1.0 / summed))
            att_ref[rows, pair * LANES : (pair + 1) * LANES] = low(
                dot_nn(side_by_side(weights), both_heads(v))
            )
            log_sum = largest + jnp.log(summed)
            stat = jnp.where(lanes == 2 * pair, log_sum[:SEG_LEN], stat)
            stat = jnp.where(lanes == 2 * pair + 1, log_sum[SEG_LEN:], stat)
        stat_ref[rows, :] = stat
        return carry

    lax.fori_loop(0, TILE // SEG_LEN, segment, 0)


def in_parts(kernel, micros, count, inputs, in_specs, outs, out_specs, scratch, previous):
    previous = list(previous or ())
    return ordered(
        kernel,
        grid=(count,),
        in_specs=in_specs + [spec_any()] * len(previous),
        out_specs=out_specs,
        out_shape=outs,
        scratch_shapes=scratch,
        input_output_aliases={len(inputs) + i: i for i in range(len(previous))},
        compiler_params=kernel_params(60),
        cost_estimate=cost(micros),
    )(*inputs, *previous)


def attend_layer(x, w_qkv, vecs, first, count, previous):
    def rows(cols):
        return tiles(cols, first)

    def kernel(x_ref, wqkv_ref, vec_ref, *refs):
        attend_kernel(x_ref, wqkv_ref, vec_ref, *refs[-3:])

    return in_parts(
        kernel,
        8 * count,
        count,
        [x, w_qkv, vecs],
        [rows(D), fixed((D, 3 * D)), fixed((VECTOR_ROWS, D))],
        [jax.ShapeDtypeStruct(v.shape, v.dtype) for v in previous],
        [rows(3 * D), rows(D), rows(LANES)],
        [],
        previous,
    )


def attend_first(x, weights, coords):
    n = x.shape[0]
    bf, f32 = jnp.bfloat16, jnp.float32
    count = len(weights.operands)

    def kernel(coords_ref, *refs):
        sources, x_ref, refs = refs[:count], refs[count], refs[count + 1 :]
        packed_ref, att_ref, stat_ref, wqkv_ref, vec_ref, staged, wide, sems = refs
        weights.start(coords_ref, sources, staged, sems)
        waited = set()
        for number in range(2):
            weights.wait(number, waited, staged, sems)
        weights.matrix(0, staged, wide, wqkv_ref)
        vec_ref[...] = jnp.zeros_like(vec_ref)
        weights.vectors(1, staged, wide, vec_ref, 0)
        attend_kernel(x_ref, wqkv_ref, vec_ref, packed_ref, att_ref, stat_ref)

    whole = [pl.BlockSpec(shape, lambda i: (0, 0)) for shape in ((D, 3 * D), (VECTOR_ROWS, D))]
    return ordered(
        kernel,
        grid=(1,),
        in_specs=[spec_smem()] + [spec_any()] * count + [tiles(D)],
        out_specs=[tiles(3 * D), tiles(D), tiles(LANES)] + whole,
        out_shape=[
            jax.ShapeDtypeStruct((n, 3 * D), bf),
            jax.ShapeDtypeStruct((n, D), bf),
            jax.ShapeDtypeStruct((n, LANES), f32),
            jax.ShapeDtypeStruct((D, 3 * D), bf),
            jax.ShapeDtypeStruct((VECTOR_ROWS, D), f32),
        ],
        scratch_shapes=weights.scratch,
        compiler_params=kernel_params(60),
        cost_estimate=cost(12),
    )(coords, *weights.operands, x)


FBLOCK = D


def feed_kernel(
    x_ref, att_ref, wout_ref, wup_ref, wdown_ref, vec_ref,
    h1low_ref, norm1_ref, g_ref, dg_ref, norm2_ref, rate_ref, h2_ref, cls_ref, res_ref, h1_ref,
):
    step = pl.program_id(0)
    segs = TILE // SEG_LEN
    lanes = lax.broadcasted_iota(jnp.int32, (SEG_LEN, LANES), 1)
    res_ref[...] = dot_nn(att_ref[...], wout_ref[...])

    def start(s, carry):
        rows = pl.ds(pl.multiple_of(s * SEG_LEN, SEG_LEN), SEG_LEN)
        resid = x_ref[rows, :].astype(jnp.float32) + res_ref[rows, :] + vec_ref[2:3, :]
        hidden, normal, rate = norm_rows(resid, vec_ref[3:4, :], vec_ref[4:5, :])
        h1_ref[rows, :] = hidden
        h1low_ref[rows, :] = low(hidden)
        norm1_ref[rows, :] = low(normal)
        rate_ref[rows, :] = jnp.broadcast_to(rate, (SEG_LEN, LANES))
        return carry

    lax.fori_loop(0, segs, start, 0)
    h = h1low_ref[...]
    for j in range(FF // FBLOCK):
        cols = slice(j * FBLOCK, (j + 1) * FBLOCK)
        act, slope = gelu_pair(dot_nn(h, wup_ref[:, cols]) + vec_ref[5 + j : 6 + j, :])
        g = low(act)
        g_ref[:, cols] = g
        dg_ref[:, cols] = low(slope)
        part = dot_nn(g, wdown_ref[cols, :])
        if j == 0:
            res_ref[...] = part
        else:
            res_ref[...] += part

    def finish(s, carry):
        rows = pl.ds(pl.multiple_of(s * SEG_LEN, SEG_LEN), SEG_LEN)
        resid = h1_ref[rows, :] + res_ref[rows, :] + vec_ref[9:10, :]
        hidden, normal, rate = norm_rows(resid, vec_ref[10:11, :], vec_ref[11:12, :])
        h2_ref[rows, :] = low(hidden)
        norm2_ref[rows, :] = low(normal)
        rate_ref[rows, :] = jnp.where(lanes == 0, rate_ref[rows, :], rate)
        cls_ref[pl.ds(step * segs + s, 1), :] = hidden[0:1, :]
        return carry

    lax.fori_loop(0, segs, finish, 0)


def feed_layer(x, att, weights, coords):
    n = x.shape[0]
    bf, f32 = jnp.bfloat16, jnp.float32
    count = len(weights.operands)
    steps = n // TILE
    shapes = [item.shape for item in weights.items if item.cols]

    def kernel(coords_ref, *refs):
        sources, refs = refs[:count], refs[count:]
        x_ref, att_ref = refs[:2]
        outs, kept = refs[2:10], refs[10:13]
        vec_ref, res_ref, h1_ref, out_sems = refs[13:17]
        held, (staged, wide, sems) = refs[17:20], refs[20:]
        step = pl.program_id(0)

        @pl.when(step == 0)
        def _():
            weights.start(coords_ref, sources, staged, sems)
            waited = set()
            vec_ref[...] = jnp.zeros_like(vec_ref)
            place = row = 0
            for number, item in enumerate(weights.items):
                weights.wait(number, waited, staged, sems)
                if item.cols:
                    weights.matrix(number, staged, wide, held[place])
                    pltpu.make_async_copy(held[place], kept[place], out_sems.at[place]).start()
                    place += 1
                else:
                    weights.vectors(number, staged, wide, vec_ref, row)
                    row += item.rows * LANES // D

        feed_kernel(x_ref, att_ref, *held, vec_ref, *outs, res_ref, h1_ref)

        @pl.when(step == steps - 1)
        def _():
            for place in range(3):
                pltpu.make_async_copy(held[place], kept[place], out_sems.at[place]).wait()

    return ordered(
        kernel,
        grid=(steps,),
        in_specs=[spec_smem()] + [spec_any()] * count + [tiles(D), tiles(D)],
        out_specs=[tiles(D), tiles(D), tiles(FF), tiles(FF), tiles(D), tiles(LANES), tiles(D)]
        + [pl.BlockSpec((n // SEG_LEN, D), lambda i: (0, 0))]
        + [spec_any()] * 3
        + [pl.BlockSpec((VECTOR_ROWS, D), lambda i: (0, 0))],
        out_shape=[
            jax.ShapeDtypeStruct((n, cols), kind)
            for cols, kind in ((D, bf), (D, bf), (FF, bf), (FF, bf), (D, bf), (LANES, f32), (D, bf))
        ]
        + [jax.ShapeDtypeStruct((n // SEG_LEN, D), f32)]
        + [jax.ShapeDtypeStruct(shape, bf) for shape in shapes]
        + [jax.ShapeDtypeStruct((VECTOR_ROWS, D), f32)],
        scratch_shapes=[
            pltpu.VMEM((TILE, D), f32),
            pltpu.VMEM((TILE, D), f32),
            pltpu.SemaphoreType.DMA((3,)),
        ]
        + [pltpu.VMEM(shape, bf) for shape in shapes]
        + weights.scratch,
        compiler_params=kernel_params(62),
        cost_estimate=cost(60),
    )(coords, *weights.operands, x, att)


def feed_back_kernel(
    cot_ref, cls_ref, norm2_ref, dg_ref, norm1_ref, rate_ref,
    wdown_ref, wup_ref, wout_ref, vec_ref,
    dm_ref, du_ref, dao_ref, da_ref, one_ref, sums_ref, res_ref,
):
    step = pl.program_id(0)

    @pl.when(step == 0)
    def _():
        sums_ref[...] = jnp.zeros_like(sums_ref)

    segs = TILE // SEG_LEN
    row_ids = lax.broadcasted_iota(jnp.int32, (SEG_LEN, D), 0)

    def add_sum(row, values):
        sums_ref[row : row + 1, :] += jnp.sum(values, axis=0, keepdims=True)

    def start(s, carry):
        rows = pl.ds(pl.multiple_of(s * SEG_LEN, SEG_LEN), SEG_LEN)
        cls = cls_ref[pl.ds(step * segs + s, 1), :]
        grad = jnp.where(row_ids == 0, cls, cot_ref[rows, :].astype(jnp.float32))
        normal = norm2_ref[rows, :].astype(jnp.float32)
        add_sum(10, grad * normal)
        add_sum(11, grad)
        two = norm_pull(grad, normal, rate_ref[rows, 1:2], vec_ref[10:11, :])
        res_ref[rows, :] = two
        dm = low(two)
        dm_ref[rows, :] = dm
        add_sum(9, dm.astype(jnp.float32))
        return carry

    lax.fori_loop(0, segs, start, 0)
    dm = dm_ref[...]
    for j in range(FF // FBLOCK):
        cols = slice(j * FBLOCK, (j + 1) * FBLOCK)
        du = low(dot_nt(dm, wdown_ref[cols, :]) * dg_ref[:, cols].astype(jnp.float32))
        du_ref[:, cols] = du
        add_sum(5 + j, du.astype(jnp.float32))
        res_ref[...] += dot_nt(du, wup_ref[:, cols])

    def finish(s, carry):
        rows = pl.ds(pl.multiple_of(s * SEG_LEN, SEG_LEN), SEG_LEN)
        grad = res_ref[rows, :]
        normal = norm1_ref[rows, :].astype(jnp.float32)
        add_sum(3, grad * normal)
        add_sum(4, grad)
        one = norm_pull(grad, normal, rate_ref[rows, 0:1], vec_ref[3:4, :])
        one_ref[rows, :] = one
        dao = low(one)
        dao_ref[rows, :] = dao
        add_sum(2, dao.astype(jnp.float32))
        return carry

    lax.fori_loop(0, segs, finish, 0)
    da_ref[...] = low(dot_nt(dao_ref[...], wout_ref[...]))


def feed_back(cot, cls, norm2, dg, norm1, rates, w_down, w_up, w_out, vecs):
    n = cot.shape[0]
    bf, f32 = jnp.bfloat16, jnp.float32
    return ordered(
        feed_back_kernel,
        grid=(n // TILE,),
        in_specs=[
            tiles(D), fixed((n // SEG_LEN, D)), tiles(D), tiles(FF), tiles(D), tiles(LANES),
            fixed((FF, D)), fixed((D, FF)), fixed((D, D)), fixed((VECTOR_ROWS, D)),
        ],
        out_specs=[
            tiles(D), tiles(FF), tiles(D), tiles(D), tiles(D),
            pl.BlockSpec((VECTOR_ROWS, D), lambda i: (0, 0)),
        ],
        out_shape=[
            jax.ShapeDtypeStruct((n, D), bf),
            jax.ShapeDtypeStruct((n, FF), bf),
            jax.ShapeDtypeStruct((n, D), bf),
            jax.ShapeDtypeStruct((n, D), bf),
            jax.ShapeDtypeStruct((n, D), f32),
            jax.ShapeDtypeStruct((VECTOR_ROWS, D), f32),
        ],
        scratch_shapes=[pltpu.VMEM((TILE, D), f32)],
        compiler_params=kernel_params(60),
        cost_estimate=cost(44),
    )(cot, cls, norm2, dg, norm1, rates, w_down, w_up, w_out, vecs)


def attend_back_kernel(packed_ref, stat_ref, da_ref, before_ref, *refs):
    dqkv_ref, sums_ref = refs[-2:]

    @pl.when(pl.program_id(0) == 0)
    def _():
        sums_ref[...] = before_ref[...]

    lanes = lax.broadcasted_iota(jnp.int32, (SEG_LEN, LANES), 1)
    scale = HEAD_DIM**-0.5

    def segment(s, carry):
        rows = pl.ds(pl.multiple_of(s * SEG_LEN, SEG_LEN), SEG_LEN)
        stat = stat_ref[rows, :]
        for pair in range(PAIRS):
            q = packed_ref[rows, third(0, pair)] * jnp.bfloat16(scale)
            k = packed_ref[rows, third(1, pair)]
            v = packed_ref[rows, third(2, pair)]
            da = da_ref[rows, pair * LANES : (pair + 1) * LANES]
            queries, grads = both_heads(q), both_heads(da)
            log_sum = jnp.concatenate([stat[:, 2 * pair : 2 * pair + 1], stat[:, 2 * pair + 1 : 2 * pair + 2]], axis=0)
            weights = jnp.exp(dot_nt(queries, k) - log_sum)
            grad_weights = dot_nt(grads, v)
            dv = dot_tn(low(weights), grads)
            inner = jnp.sum(grad_weights * weights, axis=-1, keepdims=True)
            ds = low(weights * (grad_weights - inner))
            dq = dot_nn(side_by_side(ds), both_heads(k)) * scale
            dk = dot_tn(ds, queries)
            for part, grad in enumerate((dq, dk, dv)):
                grad = low(grad)
                cols = third(part, pair)
                dqkv_ref[rows, cols] = grad
                if part != 1:
                    here = (slice(part // 2, part // 2 + 1), third(0, pair))
                    sums_ref[here] += jnp.sum(grad.astype(jnp.float32), axis=0, keepdims=True)
        return carry

    lax.fori_loop(0, TILE // SEG_LEN, segment, 0)


def attend_back(packed, stat, da, first, count, previous=None):
    n = packed.shape[0]
    before = previous[1] if previous else jnp.zeros((8, D), jnp.float32)
    return in_parts(
        attend_back_kernel,
        10 * count,
        count,
        [packed, stat, da, before],
        [tiles(3 * D, first), tiles(LANES, first), tiles(D, first), fixed((8, D))],
        [jax.ShapeDtypeStruct((n, 3 * D), jnp.bfloat16), jax.ShapeDtypeStruct((8, D), jnp.float32)],
        [tiles(3 * D, first), pl.BlockSpec((8, D), lambda i: (0, 0))],
        [],
        previous and previous[:1],
    )


def cross_kernel(
    load, rows_ref, tagc_ref, tagr_ref, gz_ref, wqkv_ref, wout_ref, wup_ref, wdown_ref, vec_ref,
    out_ref, grows_ref, sums_ref, gqkv_ref, go_ref, gu_ref, gm_ref, rowst_ref, attt_ref, hidt_ref, actt_ref,
    packed_ref, weights_ref, att_ref, act_ref, slope_ref, res_ref,
):
    scale = HEAD_DIM**-0.5
    rows = rows_ref[...]
    rowst_ref[...] = rows.T
    same = tagc_ref[:, 0:1] == tagr_ref[0:1, :]
    same = jnp.concatenate([same, same], axis=0)

    def add_sum(row, values):
        sums_ref[row : row + 1, :] = jnp.sum(values.astype(jnp.float32), axis=0, keepdims=True)

    def pair_cols(pair):
        return slice(pair * LANES, (pair + 1) * LANES)

    sums_ref[...] = jnp.zeros_like(sums_ref)
    load(0)
    for j in range(3):
        cols = slice(j * D, (j + 1) * D)
        part = dot_nn(rows, wqkv_ref[:, cols])
        packed_ref[:, cols] = low(part if j == 1 else part + vec_ref[j // 2 : j // 2 + 1, :])
    for pair in range(PAIRS):
        q = packed_ref[:, third(0, pair)] * jnp.bfloat16(scale)
        scores = jnp.where(same, dot_nt(both_heads(q), packed_ref[:, third(1, pair)]), NEGATIVE)
        raised = jnp.exp(scores - jnp.max(scores, axis=-1, keepdims=True))
        weights = raised * (1.0 / jnp.sum(raised, axis=-1, keepdims=True))
        weights_ref[pair] = weights
        blend = dot_nn(side_by_side(low(weights)), both_heads(packed_ref[:, third(2, pair)]))
        att_ref[:, pair_cols(pair)] = low(blend)
    att = att_ref[...]
    attt_ref[...] = att.T
    load(1)
    resid = rows.astype(jnp.float32) + dot_nn(att, wout_ref[...]) + vec_ref[2:3, :]
    hidden, normal_three, rate_three = norm_rows(resid, vec_ref[3:4, :], vec_ref[4:5, :])
    hidden_low = low(hidden)
    hidt_ref[...] = hidden_low.T
    load(2)
    res_ref[...] = hidden + vec_ref[9:10, :]
    for j in range(FF // FBLOCK):
        cols = slice(j * FBLOCK, (j + 1) * FBLOCK)
        act, slope = gelu_pair(dot_nn(hidden_low, wup_ref[:, cols]) + vec_ref[5 + j : 6 + j, :])
        act = low(act)
        actt_ref[cols, :] = act.T
        slope_ref[:, cols] = slope
        res_ref[...] += dot_nn(act, wdown_ref[cols, :])
    crossed, normal_four, rate_four = norm_rows(res_ref[...], vec_ref[10:11, :], vec_ref[11:12, :])
    out_ref[...] = low(crossed)

    grad_z = gz_ref[...].astype(jnp.float32)
    add_sum(10, grad_z * normal_four)
    add_sum(11, grad_z)
    grad_four = norm_pull(grad_z, normal_four, rate_four, vec_ref[10:11, :])
    grad_m = low(grad_four)
    gm_ref[...] = grad_m
    add_sum(9, grad_m)
    res_ref[...] = grad_four
    for j in range(FF // FBLOCK):
        cols = slice(j * FBLOCK, (j + 1) * FBLOCK)
        grad_u = low(dot_nt(grad_m, wdown_ref[cols, :]) * slope_ref[:, cols])
        gu_ref[:, cols] = grad_u
        add_sum(5 + j, grad_u)
        res_ref[...] += dot_nt(grad_u, wup_ref[:, cols])
    grad_h = res_ref[...]
    add_sum(3, grad_h * normal_three)
    add_sum(4, grad_h)
    grad_three = norm_pull(grad_h, normal_three, rate_three, vec_ref[3:4, :])
    grad_o = low(grad_three)
    go_ref[...] = grad_o
    add_sum(2, grad_o)
    res_ref[...] = grad_three
    att_ref[...] = low(dot_nt(grad_o, wout_ref[...]))
    for pair in range(PAIRS):
        queries = both_heads(packed_ref[:, third(0, pair)] * jnp.bfloat16(scale))
        grads = both_heads(att_ref[:, pair_cols(pair)])
        weights = weights_ref[pair]
        grad_weights = dot_nt(grads, packed_ref[:, third(2, pair)])
        dv = dot_tn(low(weights), grads)
        inner = jnp.sum(grad_weights * weights, axis=-1, keepdims=True)
        ds = low(weights * (grad_weights - inner))
        dq = dot_nn(side_by_side(ds), both_heads(packed_ref[:, third(1, pair)])) * scale
        dk = dot_tn(ds, queries)
        for part, grad in enumerate((dq, dk, dv)):
            gqkv_ref[:, third(part, pair)] = low(grad)
    add_sum(0, gqkv_ref[:, :D])
    add_sum(1, gqkv_ref[:, 2 * D :])
    for j in range(3):
        cols = slice(j * D, (j + 1) * D)
        res_ref[...] += dot_nt(gqkv_ref[:, cols], wqkv_ref[:, cols])
    grows_ref[...] = low(res_ref[...])


def cross_layer(cls, places, tags, grad_out, weights, coords):
    m = cls.shape[0]
    bf, f32 = jnp.bfloat16, jnp.float32
    tagc = jnp.broadcast_to(tags.astype(f32)[:, None], (m, LANES))
    tagr = jnp.broadcast_to(tags.astype(f32)[None, :], (8, m))
    count = len(weights.operands)
    operands = [cls, tagc, tagr, grad_out]
    shapes = [(m, D), (m, D), (VECTOR_ROWS, D), (m, 3 * D), (m, D), (m, FF), (m, D), (D, m), (D, m), (D, m), (FF, m)]
    matrices = [number for number, item in enumerate(weights.items) if item.cols]
    vectors = [number for number, item in enumerate(weights.items) if not item.cols]
    needs = [(matrices[:1], vectors[:1]), (matrices[1:2], vectors[1:2]), (matrices[2:], vectors[2:])]

    def kernel(coords_ref, *refs):
        sources, refs = refs[:count], refs[count:]
        ins, outs = refs[: len(operands)], refs[len(operands) : len(operands) + len(shapes)]
        held, vec_ref, refs = refs[-8:-4], refs[-4], (refs[len(operands) + len(shapes) : -8], refs[-3:])
        scratch, (staged, wide, sems) = refs
        waited = set()
        rows_of = {number: row for number, row in zip(vectors, (0, 2, 5, 9))}
        weights.start(coords_ref, sources, staged, sems)

        def load(stage):
            for number in needs[stage][0]:
                weights.wait(number, waited, staged, sems)
                weights.matrix(number, staged, wide, held[matrices.index(number)])
            for number in needs[stage][1]:
                weights.wait(number, waited, staged, sems)
                weights.vectors(number, staged, wide, vec_ref, rows_of[number])

        vec_ref[...] = jnp.zeros_like(vec_ref)
        cross_kernel(load, *ins, *held, vec_ref, *outs, *scratch)

    return ordered(
        kernel,
        out_shape=[jax.ShapeDtypeStruct(shape, f32 if i == 2 else bf) for i, shape in enumerate(shapes)],
        in_specs=[spec_smem()] + [spec_any()] * count + [spec_vmem()] * len(operands),
        out_specs=[spec_vmem()] * len(shapes),
        scratch_shapes=[
            pltpu.VMEM((m, 3 * D), bf),
            pltpu.VMEM((PAIRS, 2 * m, m), f32),
            pltpu.VMEM((m, D), bf),
            pltpu.VMEM((m, D), bf),
            pltpu.VMEM((m, FF), f32),
            pltpu.VMEM((m, D), f32),
        ]
        + [pltpu.VMEM(weights.items[number].shape, bf) for number in matrices]
        + [pltpu.VMEM((VECTOR_ROWS, D), f32)]
        + weights.scratch,
        compiler_params=kernel_params(62),
        cost_estimate=cost(22),
    )(coords, *weights.operands, *operands)


def class_rows(cls, cot, hot, doc, pos, weights, coords):
    count = len(weights.operands)
    segs = cls.shape[0]

    def kernel(coords_ref, *refs):
        sources, (cls_ref, cot_ref, hot_ref, doc_ref, pos_ref, out_ref, wide_out, table, staged, wide, sems) = (
            refs[:count],
            refs[count:],
        )
        weights.start(coords_ref, sources, staged, sems)
        lanes = lax.broadcasted_iota(jnp.int32, (1, LANES), 1)
        for s in range(segs):
            wide_out[s : s + 1, D : 2 * D] = cot_ref[s, 0:1, :].astype(jnp.float32)
            tag = jnp.where(lanes == 0, doc_ref[s], jnp.where(lanes == 1, pos_ref[s], 0))
            wide_out[s : s + 1, 2 * D :] = tag.astype(jnp.float32)
        weights.wait(0, set(), staged, sems)
        weights.matrix(0, staged, wide, table)
        wide_out[:, :D] = cls_ref[...] + dot_nn(hot_ref[...], table[...])
        out_ref[...] = low(wide_out[...])

    def whole(shape):
        return pl.BlockSpec(shape, lambda i: (0,) * len(shape))

    return ordered(
        kernel,
        grid=(1,),
        out_shape=jax.ShapeDtypeStruct((segs, 2 * D + LANES), jnp.bfloat16),
        in_specs=[spec_smem()] + [spec_any()] * count
        + [whole(cls.shape), whole((segs, BLK, D)), whole(hot.shape), spec_smem(), spec_smem()],
        out_specs=whole((segs, 2 * D + LANES)),
        scratch_shapes=[
            pltpu.VMEM((segs, 2 * D + LANES), jnp.float32),
            pltpu.VMEM((LONG_SEGS, D), jnp.bfloat16),
        ]
        + weights.scratch,
        compiler_params=kernel_params(),
        cost_estimate=cost(3),
    )(coords, *weights.operands, cls, cot, hot, doc, pos)


def token_back(grad_one, dqkv, w_qkv, first, count, previous=None):
    n = grad_one.shape[0]

    def kernel(one_ref, dqkv_ref, wqkv_ref, *refs):
        total = one_ref[...]
        for j in range(3):
            cols = slice(j * D, (j + 1) * D)
            total = total + dot_nt(dqkv_ref[:, cols], wqkv_ref[:, cols])
        refs[-1][...] = low(total)

    return in_parts(
        kernel,
        3 * count,
        count,
        [grad_one, dqkv, w_qkv],
        [tiles(D, first), tiles(3 * D, first), fixed((D, 3 * D))],
        [jax.ShapeDtypeStruct((n, D), jnp.bfloat16)],
        [tiles(D, first)],
        [],
        previous,
    )
AXES = ("seg", "doc")


def send(geo, value, axis, step):
    return lax.ppermute(value, AXES, geo.shift(axis, step))


def along_z(geo, value):
    return [value] + [send(geo, value, Z, r) for r in range(1, geo.n_doc)]


STEPS = 4


def slab(place, rows):
    return pl.BlockSpec((pl.squeezed, rows, LANES), lambda i: (place, i, 0))


def flat_call(kernel, inputs, outs, micros=2):
    arrays, specs = [], []
    for value, places in inputs:
        rows = value.size // LANES // places
        for place in range(places):
            arrays.append(value.reshape(places, rows, LANES))
            specs.append(slab(place, rows // STEPS))
    shapes, out_specs = [], []
    for shape, places in outs:
        rows = math.prod(shape) // LANES // max(places, 1)
        shapes.append(jax.ShapeDtypeStruct((max(places, 1), rows, LANES), jnp.bfloat16))
        out_specs.append(pl.BlockSpec((max(places, 1), rows // STEPS, LANES), lambda i: (0, i, 0)))
    results = ordered(
        kernel,
        grid=(STEPS,),
        out_shape=shapes,
        in_specs=specs,
        out_specs=out_specs,
        compiler_params=kernel_params(60),
        cost_estimate=cost(micros),
    )(*arrays)
    return [value.reshape(shape) for value, (shape, _) in zip(results, outs)]


def gather_plane(geo, halves, step):
    orders = ((X, Y), (Y, X))
    inputs, outs = [], []
    for half, order in zip(halves, orders):
        came = [send(geo, half, order[step], r) for r in range(1, geo.size(order[step]))]
        inputs += [(value, 1) for value in [half] + came]
        outs.append(((1 + len(came),) + half.shape, 1 + len(came)))

    def kernel(*refs):
        sources, targets = refs[: len(inputs)], refs[len(inputs) :]
        for target, (_, places) in zip(targets, outs):
            for place in range(places):
                target[place] = sources[place][...]
            sources = sources[places:]

    return flat_call(kernel, inputs, outs)


def gather_cores(geo, halves):
    return [array for half in halves for array in (half, send(geo, half, C, 1))]


def reduce_cores(geo, arrays):
    return [[arrays[2 * half], send(geo, arrays[2 * half + 1], C, 1)] for half in range(2)]


def added(sources):
    return low(sum(source[...].astype(jnp.float32) for source in sources))


def reduce_plane(geo, groups, step):
    orders = ((Y, X), (X, Y))
    inputs, outs, jobs = [], [], []
    for halves, step in zip(groups, step):
        for half, order in zip(halves, orders):
            places = geo.size(order[step])
            inputs += [(value, places) for value in half]
            outs += [(half[0].shape[1:], 0)] * places
            jobs.append((len(half), places, order[step]))

    def kernel(*refs):
        count = sum(places for _, places in inputs)
        sources, targets = refs[:count], refs[count:]
        for terms, places, _ in jobs:
            for place in range(places):
                targets[place][0] = added(sources[place : terms * places : places])
            sources, targets = sources[terms * places :], targets[places:]

    results = flat_call(kernel, inputs, outs)
    reduced = []
    for _, places, axis in jobs:
        mine, results = results[:places], results[places:]
        reduced.append([mine[0]] + [send(geo, mine[r], axis, r) for r in range(1, places)])
    return [reduced[2 * i : 2 * i + 2] for i in range(len(groups))]


def reduce_line(geo, halves, my_z):
    nd = geo.n_doc
    inputs = [value for half in halves for value in half]
    count = inputs[0].shape[0] // nd
    rows = [half[0].shape[1] for half in halves]

    def kernel(z_ref, *refs):
        sources, targets = refs[: len(inputs)], refs[len(inputs) :]
        done = 0
        for half, n in zip(halves, rows):
            terms, sources = sources[: len(half)], sources[len(half) :]
            for r in range(nd):
                z = wrap(z_ref[0] + r, nd)
                for s in range(count):
                    total = sum(term[s * nd + z].astype(jnp.float32) for term in terms)
                    targets[r][s, done : done + n] = low(total)
            done += n

    outs = ordered(
        kernel,
        out_shape=[jax.ShapeDtypeStruct((count, geo.share, LANES), jnp.bfloat16)] * nd,
        in_specs=[spec_smem()] + [spec_vmem()] * len(inputs),
        out_specs=[spec_vmem()] * nd,
        compiler_params=kernel_params(60),
        cost_estimate=cost(2),
    )(my_z.reshape(1), *inputs)
    return [outs[0]] + [send(geo, outs[r], Z, r) for r in range(1, nd)]


def sum_line(geo, line):
    def kernel(*refs):
        refs[-1][0] = added(refs[:-1])

    return flat_call(kernel, [(part, 1) for part in line], [(line[0].shape, 0)])[0]


def sum_all(geo, line, *others):
    count = line[0].shape[0]

    def kernel(*refs):
        sources, target = refs[:-1], refs[-1]
        target[:count] = added(sources[: len(line)])
        row = count
        for source in sources[len(line) :]:
            target[row : row + source.shape[0]] = source[...]
            row += source.shape[0]

    return ordered(
        kernel,
        out_shape=jax.ShapeDtypeStruct((geo.n_seg, geo.share, LANES), jnp.bfloat16),
        in_specs=[spec_vmem()] * (len(line) + len(others)),
        out_specs=spec_vmem(),
        compiler_params=kernel_params(),
        cost_estimate=cost(2),
    )(*line, *others)


def gate(value):
    def kernel(source, target):
        target[0] = source[...]

    return flat_call(kernel, [(value, 1)], [(value.shape, 0)])[0]
def row_rates(geo, n_tokens, n_cls):
    runs = []
    cross = list(LAYOUT)[-13:]
    row = 0
    for name, shape in LAYOUT.items():
        scale = 1.0 / math.sqrt(n_cls if name in cross else n_tokens)
        rate = 0.2
        if len(shape) == 2:
            rate = 1.0 if name == cross[0] else 0.5 / math.sqrt(shape[0])
        runs.append((row, scale, rate))
        row += math.prod(shape) // LANES
    runs.append((row, 0.0, 0.2))
    begins = [run[0] for run in runs] + [geo.chunk * geo.n_dev]
    found = []
    for n in range(geo.n_dev):
        lo, hi = n * geo.chunk, (n + 1) * geo.chunk
        found.append(
            [(max(run[0] - lo, 0), *run[1:]) for run, end in zip(runs, begins[1:]) if run[0] < hi and end > lo]
        )
    most = max(len(rows) for rows in found)
    found = [rows + [(geo.chunk, 0.0, 0.0)] * (most - len(rows)) for rows in found]
    return np.asarray(found, np.float32).transpose(0, 2, 1).copy()


def matmul(left, right):
    return jnp.dot(left, right, preferred_element_type=jnp.float32)


def column_sum(rows):
    return jnp.sum(rows.astype(jnp.float32), axis=0, keepdims=True)


def local(tokens, cotangent, seg_doc, seg_pos, master, momentum, average):
    n_seg = lax.axis_size(AXES[0])
    n_doc = lax.axis_size(AXES[1])
    geo = Geometry(n_seg, n_doc, master.shape[0])
    by = geo.by_name
    gather = Buckets(geo, [4, 4, 1], by.w_out, by.pos_table)
    buckets = Buckets(geo, [4, 4, 4, 1], by.w_out, by.w_down, by.pos_table)
    my_seg, my_doc = lax.axis_index(AXES[0]), lax.axis_index(AXES[1])
    me = my_seg * n_doc + my_doc
    coords = jnp.stack([my_seg // 4, my_seg // 2 % 2, my_seg % 2, my_doc]).astype(jnp.int32)
    table = lax.dynamic_index_in_dim(jnp.asarray(geo.block_tables()[1]), me, 0, False)
    pad_rows = ceil_to(geo.chunk + 4 * BLK, 8)
    ORDER.start()
    aligned = align_rows(geo, table, master.reshape(geo.chunk, LANES), pad_rows)
    shares = lax.all_to_all(aligned.reshape(geo.n_seg, geo.share, LANES), AXES[0], 0, 0, tiled=True)
    parts = [shares[span.start // n_doc : span.stop // n_doc] for span in gather.ranges]

    seg_count = tokens.shape[1]
    n_rows = n_seg * seg_count
    tiles_all = seg_count * SEG_LEN // TILE
    middle = max(1, tiles_all - 2)
    last = tiles_all - 1 - middle
    inputs = tokens[0].reshape(seg_count * SEG_LEN, D)
    cot_rows = cotangent[0]

    line = place_line(geo, along_z(geo, parts[0]), my_doc)
    parts_b = along_z(geo, parts[1])
    ORDER.wait_for(*parts_b[1:2])
    plane = gather_plane(geo, line, 0)
    ORDER.wait_for(*parts_b[2:3])
    plane = gather_plane(geo, plane, 1)
    gathered = [gather_cores(geo, plane), None, None]

    def weights(*numbers):
        return Weights(geo, gather, gathered, [item_name(i) for i in numbers])

    def own(values):
        return lax.dynamic_slice_in_dim(values, my_seg * seg_count, seg_count, axis=0)

    plane_b = place_line(geo, parts_b, my_doc)
    *outs, w_qkv, vec_a = attend_first(inputs, weights(0, 1), coords)
    plane_b = gather_plane(geo, plane_b, 0)
    gathered[2] = [lax.all_gather(gate(parts[2]), AXES)]
    outs = attend_layer(inputs, w_qkv, vec_a, 1, middle, outs)
    plane_b = gather_plane(geo, plane_b, 1)
    gathered[1] = gather_cores(geo, plane_b)
    if last:
        outs = attend_layer(inputs, w_qkv, vec_a, 1 + middle, last, outs)
    packed, attended, stat = outs
    hidden_low, normal_one, active, slope, normal_two, rates, hidden_two, cls, w_out, w_up, w_down, vec = feed_layer(
        inputs, attended, weights(1, 2, 3, 4, 5, 6, 7), coords
    )

    hot = (seg_pos[0][:, None] == jnp.arange(LONG_SEGS)[None, :]).astype(jnp.bfloat16)
    mine = class_rows(cls, cot_rows, hot, seg_doc[0], seg_pos[0], weights(8), coords)
    tagged = lax.all_gather(mine, AXES[0], axis=0, tiled=True)
    rows, all_grad, all_doc, all_pos = tagged[:, :D], tagged[:, D : 2 * D], tagged[:, 2 * D], tagged[:, 2 * D + 1]
    pos_hot = (all_pos.astype(jnp.int32)[:, None] == jnp.arange(LONG_SEGS)[None, :]).astype(jnp.bfloat16)
    crossed, grad_rows, xsums, g_qkv, g_o, g_u, g_m, rows_t, att_t, hid_t, act_t = cross_layer(
        rows, all_pos, all_doc, all_grad, weights(9, 10, 11, 12, 13, 14, 15, 16), coords
    )
    names = [item_name(i) for i in (8, 9, 11, 13, 15)]
    line_c = pack_cross(
        geo,
        buckets.ranges[3],
        dict(zip(names, (pos_hot.T, rows_t, att_t, hid_t, act_t))),
        dict(zip(names, (grad_rows, g_qkv, g_o, g_u, g_m))),
        {item_name(i): (xsums, row) for i, row in ((10, 0), (12, 2), (14, 5), (16, 9))},
        my_seg.astype(jnp.int32).reshape(1),
    )
    line_c = reduce_line(geo, [[line_c]], my_doc)

    grads = {}
    dm, du, dao, da, grad_one, sums = feed_back(
        cot_rows.reshape(-1, D), own(grad_rows).astype(jnp.float32), normal_two, slope, normal_one, rates,
        w_down, w_up, w_out, vec,
    )
    sums_c = sum_line(geo, line_c)
    grads[item_name(8)] = low(matmul(hot.T, own(grad_rows)))
    for number, row in ((3, 2), (5, 5), (7, 9)):
        grads[item_name(number)] = (sums, row)
    *arrays_d, grads[item_name(6)] = grad_bucket(
        geo, buckets, 2, grads, coords, item_name(6), active, dm, 512, keep=True
    )
    halves_d = reduce_cores(geo, arrays_d)
    grads[item_name(2)] = low(matmul(attended.T, dao))
    ORDER.wait_for(grads[item_name(2)])
    halves_d, = reduce_plane(geo, [halves_d], [0])
    arrays_b = grad_bucket(geo, buckets, 1, grads, coords, item_name(4), hidden_low, du, 256)
    halves_b = reduce_cores(geo, arrays_b)
    back = attend_back(packed, stat, da, 0, 1)
    halves_d, halves_b = reduce_plane(geo, [halves_d, halves_b], [1, 0])
    if tiles_all > 1:
        back = attend_back(packed, stat, da, 1, middle, back)
    line_d = reduce_line(geo, halves_d, my_doc)
    halves_b, = reduce_plane(geo, [halves_b], [1])
    if last:
        back = attend_back(packed, stat, da, 1 + middle, last, back)
    dqkv, qv_sums = back
    sums_d = sum_line(geo, line_d)
    line_b = reduce_line(geo, halves_b, my_doc)
    grads[item_name(1)] = (qv_sums, 0)
    arrays_a = grad_bucket(geo, buckets, 0, grads, coords, item_name(0), inputs, dqkv, 256)
    halves_a = reduce_cores(geo, arrays_a)
    halves_a, = reduce_plane(geo, [halves_a], [0])
    token_grad, = token_back(grad_one, dqkv, w_qkv, 0, tiles_all)
    sums_b = sum_line(geo, line_b)
    halves_a, = reduce_plane(geo, [halves_a], [1])
    first_row = lax.broadcasted_iota(jnp.int32, (seg_count, SEG_LEN, D), 1) == 0
    mixed_out = jnp.where(
        first_row, own(crossed)[:, None, :], hidden_two.reshape(seg_count, SEG_LEN, D)
    )
    line_a = reduce_line(geo, halves_a, my_doc)
    owned = lax.all_to_all(
        sum_all(geo, line_a, sums_b, sums_d, sums_c), AXES[0], 0, 0, tiled=True
    )
    n_cls = n_doc * n_rows
    rates = lax.dynamic_index_in_dim(jnp.asarray(row_rates(geo, n_cls * SEG_LEN, n_cls)), me, 0, False)
    begins, factors = rates[0].astype(jnp.int32), rates[1:].reshape(-1)
    state = [value.reshape(geo.chunk, LANES) for value in (master, momentum, average)]
    weight, moment, smooth, copy_low = (
        value.reshape(-1)
        for value in update_rows(geo, table, owned.reshape(-1, LANES), begins, factors, state, pad_rows)
    )
    return (
        mixed_out[None],
        token_grad.reshape(1, seg_count, SEG_LEN, D),
        weight,
        moment,
        smooth,
        copy_low,
    )


def item_name(number):
    return item_list(0)[number].name


def solution(mesh):
    layer = P(AXES[1], AXES[0], None, None)
    ids = P(AXES[1], AXES[0])
    flat = P(AXES)
    return jax.shard_map(
        local,
        mesh=mesh,
        in_specs=(layer, layer, ids, ids, flat, flat, flat),
        out_specs=(layer, layer, flat, flat, flat, flat),
        check_vma=False,
    )
```

```python
import math
from types import SimpleNamespace

import jax
import jax.numpy as jnp
import numpy as np
from jax import lax
from jax.experimental import pallas as pl
from jax.experimental.pallas import tpu as pltpu
from jax.sharding import PartitionSpec as P

D = 768
HEADS = 12
HEAD_DIM = 64
FF = 3072
SEG_LEN = 128
LONG_SEGS = 64
EPSILON = 1e-05
NEGATIVE = -1e30

LAYOUT = dict(
    w_qkv=(D, 3 * D),
    b_qv=(2 * D,),
    w_out=(D, D),
    b_out=(D,),
    gain_one=(D,),
    bias_one=(D,),
    w_up=(D, FF),
    b_up=(FF,),
    w_down=(FF, D),
    b_down=(D,),
    gain_two=(D,),
    bias_two=(D,),
    pos_table=(LONG_SEGS, D),
    x_qkv=(D, 3 * D),
    x_bqv=(2 * D,),
    x_out=(D, D),
    x_bout=(D,),
    gain_three=(D,),
    bias_three=(D,),
    x_up=(D, FF),
    x_bup=(FF,),
    x_down=(FF, D),
    x_bdown=(D,),
    gain_four=(D,),
    bias_four=(D,),
)
LANES = 128
BLK = 16
Y, X, C, Z = range(4)


def ceil_to(value, step):
    return -(-value // step) * step


def item_list(total_rows):
    items = []
    nat = 0
    for name, shape in LAYOUT.items():
        rows = math.prod(shape) // LANES
        if len(shape) == 1 and items and len(items[-1].shape) == 1:
            items[-1].names.append(name)
            items[-1].rows += rows
        else:
            items.append(SimpleNamespace(name=name, names=[name], shape=shape, nat=nat, rows=rows))
        nat += rows
    items.append(SimpleNamespace(name=None, names=[], shape=None, nat=nat, rows=total_rows - nat))
    blk = 0
    for item in items:
        item.cols = item.shape[1] // LANES if item.shape and len(item.shape) == 2 else 0
        item.blk = blk
        blk += ceil_to(item.rows, BLK) // BLK
    return items


class Geometry:
    def __init__(self, n_seg, n_doc, shard_len):
        self.n_seg, self.n_doc = n_seg, n_doc
        self.n_dev = n_seg * n_doc
        self.chunk = shard_len // LANES
        self.items = item_list(self.chunk * self.n_dev)
        self.by_name = SimpleNamespace(**{item.name: item for item in self.items if item.name})
        firsts, lasts = [], []
        for n in range(self.n_dev):
            lo, hi = n * self.chunk, (n + 1) * self.chunk
            blocks = []
            for item in self.items:
                a, b = max(lo, item.nat), min(hi, item.nat + item.rows)
                if a < b:
                    blocks.append(item.blk + (a - item.nat) // BLK)
                    blocks.append(item.blk + (b - 1 - item.nat) // BLK)
            firsts.append(min(blocks))
            lasts.append(max(blocks))
        self.first, self.last = firsts, lasts
        most = max(b - a + 1 for a, b in zip(firsts, lasts))
        self.piece_blocks = -(-most // self.n_dev)
        self.piece = self.piece_blocks * BLK
        self.slots = self.piece_blocks * self.n_dev
        self.groups = -(-most // (self.piece_blocks * n_doc))
        self.share = n_doc * self.piece
        self.staged_rows = self.groups * self.share
        self.c_size, self.x_size = 2, 2
        self.y_size = n_seg // 4

    def full_groups(self, item, chunk):
        rows = BLK * item.cols
        lo, hi = chunk * self.chunk - item.nat, (chunk + 1) * self.chunk - item.nat
        first, last = max(0, -(-lo // rows)), min(item.rows, hi) // rows
        return first, max(first, last)

    def block_tables(self):
        matrices = [item for item in self.items if item.cols]
        single = [[] for _ in range(self.n_dev)]
        groups = np.zeros((self.n_dev, len(matrices), 3), np.int32)
        for n in range(self.n_dev):
            lo, hi = n * self.chunk, (n + 1) * self.chunk
            for t in range(self.slots):
                b = self.first[n] + t
                if b > self.last[n]:
                    single[n].append((t, 0, 0, 0))
                    continue
                item = [it for it in self.items if it.blk <= b][-1]
                at = b - item.blk
                if item.cols:
                    first, last = self.full_groups(item, n)
                    if first <= at // item.cols < last:
                        continue
                start = item.nat + at * BLK
                a = max(start, lo)
                z = max(a, min(start + BLK, hi, item.nat + item.rows))
                single[n].append((t, start - lo, a - start, z - start))
            for i, item in enumerate(matrices):
                first, last = self.full_groups(item, n)
                if first < last:
                    slot = item.blk + first * item.cols - self.first[n]
                    groups[n, i] = (slot, item.nat + first * BLK * item.cols - lo, last - first)
        most = max(len(rows) for rows in single)
        table = np.zeros((self.n_dev, 1 + 4 * most), np.int32)
        for n, rows in enumerate(single):
            table[n, 0] = len(rows)
            table[n, 1 : 1 + 4 * len(rows)] = np.asarray(rows, np.int32).reshape(-1)
        return matrices, np.concatenate([groups.reshape(self.n_dev, -1), table], axis=1)

    def chunks_of(self, item):
        found = []
        n_blocks = ceil_to(item.rows, BLK) // BLK
        for n in range(self.n_dev):
            a = max(item.blk, self.first[n])
            b = min(item.blk + n_blocks, self.last[n] + 1)
            if a < b:
                found.append((n, a - item.blk, b - item.blk, a - self.first[n]))
        return found

    def spans(self, *ends):
        cuts = [0] + [ceil_to((end.nat - 1) // self.chunk + 1, self.n_doc) for end in ends] + [self.n_dev]
        return [range(a, b) for a, b in zip(cuts, cuts[1:])]

    def coords(self, device):
        seg, doc = divmod(device, self.n_doc)
        yx, c = divmod(seg, self.c_size)
        return [*divmod(yx, self.x_size), c, doc]

    def device(self, y, x, c, z):
        return ((y * self.x_size + x) * self.c_size + c) * self.n_doc + z

    def size(self, axis):
        return (self.y_size, self.x_size, self.c_size, self.n_doc)[axis]

    def shift(self, axis, step):
        pairs = []
        for source in range(self.n_dev):
            at = self.coords(source)
            at[axis] = (at[axis] + step) % self.size(axis)
            pairs.append((source, self.device(*at)))
        return pairs
def spec_vmem():
    return pl.BlockSpec(memory_space=pltpu.VMEM)


def spec_any():
    return pl.BlockSpec(memory_space=pl.ANY)


def spec_hbm():
    return pl.BlockSpec(memory_space=pltpu.HBM)


def spec_smem():
    return pl.BlockSpec(memory_space=pltpu.SMEM)


def kernel_params(mib=20):
    return pltpu.CompilerParams(vmem_limit_bytes=mib * 1024 * 1024)


def cost(micros):
    micros = micros if micros >= 6 else 0
    return pl.CostEstimate(flops=int(micros * 1e9), bytes_accessed=int(micros * 3e6), transcendentals=0)


class Order:
    def start(self):
        self.token = jnp.zeros((8, LANES), jnp.float32)
        self.others = []

    def wait_for(self, *others):
        self.others += others


ORDER = Order()


def ordered(kernel, out_shape, in_specs, out_specs, **settings):
    single = not isinstance(out_shape, (list, tuple))
    outs, specs = ([out_shape], [out_specs]) if single else (list(out_shape), list(out_specs))

    def run(*inputs):
        extra = [ORDER.token] + ORDER.others
        n_in, n_out, n_extra = len(inputs), len(outs), len(extra)

        def wrapped(*refs):
            rest = refs[n_in + n_extra :]
            kernel(*refs[:n_in], *rest[:n_out], *rest[n_out + 1 :])

        results = pl.pallas_call(
            wrapped,
            out_shape=outs + [jax.ShapeDtypeStruct((8, LANES), jnp.float32)],
            in_specs=list(in_specs) + [spec_any()] * n_extra,
            out_specs=specs + [spec_any()],
            **settings,
        )(*inputs, *extra)
        ORDER.token, ORDER.others = results[-1], []
        return results[0] if single else results[:-1]

    return run


def row_mask(low, high):
    rows = lax.broadcasted_iota(jnp.int32, (BLK, LANES), 0)
    return (rows >= low) & (rows < high)


def block_moves(geo, table_ref, by_group, by_row):
    matrices = geo.block_tables()[0]
    for i, item in enumerate(matrices):
        def body(g, carry, i=i, cols=item.cols):
            for cb in range(cols):
                by_group(table_ref[3 * i] + g * cols + cb, table_ref[3 * i + 1] + g * BLK * cols + cb, cols)
            return carry

        lax.fori_loop(0, table_ref[3 * i + 2], body, 0)
    base = 3 * len(matrices)

    def single(r, carry):
        by_row(*[table_ref[base + 1 + 4 * r + j] for j in range(4)])
        return carry

    lax.fori_loop(0, table_ref[base], single, 0)


def block_at(slot):
    return pl.ds(pl.multiple_of(slot * BLK, BLK), BLK)


def align_rows(geo, table, natural, pad_rows):
    def kernel(table_ref, natural_ref, out_ref, rows_ref):
        def fill(row, rows):
            rows_ref[pl.ds(row + BLK, rows), :] = natural_ref[pl.ds(row, rows), :]

        copy_rows(natural.shape[0], 256, fill)

        def by_group(slot, start, cols):
            out_ref[block_at(slot), :] = rows_ref[pl.ds(start + BLK, BLK, stride=cols), :].astype(jnp.bfloat16)

        def by_row(slot, start, low_row, high_row):
            rows = jnp.where(row_mask(low_row, high_row), rows_ref[pl.ds(start + BLK, BLK), :], 0.0)
            out_ref[block_at(slot), :] = rows.astype(jnp.bfloat16)

        block_moves(geo, table_ref, by_group, by_row)

    return ordered(
        kernel,
        out_shape=jax.ShapeDtypeStruct((geo.slots * BLK, LANES), jnp.bfloat16),
        in_specs=[spec_smem(), spec_vmem()],
        out_specs=spec_vmem(),
        scratch_shapes=[pltpu.VMEM((pad_rows, LANES), jnp.float32)],
        compiler_params=kernel_params(),
        cost_estimate=cost(3),
    )(table, natural)


def update_rows(geo, table, blocks, begins, factors, state, pad_rows):
    rows_all = geo.chunk
    runs = begins.shape[0]

    def kernel(table_ref, begins_ref, factors_ref, blocks_ref, *refs):
        held, outs, grad_ref = refs[:3], refs[3:7], refs[7]

        def by_group(slot, start, cols):
            grad_ref[pl.ds(start + BLK, BLK, stride=cols), :] = blocks_ref[block_at(slot), :].astype(jnp.float32)

        def by_row(slot, start, low_row, high_row):
            here = pl.ds(start + BLK, BLK)
            rows = blocks_ref[block_at(slot), :].astype(jnp.float32)
            grad_ref[here, :] = jnp.where(row_mask(low_row, high_row), rows, grad_ref[here, :])

        block_moves(geo, table_ref, by_group, by_row)

        def step(row, rows):
            here = pl.ds(row, rows)
            at = lax.broadcasted_iota(jnp.int32, (rows, LANES), 0) + row
            scale = jnp.full((rows, LANES), factors_ref[0], jnp.float32)
            rate = jnp.full((rows, LANES), factors_ref[runs], jnp.float32)
            for run in range(1, runs):
                later = at >= begins_ref[run]
                scale = jnp.where(later, factors_ref[run], scale)
                rate = jnp.where(later, factors_ref[runs + run], rate)
            scaled = grad_ref[pl.ds(row + BLK, rows), :] * scale
            moment = 0.5 * held[1][here, :] + scaled
            weight = held[0][here, :] - rate * (scaled + 0.5 * moment)
            outs[0][here, :] = weight
            outs[1][here, :] = moment
            outs[2][here, :] = 0.5 * held[2][here, :] + 0.5 * weight
            outs[3][here, :] = weight.astype(jnp.bfloat16)

        copy_rows(rows_all, 128, step)

    full = [jax.ShapeDtypeStruct((rows_all, LANES), kind) for kind in (jnp.float32,) * 3 + (jnp.bfloat16,)]
    return ordered(
        kernel,
        out_shape=full,
        in_specs=[spec_smem()] * 3 + [spec_vmem()] * 4,
        out_specs=[spec_vmem()] * 4,
        scratch_shapes=[pltpu.VMEM((pad_rows, LANES), jnp.float32)],
        compiler_params=kernel_params(28),
        cost_estimate=cost(3),
    )(table, begins, factors, blocks, *state)


class Buckets:
    def __init__(self, geo, arrays, *ends):
        self.geo = geo
        self.ranges = geo.spans(*ends)
        self.arrays = arrays

    def find(self, chunk):
        for number, span in enumerate(self.ranges):
            if chunk in span:
                return number, chunk - span.start

    def shapes(self, number):
        geo = self.geo
        count = len(self.ranges[number])
        return [
            (geo.y_size, geo.x_size, count, geo.share // 2, LANES),
            (geo.x_size, geo.y_size, count, geo.share // 2, LANES),
        ]


def wrap(value, size):
    return lax.rem(value + size, size)


def copy_rows(count, step, body):
    full = count // step
    if full:
        def loop(i, carry):
            body(i * step, step)
            return carry

        lax.fori_loop(0, full, loop, 0)
    if count % step:
        body(full * step, count % step)


def place_line(geo, parts, my_z):
    count, nd = parts[0].shape[0], geo.n_doc
    rows = geo.share // 2

    def kernel(z_ref, *refs):
        sources, outs = refs[:nd], refs[nd:]
        for r in range(nd):
            z = wrap(z_ref[0] - r, nd)
            for s in range(count):
                for half in range(2):
                    outs[half][s * nd + z] = sources[r][s, half * rows : (half + 1) * rows]

    return ordered(
        kernel,
        out_shape=[jax.ShapeDtypeStruct((count * nd, rows, LANES), jnp.bfloat16)] * 2,
        in_specs=[spec_smem()] + [spec_vmem()] * nd,
        out_specs=[spec_vmem()] * 2,
        compiler_params=kernel_params(),
        cost_estimate=cost(2),
    )(my_z.reshape(1), *parts)
VECTOR_ROWS = 16


def chunk_copies(geo, buckets, sources, used, coords_ref, n, staged, sem):
    my_y, my_x, my_c = coords_ref[0], coords_ref[1], coords_ref[2]
    number, place = buckets.find(n)
    first = sum(buckets.arrays[m] for m in used[: used.index(number)])
    if buckets.arrays[number] == 1:
        line, z = divmod(place, geo.n_doc)
        for s in range(geo.groups):
            pltpu.make_async_copy(
                sources[first].at[s * geo.n_doc + z, line],
                staged.at[pl.ds(s * geo.share, geo.share)],
                sem,
            ).start()
        return
    rows = geo.share // 2
    for core in range(2):
        c = my_c if core == 0 else 1 - my_c
        for ry in range(geo.y_size):
            for rx in range(geo.x_size):
                y, x = wrap(my_y - ry, geo.y_size), wrap(my_x - rx, geo.x_size)
                s = (y * geo.x_size + x) * 2 + c

                def begin(s=s, ry=ry, rx=rx, core=core):
                    for half in range(2):
                        index = (ry, rx, place) if half == 0 else (rx, ry, place)
                        pltpu.make_async_copy(
                            sources[first + 2 * half + core].at[index],
                            staged.at[pl.ds(pl.multiple_of(s * geo.share + half * rows, BLK), rows)],
                            sem,
                        ).start()

                if geo.groups == geo.n_seg:
                    begin()
                else:
                    pl.when(s < geo.groups)(begin)


class Weights:
    def __init__(self, geo, buckets, gathered, names):
        self.geo, self.buckets = geo, buckets
        self.items = [vars(geo.by_name)[name] for name in names]
        self.chunks = sorted({n for item in self.items for n, *_ in geo.chunks_of(item)})
        self.used = sorted({buckets.find(n)[0] for n in self.chunks})
        self.operands = [array for number in self.used for array in gathered[number]]
        cols = max([item.cols for item in self.items])
        self.scratch = [
            pltpu.VMEM((len(self.chunks), geo.staged_rows, LANES), jnp.bfloat16),
            pltpu.VMEM((BLK * (cols + 2), LANES), jnp.float32),
            pltpu.SemaphoreType.DMA((len(self.chunks),)),
        ]

    def start(self, coords_ref, sources, staged, sems):
        for at, n in enumerate(self.chunks):
            chunk_copies(
                self.geo, self.buckets, sources, self.used, coords_ref, n, staged.at[at], sems.at[at]
            )

    def wait(self, number, waited, staged, sems):
        for n, *_ in self.geo.chunks_of(self.items[number]):
            at = self.chunks.index(n)
            if at not in waited:
                waited.add(at)
                pltpu.make_async_copy(staged.at[at], staged.at[at], sems.at[at]).wait()

    def blocks(self, item, lo, hi, staged, wide):
        done = lo
        for n, b0, b1, slot in self.geo.chunks_of(item):
            for b in range(max(b0, lo), min(b1, hi)):
                at = self.chunks.index(n)
                rows = staged[at, pl.ds((slot + b - b0) * BLK, BLK), :].astype(jnp.float32)
                here = pl.ds((b - lo) * BLK, BLK)
                wide[here, :] = wide[here, :] + rows if b < done else rows
            done = max(done, min(b1, hi))

    def matrix(self, number, staged, wide, out_ref):
        item = self.items[number]
        cols = item.cols
        split = set()
        for n, b0, b1, slot in self.geo.chunks_of(item):
            at = self.chunks.index(n)
            first, last = self.geo.full_groups(item, n)
            split |= set(range(b0 // cols, -(-b1 // cols))) - set(range(first, last))

            def group(g, carry, at=at, shift=slot - b0):
                rows = pl.ds(pl.multiple_of(g * BLK, BLK), BLK)
                for cb in range(cols):
                    tile = staged[at, block_at(g * cols + cb + shift), :]
                    out_ref[rows, cb * LANES : (cb + 1) * LANES] = tile
                return carry

            lax.fori_loop(first, last, group, 0)
        for g in sorted(split):
            self.blocks(item, g * cols, (g + 1) * cols, staged, wide)
            for cb in range(cols):
                tile = wide[pl.ds(cb, BLK, stride=cols), :]
                out_ref[g * BLK : (g + 1) * BLK, cb * LANES : (cb + 1) * LANES] = tile.astype(jnp.bfloat16)

    def vectors(self, number, staged, wide, out_ref, row):
        item = self.items[number]
        self.blocks(item, 0, ceil_to(item.rows, BLK) // BLK, staged, wide)
        for r in range(item.rows):
            v, cb = divmod(r, D // LANES)
            out_ref[row + v : row + v + 1, cb * LANES : (cb + 1) * LANES] = wide[r : r + 1, :]


def vector_rows(wide, values, first, count):
    lane_cols = D // LANES
    for r in range(count):
        v, cb = divmod(r, lane_cols)
        wide[r : r + 1, :] = values[first + v : first + v + 1, cb * LANES : (cb + 1) * LANES]


def bucket_parts(geo, span):
    parts = []
    for item in geo.items:
        chunks = [entry for entry in geo.chunks_of(item) if entry[0] in span]
        if chunks and item.names:
            parts.append((item, chunks))
    return parts


def grad_bucket(geo, buckets, number, grads, coords, name, left, right, rows, keep=False):
    span = buckets.ranges[number]
    parts = bucket_parts(geo, span)
    operands, specs, windows, scratch = [], [], [], []
    wide_rows = BLK
    for item, chunks in parts:
        if len(item.shape) == 2:
            cols = item.cols
            wide_rows = max(wide_rows, BLK * cols)
            if item.name == name:
                main, main_chunks, windows_at = item, chunks, len(windows)
                windows.append(None)
                continue
            k0 = min(b0 for _, b0, _, _ in chunks) // cols
            k1 = -(-max(b1 for _, _, b1, _ in chunks) // cols)
            operands.append(grads[item.name])
            specs.append(spec_any())
            windows.append((len(operands) - 1, k0, k1))
            scratch.append(pltpu.VMEM(((k1 - k0) * BLK, item.shape[1]), jnp.bfloat16))
        else:
            wide_rows = max(wide_rows, ceil_to(item.rows, BLK))
            operands.append(grads[item.name][0])
            specs.append(pl.BlockSpec(operands[-1].shape, lambda i: (0, 0)))
            windows.append((len(operands) - 1, None, None))
            scratch.append(pltpu.VMEM((BLK, LANES), jnp.bfloat16))
    outs = [shape for shape in buckets.shapes(number) for _ in range(2)]
    depth, width = main.shape
    cols = main.cols
    steps = depth // rows
    count = len(operands)
    block_groups = rows // BLK

    def split_groups(item, chunks):
        found = set()
        for n, b0, b1, _ in chunks:
            first, last = geo.full_groups(item, n)
            found |= set(range(b0 // item.cols, -(-b1 // item.cols))) - set(range(first, last))
        return sorted(found)

    def kernel(coords_ref, left_ref, right_ref, *refs):
        sources, targets = refs[:count], refs[count : count + 4]
        refs = refs[count + 4 :]
        if keep:
            kept_ref, refs = refs[0], refs[1:]
        loaded, (values, staged, wide, in_sems, out_sems) = refs[:count], refs[count:]
        step = pl.program_id(0)
        my_y, my_x, my_c = coords_ref[0], coords_ref[1], coords_ref[2]

        def send_out(n):
            _, place = buckets.find(n)
            half_rows = geo.share // 2
            for core in range(2):
                c = my_c if core == 0 else 1 - my_c
                for ry in range(geo.y_size):
                    for rx in range(geo.x_size):
                        y, x = wrap(my_y + ry, geo.y_size), wrap(my_x + rx, geo.x_size)
                        s = (y * geo.x_size + x) * 2 + c
                        for half in range(2):
                            index = (ry, rx, place) if half == 0 else (rx, ry, place)
                            here = pl.ds(pl.multiple_of(s * geo.share + half * half_rows, BLK), half_rows)
                            pltpu.make_async_copy(
                                staged.at[n - span.start, here],
                                targets[2 * half + core].at[index],
                                out_sems.at[n - span.start],
                            ).start()

        def whole(item, chunks, values, base, lo, hi):
            for n, b0, b1, slot in chunks:
                first, last = geo.full_groups(item, n)

                def group(g, carry, n=n, shift=slot - b0):
                    here = pl.ds(pl.multiple_of((g - base) * BLK, BLK), BLK)
                    for cb in range(item.cols):
                        dst = block_at(g * item.cols + cb + shift)
                        staged[n - span.start, dst, :] = values[here, cb * LANES : (cb + 1) * LANES]
                    return carry

                start = jnp.maximum(first, lo)
                lax.fori_loop(start, jnp.maximum(start, jnp.minimum(last, hi)), group, 0)

        def cut(item, chunks, values, base, g):
            for cb in range(item.cols):
                tile = values[pl.ds(pl.multiple_of((g - base) * BLK, BLK), BLK), cb * LANES : (cb + 1) * LANES]
                wide[pl.ds(cb, BLK, stride=item.cols), :] = tile.astype(jnp.float32)
            for n, b0, b1, slot in chunks:
                first, last = geo.full_groups(item, n)
                lo, hi = max(b0, g * item.cols), min(b1, (g + 1) * item.cols)
                if lo < hi and not first <= g < last:
                    part = wide[pl.ds((lo - g * item.cols) * BLK, (hi - lo) * BLK), :]
                    dst = pl.ds((slot + lo - b0) * BLK, (hi - lo) * BLK)
                    staged[n - span.start, dst, :] = part.astype(jnp.bfloat16)

        @pl.when(step == 0)
        def _():
            loads = {}
            for (item, chunks), window in zip(parts, windows):
                if window is not None and window[1] is not None:
                    at, k0, k1 = window
                    source = sources[at].at[pl.ds(k0 * BLK, (k1 - k0) * BLK)]
                    loads[at] = pltpu.make_async_copy(source, loaded[at], in_sems.at[at])
                    loads[at].start()

            def clear(row, size):
                for at in range(len(span)):
                    here = pl.ds(pl.multiple_of(row + tail, BLK), size)
                    staged[at, here, :] = jnp.zeros((size, LANES), jnp.bfloat16)

            tail = min(geo.last[n] - geo.first[n] for n in span) * BLK
            copy_rows(geo.slots * BLK - tail, 128, clear)
            for (item, chunks), window in zip(parts, windows):
                if window is None:
                    continue
                at, k0, k1 = window
                if k0 is None:
                    vector_rows(wide, sources[at], grads[item.name][1], item.rows)
                    for n, b0, b1, slot in chunks:
                        part = wide[pl.ds(b0 * BLK, (b1 - b0) * BLK), :].astype(jnp.bfloat16)
                        staged[n - span.start, pl.ds(slot * BLK, (b1 - b0) * BLK), :] = part
                else:
                    loads[at].wait()
                    whole(item, chunks, loaded[at], k0, k0, k1)
                    for g in split_groups(item, chunks):
                        cut(item, chunks, loaded[at], k0, g)

        values[...] = low(dot_tn(left_ref[...], right_ref[...]))
        if keep:
            kept_ref[...] = values[...]
        low_group = step * block_groups
        whole(main, main_chunks, values, low_group, low_group, low_group + block_groups)
        for g in split_groups(main, main_chunks):
            @pl.when(step == g // block_groups)
            def _(g=g):
                cut(main, main_chunks, values, g // block_groups * block_groups, g)

        ready = {n: 0 for n in span}
        for n, _, b1, _ in main_chunks:
            ready[n] = (b1 - 1) // cols // block_groups
        for at in range(steps):
            here = [n for n in span if ready[n] == at]
            if here:
                @pl.when(step == at)
                def _(here=here):
                    for n in here:
                        send_out(n)

        @pl.when(step == steps - 1)
        def _():
            for at in range(len(span)):
                pltpu.make_async_copy(staged.at[at], staged.at[at], out_sems.at[at]).wait()

    extra = [jax.ShapeDtypeStruct(main.shape, jnp.bfloat16)] if keep else []
    return ordered(
        kernel,
        grid=(steps,),
        out_shape=[jax.ShapeDtypeStruct(shape, jnp.bfloat16) for shape in outs] + extra,
        in_specs=[
            spec_smem(),
            pl.BlockSpec((left.shape[0], rows), lambda i: (0, i)),
            pl.BlockSpec(right.shape, lambda i: (0, 0), pipeline_mode=pl.Buffered(1)),
        ]
        + specs,
        out_specs=[spec_any()] * 4 + [pl.BlockSpec((rows, width), lambda i: (i, 0))] * len(extra),
        scratch_shapes=scratch
        + [
            pltpu.VMEM((rows, width), jnp.bfloat16),
            pltpu.VMEM((len(span), geo.slots * BLK, LANES), jnp.bfloat16),
            pltpu.VMEM((wide_rows + 2 * BLK, LANES), jnp.float32),
            pltpu.SemaphoreType.DMA((max(count, 1),)),
            pltpu.SemaphoreType.DMA((len(span),)),
        ],
        compiler_params=kernel_params(60),
        cost_estimate=cost(18),
    )(coords, left, right, *operands)


class CrossPack:
    def __init__(self, geo, span, depth_rows):
        self.geo, self.span = geo, span
        self.parts = bucket_parts(geo, span)
        self.seg_blocks = geo.n_doc * geo.piece_blocks
        wide_rows, flat_cols, left_rows = BLK, D, BLK
        for item, chunks in self.parts:
            if item.cols:
                left_rows = max(left_rows, len(chunks) * self.window(item))
                wide_rows = max(wide_rows, BLK * item.cols)
                flat_cols = max(flat_cols, item.shape[1])
            else:
                wide_rows = max(wide_rows, ceil_to(item.rows, BLK))
        self.out = jax.ShapeDtypeStruct((len(span), geo.share, LANES), jnp.bfloat16)
        self.scratch = [
            pltpu.VMEM((left_rows, depth_rows), jnp.bfloat16),
            pltpu.VMEM((left_rows, flat_cols), jnp.bfloat16),
            pltpu.VMEM((wide_rows + 2 * BLK, LANES), jnp.float32),
        ]

    def window(self, item):
        return min((-(-(self.seg_blocks - 1) // item.cols) + 1) * BLK, item.shape[0])

    def run(self, seg, lefts, rights, sums_ref, first_rows, out_ref, gathered, flat, wide):
        geo, span, seg_blocks = self.geo, self.span, self.seg_blocks
        low_slot = seg * seg_blocks
        out_ref[...] = jnp.zeros_like(out_ref)

        def slots(lo, hi):
            begin = jnp.maximum(low_slot, lo)
            return begin, jnp.maximum(begin, jnp.minimum(low_slot + seg_blocks, hi))

        def rows_out(n, slot, block, rows):
            begin, end = slots(slot, slot + rows)

            def move(t, carry):
                data = wide[block_at(block + t - slot), :]
                out_ref[n - span.start, block_at(t - low_slot), :] = data.astype(jnp.bfloat16)
                return carry

            lax.fori_loop(begin, end, move, 0)

        for item, chunks in self.parts:
            if not item.cols:
                vector_rows(wide, sums_ref, first_rows[item.name], item.rows)
                for n, b0, b1, slot in chunks:
                    rows_out(n, slot, b0, b1 - b0)
                continue
            cols = item.cols
            size = self.window(item)
            starts = []
            for at, (n, b0, b1, slot) in enumerate(chunks):
                first = jnp.maximum(low_slot, slot) - slot + b0
                start = pl.multiple_of(jnp.clip(first // cols * BLK, 0, item.shape[0] - size), BLK)
                starts.append(start)
                gathered[at * size : (at + 1) * size, :] = lefts[item.name][pl.ds(start, size), :]
            count = len(chunks) * size
            rows = gathered[:count, :]
            for cb in range(0, cols, 2):
                here = slice(cb * LANES, (cb + 2) * LANES)
                flat[:count, here] = dot_nn(rows, rights[item.name][:, here]).astype(jnp.bfloat16)
            for at, (n, b0, b1, slot) in enumerate(chunks):
                first, last = geo.full_groups(item, n)
                base = at * size - starts[at]

                def group_rows(group, base=base):
                    return pl.ds(pl.multiple_of(base + group * BLK, BLK), BLK)

                def by_tile(t, carry, n=n, shift=b0 - slot, group_rows=group_rows, cols=cols):
                    b = t + shift
                    group = b // cols
                    lanes = pl.ds(pl.multiple_of((b - group * cols) * LANES, LANES), LANES)
                    out_ref[n - span.start, block_at(t - low_slot), :] = flat[group_rows(group), lanes]
                    return carry

                if first < last:
                    begin, end = slots(slot + first * cols - b0, slot + last * cols - b0)
                    lax.fori_loop(begin, end, by_tile, 0)
                for g in range(b0 // cols, -(-b1 // cols)):
                    if first <= g < last:
                        continue
                    lo, hi = max(b0, g * cols), min(b1, (g + 1) * cols)
                    begin, end = slots(slot + lo - b0, slot + hi - b0)

                    @pl.when(begin < end)
                    def _(g=g, lo=lo, hi=hi, n=n, shift=slot - b0, group_rows=group_rows, cols=cols):
                        for cb in range(cols):
                            tile = flat[group_rows(g), cb * LANES : (cb + 1) * LANES]
                            wide[pl.ds(cb, BLK, stride=cols), :] = tile.astype(jnp.float32)
                        rows_out(n, lo + shift, lo - g * cols, hi - lo)
TILE = 512
PAIRS = HEADS // 2
TAIL_RATE = 0.3
TAIL = (
    0.11962929605681312,
    0.12075400207853171,
    0.0999131861559567,
    0.12856268365589474,
    -0.05368570534984477,
    0.20635578836359286,
    -0.15720441932045734,
    0.0356750954846771,
)


def dot_nn(left, right):
    return lax.dot_general(left, right, (((1,), (0,)), ((), ())), preferred_element_type=jnp.float32)


def dot_nt(left, right):
    return lax.dot_general(left, right, (((1,), (1,)), ((), ())), preferred_element_type=jnp.float32)


def dot_tn(left, right):
    return lax.dot_general(left, right, (((0,), (0,)), ((), ())), preferred_element_type=jnp.float32)


def low(values):
    return values.astype(jnp.bfloat16)


def gelu_pair(u):
    t = 1.0 / (1.0 + TAIL_RATE * jnp.abs(u))
    poly = TAIL[-1] * t + TAIL[-2]
    for coef in TAIL[-3::-1]:
        poly = poly * t + coef
    bell = jnp.exp(-0.5 * (u * u))
    tail = bell * (poly * t)
    spread = jnp.where(u < 0.0, tail, 1.0 - tail)
    return u * spread, spread + u * bell * (1.0 / math.sqrt(2.0 * math.pi))


def norm_rows(values, gain, shift):
    center = values - jnp.mean(values, axis=-1, keepdims=True)
    rate = lax.rsqrt(jnp.mean(center * center, axis=-1, keepdims=True) + EPSILON)
    normal = center * rate
    return normal * gain + shift, normal, rate


def norm_pull(grad, normal, rate, gain):
    scaled = grad * gain
    return rate * (
        scaled
        - jnp.mean(scaled, axis=-1, keepdims=True)
        - normal * jnp.mean(scaled * normal, axis=-1, keepdims=True)
    )


def fixed(shape):
    return pl.BlockSpec(shape, lambda i: (0,) * len(shape), pipeline_mode=pl.Buffered(1))


def tiles(cols, first=0):
    return pl.BlockSpec((TILE, cols), lambda i: (i + first, 0))


def both_heads(values):
    first = lax.broadcasted_iota(jnp.int32, values.shape, 1) < HEAD_DIM
    zero = jnp.zeros_like(values)
    return jnp.concatenate([jnp.where(first, values, zero), jnp.where(first, zero, values)], axis=0)


def side_by_side(stacked):
    half = stacked.shape[0] // 2
    return jnp.concatenate([stacked[:half], stacked[half:]], axis=1)


def third(part, pair):
    start = part * D + pair * LANES
    return slice(start, start + LANES)


def attend_kernel(x_ref, wqkv_ref, vec_ref, packed_ref, att_ref, stat_ref):
    x = x_ref[...]
    for j in range(3):
        cols = slice(j * D, (j + 1) * D)
        part = dot_nn(x, wqkv_ref[:, cols])
        packed_ref[:, cols] = low(part if j == 1 else part + vec_ref[j // 2 : j // 2 + 1, :])
    lanes = lax.broadcasted_iota(jnp.int32, (SEG_LEN, LANES), 1)

    def segment(s, carry):
        rows = pl.ds(pl.multiple_of(s * SEG_LEN, SEG_LEN), SEG_LEN)
        stat = jnp.zeros((SEG_LEN, LANES), jnp.float32)
        for pair in range(PAIRS):
            q = packed_ref[rows, third(0, pair)] * jnp.bfloat16(HEAD_DIM**-0.5)
            k = packed_ref[rows, third(1, pair)]
            v = packed_ref[rows, third(2, pair)]
            scores = dot_nt(both_heads(q), k)
            largest = jnp.max(scores, axis=-1, keepdims=True)
            raised = jnp.exp(scores - largest)
            summed = jnp.sum(raised, axis=-1, keepdims=True)
            weights = low(raised * (1.0 / summed))
            att_ref[rows, pair * LANES : (pair + 1) * LANES] = low(
                dot_nn(side_by_side(weights), both_heads(v))
            )
            log_sum = largest + jnp.log(summed)
            stat = jnp.where(lanes == 2 * pair, log_sum[:SEG_LEN], stat)
            stat = jnp.where(lanes == 2 * pair + 1, log_sum[SEG_LEN:], stat)
        stat_ref[rows, :] = stat
        return carry

    lax.fori_loop(0, TILE // SEG_LEN, segment, 0)


def in_parts(kernel, micros, count, inputs, in_specs, outs, out_specs, scratch, previous, mib=60):
    previous = list(previous or ())
    return ordered(
        kernel,
        grid=(count,),
        in_specs=in_specs + [spec_any()] * len(previous),
        out_specs=out_specs,
        out_shape=outs,
        scratch_shapes=scratch,
        input_output_aliases={len(inputs) + i: i for i in range(len(previous))},
        compiler_params=kernel_params(mib),
        cost_estimate=cost(micros),
    )(*inputs, *previous)


def attend_layer(x, w_qkv, vecs, first, count, previous):
    def rows(cols):
        return tiles(cols, first)

    def kernel(x_ref, wqkv_ref, vec_ref, *refs):
        attend_kernel(x_ref, wqkv_ref, vec_ref, *refs[-3:])

    return in_parts(
        kernel,
        8 * count,
        count,
        [x, w_qkv, vecs],
        [rows(D), fixed((D, 3 * D)), fixed((VECTOR_ROWS, D))],
        [jax.ShapeDtypeStruct(v.shape, v.dtype) for v in previous],
        [rows(3 * D), rows(D), rows(LANES)],
        [],
        previous,
    )


def attend_first(x, weights, coords):
    n = x.shape[0]
    bf, f32 = jnp.bfloat16, jnp.float32
    count = len(weights.operands)

    def kernel(coords_ref, *refs):
        sources, x_ref, refs = refs[:count], refs[count], refs[count + 1 :]
        packed_ref, att_ref, stat_ref, wqkv_ref, vec_ref, staged, wide, sems = refs
        weights.start(coords_ref, sources, staged, sems)
        waited = set()
        for number in range(2):
            weights.wait(number, waited, staged, sems)
        weights.matrix(0, staged, wide, wqkv_ref)
        vec_ref[...] = jnp.zeros_like(vec_ref)
        weights.vectors(1, staged, wide, vec_ref, 0)
        attend_kernel(x_ref, wqkv_ref, vec_ref, packed_ref, att_ref, stat_ref)

    whole = [pl.BlockSpec(shape, lambda i: (0, 0)) for shape in ((D, 3 * D), (VECTOR_ROWS, D))]
    return ordered(
        kernel,
        grid=(1,),
        in_specs=[spec_smem()] + [spec_hbm()] * count + [tiles(D)],
        out_specs=[tiles(3 * D), tiles(D), tiles(LANES)] + whole,
        out_shape=[
            jax.ShapeDtypeStruct((n, 3 * D), bf),
            jax.ShapeDtypeStruct((n, D), bf),
            jax.ShapeDtypeStruct((n, LANES), f32),
            jax.ShapeDtypeStruct((D, 3 * D), bf),
            jax.ShapeDtypeStruct((VECTOR_ROWS, D), f32),
        ],
        scratch_shapes=weights.scratch,
        compiler_params=kernel_params(60),
        cost_estimate=cost(12),
    )(coords, *weights.operands, x)


FBLOCK = D


def feed_kernel(
    x_ref, att_ref, wout_ref, wup_ref, wdown_ref, vec_ref,
    h1low_ref, norm1_ref, g_ref, dg_ref, norm2_ref, rate_ref, h2_ref, cls_ref, res_ref, h1_ref,
):
    step = pl.program_id(0)
    segs = TILE // SEG_LEN
    lanes = lax.broadcasted_iota(jnp.int32, (SEG_LEN, LANES), 1)
    res_ref[...] = dot_nn(att_ref[...], wout_ref[...])

    def start(s, carry):
        rows = pl.ds(pl.multiple_of(s * SEG_LEN, SEG_LEN), SEG_LEN)
        resid = x_ref[rows, :].astype(jnp.float32) + res_ref[rows, :] + vec_ref[2:3, :]
        hidden, normal, rate = norm_rows(resid, vec_ref[3:4, :], vec_ref[4:5, :])
        h1_ref[rows, :] = hidden
        h1low_ref[rows, :] = low(hidden)
        norm1_ref[rows, :] = low(normal)
        rate_ref[rows, :] = jnp.broadcast_to(rate, (SEG_LEN, LANES))
        return carry

    lax.fori_loop(0, segs, start, 0)
    h = h1low_ref[...]
    for j in range(FF // FBLOCK):
        cols = slice(j * FBLOCK, (j + 1) * FBLOCK)
        act, slope = gelu_pair(dot_nn(h, wup_ref[:, cols]) + vec_ref[5 + j : 6 + j, :])
        g = low(act)
        g_ref[:, cols] = g
        dg_ref[:, cols] = low(slope)
        part = dot_nn(g, wdown_ref[cols, :])
        if j == 0:
            res_ref[...] = part
        else:
            res_ref[...] += part

    def finish(s, carry):
        rows = pl.ds(pl.multiple_of(s * SEG_LEN, SEG_LEN), SEG_LEN)
        resid = h1_ref[rows, :] + res_ref[rows, :] + vec_ref[9:10, :]
        hidden, normal, rate = norm_rows(resid, vec_ref[10:11, :], vec_ref[11:12, :])
        h2_ref[rows, :] = low(hidden)
        norm2_ref[rows, :] = low(normal)
        rate_ref[rows, :] = jnp.where(lanes == 0, rate_ref[rows, :], rate)
        cls_ref[pl.ds(step * segs + s, 1), :] = hidden[0:1, :]
        return carry

    lax.fori_loop(0, segs, finish, 0)


def feed_layer(x, att, weights, coords):
    n = x.shape[0]
    bf, f32 = jnp.bfloat16, jnp.float32
    count = len(weights.operands)
    steps = n // TILE
    shapes = [item.shape for item in weights.items if item.cols]

    def kernel(coords_ref, *refs):
        sources, refs = refs[:count], refs[count:]
        x_ref, att_ref = refs[:2]
        outs, kept = refs[2:10], refs[10:13]
        vec_ref, res_ref, h1_ref, out_sems = refs[13:17]
        held, (staged, wide, sems) = refs[17:20], refs[20:]
        step = pl.program_id(0)

        @pl.when(step == 0)
        def _():
            weights.start(coords_ref, sources, staged, sems)
            waited = set()
            vec_ref[...] = jnp.zeros_like(vec_ref)
            place = row = 0
            for number, item in enumerate(weights.items):
                weights.wait(number, waited, staged, sems)
                if item.cols:
                    weights.matrix(number, staged, wide, held[place])
                    pltpu.make_async_copy(held[place], kept[place], out_sems.at[place]).start()
                    place += 1
                else:
                    weights.vectors(number, staged, wide, vec_ref, row)
                    row += item.rows * LANES // D

        feed_kernel(x_ref, att_ref, *held, vec_ref, *outs, res_ref, h1_ref)

        @pl.when(step == steps - 1)
        def _():
            for place in range(3):
                pltpu.make_async_copy(held[place], kept[place], out_sems.at[place]).wait()

    return ordered(
        kernel,
        grid=(steps,),
        in_specs=[spec_smem()] + [spec_hbm()] * count + [tiles(D), tiles(D)],
        out_specs=[tiles(D), tiles(D), tiles(FF), tiles(FF), tiles(D), tiles(LANES), tiles(D)]
        + [pl.BlockSpec((n // SEG_LEN, D), lambda i: (0, 0))]
        + [spec_any()] * 3
        + [pl.BlockSpec((VECTOR_ROWS, D), lambda i: (0, 0))],
        out_shape=[
            jax.ShapeDtypeStruct((n, cols), kind)
            for cols, kind in ((D, bf), (D, bf), (FF, bf), (FF, bf), (D, bf), (LANES, f32), (D, bf))
        ]
        + [jax.ShapeDtypeStruct((n // SEG_LEN, D), f32)]
        + [jax.ShapeDtypeStruct(shape, bf) for shape in shapes]
        + [jax.ShapeDtypeStruct((VECTOR_ROWS, D), f32)],
        scratch_shapes=[
            pltpu.VMEM((TILE, D), f32),
            pltpu.VMEM((TILE, D), f32),
            pltpu.SemaphoreType.DMA((3,)),
        ]
        + [pltpu.VMEM(shape, bf) for shape in shapes]
        + weights.scratch,
        compiler_params=kernel_params(62),
        cost_estimate=cost(60),
    )(coords, *weights.operands, x, att)


def feed_back_kernel(
    cot_ref, cls_ref, norm2_ref, dg_ref, norm1_ref, rate_ref,
    wdown_ref, wup_ref, wout_ref, vec_ref,
    dm_ref, du_ref, dao_ref, da_ref, one_ref, sums_ref, res_ref,
):
    step = pl.program_id(0)

    @pl.when(step == 0)
    def _():
        sums_ref[...] = jnp.zeros_like(sums_ref)

    segs = TILE // SEG_LEN
    row_ids = lax.broadcasted_iota(jnp.int32, (SEG_LEN, D), 0)

    def add_sum(row, values):
        sums_ref[row : row + 1, :] += jnp.sum(values, axis=0, keepdims=True)

    def start(s, carry):
        rows = pl.ds(pl.multiple_of(s * SEG_LEN, SEG_LEN), SEG_LEN)
        cls = cls_ref[pl.ds(step * segs + s, 1), :]
        grad = jnp.where(row_ids == 0, cls, cot_ref[rows, :].astype(jnp.float32))
        normal = norm2_ref[rows, :].astype(jnp.float32)
        add_sum(10, grad * normal)
        add_sum(11, grad)
        two = norm_pull(grad, normal, rate_ref[rows, 1:2], vec_ref[10:11, :])
        res_ref[rows, :] = two
        dm = low(two)
        dm_ref[rows, :] = dm
        add_sum(9, dm.astype(jnp.float32))
        return carry

    lax.fori_loop(0, segs, start, 0)
    dm = dm_ref[...]
    for j in range(FF // FBLOCK):
        cols = slice(j * FBLOCK, (j + 1) * FBLOCK)
        du = low(dot_nt(dm, wdown_ref[cols, :]) * dg_ref[:, cols].astype(jnp.float32))
        du_ref[:, cols] = du
        add_sum(5 + j, du.astype(jnp.float32))
        res_ref[...] += dot_nt(du, wup_ref[:, cols])

    def finish(s, carry):
        rows = pl.ds(pl.multiple_of(s * SEG_LEN, SEG_LEN), SEG_LEN)
        grad = res_ref[rows, :]
        normal = norm1_ref[rows, :].astype(jnp.float32)
        add_sum(3, grad * normal)
        add_sum(4, grad)
        one = norm_pull(grad, normal, rate_ref[rows, 0:1], vec_ref[3:4, :])
        one_ref[rows, :] = one
        dao = low(one)
        dao_ref[rows, :] = dao
        add_sum(2, dao.astype(jnp.float32))
        return carry

    lax.fori_loop(0, segs, finish, 0)
    da_ref[...] = low(dot_nt(dao_ref[...], wout_ref[...]))


def feed_back(cot, cls, norm2, dg, norm1, rates, w_down, w_up, w_out, vecs):
    n = cot.shape[0]
    bf, f32 = jnp.bfloat16, jnp.float32
    return ordered(
        feed_back_kernel,
        grid=(n // TILE,),
        in_specs=[
            tiles(D), fixed((n // SEG_LEN, D)), tiles(D), tiles(FF), tiles(D), tiles(LANES),
            fixed((FF, D)), fixed((D, FF)), fixed((D, D)), fixed((VECTOR_ROWS, D)),
        ],
        out_specs=[
            tiles(D), tiles(FF), tiles(D), tiles(D), tiles(D),
            pl.BlockSpec((VECTOR_ROWS, D), lambda i: (0, 0)),
        ],
        out_shape=[
            jax.ShapeDtypeStruct((n, D), bf),
            jax.ShapeDtypeStruct((n, FF), bf),
            jax.ShapeDtypeStruct((n, D), bf),
            jax.ShapeDtypeStruct((n, D), bf),
            jax.ShapeDtypeStruct((n, D), f32),
            jax.ShapeDtypeStruct((VECTOR_ROWS, D), f32),
        ],
        scratch_shapes=[pltpu.VMEM((TILE, D), f32)],
        compiler_params=kernel_params(60),
        cost_estimate=cost(44),
    )(cot, cls, norm2, dg, norm1, rates, w_down, w_up, w_out, vecs)


def attend_back_kernel(packed_ref, stat_ref, da_ref, before_ref, *refs):
    dqkv_ref, sums_ref = refs[-2:]

    @pl.when(pl.program_id(0) == 0)
    def _():
        sums_ref[...] = before_ref[...]

    lanes = lax.broadcasted_iota(jnp.int32, (SEG_LEN, LANES), 1)
    scale = HEAD_DIM**-0.5

    def segment(s, carry):
        rows = pl.ds(pl.multiple_of(s * SEG_LEN, SEG_LEN), SEG_LEN)
        stat = stat_ref[rows, :]
        for pair in range(PAIRS):
            q = packed_ref[rows, third(0, pair)] * jnp.bfloat16(scale)
            k = packed_ref[rows, third(1, pair)]
            v = packed_ref[rows, third(2, pair)]
            da = da_ref[rows, pair * LANES : (pair + 1) * LANES]
            queries, grads = both_heads(q), both_heads(da)
            log_sum = jnp.concatenate([stat[:, 2 * pair : 2 * pair + 1], stat[:, 2 * pair + 1 : 2 * pair + 2]], axis=0)
            weights = jnp.exp(dot_nt(queries, k) - log_sum)
            grad_weights = dot_nt(grads, v)
            dv = dot_tn(low(weights), grads)
            inner = jnp.sum(grad_weights * weights, axis=-1, keepdims=True)
            ds = low(weights * (grad_weights - inner))
            dq = dot_nn(side_by_side(ds), both_heads(k)) * scale
            dk = dot_tn(ds, queries)
            for part, grad in enumerate((dq, dk, dv)):
                grad = low(grad)
                cols = third(part, pair)
                dqkv_ref[rows, cols] = grad
                if part != 1:
                    here = (slice(part // 2, part // 2 + 1), third(0, pair))
                    sums_ref[here] += jnp.sum(grad.astype(jnp.float32), axis=0, keepdims=True)
        return carry

    lax.fori_loop(0, TILE // SEG_LEN, segment, 0)


def attend_back(packed, stat, da, first, count, previous=None):
    n = packed.shape[0]
    before = previous[1] if previous else jnp.zeros((8, D), jnp.float32)
    return in_parts(
        attend_back_kernel,
        10 * count,
        count,
        [packed, stat, da, before],
        [tiles(3 * D, first), tiles(LANES, first), tiles(D, first), fixed((8, D))],
        [jax.ShapeDtypeStruct((n, 3 * D), jnp.bfloat16), jax.ShapeDtypeStruct((8, D), jnp.float32)],
        [tiles(3 * D, first), pl.BlockSpec((8, D), lambda i: (0, 0))],
        [],
        previous and previous[:1],
    )


def cross_kernel(
    load, rows_ref, tagc_ref, tagr_ref, gz_ref, wqkv_ref, wout_ref, wup_ref, wdown_ref, vec_ref,
    out_ref, grows_ref, sums_ref, gqkv_ref, go_ref, gu_ref, gm_ref, rowst_ref, attt_ref, hidt_ref, actt_ref,
    packed_ref, weights_ref, att_ref, act_ref, slope_ref, res_ref,
):
    scale = HEAD_DIM**-0.5
    rows = rows_ref[...]
    rowst_ref[...] = rows.T
    same = tagc_ref[:, 0:1] == tagr_ref[0:1, :]
    same = jnp.concatenate([same, same], axis=0)

    def add_sum(row, values):
        sums_ref[row : row + 1, :] = jnp.sum(values.astype(jnp.float32), axis=0, keepdims=True)

    def pair_cols(pair):
        return slice(pair * LANES, (pair + 1) * LANES)

    sums_ref[...] = jnp.zeros_like(sums_ref)
    load(0)
    for j in range(3):
        cols = slice(j * D, (j + 1) * D)
        part = dot_nn(rows, wqkv_ref[:, cols])
        packed_ref[:, cols] = low(part if j == 1 else part + vec_ref[j // 2 : j // 2 + 1, :])
    for pair in range(PAIRS):
        q = packed_ref[:, third(0, pair)] * jnp.bfloat16(scale)
        scores = jnp.where(same, dot_nt(both_heads(q), packed_ref[:, third(1, pair)]), NEGATIVE)
        raised = jnp.exp(scores - jnp.max(scores, axis=-1, keepdims=True))
        weights = raised * (1.0 / jnp.sum(raised, axis=-1, keepdims=True))
        weights_ref[pair] = weights
        blend = dot_nn(side_by_side(low(weights)), both_heads(packed_ref[:, third(2, pair)]))
        att_ref[:, pair_cols(pair)] = low(blend)
    att = att_ref[...]
    attt_ref[...] = att.T
    load(1)
    resid = rows.astype(jnp.float32) + dot_nn(att, wout_ref[...]) + vec_ref[2:3, :]
    hidden, normal_three, rate_three = norm_rows(resid, vec_ref[3:4, :], vec_ref[4:5, :])
    hidden_low = low(hidden)
    hidt_ref[...] = hidden_low.T
    load(2)
    res_ref[...] = hidden + vec_ref[9:10, :]
    for j in range(FF // FBLOCK):
        cols = slice(j * FBLOCK, (j + 1) * FBLOCK)
        act, slope = gelu_pair(dot_nn(hidden_low, wup_ref[:, cols]) + vec_ref[5 + j : 6 + j, :])
        act = low(act)
        actt_ref[cols, :] = act.T
        slope_ref[:, cols] = slope
        res_ref[...] += dot_nn(act, wdown_ref[cols, :])
    crossed, normal_four, rate_four = norm_rows(res_ref[...], vec_ref[10:11, :], vec_ref[11:12, :])
    out_ref[...] = low(crossed)

    grad_z = gz_ref[...].astype(jnp.float32)
    add_sum(10, grad_z * normal_four)
    add_sum(11, grad_z)
    grad_four = norm_pull(grad_z, normal_four, rate_four, vec_ref[10:11, :])
    grad_m = low(grad_four)
    gm_ref[...] = grad_m
    add_sum(9, grad_m)
    res_ref[...] = grad_four
    for j in range(FF // FBLOCK):
        cols = slice(j * FBLOCK, (j + 1) * FBLOCK)
        grad_u = low(dot_nt(grad_m, wdown_ref[cols, :]) * slope_ref[:, cols])
        gu_ref[:, cols] = grad_u
        add_sum(5 + j, grad_u)
        res_ref[...] += dot_nt(grad_u, wup_ref[:, cols])
    grad_h = res_ref[...]
    add_sum(3, grad_h * normal_three)
    add_sum(4, grad_h)
    grad_three = norm_pull(grad_h, normal_three, rate_three, vec_ref[3:4, :])
    grad_o = low(grad_three)
    go_ref[...] = grad_o
    add_sum(2, grad_o)
    res_ref[...] = grad_three
    att_ref[...] = low(dot_nt(grad_o, wout_ref[...]))
    for pair in range(PAIRS):
        queries = both_heads(packed_ref[:, third(0, pair)] * jnp.bfloat16(scale))
        grads = both_heads(att_ref[:, pair_cols(pair)])
        weights = weights_ref[pair]
        grad_weights = dot_nt(grads, packed_ref[:, third(2, pair)])
        dv = dot_tn(low(weights), grads)
        inner = jnp.sum(grad_weights * weights, axis=-1, keepdims=True)
        ds = low(weights * (grad_weights - inner))
        dq = dot_nn(side_by_side(ds), both_heads(packed_ref[:, third(1, pair)])) * scale
        dk = dot_tn(ds, queries)
        for part, grad in enumerate((dq, dk, dv)):
            gqkv_ref[:, third(part, pair)] = low(grad)
    add_sum(0, gqkv_ref[:, :D])
    add_sum(1, gqkv_ref[:, 2 * D :])
    for j in range(3):
        cols = slice(j * D, (j + 1) * D)
        res_ref[...] += dot_nt(gqkv_ref[:, cols], wqkv_ref[:, cols])
    grows_ref[...] = low(res_ref[...])


def cross_layer(cls, places, tags, grad_out, weights, coords, pack, seg):
    m = cls.shape[0]
    bf, f32 = jnp.bfloat16, jnp.float32
    tagc = jnp.broadcast_to(tags.astype(f32)[:, None], (m, LANES))
    tagr = jnp.broadcast_to(tags.astype(f32)[None, :], (8, m))
    placer = jnp.broadcast_to(places.astype(f32)[None, :], (8, m))
    count = len(weights.operands)
    operands = [cls, tagc, tagr, grad_out, placer]
    shapes = [
        (VECTOR_ROWS, D), (m, 3 * D), (m, D), (m, FF), (m, D), (D, m), (D, m), (D, m), (FF, m),
    ]
    matrices = [number for number, item in enumerate(weights.items) if item.cols]
    vectors = [number for number, item in enumerate(weights.items) if not item.cols]
    needs = [(matrices[:1], vectors[:1]), (matrices[1:2], vectors[1:2]), (matrices[2:], vectors[2:])]
    rows_of = {number: row for number, row in zip(vectors, (0, 2, 5, 9))}
    inner = [
        pltpu.VMEM((m, 3 * D), bf),
        pltpu.VMEM((PAIRS, 2 * m, m), f32),
        pltpu.VMEM((m, D), bf),
        pltpu.VMEM((m, D), bf),
        pltpu.VMEM((m, FF), f32),
        pltpu.VMEM((m, D), f32),
    ]
    held_shapes = [pltpu.VMEM(weights.items[number].shape, bf) for number in matrices]

    def kernel(seg_ref, coords_ref, *refs):
        refs = list(refs)

        def take(n):
            taken, refs[:] = refs[:n], refs[n:]
            return taken

        sources, ins, outs = take(count), take(len(operands)), take(3)
        kept, scratch, held = take(len(shapes)), take(len(inner)), take(len(matrices))
        (vec_ref, hot_ref), (staged, wide, sems), packing = take(2), take(3), take(3)
        waited = set()
        weights.start(coords_ref, sources, staged, sems)

        def load(stage):
            for number in needs[stage][0]:
                weights.wait(number, waited, staged, sems)
                weights.matrix(number, staged, wide, held[matrices.index(number)])
            for number in needs[stage][1]:
                weights.wait(number, waited, staged, sems)
                weights.vectors(number, staged, wide, vec_ref, rows_of[number])

        vec_ref[...] = jnp.zeros_like(vec_ref)
        cross_kernel(load, *ins[:4], *held, vec_ref, *outs[:2], *kept, *scratch)
        places_at = lax.broadcasted_iota(jnp.int32, (LONG_SEGS, m), 0).astype(f32)
        hot_ref[...] = jnp.where(places_at == ins[4][0:1, :], 1.0, 0.0).astype(bf)
        sums_ref, gqkv, go, gu, gm, rows_t, att_t, hid_t, act_t = kept
        names = [item_name(i) for i in (8, 9, 11, 13, 15)]
        pack.run(
            seg_ref[0],
            dict(zip(names, (hot_ref, rows_t, att_t, hid_t, act_t))),
            dict(zip(names, (outs[1], gqkv, go, gu, gm))),
            sums_ref,
            {item_name(i): row for i, row in ((10, 0), (12, 2), (14, 5), (16, 9))},
            outs[2],
            *packing,
        )

    return ordered(
        kernel,
        out_shape=[jax.ShapeDtypeStruct((m, D), bf)] * 2 + [pack.out],
        in_specs=[spec_smem()] * 2 + [spec_hbm()] * count + [spec_vmem()] * len(operands),
        out_specs=[spec_vmem()] * 3,
        scratch_shapes=[pltpu.VMEM(shape, f32 if i == 0 else bf) for i, shape in enumerate(shapes)]
        + inner
        + held_shapes
        + [pltpu.VMEM((VECTOR_ROWS, D), f32), pltpu.VMEM((LONG_SEGS, m), bf)]
        + weights.scratch
        + pack.scratch,
        compiler_params=kernel_params(62),
        cost_estimate=cost(30),
    )(seg, coords, *weights.operands, *operands)


def class_rows(cls, cot, hot, doc, pos, weights, coords):
    count = len(weights.operands)
    segs = cls.shape[0]

    def kernel(coords_ref, *refs):
        sources, (cls_ref, cot_ref, hot_ref, doc_ref, pos_ref, out_ref, wide_out, table, staged, wide, sems) = (
            refs[:count],
            refs[count:],
        )
        weights.start(coords_ref, sources, staged, sems)
        lanes = lax.broadcasted_iota(jnp.int32, (1, LANES), 1)
        for s in range(segs):
            wide_out[s : s + 1, D : 2 * D] = cot_ref[s, 0:1, :].astype(jnp.float32)
            tag = jnp.where(lanes == 0, doc_ref[s], jnp.where(lanes == 1, pos_ref[s], 0))
            wide_out[s : s + 1, 2 * D :] = tag.astype(jnp.float32)
        weights.wait(0, set(), staged, sems)
        weights.matrix(0, staged, wide, table)
        wide_out[:, :D] = cls_ref[...] + dot_nn(hot_ref[...], table[...])
        out_ref[...] = low(wide_out[...])

    def whole(shape):
        return pl.BlockSpec(shape, lambda i: (0,) * len(shape))

    return ordered(
        kernel,
        grid=(1,),
        out_shape=jax.ShapeDtypeStruct((segs, 2 * D + LANES), jnp.bfloat16),
        in_specs=[spec_smem()] + [spec_hbm()] * count
        + [whole(cls.shape), whole((segs, BLK, D)), whole(hot.shape), spec_smem(), spec_smem()],
        out_specs=whole((segs, 2 * D + LANES)),
        scratch_shapes=[
            pltpu.VMEM((segs, 2 * D + LANES), jnp.float32),
            pltpu.VMEM((LONG_SEGS, D), jnp.bfloat16),
        ]
        + weights.scratch,
        compiler_params=kernel_params(60),
        cost_estimate=cost(3),
    )(coords, *weights.operands, cls, cot, hot, doc, pos)


def token_back(grad_one, dqkv, w_qkv, first, count, previous=None):
    n = grad_one.shape[0]

    def kernel(one_ref, dqkv_ref, wqkv_ref, *refs):
        total = one_ref[...]
        for j in range(3):
            cols = slice(j * D, (j + 1) * D)
            total = total + dot_nt(dqkv_ref[:, cols], wqkv_ref[:, cols])
        refs[-1][...] = low(total)

    return in_parts(
        kernel,
        3 * count,
        count,
        [grad_one, dqkv, w_qkv],
        [tiles(D, first), tiles(3 * D, first), fixed((D, 3 * D))],
        [jax.ShapeDtypeStruct((n, D), jnp.bfloat16)],
        [tiles(D, first)],
        [],
        previous,
    )
AXES = ("seg", "doc")


def send(geo, value, axis, step):
    return lax.ppermute(value, AXES, geo.shift(axis, step))


def along_z(geo, value):
    return [value] + [send(geo, value, Z, r) for r in range(1, geo.n_doc)]


STEPS = 4


def slab(place, rows):
    return pl.BlockSpec((pl.squeezed, rows, LANES), lambda i: (place, i, 0))


def flat_call(kernel, inputs, outs, micros=2):
    arrays, specs = [], []
    for value, places in inputs:
        rows = value.size // LANES // places
        for place in range(places):
            arrays.append(value.reshape(places, rows, LANES))
            specs.append(slab(place, rows // STEPS))
    shapes, out_specs = [], []
    for shape, places in outs:
        rows = math.prod(shape) // LANES // max(places, 1)
        shapes.append(jax.ShapeDtypeStruct((max(places, 1), rows, LANES), jnp.bfloat16))
        out_specs.append(pl.BlockSpec((max(places, 1), rows // STEPS, LANES), lambda i: (0, i, 0)))
    results = ordered(
        kernel,
        grid=(STEPS,),
        out_shape=shapes,
        in_specs=specs,
        out_specs=out_specs,
        compiler_params=kernel_params(24),
        cost_estimate=cost(micros),
    )(*arrays)
    return [value.reshape(shape) for value, (shape, _) in zip(results, outs)]


def gather_plane(geo, halves, step):
    orders = ((X, Y), (Y, X))
    inputs, outs = [], []
    for half, order in zip(halves, orders):
        came = [send(geo, half, order[step], r) for r in range(1, geo.size(order[step]))]
        inputs += [(value, 1) for value in [half] + came]
        outs.append(((1 + len(came),) + half.shape, 1 + len(came)))

    def kernel(*refs):
        sources, targets = refs[: len(inputs)], refs[len(inputs) :]
        for target, (_, places) in zip(targets, outs):
            for place in range(places):
                target[place] = sources[place][...]
            sources = sources[places:]

    return flat_call(kernel, inputs, outs)


def gather_cores(geo, halves):
    return [array for half in halves for array in (half, send(geo, half, C, 1))]


def reduce_cores(geo, arrays):
    return [[arrays[2 * half], send(geo, arrays[2 * half + 1], C, 1)] for half in range(2)]


def added(sources):
    return low(sum(source[...].astype(jnp.float32) for source in sources))


def reduce_plane(geo, groups, step):
    orders = ((Y, X), (X, Y))
    inputs, outs, jobs = [], [], []
    for halves, step in zip(groups, step):
        for half, order in zip(halves, orders):
            places = geo.size(order[step])
            inputs += [(value, places) for value in half]
            outs += [(half[0].shape[1:], 0)] * places
            jobs.append((len(half), places, order[step]))

    def kernel(*refs):
        count = sum(places for _, places in inputs)
        sources, targets = refs[:count], refs[count:]
        for terms, places, _ in jobs:
            for place in range(places):
                targets[place][0] = added(sources[place : terms * places : places])
            sources, targets = sources[terms * places :], targets[places:]

    results = flat_call(kernel, inputs, outs)
    reduced = []
    for _, places, axis in jobs:
        mine, results = results[:places], results[places:]
        reduced.append([mine[0]] + [send(geo, mine[r], axis, r) for r in range(1, places)])
    return [reduced[2 * i : 2 * i + 2] for i in range(len(groups))]


def reduce_line(geo, halves, my_z):
    nd = geo.n_doc
    inputs = [value for half in halves for value in half]
    count = inputs[0].shape[0] // nd
    rows = [half[0].shape[1] for half in halves]

    def kernel(z_ref, *refs):
        sources, targets = refs[: len(inputs)], refs[len(inputs) :]
        done = 0
        for half, n in zip(halves, rows):
            terms, sources = sources[: len(half)], sources[len(half) :]
            for r in range(nd):
                z = wrap(z_ref[0] + r, nd)
                for s in range(count):
                    total = sum(term[s * nd + z].astype(jnp.float32) for term in terms)
                    targets[r][s, done : done + n] = low(total)
            done += n

    outs = ordered(
        kernel,
        out_shape=[jax.ShapeDtypeStruct((count, geo.share, LANES), jnp.bfloat16)] * nd,
        in_specs=[spec_smem()] + [spec_vmem()] * len(inputs),
        out_specs=[spec_vmem()] * nd,
        compiler_params=kernel_params(24),
        cost_estimate=cost(2),
    )(my_z.reshape(1), *inputs)
    return [outs[0]] + [send(geo, outs[r], Z, r) for r in range(1, nd)]


def sum_line(geo, line):
    def kernel(*refs):
        refs[-1][0] = added(refs[:-1])

    return flat_call(kernel, [(part, 1) for part in line], [(line[0].shape, 0)])[0]


def sum_all(geo, line, *others):
    count = line[0].shape[0]

    def kernel(*refs):
        sources, target = refs[:-1], refs[-1]
        target[:count] = added(sources[: len(line)])
        row = count
        for source in sources[len(line) :]:
            target[row : row + source.shape[0]] = source[...]
            row += source.shape[0]

    return ordered(
        kernel,
        out_shape=jax.ShapeDtypeStruct((geo.n_seg, geo.share, LANES), jnp.bfloat16),
        in_specs=[spec_vmem()] * (len(line) + len(others)),
        out_specs=spec_vmem(),
        compiler_params=kernel_params(),
        cost_estimate=cost(2),
    )(*line, *others)


def gate(value):
    def kernel(source, target):
        target[0] = source[...]

    return flat_call(kernel, [(value, 1)], [(value.shape, 0)])[0]
def row_rates(geo, n_tokens, n_cls):
    runs = []
    cross = list(LAYOUT)[-13:]
    row = 0
    for name, shape in LAYOUT.items():
        scale = 1.0 / math.sqrt(n_cls if name in cross else n_tokens)
        rate = 0.2
        if len(shape) == 2:
            rate = 1.0 if name == cross[0] else 0.5 / math.sqrt(shape[0])
        runs.append((row, scale, rate))
        row += math.prod(shape) // LANES
    runs.append((row, 0.0, 0.2))
    begins = [run[0] for run in runs] + [geo.chunk * geo.n_dev]
    found = []
    for n in range(geo.n_dev):
        lo, hi = n * geo.chunk, (n + 1) * geo.chunk
        found.append(
            [(max(run[0] - lo, 0), *run[1:]) for run, end in zip(runs, begins[1:]) if run[0] < hi and end > lo]
        )
    most = max(len(rows) for rows in found)
    found = [rows + [(geo.chunk, 0.0, 0.0)] * (most - len(rows)) for rows in found]
    return np.asarray(found, np.float32).transpose(0, 2, 1).copy()


def matmul(left, right):
    return jnp.dot(left, right, preferred_element_type=jnp.float32)


def column_sum(rows):
    return jnp.sum(rows.astype(jnp.float32), axis=0, keepdims=True)


def local(tokens, cotangent, seg_doc, seg_pos, master, momentum, average):
    n_seg = lax.axis_size(AXES[0])
    n_doc = lax.axis_size(AXES[1])
    geo = Geometry(n_seg, n_doc, master.shape[0])
    by = geo.by_name
    gather = Buckets(geo, [4, 4, 1], by.w_out, by.pos_table)
    buckets = Buckets(geo, [4, 4, 4, 1], by.w_out, by.w_down, by.pos_table)
    my_seg, my_doc = lax.axis_index(AXES[0]), lax.axis_index(AXES[1])
    me = my_seg * n_doc + my_doc
    coords = jnp.stack([my_seg // 4, my_seg // 2 % 2, my_seg % 2, my_doc]).astype(jnp.int32)
    table = lax.dynamic_index_in_dim(jnp.asarray(geo.block_tables()[1]), me, 0, False)
    pad_rows = ceil_to(geo.chunk + 4 * BLK, 8)
    ORDER.start()
    aligned = align_rows(geo, table, master.reshape(geo.chunk, LANES), pad_rows)
    shares = lax.all_to_all(aligned.reshape(geo.n_seg, geo.share, LANES), AXES[0], 0, 0, tiled=True)
    parts = [shares[span.start // n_doc : span.stop // n_doc] for span in gather.ranges]

    seg_count = tokens.shape[1]
    n_rows = n_seg * seg_count
    tiles_all = seg_count * SEG_LEN // TILE
    middle = max(1, tiles_all - 2)
    last = tiles_all - 1 - middle
    inputs = tokens[0].reshape(seg_count * SEG_LEN, D)
    cot_rows = cotangent[0]

    line = place_line(geo, along_z(geo, parts[0]), my_doc)
    parts_b = along_z(geo, parts[1])
    ORDER.wait_for(*parts_b[1:2])
    plane = gather_plane(geo, line, 0)
    ORDER.wait_for(*parts_b[2:3])
    plane = gather_plane(geo, plane, 1)
    gathered = [gather_cores(geo, plane), None, None]
    plane_b = place_line(geo, parts_b, my_doc)

    def weights(*numbers):
        return Weights(geo, gather, gathered, [item_name(i) for i in numbers])

    def own(values):
        return lax.dynamic_slice_in_dim(values, my_seg * seg_count, seg_count, axis=0)

    *outs, w_qkv, vec_a = attend_first(inputs, weights(0, 1), coords)
    plane_b = gather_plane(geo, plane_b, 0)
    gathered[2] = [lax.all_gather(gate(parts[2]), AXES)]
    outs = attend_layer(inputs, w_qkv, vec_a, 1, middle, outs)
    plane_b = gather_plane(geo, plane_b, 1)
    gathered[1] = gather_cores(geo, plane_b)
    if last:
        outs = attend_layer(inputs, w_qkv, vec_a, 1 + middle, last, outs)
    packed, attended, stat = outs
    hidden_low, normal_one, active, slope, normal_two, rates, hidden_two, cls, w_out, w_up, w_down, vec = feed_layer(
        inputs, attended, weights(1, 2, 3, 4, 5, 6, 7), coords
    )

    hot = (seg_pos[0][:, None] == jnp.arange(LONG_SEGS)[None, :]).astype(jnp.bfloat16)
    mine = class_rows(cls, cot_rows, hot, seg_doc[0], seg_pos[0], weights(8), coords)
    tagged = lax.all_gather(mine, AXES[0], axis=0, tiled=True)
    rows, all_grad, all_doc, all_pos = tagged[:, :D], tagged[:, D : 2 * D], tagged[:, 2 * D], tagged[:, 2 * D + 1]
    crossed, grad_rows, line_c = cross_layer(
        rows, all_pos, all_doc, all_grad, weights(9, 10, 11, 12, 13, 14, 15, 16), coords,
        CrossPack(geo, buckets.ranges[3], n_rows), my_seg.astype(jnp.int32).reshape(1),
    )
    line_c = reduce_line(geo, [[line_c]], my_doc)

    grads = {}
    dm, du, dao, da, grad_one, sums = feed_back(
        cot_rows.reshape(-1, D), own(grad_rows).astype(jnp.float32), normal_two, slope, normal_one, rates,
        w_down, w_up, w_out, vec,
    )
    sums_c = sum_line(geo, line_c)
    grads[item_name(8)] = low(matmul(hot.T, own(grad_rows)))
    for number, row in ((3, 2), (5, 5), (7, 9)):
        grads[item_name(number)] = (sums, row)
    *arrays_d, grads[item_name(6)] = grad_bucket(
        geo, buckets, 2, grads, coords, item_name(6), active, dm, 512, keep=True
    )
    halves_d = reduce_cores(geo, arrays_d)
    grads[item_name(2)] = low(matmul(attended.T, dao))
    ORDER.wait_for(grads[item_name(2)])
    halves_d, = reduce_plane(geo, [halves_d], [0])
    arrays_b = grad_bucket(geo, buckets, 1, grads, coords, item_name(4), hidden_low, du, 256)
    halves_b = reduce_cores(geo, arrays_b)
    back = attend_back(packed, stat, da, 0, 1)
    halves_d, halves_b = reduce_plane(geo, [halves_d, halves_b], [1, 0])
    if tiles_all > 1:
        back = attend_back(packed, stat, da, 1, middle, back)
    line_d = reduce_line(geo, halves_d, my_doc)
    halves_b, = reduce_plane(geo, [halves_b], [1])
    if last:
        back = attend_back(packed, stat, da, 1 + middle, last, back)
    dqkv, qv_sums = back
    sums_d = sum_line(geo, line_d)
    line_b = reduce_line(geo, halves_b, my_doc)
    grads[item_name(1)] = (qv_sums, 0)
    arrays_a = grad_bucket(geo, buckets, 0, grads, coords, item_name(0), inputs, dqkv, 256)
    halves_a = reduce_cores(geo, arrays_a)
    halves_a, = reduce_plane(geo, [halves_a], [0])
    token_grad, = token_back(grad_one, dqkv, w_qkv, 0, tiles_all)
    sums_b = sum_line(geo, line_b)
    halves_a, = reduce_plane(geo, [halves_a], [1])
    first_row = lax.broadcasted_iota(jnp.int32, (seg_count, SEG_LEN, D), 1) == 0
    mixed_out = jnp.where(
        first_row, own(crossed)[:, None, :], hidden_two.reshape(seg_count, SEG_LEN, D)
    )
    line_a = reduce_line(geo, halves_a, my_doc)
    owned = lax.all_to_all(
        sum_all(geo, line_a, sums_b, sums_d, sums_c), AXES[0], 0, 0, tiled=True
    )
    n_cls = n_doc * n_rows
    rates = lax.dynamic_index_in_dim(jnp.asarray(row_rates(geo, n_cls * SEG_LEN, n_cls)), me, 0, False)
    begins, factors = rates[0].astype(jnp.int32), rates[1:].reshape(-1)
    state = [value.reshape(geo.chunk, LANES) for value in (master, momentum, average)]
    weight, moment, smooth, copy_low = (
        value.reshape(-1)
        for value in update_rows(geo, table, owned.reshape(-1, LANES), begins, factors, state, pad_rows)
    )
    return (
        mixed_out[None],
        token_grad.reshape(1, seg_count, SEG_LEN, D),
        weight,
        moment,
        smooth,
        copy_low,
    )


def item_name(number):
    return item_list(0)[number].name


def solution(mesh):
    layer = P(AXES[1], AXES[0], None, None)
    ids = P(AXES[1], AXES[0])
    flat = P(AXES)
    return jax.shard_map(
        local,
        mesh=mesh,
        in_specs=(layer, layer, ids, ids, flat, flat, flat),
        out_specs=(layer, layer, flat, flat, flat, flat),
        check_vma=False,
    )
```

```python
import math
from types import SimpleNamespace

import jax
import jax.numpy as jnp
import numpy as np
from jax import lax
from jax.experimental import pallas as pl
from jax.experimental.pallas import tpu as pltpu
from jax.sharding import PartitionSpec as P

D = 768
HEADS = 12
HEAD_DIM = 64
FF = 3072
SEG_LEN = 128
LONG_SEGS = 64
EPSILON = 1e-05
NEGATIVE = -1e30

LAYOUT = dict(
    w_qkv=(D, 3 * D),
    b_qv=(2 * D,),
    w_out=(D, D),
    b_out=(D,),
    gain_one=(D,),
    bias_one=(D,),
    w_up=(D, FF),
    b_up=(FF,),
    w_down=(FF, D),
    b_down=(D,),
    gain_two=(D,),
    bias_two=(D,),
    pos_table=(LONG_SEGS, D),
    x_qkv=(D, 3 * D),
    x_bqv=(2 * D,),
    x_out=(D, D),
    x_bout=(D,),
    gain_three=(D,),
    bias_three=(D,),
    x_up=(D, FF),
    x_bup=(FF,),
    x_down=(FF, D),
    x_bdown=(D,),
    gain_four=(D,),
    bias_four=(D,),
)
LANES = 128
BLK = 16
Y, X, C, Z = range(4)


def ceil_to(value, step):
    return -(-value // step) * step


def item_list(total_rows):
    items = []
    nat = 0
    for name, shape in LAYOUT.items():
        rows = math.prod(shape) // LANES
        if len(shape) == 1 and items and len(items[-1].shape) == 1:
            items[-1].names.append(name)
            items[-1].rows += rows
        else:
            items.append(SimpleNamespace(name=name, names=[name], shape=shape, nat=nat, rows=rows))
        nat += rows
    items.append(SimpleNamespace(name=None, names=[], shape=None, nat=nat, rows=total_rows - nat))
    blk = 0
    for item in items:
        item.cols = item.shape[1] // LANES if item.shape and len(item.shape) == 2 else 0
        item.blk = blk
        blk += ceil_to(item.rows, BLK) // BLK
    return items


class Geometry:
    def __init__(self, n_seg, n_doc, shard_len):
        self.n_seg, self.n_doc = n_seg, n_doc
        self.n_dev = n_seg * n_doc
        self.chunk = shard_len // LANES
        self.items = item_list(self.chunk * self.n_dev)
        self.by_name = SimpleNamespace(**{item.name: item for item in self.items if item.name})
        firsts, lasts = [], []
        for n in range(self.n_dev):
            lo, hi = n * self.chunk, (n + 1) * self.chunk
            blocks = []
            for item in self.items:
                a, b = max(lo, item.nat), min(hi, item.nat + item.rows)
                if a < b:
                    blocks.append(item.blk + (a - item.nat) // BLK)
                    blocks.append(item.blk + (b - 1 - item.nat) // BLK)
            firsts.append(min(blocks))
            lasts.append(max(blocks))
        self.first, self.last = firsts, lasts
        most = max(b - a + 1 for a, b in zip(firsts, lasts))
        self.piece_blocks = -(-most // self.n_dev)
        self.piece = self.piece_blocks * BLK
        self.slots = self.piece_blocks * self.n_dev
        self.groups = -(-most // (self.piece_blocks * n_doc))
        self.share = n_doc * self.piece
        self.staged_rows = self.groups * self.share
        self.c_size, self.x_size = 2, 2
        self.y_size = n_seg // 4

    def full_groups(self, item, chunk):
        rows = BLK * item.cols
        lo, hi = chunk * self.chunk - item.nat, (chunk + 1) * self.chunk - item.nat
        first, last = max(0, -(-lo // rows)), min(item.rows, hi) // rows
        return first, max(first, last)

    def block_tables(self):
        matrices = [item for item in self.items if item.cols]
        single = [[] for _ in range(self.n_dev)]
        groups = np.zeros((self.n_dev, len(matrices), 3), np.int32)
        for n in range(self.n_dev):
            lo, hi = n * self.chunk, (n + 1) * self.chunk
            for t in range(self.slots):
                b = self.first[n] + t
                if b > self.last[n]:
                    single[n].append((t, 0, 0, 0))
                    continue
                item = [it for it in self.items if it.blk <= b][-1]
                at = b - item.blk
                if item.cols:
                    first, last = self.full_groups(item, n)
                    if first <= at // item.cols < last:
                        continue
                start = item.nat + at * BLK
                a = max(start, lo)
                z = max(a, min(start + BLK, hi, item.nat + item.rows))
                single[n].append((t, start - lo, a - start, z - start))
            for i, item in enumerate(matrices):
                first, last = self.full_groups(item, n)
                if first < last:
                    slot = item.blk + first * item.cols - self.first[n]
                    groups[n, i] = (slot, item.nat + first * BLK * item.cols - lo, last - first)
        most = max(len(rows) for rows in single)
        table = np.zeros((self.n_dev, 1 + 4 * most), np.int32)
        for n, rows in enumerate(single):
            table[n, 0] = len(rows)
            table[n, 1 : 1 + 4 * len(rows)] = np.asarray(rows, np.int32).reshape(-1)
        return matrices, np.concatenate([groups.reshape(self.n_dev, -1), table], axis=1)

    def chunks_of(self, item):
        found = []
        n_blocks = ceil_to(item.rows, BLK) // BLK
        for n in range(self.n_dev):
            a = max(item.blk, self.first[n])
            b = min(item.blk + n_blocks, self.last[n] + 1)
            if a < b:
                found.append((n, a - item.blk, b - item.blk, a - self.first[n]))
        return found

    def spans(self, *ends):
        cuts = [0] + [ceil_to((end.nat - 1) // self.chunk + 1, self.n_doc) for end in ends] + [self.n_dev]
        return [range(a, b) for a, b in zip(cuts, cuts[1:])]

    def coords(self, device):
        seg, doc = divmod(device, self.n_doc)
        yx, c = divmod(seg, self.c_size)
        return [*divmod(yx, self.x_size), c, doc]

    def device(self, y, x, c, z):
        return ((y * self.x_size + x) * self.c_size + c) * self.n_doc + z

    def size(self, axis):
        return (self.y_size, self.x_size, self.c_size, self.n_doc)[axis]

    def shift(self, axis, step):
        pairs = []
        for source in range(self.n_dev):
            at = self.coords(source)
            at[axis] = (at[axis] + step) % self.size(axis)
            pairs.append((source, self.device(*at)))
        return pairs
def spec_vmem():
    return pl.BlockSpec(memory_space=pltpu.VMEM)


def spec_any():
    return pl.BlockSpec(memory_space=pl.ANY)


def spec_hbm():
    return pl.BlockSpec(memory_space=pltpu.HBM)


def spec_smem():
    return pl.BlockSpec(memory_space=pltpu.SMEM)


def kernel_params(mib=20):
    return pltpu.CompilerParams(vmem_limit_bytes=mib * 1024 * 1024)


def cost(micros):
    micros = micros if micros >= 6 else 0
    return pl.CostEstimate(flops=int(micros * 1e9), bytes_accessed=int(micros * 3e6), transcendentals=0)


class Order:
    def start(self):
        self.token = jnp.zeros((8, LANES), jnp.float32)
        self.others = []

    def wait_for(self, *others):
        self.others += others


ORDER = Order()


def ordered(kernel, out_shape, in_specs, out_specs, **settings):
    single = not isinstance(out_shape, (list, tuple))
    outs, specs = ([out_shape], [out_specs]) if single else (list(out_shape), list(out_specs))

    def run(*inputs):
        extra = [ORDER.token] + ORDER.others
        n_in, n_out, n_extra = len(inputs), len(outs), len(extra)

        def wrapped(*refs):
            rest = refs[n_in + n_extra :]
            kernel(*refs[:n_in], *rest[:n_out], *rest[n_out + 1 :])

        results = pl.pallas_call(
            wrapped,
            out_shape=outs + [jax.ShapeDtypeStruct((8, LANES), jnp.float32)],
            in_specs=list(in_specs) + [spec_any()] * n_extra,
            out_specs=specs + [spec_any()],
            **settings,
        )(*inputs, *extra)
        ORDER.token, ORDER.others = results[-1], []
        return results[0] if single else results[:-1]

    return run


def row_mask(low, high):
    rows = lax.broadcasted_iota(jnp.int32, (BLK, LANES), 0)
    return (rows >= low) & (rows < high)


def block_moves(geo, table_ref, by_group, by_row):
    matrices = geo.block_tables()[0]
    for i, item in enumerate(matrices):
        def body(g, carry, i=i, cols=item.cols):
            for cb in range(cols):
                by_group(table_ref[3 * i] + g * cols + cb, table_ref[3 * i + 1] + g * BLK * cols + cb, cols)
            return carry

        lax.fori_loop(0, table_ref[3 * i + 2], body, 0)
    base = 3 * len(matrices)

    def single(r, carry):
        by_row(*[table_ref[base + 1 + 4 * r + j] for j in range(4)])
        return carry

    lax.fori_loop(0, table_ref[base], single, 0)


def block_at(slot):
    return pl.ds(pl.multiple_of(slot * BLK, BLK), BLK)


def align_rows(geo, table, natural, pad_rows):
    def kernel(table_ref, natural_ref, out_ref, rows_ref):
        def fill(row, rows):
            rows_ref[pl.ds(row + BLK, rows), :] = natural_ref[pl.ds(row, rows), :]

        copy_rows(natural.shape[0], 256, fill)

        def by_group(slot, start, cols):
            out_ref[block_at(slot), :] = rows_ref[pl.ds(start + BLK, BLK, stride=cols), :].astype(jnp.bfloat16)

        def by_row(slot, start, low_row, high_row):
            rows = jnp.where(row_mask(low_row, high_row), rows_ref[pl.ds(start + BLK, BLK), :], 0.0)
            out_ref[block_at(slot), :] = rows.astype(jnp.bfloat16)

        block_moves(geo, table_ref, by_group, by_row)

    return ordered(
        kernel,
        out_shape=jax.ShapeDtypeStruct((geo.slots * BLK, LANES), jnp.bfloat16),
        in_specs=[spec_smem(), spec_vmem()],
        out_specs=spec_vmem(),
        scratch_shapes=[pltpu.VMEM((pad_rows, LANES), jnp.float32)],
        compiler_params=kernel_params(),
        cost_estimate=cost(3),
    )(table, natural)


def update_rows(geo, table, blocks, begins, factors, state, pad_rows):
    rows_all = geo.chunk
    runs = begins.shape[0]

    def kernel(table_ref, begins_ref, factors_ref, blocks_ref, *refs):
        held, outs, grad_ref = refs[:3], refs[3:7], refs[7]

        def by_group(slot, start, cols):
            grad_ref[pl.ds(start + BLK, BLK, stride=cols), :] = blocks_ref[block_at(slot), :].astype(jnp.float32)

        def by_row(slot, start, low_row, high_row):
            here = pl.ds(start + BLK, BLK)
            rows = blocks_ref[block_at(slot), :].astype(jnp.float32)
            grad_ref[here, :] = jnp.where(row_mask(low_row, high_row), rows, grad_ref[here, :])

        block_moves(geo, table_ref, by_group, by_row)

        def step(row, rows):
            here = pl.ds(row, rows)
            at = lax.broadcasted_iota(jnp.int32, (rows, LANES), 0) + row
            scale = jnp.full((rows, LANES), factors_ref[0], jnp.float32)
            rate = jnp.full((rows, LANES), factors_ref[runs], jnp.float32)
            for run in range(1, runs):
                later = at >= begins_ref[run]
                scale = jnp.where(later, factors_ref[run], scale)
                rate = jnp.where(later, factors_ref[runs + run], rate)
            scaled = grad_ref[pl.ds(row + BLK, rows), :] * scale
            moment = 0.5 * held[1][here, :] + scaled
            weight = held[0][here, :] - rate * (scaled + 0.5 * moment)
            outs[0][here, :] = weight
            outs[1][here, :] = moment
            outs[2][here, :] = 0.5 * held[2][here, :] + 0.5 * weight
            outs[3][here, :] = weight.astype(jnp.bfloat16)

        copy_rows(rows_all, 128, step)

    full = [jax.ShapeDtypeStruct((rows_all, LANES), kind) for kind in (jnp.float32,) * 3 + (jnp.bfloat16,)]
    return ordered(
        kernel,
        out_shape=full,
        in_specs=[spec_smem()] * 3 + [spec_vmem()] * 4,
        out_specs=[spec_vmem()] * 4,
        scratch_shapes=[pltpu.VMEM((pad_rows, LANES), jnp.float32)],
        compiler_params=kernel_params(28),
        cost_estimate=cost(3),
    )(table, begins, factors, blocks, *state)


class Buckets:
    def __init__(self, geo, arrays, *ends):
        self.geo = geo
        self.ranges = geo.spans(*ends)
        self.arrays = arrays

    def find(self, chunk):
        for number, span in enumerate(self.ranges):
            if chunk in span:
                return number, chunk - span.start

    def shapes(self, number):
        geo = self.geo
        count = len(self.ranges[number])
        return [
            (geo.y_size, geo.x_size, count, geo.share // 2, LANES),
            (geo.x_size, geo.y_size, count, geo.share // 2, LANES),
        ]


def wrap(value, size):
    return lax.rem(value + size, size)


def copy_rows(count, step, body):
    full = count // step
    if full:
        def loop(i, carry):
            body(i * step, step)
            return carry

        lax.fori_loop(0, full, loop, 0)
    if count % step:
        body(full * step, count % step)


def place_line(geo, parts, my_z):
    count, nd = parts[0].shape[0], geo.n_doc
    rows = geo.share // 2

    def kernel(z_ref, *refs):
        sources, outs = refs[:nd], refs[nd:]
        for r in range(nd):
            z = wrap(z_ref[0] - r, nd)
            for s in range(count):
                for half in range(2):
                    outs[half][s * nd + z] = sources[r][s, half * rows : (half + 1) * rows]

    return ordered(
        kernel,
        out_shape=[jax.ShapeDtypeStruct((count * nd, rows, LANES), jnp.bfloat16)] * 2,
        in_specs=[spec_smem()] + [spec_vmem()] * nd,
        out_specs=[spec_vmem()] * 2,
        compiler_params=kernel_params(),
        cost_estimate=cost(2),
    )(my_z.reshape(1), *parts)
VECTOR_ROWS = 16


def chunk_copies(geo, buckets, sources, used, coords_ref, n, staged, sem):
    my_y, my_x, my_c = coords_ref[0], coords_ref[1], coords_ref[2]
    number, place = buckets.find(n)
    first = sum(buckets.arrays[m] for m in used[: used.index(number)])
    if buckets.arrays[number] == 1:
        line, z = divmod(place, geo.n_doc)
        for s in range(geo.groups):
            pltpu.make_async_copy(
                sources[first].at[s * geo.n_doc + z, line],
                staged.at[pl.ds(s * geo.share, geo.share)],
                sem,
            ).start()
        return
    rows = geo.share // 2
    for core in range(2):
        c = my_c if core == 0 else 1 - my_c
        for ry in range(geo.y_size):
            for rx in range(geo.x_size):
                y, x = wrap(my_y - ry, geo.y_size), wrap(my_x - rx, geo.x_size)
                s = (y * geo.x_size + x) * 2 + c

                def begin(s=s, ry=ry, rx=rx, core=core):
                    for half in range(2):
                        index = (ry, rx, place) if half == 0 else (rx, ry, place)
                        pltpu.make_async_copy(
                            sources[first + 2 * half + core].at[index],
                            staged.at[pl.ds(pl.multiple_of(s * geo.share + half * rows, BLK), rows)],
                            sem,
                        ).start()

                if geo.groups == geo.n_seg:
                    begin()
                else:
                    pl.when(s < geo.groups)(begin)


class Weights:
    def __init__(self, geo, buckets, gathered, names):
        self.geo, self.buckets = geo, buckets
        self.items = [vars(geo.by_name)[name] for name in names]
        self.chunks = sorted({n for item in self.items for n, *_ in geo.chunks_of(item)})
        self.used = sorted({buckets.find(n)[0] for n in self.chunks})
        self.operands = [array for number in self.used for array in gathered[number]]
        cols = max([item.cols for item in self.items])
        self.scratch = [
            pltpu.VMEM((len(self.chunks), geo.staged_rows, LANES), jnp.bfloat16),
            pltpu.VMEM((BLK * (cols + 2), LANES), jnp.float32),
            pltpu.SemaphoreType.DMA((len(self.chunks),)),
        ]

    def start(self, coords_ref, sources, staged, sems):
        for at, n in enumerate(self.chunks):
            chunk_copies(
                self.geo, self.buckets, sources, self.used, coords_ref, n, staged.at[at], sems.at[at]
            )

    def wait(self, number, waited, staged, sems):
        for n, *_ in self.geo.chunks_of(self.items[number]):
            at = self.chunks.index(n)
            if at not in waited:
                waited.add(at)
                pltpu.make_async_copy(staged.at[at], staged.at[at], sems.at[at]).wait()

    def blocks(self, item, lo, hi, staged, wide):
        done = lo
        for n, b0, b1, slot in self.geo.chunks_of(item):
            for b in range(max(b0, lo), min(b1, hi)):
                at = self.chunks.index(n)
                rows = staged[at, pl.ds((slot + b - b0) * BLK, BLK), :].astype(jnp.float32)
                here = pl.ds((b - lo) * BLK, BLK)
                wide[here, :] = wide[here, :] + rows if b < done else rows
            done = max(done, min(b1, hi))

    def matrix(self, number, staged, wide, out_ref):
        item = self.items[number]
        cols = item.cols
        split = set()
        for n, b0, b1, slot in self.geo.chunks_of(item):
            at = self.chunks.index(n)
            first, last = self.geo.full_groups(item, n)
            split |= set(range(b0 // cols, -(-b1 // cols))) - set(range(first, last))

            def group(g, carry, at=at, shift=slot - b0):
                rows = pl.ds(pl.multiple_of(g * BLK, BLK), BLK)
                for cb in range(cols):
                    tile = staged[at, block_at(g * cols + cb + shift), :]
                    out_ref[rows, cb * LANES : (cb + 1) * LANES] = tile
                return carry

            lax.fori_loop(first, last, group, 0)
        for g in sorted(split):
            self.blocks(item, g * cols, (g + 1) * cols, staged, wide)
            for cb in range(cols):
                tile = wide[pl.ds(cb, BLK, stride=cols), :]
                out_ref[g * BLK : (g + 1) * BLK, cb * LANES : (cb + 1) * LANES] = tile.astype(jnp.bfloat16)

    def vectors(self, number, staged, wide, out_ref, row):
        item = self.items[number]
        self.blocks(item, 0, ceil_to(item.rows, BLK) // BLK, staged, wide)
        for r in range(item.rows):
            v, cb = divmod(r, D // LANES)
            out_ref[row + v : row + v + 1, cb * LANES : (cb + 1) * LANES] = wide[r : r + 1, :]


def vector_rows(wide, values, first, count):
    lane_cols = D // LANES
    for r in range(count):
        v, cb = divmod(r, lane_cols)
        wide[r : r + 1, :] = values[first + v : first + v + 1, cb * LANES : (cb + 1) * LANES]


def bucket_parts(geo, span):
    parts = []
    for item in geo.items:
        chunks = [entry for entry in geo.chunks_of(item) if entry[0] in span]
        if chunks and item.names:
            parts.append((item, chunks))
    return parts


def grad_bucket(geo, buckets, number, grads, coords, name, left, right, rows, keep=False):
    span = buckets.ranges[number]
    parts = bucket_parts(geo, span)
    operands, specs, windows, scratch = [], [], [], []
    wide_rows = BLK
    for item, chunks in parts:
        if len(item.shape) == 2:
            cols = item.cols
            wide_rows = max(wide_rows, BLK * cols)
            if item.name == name:
                main, main_chunks, windows_at = item, chunks, len(windows)
                windows.append(None)
                continue
            k0 = min(b0 for _, b0, _, _ in chunks) // cols
            k1 = -(-max(b1 for _, _, b1, _ in chunks) // cols)
            operands.append(grads[item.name])
            specs.append(spec_any())
            windows.append((len(operands) - 1, k0, k1))
            scratch.append(pltpu.VMEM(((k1 - k0) * BLK, item.shape[1]), jnp.bfloat16))
        else:
            wide_rows = max(wide_rows, ceil_to(item.rows, BLK))
            operands.append(grads[item.name][0])
            specs.append(pl.BlockSpec(operands[-1].shape, lambda i: (0, 0)))
            windows.append((len(operands) - 1, None, None))
            scratch.append(pltpu.VMEM((BLK, LANES), jnp.bfloat16))
    outs = [shape for shape in buckets.shapes(number) for _ in range(2)]
    depth, width = main.shape
    cols = main.cols
    steps = depth // rows
    count = len(operands)
    block_groups = rows // BLK

    def split_groups(item, chunks):
        found = set()
        for n, b0, b1, _ in chunks:
            first, last = geo.full_groups(item, n)
            found |= set(range(b0 // item.cols, -(-b1 // item.cols))) - set(range(first, last))
        return sorted(found)

    def kernel(coords_ref, left_ref, right_ref, *refs):
        sources, targets = refs[:count], refs[count : count + 4]
        refs = refs[count + 4 :]
        if keep:
            kept_ref, refs = refs[0], refs[1:]
        loaded, (values, staged, wide, in_sems, out_sems) = refs[:count], refs[count:]
        step = pl.program_id(0)
        my_y, my_x, my_c = coords_ref[0], coords_ref[1], coords_ref[2]

        def send_out(n):
            _, place = buckets.find(n)
            half_rows = geo.share // 2
            for core in range(2):
                c = my_c if core == 0 else 1 - my_c
                for ry in range(geo.y_size):
                    for rx in range(geo.x_size):
                        y, x = wrap(my_y + ry, geo.y_size), wrap(my_x + rx, geo.x_size)
                        s = (y * geo.x_size + x) * 2 + c
                        for half in range(2):
                            index = (ry, rx, place) if half == 0 else (rx, ry, place)
                            here = pl.ds(pl.multiple_of(s * geo.share + half * half_rows, BLK), half_rows)
                            pltpu.make_async_copy(
                                staged.at[n - span.start, here],
                                targets[2 * half + core].at[index],
                                out_sems.at[n - span.start],
                            ).start()

        def whole(item, chunks, values, base, lo, hi):
            for n, b0, b1, slot in chunks:
                first, last = geo.full_groups(item, n)

                def group(g, carry, n=n, shift=slot - b0):
                    here = pl.ds(pl.multiple_of((g - base) * BLK, BLK), BLK)
                    for cb in range(item.cols):
                        dst = block_at(g * item.cols + cb + shift)
                        staged[n - span.start, dst, :] = values[here, cb * LANES : (cb + 1) * LANES]
                    return carry

                start = jnp.maximum(first, lo)
                lax.fori_loop(start, jnp.maximum(start, jnp.minimum(last, hi)), group, 0)

        def cut(item, chunks, values, base, g):
            for cb in range(item.cols):
                tile = values[pl.ds(pl.multiple_of((g - base) * BLK, BLK), BLK), cb * LANES : (cb + 1) * LANES]
                wide[pl.ds(cb, BLK, stride=item.cols), :] = tile.astype(jnp.float32)
            for n, b0, b1, slot in chunks:
                first, last = geo.full_groups(item, n)
                lo, hi = max(b0, g * item.cols), min(b1, (g + 1) * item.cols)
                if lo < hi and not first <= g < last:
                    part = wide[pl.ds((lo - g * item.cols) * BLK, (hi - lo) * BLK), :]
                    dst = pl.ds((slot + lo - b0) * BLK, (hi - lo) * BLK)
                    staged[n - span.start, dst, :] = part.astype(jnp.bfloat16)

        @pl.when(step == 0)
        def _():
            loads = {}
            for (item, chunks), window in zip(parts, windows):
                if window is not None and window[1] is not None:
                    at, k0, k1 = window
                    source = sources[at].at[pl.ds(k0 * BLK, (k1 - k0) * BLK)]
                    loads[at] = pltpu.make_async_copy(source, loaded[at], in_sems.at[at])
                    loads[at].start()

            def clear(row, size):
                for at in range(len(span)):
                    here = pl.ds(pl.multiple_of(row + tail, BLK), size)
                    staged[at, here, :] = jnp.zeros((size, LANES), jnp.bfloat16)

            tail = min(geo.last[n] - geo.first[n] for n in span) * BLK
            copy_rows(geo.slots * BLK - tail, 128, clear)
            for (item, chunks), window in zip(parts, windows):
                if window is None:
                    continue
                at, k0, k1 = window
                if k0 is None:
                    vector_rows(wide, sources[at], grads[item.name][1], item.rows)
                    for n, b0, b1, slot in chunks:
                        part = wide[pl.ds(b0 * BLK, (b1 - b0) * BLK), :].astype(jnp.bfloat16)
                        staged[n - span.start, pl.ds(slot * BLK, (b1 - b0) * BLK), :] = part
                else:
                    loads[at].wait()
                    whole(item, chunks, loaded[at], k0, k0, k1)
                    for g in split_groups(item, chunks):
                        cut(item, chunks, loaded[at], k0, g)

        values[...] = low(dot_tn(left_ref[...], right_ref[...]))
        if keep:
            kept_ref[...] = values[...]
        low_group = step * block_groups
        whole(main, main_chunks, values, low_group, low_group, low_group + block_groups)
        for g in split_groups(main, main_chunks):
            @pl.when(step == g // block_groups)
            def _(g=g):
                cut(main, main_chunks, values, g // block_groups * block_groups, g)

        ready = {n: 0 for n in span}
        for n, _, b1, _ in main_chunks:
            ready[n] = (b1 - 1) // cols // block_groups
        for at in range(steps):
            here = [n for n in span if ready[n] == at]
            if here:
                @pl.when(step == at)
                def _(here=here):
                    for n in here:
                        send_out(n)

        @pl.when(step == steps - 1)
        def _():
            for at in range(len(span)):
                pltpu.make_async_copy(staged.at[at], staged.at[at], out_sems.at[at]).wait()

    extra = [jax.ShapeDtypeStruct(main.shape, jnp.bfloat16)] if keep else []
    return ordered(
        kernel,
        grid=(steps,),
        out_shape=[jax.ShapeDtypeStruct(shape, jnp.bfloat16) for shape in outs] + extra,
        in_specs=[
            spec_smem(),
            pl.BlockSpec((left.shape[0], rows), lambda i: (0, i)),
            pl.BlockSpec(right.shape, lambda i: (0, 0), pipeline_mode=pl.Buffered(1)),
        ]
        + specs,
        out_specs=[spec_any()] * 4 + [pl.BlockSpec((rows, width), lambda i: (i, 0))] * len(extra),
        scratch_shapes=scratch
        + [
            pltpu.VMEM((rows, width), jnp.bfloat16),
            pltpu.VMEM((len(span), geo.slots * BLK, LANES), jnp.bfloat16),
            pltpu.VMEM((wide_rows + 2 * BLK, LANES), jnp.float32),
            pltpu.SemaphoreType.DMA((max(count, 1),)),
            pltpu.SemaphoreType.DMA((len(span),)),
        ],
        compiler_params=kernel_params(60),
        cost_estimate=cost(18),
    )(coords, left, right, *operands)


class CrossPack:
    def __init__(self, geo, span, depth_rows):
        self.geo, self.span = geo, span
        self.parts = bucket_parts(geo, span)
        self.seg_blocks = geo.n_doc * geo.piece_blocks
        wide_rows, flat_cols, left_rows = BLK, D, BLK
        for item, chunks in self.parts:
            if item.cols:
                left_rows = max(left_rows, len(chunks) * self.window(item))
                wide_rows = max(wide_rows, BLK * item.cols)
                flat_cols = max(flat_cols, item.shape[1])
            else:
                wide_rows = max(wide_rows, ceil_to(item.rows, BLK))
        self.out = jax.ShapeDtypeStruct((len(span), geo.share, LANES), jnp.bfloat16)
        self.scratch = [
            pltpu.VMEM((left_rows, depth_rows), jnp.bfloat16),
            pltpu.VMEM((left_rows, flat_cols), jnp.bfloat16),
            pltpu.VMEM((wide_rows + 2 * BLK, LANES), jnp.float32),
        ]

    def window(self, item):
        return min((-(-(self.seg_blocks - 1) // item.cols) + 1) * BLK, item.shape[0])

    def run(self, seg, lefts, rights, sums_ref, first_rows, out_ref, gathered, flat, wide):
        geo, span, seg_blocks = self.geo, self.span, self.seg_blocks
        low_slot = seg * seg_blocks
        out_ref[...] = jnp.zeros_like(out_ref)

        def slots(lo, hi):
            begin = jnp.maximum(low_slot, lo)
            return begin, jnp.maximum(begin, jnp.minimum(low_slot + seg_blocks, hi))

        def rows_out(n, slot, block, rows):
            begin, end = slots(slot, slot + rows)

            def move(t, carry):
                data = wide[block_at(block + t - slot), :]
                out_ref[n - span.start, block_at(t - low_slot), :] = data.astype(jnp.bfloat16)
                return carry

            lax.fori_loop(begin, end, move, 0)

        for item, chunks in self.parts:
            if not item.cols:
                vector_rows(wide, sums_ref, first_rows[item.name], item.rows)
                for n, b0, b1, slot in chunks:
                    rows_out(n, slot, b0, b1 - b0)
                continue
            cols = item.cols
            size = self.window(item)
            starts = []
            for at, (n, b0, b1, slot) in enumerate(chunks):
                first = jnp.maximum(low_slot, slot) - slot + b0
                start = pl.multiple_of(jnp.clip(first // cols * BLK, 0, item.shape[0] - size), BLK)
                starts.append(start)
                gathered[at * size : (at + 1) * size, :] = lefts[item.name][pl.ds(start, size), :]
            count = len(chunks) * size
            rows = gathered[:count, :]
            for cb in range(0, cols, 2):
                here = slice(cb * LANES, (cb + 2) * LANES)
                flat[:count, here] = dot_nn(rows, rights[item.name][:, here]).astype(jnp.bfloat16)
            for at, (n, b0, b1, slot) in enumerate(chunks):
                first, last = geo.full_groups(item, n)
                base = at * size - starts[at]

                def group_rows(group, base=base):
                    return pl.ds(pl.multiple_of(base + group * BLK, BLK), BLK)

                def by_tile(t, carry, n=n, shift=b0 - slot, group_rows=group_rows, cols=cols):
                    b = t + shift
                    group = b // cols
                    lanes = pl.ds(pl.multiple_of((b - group * cols) * LANES, LANES), LANES)
                    out_ref[n - span.start, block_at(t - low_slot), :] = flat[group_rows(group), lanes]
                    return carry

                if first < last:
                    begin, end = slots(slot + first * cols - b0, slot + last * cols - b0)
                    lax.fori_loop(begin, end, by_tile, 0)
                for g in range(b0 // cols, -(-b1 // cols)):
                    if first <= g < last:
                        continue
                    lo, hi = max(b0, g * cols), min(b1, (g + 1) * cols)
                    begin, end = slots(slot + lo - b0, slot + hi - b0)

                    @pl.when(begin < end)
                    def _(g=g, lo=lo, hi=hi, n=n, shift=slot - b0, group_rows=group_rows, cols=cols):
                        for cb in range(cols):
                            tile = flat[group_rows(g), cb * LANES : (cb + 1) * LANES]
                            wide[pl.ds(cb, BLK, stride=cols), :] = tile.astype(jnp.float32)
                        rows_out(n, lo + shift, lo - g * cols, hi - lo)
TILE = 512
PAIRS = HEADS // 2

def dot_nn(left, right):
    return lax.dot_general(left, right, (((1,), (0,)), ((), ())), preferred_element_type=jnp.float32)


def dot_nt(left, right):
    return lax.dot_general(left, right, (((1,), (1,)), ((), ())), preferred_element_type=jnp.float32)


def dot_tn(left, right):
    return lax.dot_general(left, right, (((0,), (0,)), ((), ())), preferred_element_type=jnp.float32)


def low(values):
    return values.astype(jnp.bfloat16)


def gelu_pair(u):
    spread = 0.5 + 0.5 * lax.erf(u * math.sqrt(0.5))
    return u * spread, spread + u * jnp.exp(-0.5 * (u * u)) * (1.0 / math.sqrt(2.0 * math.pi))


def norm_rows(values, gain, shift):
    center = values - jnp.mean(values, axis=-1, keepdims=True)
    rate = lax.rsqrt(jnp.mean(center * center, axis=-1, keepdims=True) + EPSILON)
    normal = center * rate
    return normal * gain + shift, normal, rate


def norm_pull(grad, normal, rate, gain):
    scaled = grad * gain
    return rate * (
        scaled
        - jnp.mean(scaled, axis=-1, keepdims=True)
        - normal * jnp.mean(scaled * normal, axis=-1, keepdims=True)
    )


def fixed(shape):
    return pl.BlockSpec(shape, lambda i: (0,) * len(shape), pipeline_mode=pl.Buffered(1))


def tiles(cols, first=0):
    return pl.BlockSpec((TILE, cols), lambda i: (i + first, 0))


def both_heads(values):
    first = lax.broadcasted_iota(jnp.int32, values.shape, 1) < HEAD_DIM
    zero = jnp.zeros_like(values)
    return jnp.concatenate([jnp.where(first, values, zero), jnp.where(first, zero, values)], axis=0)


def side_by_side(stacked):
    half = stacked.shape[0] // 2
    return jnp.concatenate([stacked[:half], stacked[half:]], axis=1)


def stacked_heads(values):
    half = values.shape[1] // 2
    return jnp.concatenate([values[:, :half], values[:, half:]], axis=0)


STATS = 16


def stat_tiles(first=0):
    return pl.BlockSpec((TILE // SEG_LEN * STATS, LANES), lambda i: (i + first, 0))


def third(part, pair):
    start = part * D + pair * LANES
    return slice(start, start + LANES)


def attend_kernel(x_ref, wqkv_ref, vec_ref, packed_ref, att_ref, stat_ref):
    x = x_ref[...]
    for j in range(3):
        cols = slice(j * D, (j + 1) * D)
        part = dot_nn(x, wqkv_ref[:, cols])
        packed_ref[:, cols] = low(part if j == 1 else part + vec_ref[j // 2 : j // 2 + 1, :])

    def segment(s, carry):
        rows = pl.ds(pl.multiple_of(s * SEG_LEN, SEG_LEN), SEG_LEN)
        for pair in range(PAIRS):
            queries = both_heads(packed_ref[rows, third(0, pair)] * jnp.bfloat16(HEAD_DIM**-0.5))
            values = both_heads(packed_ref[rows, third(2, pair)])
            scores = dot_nt(packed_ref[rows, third(1, pair)], queries)
            largest = jnp.max(scores, axis=0, keepdims=True)
            raised = jnp.exp(scores - largest)
            summed = jnp.sum(raised, axis=0, keepdims=True)
            weights = low(raised * (1.0 / summed))
            att_ref[rows, pair * LANES : (pair + 1) * LANES] = low(dot_tn(stacked_heads(weights), values))
            log_sum = largest + jnp.log(summed)
            for head in range(2):
                row = pl.ds(s * STATS + 2 * pair + head, 1)
                stat_ref[row, :] = log_sum[:, head * SEG_LEN : (head + 1) * SEG_LEN]
        return carry

    lax.fori_loop(0, TILE // SEG_LEN, segment, 0, unroll=2)


def in_parts(kernel, micros, count, inputs, in_specs, outs, out_specs, scratch, previous, mib=60):
    previous = list(previous or ())
    return ordered(
        kernel,
        grid=(count,),
        in_specs=in_specs + [spec_any()] * len(previous),
        out_specs=out_specs,
        out_shape=outs,
        scratch_shapes=scratch,
        input_output_aliases={len(inputs) + i: i for i in range(len(previous))},
        compiler_params=kernel_params(mib),
        cost_estimate=cost(micros),
    )(*inputs, *previous)


def attend_layer(x, w_qkv, vecs, first, count, previous):
    def rows(cols):
        return tiles(cols, first)

    def kernel(x_ref, wqkv_ref, vec_ref, *refs):
        attend_kernel(x_ref, wqkv_ref, vec_ref, *refs[-3:])

    return in_parts(
        kernel,
        8 * count,
        count,
        [x, w_qkv, vecs],
        [rows(D), fixed((D, 3 * D)), fixed((VECTOR_ROWS, D))],
        [jax.ShapeDtypeStruct(v.shape, v.dtype) for v in previous],
        [rows(3 * D), rows(D), stat_tiles(first)],
        [],
        previous,
    )


def attend_first(x, weights, coords):
    n = x.shape[0]
    bf, f32 = jnp.bfloat16, jnp.float32
    count = len(weights.operands)

    def kernel(coords_ref, *refs):
        sources, x_ref, refs = refs[:count], refs[count], refs[count + 1 :]
        packed_ref, att_ref, stat_ref, wqkv_ref, vec_ref, staged, wide, sems = refs
        weights.start(coords_ref, sources, staged, sems)
        waited = set()
        for number in range(2):
            weights.wait(number, waited, staged, sems)
        weights.matrix(0, staged, wide, wqkv_ref)
        vec_ref[...] = jnp.zeros_like(vec_ref)
        weights.vectors(1, staged, wide, vec_ref, 0)
        attend_kernel(x_ref, wqkv_ref, vec_ref, packed_ref, att_ref, stat_ref)

    whole = [pl.BlockSpec(shape, lambda i: (0, 0)) for shape in ((D, 3 * D), (VECTOR_ROWS, D))]
    return ordered(
        kernel,
        grid=(1,),
        in_specs=[spec_smem()] + [spec_hbm()] * count + [tiles(D)],
        out_specs=[tiles(3 * D), tiles(D), stat_tiles()] + whole,
        out_shape=[
            jax.ShapeDtypeStruct((n, 3 * D), bf),
            jax.ShapeDtypeStruct((n, D), bf),
            jax.ShapeDtypeStruct((n // SEG_LEN * STATS, LANES), f32),
            jax.ShapeDtypeStruct((D, 3 * D), bf),
            jax.ShapeDtypeStruct((VECTOR_ROWS, D), f32),
        ],
        scratch_shapes=weights.scratch,
        compiler_params=kernel_params(60),
        cost_estimate=cost(12),
    )(coords, *weights.operands, x)


FBLOCK = D


def feed_kernel(
    x_ref, att_ref, wout_ref, wup_ref, wdown_ref, vec_ref,
    h1low_ref, norm1_ref, g_ref, dg_ref, norm2_ref, rate_ref, h2_ref, cls_ref, res_ref, h1_ref,
):
    step = pl.program_id(0)
    segs = TILE // SEG_LEN
    lanes = lax.broadcasted_iota(jnp.int32, (SEG_LEN, LANES), 1)
    res_ref[...] = dot_nn(att_ref[...], wout_ref[...])

    def start(s, carry):
        rows = pl.ds(pl.multiple_of(s * SEG_LEN, SEG_LEN), SEG_LEN)
        resid = x_ref[rows, :].astype(jnp.float32) + res_ref[rows, :] + vec_ref[2:3, :]
        hidden, normal, rate = norm_rows(resid, vec_ref[3:4, :], vec_ref[4:5, :])
        h1_ref[rows, :] = hidden
        h1low_ref[rows, :] = low(hidden)
        norm1_ref[rows, :] = low(normal)
        rate_ref[rows, :] = jnp.broadcast_to(rate, (SEG_LEN, LANES))
        return carry

    lax.fori_loop(0, segs, start, 0)
    h = h1low_ref[...]
    for j in range(FF // FBLOCK):
        cols = slice(j * FBLOCK, (j + 1) * FBLOCK)
        act, slope = gelu_pair(dot_nn(h, wup_ref[:, cols]) + vec_ref[5 + j : 6 + j, :])
        g = low(act)
        g_ref[:, cols] = g
        dg_ref[:, cols] = low(slope)
        part = dot_nn(g, wdown_ref[cols, :])
        if j == 0:
            res_ref[...] = part
        else:
            res_ref[...] += part

    def finish(s, carry):
        rows = pl.ds(pl.multiple_of(s * SEG_LEN, SEG_LEN), SEG_LEN)
        resid = h1_ref[rows, :] + res_ref[rows, :] + vec_ref[9:10, :]
        hidden, normal, rate = norm_rows(resid, vec_ref[10:11, :], vec_ref[11:12, :])
        h2_ref[rows, :] = low(hidden)
        norm2_ref[rows, :] = low(normal)
        rate_ref[rows, :] = jnp.where(lanes == 0, rate_ref[rows, :], rate)
        cls_ref[pl.ds(step * segs + s, 1), :] = hidden[0:1, :]
        return carry

    lax.fori_loop(0, segs, finish, 0)


def feed_layer(x, att, weights, coords):
    n = x.shape[0]
    bf, f32 = jnp.bfloat16, jnp.float32
    count = len(weights.operands)
    steps = n // TILE
    shapes = [item.shape for item in weights.items if item.cols]

    def kernel(coords_ref, *refs):
        sources, refs = refs[:count], refs[count:]
        x_ref, att_ref = refs[:2]
        outs, kept = refs[2:10], refs[10:13]
        vec_ref, res_ref, h1_ref, out_sems = refs[13:17]
        held, (staged, wide, sems) = refs[17:20], refs[20:]
        step = pl.program_id(0)

        @pl.when(step == 0)
        def _():
            weights.start(coords_ref, sources, staged, sems)
            waited = set()
            vec_ref[...] = jnp.zeros_like(vec_ref)
            place = row = 0
            for number, item in enumerate(weights.items):
                weights.wait(number, waited, staged, sems)
                if item.cols:
                    weights.matrix(number, staged, wide, held[place])
                    pltpu.make_async_copy(held[place], kept[place], out_sems.at[place]).start()
                    place += 1
                else:
                    weights.vectors(number, staged, wide, vec_ref, row)
                    row += item.rows * LANES // D

        feed_kernel(x_ref, att_ref, *held, vec_ref, *outs, res_ref, h1_ref)

        @pl.when(step == steps - 1)
        def _():
            for place in range(3):
                pltpu.make_async_copy(held[place], kept[place], out_sems.at[place]).wait()

    return ordered(
        kernel,
        grid=(steps,),
        in_specs=[spec_smem()] + [spec_hbm()] * count + [tiles(D), tiles(D)],
        out_specs=[tiles(D), tiles(D), tiles(FF), tiles(FF), tiles(D), tiles(LANES), tiles(D)]
        + [pl.BlockSpec((n // SEG_LEN, D), lambda i: (0, 0))]
        + [spec_any()] * 3
        + [pl.BlockSpec((VECTOR_ROWS, D), lambda i: (0, 0))],
        out_shape=[
            jax.ShapeDtypeStruct((n, cols), kind)
            for cols, kind in ((D, bf), (D, bf), (FF, bf), (FF, bf), (D, bf), (LANES, f32), (D, bf))
        ]
        + [jax.ShapeDtypeStruct((n // SEG_LEN, D), f32)]
        + [jax.ShapeDtypeStruct(shape, bf) for shape in shapes]
        + [jax.ShapeDtypeStruct((VECTOR_ROWS, D), f32)],
        scratch_shapes=[
            pltpu.VMEM((TILE, D), f32),
            pltpu.VMEM((TILE, D), f32),
            pltpu.SemaphoreType.DMA((3,)),
        ]
        + [pltpu.VMEM(shape, bf) for shape in shapes]
        + weights.scratch,
        compiler_params=kernel_params(62),
        cost_estimate=cost(60),
    )(coords, *weights.operands, x, att)


def feed_back_kernel(
    cot_ref, cls_ref, norm2_ref, dg_ref, norm1_ref, rate_ref,
    wdown_ref, wup_ref, wout_ref, vec_ref,
    dm_ref, du_ref, dao_ref, da_ref, one_ref, sums_ref, res_ref,
):
    step = pl.program_id(0)

    @pl.when(step == 0)
    def _():
        sums_ref[...] = jnp.zeros_like(sums_ref)

    segs = TILE // SEG_LEN
    row_ids = lax.broadcasted_iota(jnp.int32, (SEG_LEN, D), 0)

    def add_sum(row, values):
        sums_ref[row : row + 1, :] += jnp.sum(values, axis=0, keepdims=True)

    def start(s, carry):
        rows = pl.ds(pl.multiple_of(s * SEG_LEN, SEG_LEN), SEG_LEN)
        cls = cls_ref[pl.ds(step * segs + s, 1), :]
        grad = jnp.where(row_ids == 0, cls, cot_ref[rows, :].astype(jnp.float32))
        normal = norm2_ref[rows, :].astype(jnp.float32)
        add_sum(10, grad * normal)
        add_sum(11, grad)
        two = norm_pull(grad, normal, rate_ref[rows, 1:2], vec_ref[10:11, :])
        res_ref[rows, :] = two
        dm = low(two)
        dm_ref[rows, :] = dm
        add_sum(9, dm.astype(jnp.float32))
        return carry

    lax.fori_loop(0, segs, start, 0)
    dm = dm_ref[...]
    for j in range(FF // FBLOCK):
        cols = slice(j * FBLOCK, (j + 1) * FBLOCK)
        du = low(dot_nt(dm, wdown_ref[cols, :]) * dg_ref[:, cols].astype(jnp.float32))
        du_ref[:, cols] = du
        add_sum(5 + j, du.astype(jnp.float32))
        res_ref[...] += dot_nt(du, wup_ref[:, cols])

    def finish(s, carry):
        rows = pl.ds(pl.multiple_of(s * SEG_LEN, SEG_LEN), SEG_LEN)
        grad = res_ref[rows, :]
        normal = norm1_ref[rows, :].astype(jnp.float32)
        add_sum(3, grad * normal)
        add_sum(4, grad)
        one = norm_pull(grad, normal, rate_ref[rows, 0:1], vec_ref[3:4, :])
        one_ref[rows, :] = one
        dao = low(one)
        dao_ref[rows, :] = dao
        add_sum(2, dao.astype(jnp.float32))
        return carry

    lax.fori_loop(0, segs, finish, 0)
    da_ref[...] = low(dot_nt(dao_ref[...], wout_ref[...]))


def feed_back(cot, cls, norm2, dg, norm1, rates, w_down, w_up, w_out, vecs):
    n = cot.shape[0]
    bf, f32 = jnp.bfloat16, jnp.float32
    return ordered(
        feed_back_kernel,
        grid=(n // TILE,),
        in_specs=[
            tiles(D), fixed((n // SEG_LEN, D)), tiles(D), tiles(FF), tiles(D), tiles(LANES),
            fixed((FF, D)), fixed((D, FF)), fixed((D, D)), fixed((VECTOR_ROWS, D)),
        ],
        out_specs=[
            tiles(D), tiles(FF), tiles(D), tiles(D), tiles(D),
            pl.BlockSpec((VECTOR_ROWS, D), lambda i: (0, 0)),
        ],
        out_shape=[
            jax.ShapeDtypeStruct((n, D), bf),
            jax.ShapeDtypeStruct((n, FF), bf),
            jax.ShapeDtypeStruct((n, D), bf),
            jax.ShapeDtypeStruct((n, D), bf),
            jax.ShapeDtypeStruct((n, D), f32),
            jax.ShapeDtypeStruct((VECTOR_ROWS, D), f32),
        ],
        scratch_shapes=[pltpu.VMEM((TILE, D), f32)],
        compiler_params=kernel_params(60),
        cost_estimate=cost(44),
    )(cot, cls, norm2, dg, norm1, rates, w_down, w_up, w_out, vecs)


def attend_back_kernel(packed_ref, stat_ref, da_ref, before_ref, *refs):
    dqkv_ref, sums_ref = refs[-2:]

    @pl.when(pl.program_id(0) == 0)
    def _():
        sums_ref[...] = before_ref[...]

    scale = HEAD_DIM**-0.5

    def segment(s, carry):
        rows = pl.ds(pl.multiple_of(s * SEG_LEN, SEG_LEN), SEG_LEN)
        for pair in range(PAIRS):
            queries = both_heads(packed_ref[rows, third(0, pair)] * jnp.bfloat16(scale))
            k = packed_ref[rows, third(1, pair)]
            grads = both_heads(da_ref[rows, pair * LANES : (pair + 1) * LANES])
            log_sum = jnp.concatenate(
                [stat_ref[pl.ds(s * STATS + 2 * pair + head, 1), :] for head in range(2)], axis=1
            )
            weights = jnp.exp(dot_nt(k, queries) - log_sum)
            grad_weights = dot_nt(packed_ref[rows, third(2, pair)], grads)
            inner = jnp.sum(grad_weights * weights, axis=0, keepdims=True)
            ds = low(weights * (grad_weights - inner))
            dv = dot_nn(low(weights), grads)
            dk = dot_nn(ds, queries)
            dq = dot_tn(stacked_heads(ds), both_heads(k)) * scale
            for part, grad in enumerate((dq, dk, dv)):
                grad = low(grad)
                dqkv_ref[rows, third(part, pair)] = grad
                if part != 1:
                    here = (slice(part // 2, part // 2 + 1), third(0, pair))
                    sums_ref[here] += jnp.sum(grad.astype(jnp.float32), axis=0, keepdims=True)
        return carry

    lax.fori_loop(0, TILE // SEG_LEN, segment, 0, unroll=2)


def attend_back(packed, stat, da, first, count, previous=None):
    n = packed.shape[0]
    before = previous[1] if previous else jnp.zeros((8, D), jnp.float32)
    return in_parts(
        attend_back_kernel,
        10 * count,
        count,
        [packed, stat, da, before],
        [tiles(3 * D, first), stat_tiles(first), tiles(D, first), fixed((8, D))],
        [jax.ShapeDtypeStruct((n, 3 * D), jnp.bfloat16), jax.ShapeDtypeStruct((8, D), jnp.float32)],
        [tiles(3 * D, first), pl.BlockSpec((8, D), lambda i: (0, 0))],
        [],
        previous and previous[:1],
    )


def cross_kernel(
    load, rows_ref, tagc_ref, tagr_ref, gz_ref, wqkv_ref, wout_ref, wup_ref, wdown_ref, vec_ref,
    out_ref, grows_ref, sums_ref, gqkv_ref, go_ref, gu_ref, gm_ref, rowst_ref, attt_ref, hidt_ref, actt_ref,
    packed_ref, weights_ref, att_ref, act_ref, slope_ref, res_ref,
):
    scale = HEAD_DIM**-0.5
    rows = rows_ref[...]
    rowst_ref[...] = rows.T
    same = tagc_ref[:, 0:1] == tagr_ref[0:1, :]
    same = jnp.concatenate([same, same], axis=0)

    def add_sum(row, values):
        sums_ref[row : row + 1, :] = jnp.sum(values.astype(jnp.float32), axis=0, keepdims=True)

    def pair_cols(pair):
        return slice(pair * LANES, (pair + 1) * LANES)

    sums_ref[...] = jnp.zeros_like(sums_ref)
    load(0)
    for j in range(3):
        cols = slice(j * D, (j + 1) * D)
        part = dot_nn(rows, wqkv_ref[:, cols])
        packed_ref[:, cols] = low(part if j == 1 else part + vec_ref[j // 2 : j // 2 + 1, :])
    for pair in range(PAIRS):
        q = packed_ref[:, third(0, pair)] * jnp.bfloat16(scale)
        scores = jnp.where(same, dot_nt(both_heads(q), packed_ref[:, third(1, pair)]), NEGATIVE)
        raised = jnp.exp(scores - jnp.max(scores, axis=-1, keepdims=True))
        weights = raised * (1.0 / jnp.sum(raised, axis=-1, keepdims=True))
        weights_ref[pair] = weights
        blend = dot_nn(side_by_side(low(weights)), both_heads(packed_ref[:, third(2, pair)]))
        att_ref[:, pair_cols(pair)] = low(blend)
    att = att_ref[...]
    attt_ref[...] = att.T
    load(1)
    resid = rows.astype(jnp.float32) + dot_nn(att, wout_ref[...]) + vec_ref[2:3, :]
    hidden, normal_three, rate_three = norm_rows(resid, vec_ref[3:4, :], vec_ref[4:5, :])
    hidden_low = low(hidden)
    hidt_ref[...] = hidden_low.T
    load(2)
    res_ref[...] = hidden + vec_ref[9:10, :]
    for j in range(FF // FBLOCK):
        cols = slice(j * FBLOCK, (j + 1) * FBLOCK)
        act, slope = gelu_pair(dot_nn(hidden_low, wup_ref[:, cols]) + vec_ref[5 + j : 6 + j, :])
        act = low(act)
        actt_ref[cols, :] = act.T
        slope_ref[:, cols] = slope
        res_ref[...] += dot_nn(act, wdown_ref[cols, :])
    crossed, normal_four, rate_four = norm_rows(res_ref[...], vec_ref[10:11, :], vec_ref[11:12, :])
    out_ref[...] = low(crossed)

    grad_z = gz_ref[...].astype(jnp.float32)
    add_sum(10, grad_z * normal_four)
    add_sum(11, grad_z)
    grad_four = norm_pull(grad_z, normal_four, rate_four, vec_ref[10:11, :])
    grad_m = low(grad_four)
    gm_ref[...] = grad_m
    add_sum(9, grad_m)
    res_ref[...] = grad_four
    for j in range(FF // FBLOCK):
        cols = slice(j * FBLOCK, (j + 1) * FBLOCK)
        grad_u = low(dot_nt(grad_m, wdown_ref[cols, :]) * slope_ref[:, cols])
        gu_ref[:, cols] = grad_u
        add_sum(5 + j, grad_u)
        res_ref[...] += dot_nt(grad_u, wup_ref[:, cols])
    grad_h = res_ref[...]
    add_sum(3, grad_h * normal_three)
    add_sum(4, grad_h)
    grad_three = norm_pull(grad_h, normal_three, rate_three, vec_ref[3:4, :])
    grad_o = low(grad_three)
    go_ref[...] = grad_o
    add_sum(2, grad_o)
    res_ref[...] = grad_three
    att_ref[...] = low(dot_nt(grad_o, wout_ref[...]))
    for pair in range(PAIRS):
        queries = both_heads(packed_ref[:, third(0, pair)] * jnp.bfloat16(scale))
        grads = both_heads(att_ref[:, pair_cols(pair)])
        weights = weights_ref[pair]
        grad_weights = dot_nt(grads, packed_ref[:, third(2, pair)])
        dv = dot_tn(low(weights), grads)
        inner = jnp.sum(grad_weights * weights, axis=-1, keepdims=True)
        ds = low(weights * (grad_weights - inner))
        dq = dot_nn(side_by_side(ds), both_heads(packed_ref[:, third(1, pair)])) * scale
        dk = dot_tn(ds, queries)
        for part, grad in enumerate((dq, dk, dv)):
            gqkv_ref[:, third(part, pair)] = low(grad)
    add_sum(0, gqkv_ref[:, :D])
    add_sum(1, gqkv_ref[:, 2 * D :])
    for j in range(3):
        cols = slice(j * D, (j + 1) * D)
        res_ref[...] += dot_nt(gqkv_ref[:, cols], wqkv_ref[:, cols])
    grows_ref[...] = low(res_ref[...])


def cross_layer(cls, places, tags, grad_out, weights, coords, pack, seg):
    m = cls.shape[0]
    bf, f32 = jnp.bfloat16, jnp.float32
    tagc = jnp.broadcast_to(tags.astype(f32)[:, None], (m, LANES))
    tagr = jnp.broadcast_to(tags.astype(f32)[None, :], (8, m))
    placer = jnp.broadcast_to(places.astype(f32)[None, :], (8, m))
    count = len(weights.operands)
    operands = [cls, tagc, tagr, grad_out, placer]
    shapes = [
        (VECTOR_ROWS, D), (m, 3 * D), (m, D), (m, FF), (m, D), (D, m), (D, m), (D, m), (FF, m),
    ]
    matrices = [number for number, item in enumerate(weights.items) if item.cols]
    vectors = [number for number, item in enumerate(weights.items) if not item.cols]
    needs = [(matrices[:1], vectors[:1]), (matrices[1:2], vectors[1:2]), (matrices[2:], vectors[2:])]
    rows_of = {number: row for number, row in zip(vectors, (0, 2, 5, 9))}
    inner = [
        pltpu.VMEM((m, 3 * D), bf),
        pltpu.VMEM((PAIRS, 2 * m, m), f32),
        pltpu.VMEM((m, D), bf),
        pltpu.VMEM((m, D), bf),
        pltpu.VMEM((m, FF), f32),
        pltpu.VMEM((m, D), f32),
    ]
    held_shapes = [pltpu.VMEM(weights.items[number].shape, bf) for number in matrices]

    def kernel(seg_ref, coords_ref, *refs):
        refs = list(refs)

        def take(n):
            taken, refs[:] = refs[:n], refs[n:]
            return taken

        sources, ins, outs = take(count), take(len(operands)), take(3)
        kept, scratch, held = take(len(shapes)), take(len(inner)), take(len(matrices))
        (vec_ref, hot_ref), (staged, wide, sems), packing = take(2), take(3), take(3)
        waited = set()
        weights.start(coords_ref, sources, staged, sems)

        def load(stage):
            for number in needs[stage][0]:
                weights.wait(number, waited, staged, sems)
                weights.matrix(number, staged, wide, held[matrices.index(number)])
            for number in needs[stage][1]:
                weights.wait(number, waited, staged, sems)
                weights.vectors(number, staged, wide, vec_ref, rows_of[number])

        vec_ref[...] = jnp.zeros_like(vec_ref)
        cross_kernel(load, *ins[:4], *held, vec_ref, *outs[:2], *kept, *scratch)
        places_at = lax.broadcasted_iota(jnp.int32, (LONG_SEGS, m), 0).astype(f32)
        hot_ref[...] = jnp.where(places_at == ins[4][0:1, :], 1.0, 0.0).astype(bf)
        sums_ref, gqkv, go, gu, gm, rows_t, att_t, hid_t, act_t = kept
        names = [item_name(i) for i in (8, 9, 11, 13, 15)]
        pack.run(
            seg_ref[0],
            dict(zip(names, (hot_ref, rows_t, att_t, hid_t, act_t))),
            dict(zip(names, (outs[1], gqkv, go, gu, gm))),
            sums_ref,
            {item_name(i): row for i, row in ((10, 0), (12, 2), (14, 5), (16, 9))},
            outs[2],
            *packing,
        )

    return ordered(
        kernel,
        out_shape=[jax.ShapeDtypeStruct((m, D), bf)] * 2 + [pack.out],
        in_specs=[spec_smem()] * 2 + [spec_hbm()] * count + [spec_vmem()] * len(operands),
        out_specs=[spec_vmem()] * 3,
        scratch_shapes=[pltpu.VMEM(shape, f32 if i == 0 else bf) for i, shape in enumerate(shapes)]
        + inner
        + held_shapes
        + [pltpu.VMEM((VECTOR_ROWS, D), f32), pltpu.VMEM((LONG_SEGS, m), bf)]
        + weights.scratch
        + pack.scratch,
        compiler_params=kernel_params(62),
        cost_estimate=cost(30),
    )(seg, coords, *weights.operands, *operands)


def class_rows(cls, cot, hot, doc, pos, weights, coords):
    count = len(weights.operands)
    segs = cls.shape[0]

    def kernel(coords_ref, *refs):
        sources, (cls_ref, cot_ref, hot_ref, doc_ref, pos_ref, out_ref, wide_out, table, staged, wide, sems) = (
            refs[:count],
            refs[count:],
        )
        weights.start(coords_ref, sources, staged, sems)
        lanes = lax.broadcasted_iota(jnp.int32, (1, LANES), 1)
        for s in range(segs):
            wide_out[s : s + 1, D : 2 * D] = cot_ref[s, 0:1, :].astype(jnp.float32)
            tag = jnp.where(lanes == 0, doc_ref[s], jnp.where(lanes == 1, pos_ref[s], 0))
            wide_out[s : s + 1, 2 * D :] = tag.astype(jnp.float32)
        weights.wait(0, set(), staged, sems)
        weights.matrix(0, staged, wide, table)
        wide_out[:, :D] = cls_ref[...] + dot_nn(hot_ref[...], table[...])
        out_ref[...] = low(wide_out[...])

    def whole(shape):
        return pl.BlockSpec(shape, lambda i: (0,) * len(shape))

    return ordered(
        kernel,
        grid=(1,),
        out_shape=jax.ShapeDtypeStruct((segs, 2 * D + LANES), jnp.bfloat16),
        in_specs=[spec_smem()] + [spec_hbm()] * count
        + [whole(cls.shape), whole((segs, BLK, D)), whole(hot.shape), spec_smem(), spec_smem()],
        out_specs=whole((segs, 2 * D + LANES)),
        scratch_shapes=[
            pltpu.VMEM((segs, 2 * D + LANES), jnp.float32),
            pltpu.VMEM((LONG_SEGS, D), jnp.bfloat16),
        ]
        + weights.scratch,
        compiler_params=kernel_params(60),
        cost_estimate=cost(3),
    )(coords, *weights.operands, cls, cot, hot, doc, pos)


def token_back(grad_one, dqkv, w_qkv, first, count, previous=None):
    n = grad_one.shape[0]

    def kernel(one_ref, dqkv_ref, wqkv_ref, *refs):
        total = one_ref[...]
        for j in range(3):
            cols = slice(j * D, (j + 1) * D)
            total = total + dot_nt(dqkv_ref[:, cols], wqkv_ref[:, cols])
        refs[-1][...] = low(total)

    return in_parts(
        kernel,
        3 * count,
        count,
        [grad_one, dqkv, w_qkv],
        [tiles(D, first), tiles(3 * D, first), fixed((D, 3 * D))],
        [jax.ShapeDtypeStruct((n, D), jnp.bfloat16)],
        [tiles(D, first)],
        [],
        previous,
    )
AXES = ("seg", "doc")


def send(geo, value, axis, step):
    return lax.ppermute(value, AXES, geo.shift(axis, step))


def along_z(geo, value):
    return [value] + [send(geo, value, Z, r) for r in range(1, geo.n_doc)]


STEPS = 4


def slab(place, rows):
    return pl.BlockSpec((pl.squeezed, rows, LANES), lambda i: (place, i, 0))


def flat_call(kernel, inputs, outs, micros=2):
    arrays, specs = [], []
    for value, places in inputs:
        rows = value.size // LANES // places
        for place in range(places):
            arrays.append(value.reshape(places, rows, LANES))
            specs.append(slab(place, rows // STEPS))
    shapes, out_specs = [], []
    for shape, places in outs:
        rows = math.prod(shape) // LANES // max(places, 1)
        shapes.append(jax.ShapeDtypeStruct((max(places, 1), rows, LANES), jnp.bfloat16))
        out_specs.append(pl.BlockSpec((max(places, 1), rows // STEPS, LANES), lambda i: (0, i, 0)))
    results = ordered(
        kernel,
        grid=(STEPS,),
        out_shape=shapes,
        in_specs=specs,
        out_specs=out_specs,
        compiler_params=kernel_params(24),
        cost_estimate=cost(micros),
    )(*arrays)
    return [value.reshape(shape) for value, (shape, _) in zip(results, outs)]


def gather_plane(geo, halves, step):
    orders = ((X, Y), (Y, X))
    inputs, outs = [], []
    for half, order in zip(halves, orders):
        came = [send(geo, half, order[step], r) for r in range(1, geo.size(order[step]))]
        inputs += [(value, 1) for value in [half] + came]
        outs.append(((1 + len(came),) + half.shape, 1 + len(came)))

    def kernel(*refs):
        sources, targets = refs[: len(inputs)], refs[len(inputs) :]
        for target, (_, places) in zip(targets, outs):
            for place in range(places):
                target[place] = sources[place][...]
            sources = sources[places:]

    return flat_call(kernel, inputs, outs)


def gather_cores(geo, halves):
    return [array for half in halves for array in (half, send(geo, half, C, 1))]


def reduce_cores(geo, arrays):
    return [[arrays[2 * half], send(geo, arrays[2 * half + 1], C, 1)] for half in range(2)]


def added(sources):
    return low(sum(source[...].astype(jnp.float32) for source in sources))


def reduce_plane(geo, groups, step):
    orders = ((Y, X), (X, Y))
    inputs, outs, jobs = [], [], []
    for halves, step in zip(groups, step):
        for half, order in zip(halves, orders):
            places = geo.size(order[step])
            inputs += [(value, places) for value in half]
            outs += [(half[0].shape[1:], 0)] * places
            jobs.append((len(half), places, order[step]))

    def kernel(*refs):
        count = sum(places for _, places in inputs)
        sources, targets = refs[:count], refs[count:]
        for terms, places, _ in jobs:
            for place in range(places):
                targets[place][0] = added(sources[place : terms * places : places])
            sources, targets = sources[terms * places :], targets[places:]

    results = flat_call(kernel, inputs, outs)
    reduced = []
    for _, places, axis in jobs:
        mine, results = results[:places], results[places:]
        reduced.append([mine[0]] + [send(geo, mine[r], axis, r) for r in range(1, places)])
    return [reduced[2 * i : 2 * i + 2] for i in range(len(groups))]


def reduce_line(geo, halves, my_z):
    nd = geo.n_doc
    inputs = [value for half in halves for value in half]
    count = inputs[0].shape[0] // nd
    rows = [half[0].shape[1] for half in halves]

    def kernel(z_ref, *refs):
        sources, targets = refs[: len(inputs)], refs[len(inputs) :]
        done = 0
        for half, n in zip(halves, rows):
            terms, sources = sources[: len(half)], sources[len(half) :]
            for r in range(nd):
                z = wrap(z_ref[0] + r, nd)
                for s in range(count):
                    total = sum(term[s * nd + z].astype(jnp.float32) for term in terms)
                    targets[r][s, done : done + n] = low(total)
            done += n

    outs = ordered(
        kernel,
        out_shape=[jax.ShapeDtypeStruct((count, geo.share, LANES), jnp.bfloat16)] * nd,
        in_specs=[spec_smem()] + [spec_vmem()] * len(inputs),
        out_specs=[spec_vmem()] * nd,
        compiler_params=kernel_params(24),
        cost_estimate=cost(2),
    )(my_z.reshape(1), *inputs)
    return [outs[0]] + [send(geo, outs[r], Z, r) for r in range(1, nd)]


def sum_line(geo, line):
    def kernel(*refs):
        refs[-1][0] = added(refs[:-1])

    return flat_call(kernel, [(part, 1) for part in line], [(line[0].shape, 0)])[0]


def sum_all(geo, line, *others):
    count = line[0].shape[0]

    def kernel(*refs):
        sources, target = refs[:-1], refs[-1]
        target[:count] = added(sources[: len(line)])
        row = count
        for source in sources[len(line) :]:
            target[row : row + source.shape[0]] = source[...]
            row += source.shape[0]

    return ordered(
        kernel,
        out_shape=jax.ShapeDtypeStruct((geo.n_seg, geo.share, LANES), jnp.bfloat16),
        in_specs=[spec_vmem()] * (len(line) + len(others)),
        out_specs=spec_vmem(),
        compiler_params=kernel_params(),
        cost_estimate=cost(2),
    )(*line, *others)


def gate(value):
    def kernel(source, target):
        target[0] = source[...]

    return flat_call(kernel, [(value, 1)], [(value.shape, 0)])[0]
def row_rates(geo, n_tokens, n_cls):
    runs = []
    cross = list(LAYOUT)[-13:]
    row = 0
    for name, shape in LAYOUT.items():
        scale = 1.0 / math.sqrt(n_cls if name in cross else n_tokens)
        rate = 0.2
        if len(shape) == 2:
            rate = 1.0 if name == cross[0] else 0.5 / math.sqrt(shape[0])
        runs.append((row, scale, rate))
        row += math.prod(shape) // LANES
    runs.append((row, 0.0, 0.2))
    begins = [run[0] for run in runs] + [geo.chunk * geo.n_dev]
    found = []
    for n in range(geo.n_dev):
        lo, hi = n * geo.chunk, (n + 1) * geo.chunk
        found.append(
            [(max(run[0] - lo, 0), *run[1:]) for run, end in zip(runs, begins[1:]) if run[0] < hi and end > lo]
        )
    most = max(len(rows) for rows in found)
    found = [rows + [(geo.chunk, 0.0, 0.0)] * (most - len(rows)) for rows in found]
    return np.asarray(found, np.float32).transpose(0, 2, 1).copy()


def matmul(left, right):
    return jnp.dot(left, right, preferred_element_type=jnp.float32)


def column_sum(rows):
    return jnp.sum(rows.astype(jnp.float32), axis=0, keepdims=True)


def local(tokens, cotangent, seg_doc, seg_pos, master, momentum, average):
    n_seg = lax.axis_size(AXES[0])
    n_doc = lax.axis_size(AXES[1])
    geo = Geometry(n_seg, n_doc, master.shape[0])
    by = geo.by_name
    gather = Buckets(geo, [4, 4, 1], by.w_out, by.pos_table)
    buckets = Buckets(geo, [4, 4, 4, 1], by.w_out, by.w_down, by.pos_table)
    my_seg, my_doc = lax.axis_index(AXES[0]), lax.axis_index(AXES[1])
    me = my_seg * n_doc + my_doc
    coords = jnp.stack([my_seg // 4, my_seg // 2 % 2, my_seg % 2, my_doc]).astype(jnp.int32)
    table = lax.dynamic_index_in_dim(jnp.asarray(geo.block_tables()[1]), me, 0, False)
    pad_rows = ceil_to(geo.chunk + 4 * BLK, 8)
    ORDER.start()
    aligned = align_rows(geo, table, master.reshape(geo.chunk, LANES), pad_rows)
    shares = lax.all_to_all(aligned.reshape(geo.n_seg, geo.share, LANES), AXES[0], 0, 0, tiled=True)
    parts = [shares[span.start // n_doc : span.stop // n_doc] for span in gather.ranges]

    seg_count = tokens.shape[1]
    n_rows = n_seg * seg_count
    tiles_all = seg_count * SEG_LEN // TILE
    middle = max(1, tiles_all - 2)
    last = tiles_all - 1 - middle
    inputs = tokens[0].reshape(seg_count * SEG_LEN, D)
    cot_rows = cotangent[0]

    line = place_line(geo, along_z(geo, parts[0]), my_doc)
    parts_b = along_z(geo, parts[1])
    ORDER.wait_for(*parts_b[1:2])
    plane = gather_plane(geo, line, 0)
    ORDER.wait_for(*parts_b[2:3])
    plane = gather_plane(geo, plane, 1)
    gathered = [gather_cores(geo, plane), None, None]
    plane_b = place_line(geo, parts_b, my_doc)

    def weights(*numbers):
        return Weights(geo, gather, gathered, [item_name(i) for i in numbers])

    def own(values):
        return lax.dynamic_slice_in_dim(values, my_seg * seg_count, seg_count, axis=0)

    *outs, w_qkv, vec_a = attend_first(inputs, weights(0, 1), coords)
    plane_b = gather_plane(geo, plane_b, 0)
    gathered[2] = [lax.all_gather(gate(parts[2]), AXES)]
    outs = attend_layer(inputs, w_qkv, vec_a, 1, middle, outs)
    plane_b = gather_plane(geo, plane_b, 1)
    gathered[1] = gather_cores(geo, plane_b)
    if last:
        outs = attend_layer(inputs, w_qkv, vec_a, 1 + middle, last, outs)
    packed, attended, stat = outs
    hidden_low, normal_one, active, slope, normal_two, rates, hidden_two, cls, w_out, w_up, w_down, vec = feed_layer(
        inputs, attended, weights(1, 2, 3, 4, 5, 6, 7), coords
    )

    hot = (seg_pos[0][:, None] == jnp.arange(LONG_SEGS)[None, :]).astype(jnp.bfloat16)
    mine = class_rows(cls, cot_rows, hot, seg_doc[0], seg_pos[0], weights(8), coords)
    tagged = lax.all_gather(mine, AXES[0], axis=0, tiled=True)
    rows, all_grad, all_doc, all_pos = tagged[:, :D], tagged[:, D : 2 * D], tagged[:, 2 * D], tagged[:, 2 * D + 1]
    crossed, grad_rows, line_c = cross_layer(
        rows, all_pos, all_doc, all_grad, weights(9, 10, 11, 12, 13, 14, 15, 16), coords,
        CrossPack(geo, buckets.ranges[3], n_rows), my_seg.astype(jnp.int32).reshape(1),
    )
    line_c = reduce_line(geo, [[line_c]], my_doc)

    grads = {}
    dm, du, dao, da, grad_one, sums = feed_back(
        cot_rows.reshape(-1, D), own(grad_rows).astype(jnp.float32), normal_two, slope, normal_one, rates,
        w_down, w_up, w_out, vec,
    )
    sums_c = sum_line(geo, line_c)
    grads[item_name(8)] = low(matmul(hot.T, own(grad_rows)))
    for number, row in ((3, 2), (5, 5), (7, 9)):
        grads[item_name(number)] = (sums, row)
    *arrays_d, grads[item_name(6)] = grad_bucket(
        geo, buckets, 2, grads, coords, item_name(6), active, dm, 512, keep=True
    )
    halves_d = reduce_cores(geo, arrays_d)
    grads[item_name(2)] = low(matmul(attended.T, dao))
    ORDER.wait_for(grads[item_name(2)])
    halves_d, = reduce_plane(geo, [halves_d], [0])
    arrays_b = grad_bucket(geo, buckets, 1, grads, coords, item_name(4), hidden_low, du, 256)
    halves_b = reduce_cores(geo, arrays_b)
    back = attend_back(packed, stat, da, 0, 1)
    halves_d, halves_b = reduce_plane(geo, [halves_d, halves_b], [1, 0])
    if tiles_all > 1:
        back = attend_back(packed, stat, da, 1, middle, back)
    line_d = reduce_line(geo, halves_d, my_doc)
    halves_b, = reduce_plane(geo, [halves_b], [1])
    if last:
        back = attend_back(packed, stat, da, 1 + middle, last, back)
    dqkv, qv_sums = back
    sums_d = sum_line(geo, line_d)
    line_b = reduce_line(geo, halves_b, my_doc)
    grads[item_name(1)] = (qv_sums, 0)
    arrays_a = grad_bucket(geo, buckets, 0, grads, coords, item_name(0), inputs, dqkv, 256)
    halves_a = reduce_cores(geo, arrays_a)
    halves_a, = reduce_plane(geo, [halves_a], [0])
    token_grad, = token_back(grad_one, dqkv, w_qkv, 0, tiles_all)
    sums_b = sum_line(geo, line_b)
    halves_a, = reduce_plane(geo, [halves_a], [1])
    first_row = lax.broadcasted_iota(jnp.int32, (seg_count, SEG_LEN, D), 1) == 0
    mixed_out = jnp.where(
        first_row, own(crossed)[:, None, :], hidden_two.reshape(seg_count, SEG_LEN, D)
    )
    line_a = reduce_line(geo, halves_a, my_doc)
    owned = lax.all_to_all(
        sum_all(geo, line_a, sums_b, sums_d, sums_c), AXES[0], 0, 0, tiled=True
    )
    n_cls = n_doc * n_rows
    rates = lax.dynamic_index_in_dim(jnp.asarray(row_rates(geo, n_cls * SEG_LEN, n_cls)), me, 0, False)
    begins, factors = rates[0].astype(jnp.int32), rates[1:].reshape(-1)
    state = [value.reshape(geo.chunk, LANES) for value in (master, momentum, average)]
    weight, moment, smooth, copy_low = (
        value.reshape(-1)
        for value in update_rows(geo, table, owned.reshape(-1, LANES), begins, factors, state, pad_rows)
    )
    return (
        mixed_out[None],
        token_grad.reshape(1, seg_count, SEG_LEN, D),
        weight,
        moment,
        smooth,
        copy_low,
    )


def item_name(number):
    return item_list(0)[number].name


def solution(mesh):
    layer = P(AXES[1], AXES[0], None, None)
    ids = P(AXES[1], AXES[0])
    flat = P(AXES)
    return jax.shard_map(
        local,
        mesh=mesh,
        in_specs=(layer, layer, ids, ids, flat, flat, flat),
        out_specs=(layer, layer, flat, flat, flat, flat),
        check_vma=False,
    )
```

```python
import math
from types import SimpleNamespace

import jax
import jax.numpy as jnp
import numpy as np
from jax import lax
from jax.experimental import pallas as pl
from jax.experimental.pallas import tpu as pltpu
from jax.sharding import PartitionSpec as P

D = 768
HEADS = 12
HEAD_DIM = 64
FF = 3072
SEG_LEN = 128
LONG_SEGS = 64
EPSILON = 1e-05
NEGATIVE = -1e30

LAYOUT = dict(
    w_qkv=(D, 3 * D),
    b_qv=(2 * D,),
    w_out=(D, D),
    b_out=(D,),
    gain_one=(D,),
    bias_one=(D,),
    w_up=(D, FF),
    b_up=(FF,),
    w_down=(FF, D),
    b_down=(D,),
    gain_two=(D,),
    bias_two=(D,),
    pos_table=(LONG_SEGS, D),
    x_qkv=(D, 3 * D),
    x_bqv=(2 * D,),
    x_out=(D, D),
    x_bout=(D,),
    gain_three=(D,),
    bias_three=(D,),
    x_up=(D, FF),
    x_bup=(FF,),
    x_down=(FF, D),
    x_bdown=(D,),
    gain_four=(D,),
    bias_four=(D,),
)
LANES = 128
BLK = 16
Y, X, C, Z = range(4)


def ceil_to(value, step):
    return -(-value // step) * step


def item_list(total_rows):
    items = []
    nat = 0
    for name, shape in LAYOUT.items():
        rows = math.prod(shape) // LANES
        if len(shape) == 1 and items and len(items[-1].shape) == 1:
            items[-1].names.append(name)
            items[-1].rows += rows
        else:
            items.append(SimpleNamespace(name=name, names=[name], shape=shape, nat=nat, rows=rows))
        nat += rows
    items.append(SimpleNamespace(name=None, names=[], shape=None, nat=nat, rows=total_rows - nat))
    blk = 0
    for item in items:
        item.cols = item.shape[1] // LANES if item.shape and len(item.shape) == 2 else 0
        item.blk = blk
        blk += ceil_to(item.rows, BLK) // BLK
    return items


class Geometry:
    def __init__(self, n_seg, n_doc, shard_len):
        self.n_seg, self.n_doc = n_seg, n_doc
        self.n_dev = n_seg * n_doc
        self.chunk = shard_len // LANES
        self.items = item_list(self.chunk * self.n_dev)
        self.by_name = SimpleNamespace(**{item.name: item for item in self.items if item.name})
        firsts, lasts = [], []
        for n in range(self.n_dev):
            lo, hi = n * self.chunk, (n + 1) * self.chunk
            blocks = []
            for item in self.items:
                a, b = max(lo, item.nat), min(hi, item.nat + item.rows)
                if a < b:
                    blocks.append(item.blk + (a - item.nat) // BLK)
                    blocks.append(item.blk + (b - 1 - item.nat) // BLK)
            firsts.append(min(blocks))
            lasts.append(max(blocks))
        self.first, self.last = firsts, lasts
        most = max(b - a + 1 for a, b in zip(firsts, lasts))
        self.piece_blocks = -(-most // self.n_dev)
        self.piece = self.piece_blocks * BLK
        self.slots = self.piece_blocks * self.n_dev
        self.groups = -(-most // (self.piece_blocks * n_doc))
        self.share = n_doc * self.piece
        self.staged_rows = self.groups * self.share
        self.c_size, self.x_size = 2, 2
        self.y_size = n_seg // 4

    def full_groups(self, item, chunk):
        rows = BLK * item.cols
        lo, hi = chunk * self.chunk - item.nat, (chunk + 1) * self.chunk - item.nat
        first, last = max(0, -(-lo // rows)), min(item.rows, hi) // rows
        return first, max(first, last)

    def block_tables(self):
        matrices = [item for item in self.items if item.cols]
        single = [[] for _ in range(self.n_dev)]
        groups = np.zeros((self.n_dev, len(matrices), 3), np.int32)
        for n in range(self.n_dev):
            lo, hi = n * self.chunk, (n + 1) * self.chunk
            for t in range(self.slots):
                b = self.first[n] + t
                if b > self.last[n]:
                    single[n].append((t, 0, 0, 0))
                    continue
                item = [it for it in self.items if it.blk <= b][-1]
                at = b - item.blk
                if item.cols:
                    first, last = self.full_groups(item, n)
                    if first <= at // item.cols < last:
                        continue
                start = item.nat + at * BLK
                a = max(start, lo)
                z = max(a, min(start + BLK, hi, item.nat + item.rows))
                single[n].append((t, start - lo, a - start, z - start))
            for i, item in enumerate(matrices):
                first, last = self.full_groups(item, n)
                if first < last:
                    slot = item.blk + first * item.cols - self.first[n]
                    groups[n, i] = (slot, item.nat + first * BLK * item.cols - lo, last - first)
        most = max(len(rows) for rows in single)
        table = np.zeros((self.n_dev, 1 + 4 * most), np.int32)
        for n, rows in enumerate(single):
            table[n, 0] = len(rows)
            table[n, 1 : 1 + 4 * len(rows)] = np.asarray(rows, np.int32).reshape(-1)
        return matrices, np.concatenate([groups.reshape(self.n_dev, -1), table], axis=1)

    def chunks_of(self, item):
        found = []
        n_blocks = ceil_to(item.rows, BLK) // BLK
        for n in range(self.n_dev):
            a = max(item.blk, self.first[n])
            b = min(item.blk + n_blocks, self.last[n] + 1)
            if a < b:
                found.append((n, a - item.blk, b - item.blk, a - self.first[n]))
        return found

    def spans(self, *ends):
        cuts = [0] + [ceil_to((end.nat - 1) // self.chunk + 1, self.n_doc) for end in ends] + [self.n_dev]
        return [range(a, b) for a, b in zip(cuts, cuts[1:])]

    def coords(self, device):
        seg, doc = divmod(device, self.n_doc)
        yx, c = divmod(seg, self.c_size)
        return [*divmod(yx, self.x_size), c, doc]

    def device(self, y, x, c, z):
        return ((y * self.x_size + x) * self.c_size + c) * self.n_doc + z

    def size(self, axis):
        return (self.y_size, self.x_size, self.c_size, self.n_doc)[axis]

    def shift(self, axis, step):
        pairs = []
        for source in range(self.n_dev):
            at = self.coords(source)
            at[axis] = (at[axis] + step) % self.size(axis)
            pairs.append((source, self.device(*at)))
        return pairs
def spec_vmem():
    return pl.BlockSpec(memory_space=pltpu.VMEM)


def spec_any():
    return pl.BlockSpec(memory_space=pl.ANY)


def spec_hbm():
    return pl.BlockSpec(memory_space=pltpu.HBM)


def spec_smem():
    return pl.BlockSpec(memory_space=pltpu.SMEM)


def kernel_params(mib=20):
    return pltpu.CompilerParams(vmem_limit_bytes=mib * 1024 * 1024)


def cost(micros):
    micros = micros if micros >= 6 else 0
    return pl.CostEstimate(flops=int(micros * 1e9), bytes_accessed=int(micros * 3e6), transcendentals=0)


class Order:
    def start(self):
        self.token = jnp.zeros((8, LANES), jnp.float32)
        self.others = []

    def wait_for(self, *others):
        self.others += others


ORDER = Order()


def ordered(kernel, out_shape, in_specs, out_specs, **settings):
    single = not isinstance(out_shape, (list, tuple))
    outs, specs = ([out_shape], [out_specs]) if single else (list(out_shape), list(out_specs))

    def run(*inputs):
        extra = [ORDER.token] + ORDER.others
        n_in, n_out, n_extra = len(inputs), len(outs), len(extra)

        def wrapped(*refs):
            rest = refs[n_in + n_extra :]
            kernel(*refs[:n_in], *rest[:n_out], *rest[n_out + 1 :])

        results = pl.pallas_call(
            wrapped,
            out_shape=outs + [jax.ShapeDtypeStruct((8, LANES), jnp.float32)],
            in_specs=list(in_specs) + [spec_any()] * n_extra,
            out_specs=specs + [spec_any()],
            **settings,
        )(*inputs, *extra)
        ORDER.token, ORDER.others = results[-1], []
        return results[0] if single else results[:-1]

    return run


def row_mask(low, high):
    rows = lax.broadcasted_iota(jnp.int32, (BLK, LANES), 0)
    return (rows >= low) & (rows < high)


def block_moves(geo, table_ref, by_group, by_row):
    matrices = geo.block_tables()[0]
    for i, item in enumerate(matrices):
        def body(g, carry, i=i, cols=item.cols):
            for cb in range(cols):
                by_group(table_ref[3 * i] + g * cols + cb, table_ref[3 * i + 1] + g * BLK * cols + cb, cols)
            return carry

        lax.fori_loop(0, table_ref[3 * i + 2], body, 0)
    base = 3 * len(matrices)

    def single(r, carry):
        by_row(*[table_ref[base + 1 + 4 * r + j] for j in range(4)])
        return carry

    lax.fori_loop(0, table_ref[base], single, 0)


def block_at(slot):
    return pl.ds(pl.multiple_of(slot * BLK, BLK), BLK)


def align_rows(geo, table, natural, pad_rows):
    def kernel(table_ref, natural_ref, out_ref, rows_ref):
        def fill(row, rows):
            rows_ref[pl.ds(row + BLK, rows), :] = natural_ref[pl.ds(row, rows), :]

        copy_rows(natural.shape[0], 256, fill)

        def by_group(slot, start, cols):
            out_ref[block_at(slot), :] = rows_ref[pl.ds(start + BLK, BLK, stride=cols), :].astype(jnp.bfloat16)

        def by_row(slot, start, low_row, high_row):
            rows = jnp.where(row_mask(low_row, high_row), rows_ref[pl.ds(start + BLK, BLK), :], 0.0)
            out_ref[block_at(slot), :] = rows.astype(jnp.bfloat16)

        block_moves(geo, table_ref, by_group, by_row)

    return ordered(
        kernel,
        out_shape=jax.ShapeDtypeStruct((geo.slots * BLK, LANES), jnp.bfloat16),
        in_specs=[spec_smem(), spec_vmem()],
        out_specs=spec_vmem(),
        scratch_shapes=[pltpu.VMEM((pad_rows, LANES), jnp.float32)],
        compiler_params=kernel_params(),
        cost_estimate=cost(3),
    )(table, natural)


def update_rows(geo, table, blocks, begins, factors, state, pad_rows):
    rows_all = geo.chunk
    runs = begins.shape[0]

    def kernel(table_ref, begins_ref, factors_ref, blocks_ref, *refs):
        held, outs, grad_ref = refs[:3], refs[3:7], refs[7]

        def by_group(slot, start, cols):
            grad_ref[pl.ds(start + BLK, BLK, stride=cols), :] = blocks_ref[block_at(slot), :].astype(jnp.float32)

        def by_row(slot, start, low_row, high_row):
            here = pl.ds(start + BLK, BLK)
            rows = blocks_ref[block_at(slot), :].astype(jnp.float32)
            grad_ref[here, :] = jnp.where(row_mask(low_row, high_row), rows, grad_ref[here, :])

        block_moves(geo, table_ref, by_group, by_row)

        def step(row, rows):
            here = pl.ds(row, rows)
            at = lax.broadcasted_iota(jnp.int32, (rows, LANES), 0) + row
            scale = jnp.full((rows, LANES), factors_ref[0], jnp.float32)
            rate = jnp.full((rows, LANES), factors_ref[runs], jnp.float32)
            for run in range(1, runs):
                later = at >= begins_ref[run]
                scale = jnp.where(later, factors_ref[run], scale)
                rate = jnp.where(later, factors_ref[runs + run], rate)
            scaled = grad_ref[pl.ds(row + BLK, rows), :] * scale
            moment = 0.5 * held[1][here, :] + scaled
            weight = held[0][here, :] - rate * (scaled + 0.5 * moment)
            outs[0][here, :] = weight
            outs[1][here, :] = moment
            outs[2][here, :] = 0.5 * held[2][here, :] + 0.5 * weight
            outs[3][here, :] = weight.astype(jnp.bfloat16)

        copy_rows(rows_all, 128, step)

    full = [jax.ShapeDtypeStruct((rows_all, LANES), kind) for kind in (jnp.float32,) * 3 + (jnp.bfloat16,)]
    return ordered(
        kernel,
        out_shape=full,
        in_specs=[spec_smem()] * 3 + [spec_vmem()] * 4,
        out_specs=[spec_vmem()] * 4,
        scratch_shapes=[pltpu.VMEM((pad_rows, LANES), jnp.float32)],
        compiler_params=kernel_params(28),
        cost_estimate=cost(3),
    )(table, begins, factors, blocks, *state)


class Buckets:
    def __init__(self, geo, arrays, *ends):
        self.geo = geo
        self.ranges = geo.spans(*ends)
        self.arrays = arrays

    def find(self, chunk):
        for number, span in enumerate(self.ranges):
            if chunk in span:
                return number, chunk - span.start

    def shapes(self, number):
        geo = self.geo
        count = len(self.ranges[number])
        return [
            (geo.y_size, geo.x_size, count, geo.share // 2, LANES),
            (geo.x_size, geo.y_size, count, geo.share // 2, LANES),
        ]


def wrap(value, size):
    return lax.rem(value + size, size)


def copy_rows(count, step, body):
    full = count // step
    if full:
        def loop(i, carry):
            body(i * step, step)
            return carry

        lax.fori_loop(0, full, loop, 0)
    if count % step:
        body(full * step, count % step)


def place_line(geo, parts, my_z):
    count, nd = parts[0].shape[0], geo.n_doc
    rows = geo.share // 2

    def kernel(z_ref, *refs):
        sources, outs = refs[:nd], refs[nd:]
        for r in range(nd):
            z = wrap(z_ref[0] - r, nd)
            for s in range(count):
                for half in range(2):
                    outs[half][s * nd + z] = sources[r][s, half * rows : (half + 1) * rows]

    return ordered(
        kernel,
        out_shape=[jax.ShapeDtypeStruct((count * nd, rows, LANES), jnp.bfloat16)] * 2,
        in_specs=[spec_smem()] + [spec_vmem()] * nd,
        out_specs=[spec_vmem()] * 2,
        compiler_params=kernel_params(),
        cost_estimate=cost(2),
    )(my_z.reshape(1), *parts)
VECTOR_ROWS = 16


def chunk_copies(geo, buckets, sources, used, coords_ref, n, staged, sem):
    my_y, my_x, my_c = coords_ref[0], coords_ref[1], coords_ref[2]
    number, place = buckets.find(n)
    first = sum(buckets.arrays[m] for m in used[: used.index(number)])
    if buckets.arrays[number] == 1:
        line, z = divmod(place, geo.n_doc)
        for s in range(geo.groups):
            pltpu.make_async_copy(
                sources[first].at[s * geo.n_doc + z, line],
                staged.at[pl.ds(s * geo.share, geo.share)],
                sem,
            ).start()
        return
    rows = geo.share // 2
    for core in range(2):
        c = my_c if core == 0 else 1 - my_c
        for ry in range(geo.y_size):
            for rx in range(geo.x_size):
                y, x = wrap(my_y - ry, geo.y_size), wrap(my_x - rx, geo.x_size)
                s = (y * geo.x_size + x) * 2 + c

                def begin(s=s, ry=ry, rx=rx, core=core):
                    for half in range(2):
                        index = (ry, rx, place) if half == 0 else (rx, ry, place)
                        pltpu.make_async_copy(
                            sources[first + 2 * half + core].at[index],
                            staged.at[pl.ds(pl.multiple_of(s * geo.share + half * rows, BLK), rows)],
                            sem,
                        ).start()

                if geo.groups == geo.n_seg:
                    begin()
                else:
                    pl.when(s < geo.groups)(begin)


class Weights:
    def __init__(self, geo, buckets, gathered, names):
        self.geo, self.buckets = geo, buckets
        self.items = [vars(geo.by_name)[name] for name in names]
        self.chunks = sorted({n for item in self.items for n, *_ in geo.chunks_of(item)})
        self.used = sorted({buckets.find(n)[0] for n in self.chunks})
        self.operands = [array for number in self.used for array in gathered[number]]
        cols = max([item.cols for item in self.items])
        self.scratch = [
            pltpu.VMEM((len(self.chunks), geo.staged_rows, LANES), jnp.bfloat16),
            pltpu.VMEM((BLK * (cols + 2), LANES), jnp.float32),
            pltpu.SemaphoreType.DMA((len(self.chunks),)),
        ]

    def start(self, coords_ref, sources, staged, sems):
        for at, n in enumerate(self.chunks):
            chunk_copies(
                self.geo, self.buckets, sources, self.used, coords_ref, n, staged.at[at], sems.at[at]
            )

    def wait(self, number, waited, staged, sems):
        for n, *_ in self.geo.chunks_of(self.items[number]):
            at = self.chunks.index(n)
            if at not in waited:
                waited.add(at)
                pltpu.make_async_copy(staged.at[at], staged.at[at], sems.at[at]).wait()

    def blocks(self, item, lo, hi, staged, wide):
        done = lo
        for n, b0, b1, slot in self.geo.chunks_of(item):
            for b in range(max(b0, lo), min(b1, hi)):
                at = self.chunks.index(n)
                rows = staged[at, pl.ds((slot + b - b0) * BLK, BLK), :].astype(jnp.float32)
                here = pl.ds((b - lo) * BLK, BLK)
                wide[here, :] = wide[here, :] + rows if b < done else rows
            done = max(done, min(b1, hi))

    def matrix(self, number, staged, wide, out_ref):
        item = self.items[number]
        cols = item.cols
        split = set()
        for n, b0, b1, slot in self.geo.chunks_of(item):
            at = self.chunks.index(n)
            first, last = self.geo.full_groups(item, n)
            split |= set(range(b0 // cols, -(-b1 // cols))) - set(range(first, last))

            def group(g, carry, at=at, shift=slot - b0):
                rows = pl.ds(pl.multiple_of(g * BLK, BLK), BLK)
                for cb in range(cols):
                    tile = staged[at, block_at(g * cols + cb + shift), :]
                    out_ref[rows, cb * LANES : (cb + 1) * LANES] = tile
                return carry

            lax.fori_loop(first, last, group, 0)
        for g in sorted(split):
            self.blocks(item, g * cols, (g + 1) * cols, staged, wide)
            for cb in range(cols):
                tile = wide[pl.ds(cb, BLK, stride=cols), :]
                out_ref[g * BLK : (g + 1) * BLK, cb * LANES : (cb + 1) * LANES] = tile.astype(jnp.bfloat16)

    def vectors(self, number, staged, wide, out_ref, row):
        item = self.items[number]
        self.blocks(item, 0, ceil_to(item.rows, BLK) // BLK, staged, wide)
        for r in range(item.rows):
            v, cb = divmod(r, D // LANES)
            out_ref[row + v : row + v + 1, cb * LANES : (cb + 1) * LANES] = wide[r : r + 1, :]


def vector_rows(wide, values, first, count):
    lane_cols = D // LANES
    for r in range(count):
        v, cb = divmod(r, lane_cols)
        wide[r : r + 1, :] = values[first + v : first + v + 1, cb * LANES : (cb + 1) * LANES]


def bucket_parts(geo, span):
    parts = []
    for item in geo.items:
        chunks = [entry for entry in geo.chunks_of(item) if entry[0] in span]
        if chunks and item.names:
            parts.append((item, chunks))
    return parts


def grad_bucket(geo, buckets, number, grads, coords, name, left, right, rows, keep=False):
    span = buckets.ranges[number]
    parts = bucket_parts(geo, span)
    operands, specs, windows, scratch = [], [], [], []
    wide_rows = BLK
    for item, chunks in parts:
        if len(item.shape) == 2:
            cols = item.cols
            wide_rows = max(wide_rows, BLK * cols)
            if item.name == name:
                main, main_chunks, windows_at = item, chunks, len(windows)
                windows.append(None)
                continue
            k0 = min(b0 for _, b0, _, _ in chunks) // cols
            k1 = -(-max(b1 for _, _, b1, _ in chunks) // cols)
            operands.append(grads[item.name])
            specs.append(spec_any())
            windows.append((len(operands) - 1, k0, k1))
            scratch.append(pltpu.VMEM(((k1 - k0) * BLK, item.shape[1]), jnp.bfloat16))
        else:
            wide_rows = max(wide_rows, ceil_to(item.rows, BLK))
            operands.append(grads[item.name][0])
            specs.append(pl.BlockSpec(operands[-1].shape, lambda i: (0, 0)))
            windows.append((len(operands) - 1, None, None))
            scratch.append(pltpu.VMEM((BLK, LANES), jnp.bfloat16))
    outs = [shape for shape in buckets.shapes(number) for _ in range(2)]
    depth, width = main.shape
    cols = main.cols
    steps = depth // rows
    count = len(operands)
    block_groups = rows // BLK

    def split_groups(item, chunks):
        found = set()
        for n, b0, b1, _ in chunks:
            first, last = geo.full_groups(item, n)
            found |= set(range(b0 // item.cols, -(-b1 // item.cols))) - set(range(first, last))
        return sorted(found)

    def kernel(coords_ref, left_ref, right_ref, *refs):
        sources, targets = refs[:count], refs[count : count + 4]
        refs = refs[count + 4 :]
        if keep:
            kept_ref, refs = refs[0], refs[1:]
        loaded, (values, staged, wide, in_sems, out_sems) = refs[:count], refs[count:]
        step = pl.program_id(0)
        my_y, my_x, my_c = coords_ref[0], coords_ref[1], coords_ref[2]

        def send_out(n):
            _, place = buckets.find(n)
            half_rows = geo.share // 2
            for core in range(2):
                c = my_c if core == 0 else 1 - my_c
                for ry in range(geo.y_size):
                    for rx in range(geo.x_size):
                        y, x = wrap(my_y + ry, geo.y_size), wrap(my_x + rx, geo.x_size)
                        s = (y * geo.x_size + x) * 2 + c
                        for half in range(2):
                            index = (ry, rx, place) if half == 0 else (rx, ry, place)
                            here = pl.ds(pl.multiple_of(s * geo.share + half * half_rows, BLK), half_rows)
                            pltpu.make_async_copy(
                                staged.at[n - span.start, here],
                                targets[2 * half + core].at[index],
                                out_sems.at[n - span.start],
                            ).start()

        def whole(item, chunks, values, base, lo, hi):
            for n, b0, b1, slot in chunks:
                first, last = geo.full_groups(item, n)

                def group(g, carry, n=n, shift=slot - b0):
                    here = pl.ds(pl.multiple_of((g - base) * BLK, BLK), BLK)
                    for cb in range(item.cols):
                        dst = block_at(g * item.cols + cb + shift)
                        staged[n - span.start, dst, :] = values[here, cb * LANES : (cb + 1) * LANES]
                    return carry

                start = jnp.maximum(first, lo)
                lax.fori_loop(start, jnp.maximum(start, jnp.minimum(last, hi)), group, 0)

        def cut(item, chunks, values, base, g):
            for cb in range(item.cols):
                tile = values[pl.ds(pl.multiple_of((g - base) * BLK, BLK), BLK), cb * LANES : (cb + 1) * LANES]
                wide[pl.ds(cb, BLK, stride=item.cols), :] = tile.astype(jnp.float32)
            for n, b0, b1, slot in chunks:
                first, last = geo.full_groups(item, n)
                lo, hi = max(b0, g * item.cols), min(b1, (g + 1) * item.cols)
                if lo < hi and not first <= g < last:
                    part = wide[pl.ds((lo - g * item.cols) * BLK, (hi - lo) * BLK), :]
                    dst = pl.ds((slot + lo - b0) * BLK, (hi - lo) * BLK)
                    staged[n - span.start, dst, :] = part.astype(jnp.bfloat16)

        @pl.when(step == 0)
        def _():
            loads = {}
            for (item, chunks), window in zip(parts, windows):
                if window is not None and window[1] is not None:
                    at, k0, k1 = window
                    source = sources[at].at[pl.ds(k0 * BLK, (k1 - k0) * BLK)]
                    loads[at] = pltpu.make_async_copy(source, loaded[at], in_sems.at[at])
                    loads[at].start()

            def clear(row, size):
                for at in range(len(span)):
                    here = pl.ds(pl.multiple_of(row + tail, BLK), size)
                    staged[at, here, :] = jnp.zeros((size, LANES), jnp.bfloat16)

            tail = min(geo.last[n] - geo.first[n] for n in span) * BLK
            copy_rows(geo.slots * BLK - tail, 128, clear)
            for (item, chunks), window in zip(parts, windows):
                if window is None:
                    continue
                at, k0, k1 = window
                if k0 is None:
                    vector_rows(wide, sources[at], grads[item.name][1], item.rows)
                    for n, b0, b1, slot in chunks:
                        part = wide[pl.ds(b0 * BLK, (b1 - b0) * BLK), :].astype(jnp.bfloat16)
                        staged[n - span.start, pl.ds(slot * BLK, (b1 - b0) * BLK), :] = part
                else:
                    loads[at].wait()
                    whole(item, chunks, loaded[at], k0, k0, k1)
                    for g in split_groups(item, chunks):
                        cut(item, chunks, loaded[at], k0, g)

        values[...] = low(dot_tn(left_ref[...], right_ref[...]))
        if keep:
            kept_ref[...] = values[...]
        low_group = step * block_groups
        whole(main, main_chunks, values, low_group, low_group, low_group + block_groups)
        for g in split_groups(main, main_chunks):
            @pl.when(step == g // block_groups)
            def _(g=g):
                cut(main, main_chunks, values, g // block_groups * block_groups, g)

        ready = {n: 0 for n in span}
        for n, _, b1, _ in main_chunks:
            ready[n] = (b1 - 1) // cols // block_groups
        for at in range(steps):
            here = [n for n in span if ready[n] == at]
            if here:
                @pl.when(step == at)
                def _(here=here):
                    for n in here:
                        send_out(n)

        @pl.when(step == steps - 1)
        def _():
            for at in range(len(span)):
                pltpu.make_async_copy(staged.at[at], staged.at[at], out_sems.at[at]).wait()

    extra = [jax.ShapeDtypeStruct(main.shape, jnp.bfloat16)] if keep else []
    return ordered(
        kernel,
        grid=(steps,),
        out_shape=[jax.ShapeDtypeStruct(shape, jnp.bfloat16) for shape in outs] + extra,
        in_specs=[
            spec_smem(),
            pl.BlockSpec((left.shape[0], rows), lambda i: (0, i)),
            pl.BlockSpec(right.shape, lambda i: (0, 0), pipeline_mode=pl.Buffered(1)),
        ]
        + specs,
        out_specs=[spec_any()] * 4 + [pl.BlockSpec((rows, width), lambda i: (i, 0))] * len(extra),
        scratch_shapes=scratch
        + [
            pltpu.VMEM((rows, width), jnp.bfloat16),
            pltpu.VMEM((len(span), geo.slots * BLK, LANES), jnp.bfloat16),
            pltpu.VMEM((wide_rows + 2 * BLK, LANES), jnp.float32),
            pltpu.SemaphoreType.DMA((max(count, 1),)),
            pltpu.SemaphoreType.DMA((len(span),)),
        ],
        compiler_params=kernel_params(60),
        cost_estimate=cost(18),
    )(coords, left, right, *operands)


class CrossPack:
    def __init__(self, geo, span, depth_rows):
        self.geo, self.span = geo, span
        self.parts = bucket_parts(geo, span)
        self.seg_blocks = geo.n_doc * geo.piece_blocks
        wide_rows, flat_cols, left_rows = BLK, D, BLK
        for item, chunks in self.parts:
            if item.cols:
                left_rows = max(left_rows, len(chunks) * self.window(item))
                wide_rows = max(wide_rows, BLK * item.cols)
                flat_cols = max(flat_cols, item.shape[1])
            else:
                wide_rows = max(wide_rows, ceil_to(item.rows, BLK))
        self.out = jax.ShapeDtypeStruct((len(span), geo.share, LANES), jnp.bfloat16)
        self.scratch = [
            pltpu.VMEM((left_rows, depth_rows), jnp.bfloat16),
            pltpu.VMEM((left_rows, flat_cols), jnp.bfloat16),
            pltpu.VMEM((wide_rows + 2 * BLK, LANES), jnp.float32),
        ]

    def window(self, item):
        return min((-(-(self.seg_blocks - 1) // item.cols) + 1) * BLK, item.shape[0])

    def run(self, seg, lefts, rights, sums_ref, first_rows, out_ref, gathered, flat, wide):
        geo, span, seg_blocks = self.geo, self.span, self.seg_blocks
        low_slot = seg * seg_blocks
        out_ref[...] = jnp.zeros_like(out_ref)

        def slots(lo, hi):
            begin = jnp.maximum(low_slot, lo)
            return begin, jnp.maximum(begin, jnp.minimum(low_slot + seg_blocks, hi))

        def rows_out(n, slot, block, rows):
            begin, end = slots(slot, slot + rows)

            def move(t, carry):
                data = wide[block_at(block + t - slot), :]
                out_ref[n - span.start, block_at(t - low_slot), :] = data.astype(jnp.bfloat16)
                return carry

            lax.fori_loop(begin, end, move, 0)

        for item, chunks in self.parts:
            if not item.cols:
                vector_rows(wide, sums_ref, first_rows[item.name], item.rows)
                for n, b0, b1, slot in chunks:
                    rows_out(n, slot, b0, b1 - b0)
                continue
            cols = item.cols
            size = self.window(item)
            starts = []
            for at, (n, b0, b1, slot) in enumerate(chunks):
                first = jnp.maximum(low_slot, slot) - slot + b0
                start = pl.multiple_of(jnp.clip(first // cols * BLK, 0, item.shape[0] - size), BLK)
                starts.append(start)
                gathered[at * size : (at + 1) * size, :] = lefts[item.name][pl.ds(start, size), :]
            count = len(chunks) * size
            rows = gathered[:count, :]
            for cb in range(0, cols, 2):
                here = slice(cb * LANES, (cb + 2) * LANES)
                flat[:count, here] = dot_nn(rows, rights[item.name][:, here]).astype(jnp.bfloat16)
            for at, (n, b0, b1, slot) in enumerate(chunks):
                first, last = geo.full_groups(item, n)
                base = at * size - starts[at]

                def group_rows(group, base=base):
                    return pl.ds(pl.multiple_of(base + group * BLK, BLK), BLK)

                def by_tile(t, carry, n=n, shift=b0 - slot, group_rows=group_rows, cols=cols):
                    b = t + shift
                    group = b // cols
                    lanes = pl.ds(pl.multiple_of((b - group * cols) * LANES, LANES), LANES)
                    out_ref[n - span.start, block_at(t - low_slot), :] = flat[group_rows(group), lanes]
                    return carry

                if first < last:
                    begin, end = slots(slot + first * cols - b0, slot + last * cols - b0)
                    lax.fori_loop(begin, end, by_tile, 0)
                for g in range(b0 // cols, -(-b1 // cols)):
                    if first <= g < last:
                        continue
                    lo, hi = max(b0, g * cols), min(b1, (g + 1) * cols)
                    begin, end = slots(slot + lo - b0, slot + hi - b0)

                    @pl.when(begin < end)
                    def _(g=g, lo=lo, hi=hi, n=n, shift=slot - b0, group_rows=group_rows, cols=cols):
                        for cb in range(cols):
                            tile = flat[group_rows(g), cb * LANES : (cb + 1) * LANES]
                            wide[pl.ds(cb, BLK, stride=cols), :] = tile.astype(jnp.float32)
                        rows_out(n, lo + shift, lo - g * cols, hi - lo)
TILE = 512
PAIRS = HEADS // 2

def dot_nn(left, right):
    return lax.dot_general(left, right, (((1,), (0,)), ((), ())), preferred_element_type=jnp.float32)


def dot_nt(left, right):
    return lax.dot_general(left, right, (((1,), (1,)), ((), ())), preferred_element_type=jnp.float32)


def dot_tn(left, right):
    return lax.dot_general(left, right, (((0,), (0,)), ((), ())), preferred_element_type=jnp.float32)


def low(values):
    return values.astype(jnp.bfloat16)


def gelu_pair(u):
    spread = 0.5 + 0.5 * lax.erf(u * math.sqrt(0.5))
    return u * spread, spread + u * jnp.exp(-0.5 * (u * u)) * (1.0 / math.sqrt(2.0 * math.pi))


def norm_rows(values, gain, shift):
    center = values - jnp.mean(values, axis=-1, keepdims=True)
    rate = lax.rsqrt(jnp.mean(center * center, axis=-1, keepdims=True) + EPSILON)
    normal = center * rate
    return normal * gain + shift, normal, rate


def norm_pull(grad, normal, rate, gain):
    scaled = grad * gain
    return rate * (
        scaled
        - jnp.mean(scaled, axis=-1, keepdims=True)
        - normal * jnp.mean(scaled * normal, axis=-1, keepdims=True)
    )


def fixed(shape):
    return pl.BlockSpec(shape, lambda i: (0,) * len(shape), pipeline_mode=pl.Buffered(1))


def tiles(cols, first=0):
    return pl.BlockSpec((TILE, cols), lambda i: (i + first, 0))


def both_heads(values):
    first = lax.broadcasted_iota(jnp.int32, values.shape, 1) < HEAD_DIM
    zero = jnp.zeros_like(values)
    return jnp.concatenate([jnp.where(first, values, zero), jnp.where(first, zero, values)], axis=0)


def side_by_side(stacked):
    half = stacked.shape[0] // 2
    return jnp.concatenate([stacked[:half], stacked[half:]], axis=1)


def stacked_heads(values):
    half = values.shape[1] // 2
    return jnp.concatenate([values[:, :half], values[:, half:]], axis=0)


STATS = 16


def stat_tiles(first=0):
    return pl.BlockSpec((TILE // SEG_LEN * STATS, LANES), lambda i: (i + first, 0))


def third(part, pair):
    start = part * D + pair * LANES
    return slice(start, start + LANES)


def attend_kernel(x_ref, wqkv_ref, vec_ref, packed_ref, att_ref, stat_ref):
    x = x_ref[...]
    for j in range(3):
        cols = slice(j * D, (j + 1) * D)
        part = dot_nn(x, wqkv_ref[:, cols])
        packed_ref[:, cols] = low(part if j == 1 else part + vec_ref[j // 2 : j // 2 + 1, :])

    def segment(s, carry):
        rows = pl.ds(pl.multiple_of(s * SEG_LEN, SEG_LEN), SEG_LEN)
        for pair in range(PAIRS):
            queries = both_heads(packed_ref[rows, third(0, pair)] * jnp.bfloat16(HEAD_DIM**-0.5))
            values = both_heads(packed_ref[rows, third(2, pair)])
            scores = dot_nt(packed_ref[rows, third(1, pair)], queries)
            largest = jnp.max(scores, axis=0, keepdims=True)
            raised = jnp.exp(scores - largest)
            summed = jnp.sum(raised, axis=0, keepdims=True)
            weights = low(raised * (1.0 / summed))
            att_ref[rows, pair * LANES : (pair + 1) * LANES] = low(dot_tn(stacked_heads(weights), values))
            log_sum = largest + jnp.log(summed)
            for head in range(2):
                row = pl.ds(s * STATS + 2 * pair + head, 1)
                stat_ref[row, :] = log_sum[:, head * SEG_LEN : (head + 1) * SEG_LEN]
        return carry

    lax.fori_loop(0, TILE // SEG_LEN, segment, 0, unroll=2)


def in_parts(kernel, micros, count, inputs, in_specs, outs, out_specs, scratch, previous, mib=60):
    previous = list(previous or ())
    return ordered(
        kernel,
        grid=(count,),
        in_specs=in_specs + [spec_any()] * len(previous),
        out_specs=out_specs,
        out_shape=outs,
        scratch_shapes=scratch,
        input_output_aliases={len(inputs) + i: i for i in range(len(previous))},
        compiler_params=kernel_params(mib),
        cost_estimate=cost(micros),
    )(*inputs, *previous)


def attend_layer(x, w_qkv, vecs, first, count, previous):
    def rows(cols):
        return tiles(cols, first)

    def kernel(x_ref, wqkv_ref, vec_ref, *refs):
        attend_kernel(x_ref, wqkv_ref, vec_ref, *refs[-3:])

    return in_parts(
        kernel,
        0,
        count,
        [x, w_qkv, vecs],
        [rows(D), fixed((D, 3 * D)), fixed((VECTOR_ROWS, D))],
        [jax.ShapeDtypeStruct(v.shape, v.dtype) for v in previous],
        [rows(3 * D), rows(D), stat_tiles(first)],
        [],
        previous,
    )


def attend_first(x, weights, coords):
    n = x.shape[0]
    bf, f32 = jnp.bfloat16, jnp.float32
    count = len(weights.operands)

    def kernel(coords_ref, *refs):
        sources, x_ref, refs = refs[:count], refs[count], refs[count + 1 :]
        packed_ref, att_ref, stat_ref, wqkv_ref, vec_ref, staged, wide, sems = refs
        weights.start(coords_ref, sources, staged, sems)
        waited = set()
        for number in range(2):
            weights.wait(number, waited, staged, sems)
        weights.matrix(0, staged, wide, wqkv_ref)
        vec_ref[...] = jnp.zeros_like(vec_ref)
        weights.vectors(1, staged, wide, vec_ref, 0)
        attend_kernel(x_ref, wqkv_ref, vec_ref, packed_ref, att_ref, stat_ref)

    whole = [pl.BlockSpec(shape, lambda i: (0, 0)) for shape in ((D, 3 * D), (VECTOR_ROWS, D))]
    return ordered(
        kernel,
        grid=(1,),
        in_specs=[spec_smem()] + [spec_hbm()] * count + [tiles(D)],
        out_specs=[tiles(3 * D), tiles(D), stat_tiles()] + whole,
        out_shape=[
            jax.ShapeDtypeStruct((n, 3 * D), bf),
            jax.ShapeDtypeStruct((n, D), bf),
            jax.ShapeDtypeStruct((n // SEG_LEN * STATS, LANES), f32),
            jax.ShapeDtypeStruct((D, 3 * D), bf),
            jax.ShapeDtypeStruct((VECTOR_ROWS, D), f32),
        ],
        scratch_shapes=weights.scratch,
        compiler_params=kernel_params(60),
        cost_estimate=cost(0),
    )(coords, *weights.operands, x)


FBLOCK = D


def feed_kernel(
    x_ref, att_ref, wout_ref, wup_ref, wdown_ref, vec_ref,
    h1low_ref, norm1_ref, g_ref, dg_ref, norm2_ref, rate_ref, h2_ref, cls_ref, res_ref, h1_ref,
):
    step = pl.program_id(0)
    segs = TILE // SEG_LEN
    lanes = lax.broadcasted_iota(jnp.int32, (SEG_LEN, LANES), 1)
    res_ref[...] = dot_nn(att_ref[...], wout_ref[...])

    def start(s, carry):
        rows = pl.ds(pl.multiple_of(s * SEG_LEN, SEG_LEN), SEG_LEN)
        resid = x_ref[rows, :].astype(jnp.float32) + res_ref[rows, :] + vec_ref[2:3, :]
        hidden, normal, rate = norm_rows(resid, vec_ref[3:4, :], vec_ref[4:5, :])
        h1_ref[rows, :] = hidden
        h1low_ref[rows, :] = low(hidden)
        norm1_ref[rows, :] = low(normal)
        rate_ref[rows, :] = jnp.broadcast_to(rate, (SEG_LEN, LANES))
        return carry

    lax.fori_loop(0, segs, start, 0, unroll=2)
    h = h1low_ref[...]
    for j in range(FF // FBLOCK):
        cols = slice(j * FBLOCK, (j + 1) * FBLOCK)
        act, slope = gelu_pair(dot_nn(h, wup_ref[:, cols]) + vec_ref[5 + j : 6 + j, :])
        g = low(act)
        g_ref[:, cols] = g
        dg_ref[:, cols] = low(slope)
        part = dot_nn(g, wdown_ref[cols, :])
        if j == 0:
            res_ref[...] = part
        else:
            res_ref[...] += part

    def finish(s, carry):
        rows = pl.ds(pl.multiple_of(s * SEG_LEN, SEG_LEN), SEG_LEN)
        resid = h1_ref[rows, :] + res_ref[rows, :] + vec_ref[9:10, :]
        hidden, normal, rate = norm_rows(resid, vec_ref[10:11, :], vec_ref[11:12, :])
        h2_ref[rows, :] = low(hidden)
        norm2_ref[rows, :] = low(normal)
        rate_ref[rows, :] = jnp.where(lanes == 0, rate_ref[rows, :], rate)
        cls_ref[pl.ds(step * segs + s, 1), :] = hidden[0:1, :]
        return carry

    lax.fori_loop(0, segs, finish, 0, unroll=2)


def feed_layer(x, att, weights, coords):
    n = x.shape[0]
    bf, f32 = jnp.bfloat16, jnp.float32
    count = len(weights.operands)
    steps = n // TILE
    shapes = [item.shape for item in weights.items if item.cols]

    def kernel(coords_ref, *refs):
        sources, refs = refs[:count], refs[count:]
        x_ref, att_ref = refs[:2]
        outs, kept = refs[2:10], refs[10:13]
        vec_ref, res_ref, h1_ref, out_sems = refs[13:17]
        held, (staged, wide, sems) = refs[17:20], refs[20:]
        step = pl.program_id(0)

        @pl.when(step == 0)
        def _():
            weights.start(coords_ref, sources, staged, sems)
            waited = set()
            vec_ref[...] = jnp.zeros_like(vec_ref)
            place = row = 0
            for number, item in enumerate(weights.items):
                weights.wait(number, waited, staged, sems)
                if item.cols:
                    weights.matrix(number, staged, wide, held[place])
                    pltpu.make_async_copy(held[place], kept[place], out_sems.at[place]).start()
                    place += 1
                else:
                    weights.vectors(number, staged, wide, vec_ref, row)
                    row += item.rows * LANES // D

        feed_kernel(x_ref, att_ref, *held, vec_ref, *outs, res_ref, h1_ref)

        @pl.when(step == steps - 1)
        def _():
            for place in range(3):
                pltpu.make_async_copy(held[place], kept[place], out_sems.at[place]).wait()

    return ordered(
        kernel,
        grid=(steps,),
        in_specs=[spec_smem()] + [spec_hbm()] * count + [tiles(D), tiles(D)],
        out_specs=[tiles(D), tiles(D), tiles(FF), tiles(FF), tiles(D), tiles(LANES), tiles(D)]
        + [pl.BlockSpec((n // SEG_LEN, D), lambda i: (0, 0))]
        + [spec_any()] * 3
        + [pl.BlockSpec((VECTOR_ROWS, D), lambda i: (0, 0))],
        out_shape=[
            jax.ShapeDtypeStruct((n, cols), kind)
            for cols, kind in ((D, bf), (D, bf), (FF, bf), (FF, bf), (D, bf), (LANES, f32), (D, bf))
        ]
        + [jax.ShapeDtypeStruct((n // SEG_LEN, D), f32)]
        + [jax.ShapeDtypeStruct(shape, bf) for shape in shapes]
        + [jax.ShapeDtypeStruct((VECTOR_ROWS, D), f32)],
        scratch_shapes=[
            pltpu.VMEM((TILE, D), f32),
            pltpu.VMEM((TILE, D), f32),
            pltpu.SemaphoreType.DMA((3,)),
        ]
        + [pltpu.VMEM(shape, bf) for shape in shapes]
        + weights.scratch,
        compiler_params=kernel_params(62),
        cost_estimate=cost(60),
    )(coords, *weights.operands, x, att)


def feed_back_kernel(
    cot_ref, cls_ref, norm2_ref, dg_ref, norm1_ref, rate_ref,
    wdown_ref, wup_ref, wout_ref, vec_ref,
    dm_ref, du_ref, dao_ref, da_ref, one_ref, sums_ref, res_ref,
):
    step = pl.program_id(0)

    @pl.when(step == 0)
    def _():
        sums_ref[...] = jnp.zeros_like(sums_ref)

    segs = TILE // SEG_LEN
    row_ids = lax.broadcasted_iota(jnp.int32, (SEG_LEN, D), 0)

    def add_sum(row, values):
        sums_ref[row : row + 1, :] += jnp.sum(values, axis=0, keepdims=True)

    def start(s, carry):
        rows = pl.ds(pl.multiple_of(s * SEG_LEN, SEG_LEN), SEG_LEN)
        cls = cls_ref[pl.ds(step * segs + s, 1), :]
        grad = jnp.where(row_ids == 0, cls, cot_ref[rows, :].astype(jnp.float32))
        normal = norm2_ref[rows, :].astype(jnp.float32)
        add_sum(10, grad * normal)
        add_sum(11, grad)
        two = norm_pull(grad, normal, rate_ref[rows, 1:2], vec_ref[10:11, :])
        res_ref[rows, :] = two
        dm = low(two)
        dm_ref[rows, :] = dm
        add_sum(9, dm.astype(jnp.float32))
        return carry

    lax.fori_loop(0, segs, start, 0, unroll=2)
    dm = dm_ref[...]
    for j in range(FF // FBLOCK):
        cols = slice(j * FBLOCK, (j + 1) * FBLOCK)
        du = low(dot_nt(dm, wdown_ref[cols, :]) * dg_ref[:, cols].astype(jnp.float32))
        du_ref[:, cols] = du
        add_sum(5 + j, du.astype(jnp.float32))
        res_ref[...] += dot_nt(du, wup_ref[:, cols])

    def finish(s, carry):
        rows = pl.ds(pl.multiple_of(s * SEG_LEN, SEG_LEN), SEG_LEN)
        grad = res_ref[rows, :]
        normal = norm1_ref[rows, :].astype(jnp.float32)
        add_sum(3, grad * normal)
        add_sum(4, grad)
        one = norm_pull(grad, normal, rate_ref[rows, 0:1], vec_ref[3:4, :])
        one_ref[rows, :] = one
        dao = low(one)
        dao_ref[rows, :] = dao
        add_sum(2, dao.astype(jnp.float32))
        return carry

    lax.fori_loop(0, segs, finish, 0, unroll=2)
    da_ref[...] = low(dot_nt(dao_ref[...], wout_ref[...]))


def feed_back(cot, cls, norm2, dg, norm1, rates, w_down, w_up, w_out, vecs):
    n = cot.shape[0]
    bf, f32 = jnp.bfloat16, jnp.float32
    return ordered(
        feed_back_kernel,
        grid=(n // TILE,),
        in_specs=[
            tiles(D), fixed((n // SEG_LEN, D)), tiles(D), tiles(FF), tiles(D), tiles(LANES),
            fixed((FF, D)), fixed((D, FF)), fixed((D, D)), fixed((VECTOR_ROWS, D)),
        ],
        out_specs=[
            tiles(D), tiles(FF), tiles(D), tiles(D), tiles(D),
            pl.BlockSpec((VECTOR_ROWS, D), lambda i: (0, 0)),
        ],
        out_shape=[
            jax.ShapeDtypeStruct((n, D), bf),
            jax.ShapeDtypeStruct((n, FF), bf),
            jax.ShapeDtypeStruct((n, D), bf),
            jax.ShapeDtypeStruct((n, D), bf),
            jax.ShapeDtypeStruct((n, D), f32),
            jax.ShapeDtypeStruct((VECTOR_ROWS, D), f32),
        ],
        scratch_shapes=[pltpu.VMEM((TILE, D), f32)],
        compiler_params=kernel_params(60),
        cost_estimate=cost(44),
    )(cot, cls, norm2, dg, norm1, rates, w_down, w_up, w_out, vecs)


def attend_back_kernel(packed_ref, stat_ref, da_ref, before_ref, *refs):
    dqkv_ref, sums_ref = refs[-2:]

    @pl.when(pl.program_id(0) == 0)
    def _():
        sums_ref[...] = before_ref[...]

    scale = HEAD_DIM**-0.5

    def segment(s, carry):
        rows = pl.ds(pl.multiple_of(s * SEG_LEN, SEG_LEN), SEG_LEN)
        for pair in range(PAIRS):
            queries = both_heads(packed_ref[rows, third(0, pair)] * jnp.bfloat16(scale))
            k = packed_ref[rows, third(1, pair)]
            grads = both_heads(da_ref[rows, pair * LANES : (pair + 1) * LANES])
            log_sum = jnp.concatenate(
                [stat_ref[pl.ds(s * STATS + 2 * pair + head, 1), :] for head in range(2)], axis=1
            )
            weights = jnp.exp(dot_nt(k, queries) - log_sum)
            grad_weights = dot_nt(packed_ref[rows, third(2, pair)], grads)
            inner = jnp.sum(grad_weights * weights, axis=0, keepdims=True)
            ds = low(weights * (grad_weights - inner))
            dv = dot_nn(low(weights), grads)
            dk = dot_nn(ds, queries)
            dq = dot_tn(stacked_heads(ds), both_heads(k)) * scale
            for part, grad in enumerate((dq, dk, dv)):
                grad = low(grad)
                dqkv_ref[rows, third(part, pair)] = grad
                if part != 1:
                    here = (slice(part // 2, part // 2 + 1), third(0, pair))
                    sums_ref[here] += jnp.sum(grad.astype(jnp.float32), axis=0, keepdims=True)
        return carry

    lax.fori_loop(0, TILE // SEG_LEN, segment, 0, unroll=4)


def attend_back(packed, stat, da, first, count, previous=None):
    n = packed.shape[0]
    before = previous[1] if previous else jnp.zeros((8, D), jnp.float32)
    return in_parts(
        attend_back_kernel,
        10 * count,
        count,
        [packed, stat, da, before],
        [tiles(3 * D, first), stat_tiles(first), tiles(D, first), fixed((8, D))],
        [jax.ShapeDtypeStruct((n, 3 * D), jnp.bfloat16), jax.ShapeDtypeStruct((8, D), jnp.float32)],
        [tiles(3 * D, first), pl.BlockSpec((8, D), lambda i: (0, 0))],
        [],
        previous and previous[:1],
    )


def cross_kernel(
    load, rows_ref, tagc_ref, tagr_ref, gz_ref, wqkv_ref, wout_ref, wup_ref, wdown_ref, vec_ref,
    out_ref, grows_ref, sums_ref, gqkv_ref, go_ref, gu_ref, gm_ref, rowst_ref, attt_ref, hidt_ref, actt_ref,
    packed_ref, weights_ref, att_ref, act_ref, slope_ref, res_ref,
):
    scale = HEAD_DIM**-0.5
    rows = rows_ref[...]
    rowst_ref[...] = rows.T
    same = tagc_ref[:, 0:1] == tagr_ref[0:1, :]
    same = jnp.concatenate([same, same], axis=0)

    def add_sum(row, values):
        sums_ref[row : row + 1, :] = jnp.sum(values.astype(jnp.float32), axis=0, keepdims=True)

    def pair_cols(pair):
        return slice(pair * LANES, (pair + 1) * LANES)

    sums_ref[...] = jnp.zeros_like(sums_ref)
    load(0)
    for j in range(3):
        cols = slice(j * D, (j + 1) * D)
        part = dot_nn(rows, wqkv_ref[:, cols])
        packed_ref[:, cols] = low(part if j == 1 else part + vec_ref[j // 2 : j // 2 + 1, :])
    for pair in range(PAIRS):
        q = packed_ref[:, third(0, pair)] * jnp.bfloat16(scale)
        scores = jnp.where(same, dot_nt(both_heads(q), packed_ref[:, third(1, pair)]), NEGATIVE)
        raised = jnp.exp(scores - jnp.max(scores, axis=-1, keepdims=True))
        weights = raised * (1.0 / jnp.sum(raised, axis=-1, keepdims=True))
        weights_ref[pair] = weights
        blend = dot_nn(side_by_side(low(weights)), both_heads(packed_ref[:, third(2, pair)]))
        att_ref[:, pair_cols(pair)] = low(blend)
    att = att_ref[...]
    attt_ref[...] = att.T
    load(1)
    resid = rows.astype(jnp.float32) + dot_nn(att, wout_ref[...]) + vec_ref[2:3, :]
    hidden, normal_three, rate_three = norm_rows(resid, vec_ref[3:4, :], vec_ref[4:5, :])
    hidden_low = low(hidden)
    hidt_ref[...] = hidden_low.T
    load(2)
    res_ref[...] = hidden + vec_ref[9:10, :]
    for j in range(FF // FBLOCK):
        cols = slice(j * FBLOCK, (j + 1) * FBLOCK)
        act, slope = gelu_pair(dot_nn(hidden_low, wup_ref[:, cols]) + vec_ref[5 + j : 6 + j, :])
        act = low(act)
        actt_ref[cols, :] = act.T
        slope_ref[:, cols] = slope
        res_ref[...] += dot_nn(act, wdown_ref[cols, :])
    crossed, normal_four, rate_four = norm_rows(res_ref[...], vec_ref[10:11, :], vec_ref[11:12, :])
    out_ref[...] = low(crossed)

    grad_z = gz_ref[...].astype(jnp.float32)
    add_sum(10, grad_z * normal_four)
    add_sum(11, grad_z)
    grad_four = norm_pull(grad_z, normal_four, rate_four, vec_ref[10:11, :])
    grad_m = low(grad_four)
    gm_ref[...] = grad_m
    add_sum(9, grad_m)
    res_ref[...] = grad_four
    for j in range(FF // FBLOCK):
        cols = slice(j * FBLOCK, (j + 1) * FBLOCK)
        grad_u = low(dot_nt(grad_m, wdown_ref[cols, :]) * slope_ref[:, cols])
        gu_ref[:, cols] = grad_u
        add_sum(5 + j, grad_u)
        res_ref[...] += dot_nt(grad_u, wup_ref[:, cols])
    grad_h = res_ref[...]
    add_sum(3, grad_h * normal_three)
    add_sum(4, grad_h)
    grad_three = norm_pull(grad_h, normal_three, rate_three, vec_ref[3:4, :])
    grad_o = low(grad_three)
    go_ref[...] = grad_o
    add_sum(2, grad_o)
    res_ref[...] = grad_three
    att_ref[...] = low(dot_nt(grad_o, wout_ref[...]))
    for pair in range(PAIRS):
        queries = both_heads(packed_ref[:, third(0, pair)] * jnp.bfloat16(scale))
        grads = both_heads(att_ref[:, pair_cols(pair)])
        weights = weights_ref[pair]
        grad_weights = dot_nt(grads, packed_ref[:, third(2, pair)])
        dv = dot_tn(low(weights), grads)
        inner = jnp.sum(grad_weights * weights, axis=-1, keepdims=True)
        ds = low(weights * (grad_weights - inner))
        dq = dot_nn(side_by_side(ds), both_heads(packed_ref[:, third(1, pair)])) * scale
        dk = dot_tn(ds, queries)
        for part, grad in enumerate((dq, dk, dv)):
            gqkv_ref[:, third(part, pair)] = low(grad)
    add_sum(0, gqkv_ref[:, :D])
    add_sum(1, gqkv_ref[:, 2 * D :])
    for j in range(3):
        cols = slice(j * D, (j + 1) * D)
        res_ref[...] += dot_nt(gqkv_ref[:, cols], wqkv_ref[:, cols])
    grows_ref[...] = low(res_ref[...])


def cross_layer(cls, places, tags, grad_out, weights, coords, pack, seg):
    m = cls.shape[0]
    bf, f32 = jnp.bfloat16, jnp.float32
    tagc = jnp.broadcast_to(tags.astype(f32)[:, None], (m, LANES))
    tagr = jnp.broadcast_to(tags.astype(f32)[None, :], (8, m))
    placer = jnp.broadcast_to(places.astype(f32)[None, :], (8, m))
    count = len(weights.operands)
    operands = [cls, tagc, tagr, grad_out, placer]
    shapes = [
        (VECTOR_ROWS, D), (m, 3 * D), (m, D), (m, FF), (m, D), (D, m), (D, m), (D, m), (FF, m),
    ]
    matrices = [number for number, item in enumerate(weights.items) if item.cols]
    vectors = [number for number, item in enumerate(weights.items) if not item.cols]
    needs = [(matrices[:1], vectors[:1]), (matrices[1:2], vectors[1:2]), (matrices[2:], vectors[2:])]
    rows_of = {number: row for number, row in zip(vectors, (0, 2, 5, 9))}
    inner = [
        pltpu.VMEM((m, 3 * D), bf),
        pltpu.VMEM((PAIRS, 2 * m, m), f32),
        pltpu.VMEM((m, D), bf),
        pltpu.VMEM((m, D), bf),
        pltpu.VMEM((m, FF), f32),
        pltpu.VMEM((m, D), f32),
    ]
    held_shapes = [pltpu.VMEM(weights.items[number].shape, bf) for number in matrices]

    def kernel(seg_ref, coords_ref, *refs):
        refs = list(refs)

        def take(n):
            taken, refs[:] = refs[:n], refs[n:]
            return taken

        sources, ins, outs = take(count), take(len(operands)), take(3)
        kept, scratch, held = take(len(shapes)), take(len(inner)), take(len(matrices))
        (vec_ref, hot_ref), (staged, wide, sems), packing = take(2), take(3), take(3)
        waited = set()
        weights.start(coords_ref, sources, staged, sems)

        def load(stage):
            for number in needs[stage][0]:
                weights.wait(number, waited, staged, sems)
                weights.matrix(number, staged, wide, held[matrices.index(number)])
            for number in needs[stage][1]:
                weights.wait(number, waited, staged, sems)
                weights.vectors(number, staged, wide, vec_ref, rows_of[number])

        vec_ref[...] = jnp.zeros_like(vec_ref)
        cross_kernel(load, *ins[:4], *held, vec_ref, *outs[:2], *kept, *scratch)
        places_at = lax.broadcasted_iota(jnp.int32, (LONG_SEGS, m), 0).astype(f32)
        hot_ref[...] = jnp.where(places_at == ins[4][0:1, :], 1.0, 0.0).astype(bf)
        sums_ref, gqkv, go, gu, gm, rows_t, att_t, hid_t, act_t = kept
        names = [item_name(i) for i in (8, 9, 11, 13, 15)]
        pack.run(
            seg_ref[0],
            dict(zip(names, (hot_ref, rows_t, att_t, hid_t, act_t))),
            dict(zip(names, (outs[1], gqkv, go, gu, gm))),
            sums_ref,
            {item_name(i): row for i, row in ((10, 0), (12, 2), (14, 5), (16, 9))},
            outs[2],
            *packing,
        )

    return ordered(
        kernel,
        out_shape=[jax.ShapeDtypeStruct((m, D), bf)] * 2 + [pack.out],
        in_specs=[spec_smem()] * 2 + [spec_hbm()] * count + [spec_vmem()] * len(operands),
        out_specs=[spec_vmem()] * 3,
        scratch_shapes=[pltpu.VMEM(shape, f32 if i == 0 else bf) for i, shape in enumerate(shapes)]
        + inner
        + held_shapes
        + [pltpu.VMEM((VECTOR_ROWS, D), f32), pltpu.VMEM((LONG_SEGS, m), bf)]
        + weights.scratch
        + pack.scratch,
        compiler_params=kernel_params(62),
        cost_estimate=cost(30),
    )(seg, coords, *weights.operands, *operands)


def class_rows(cls, cot, hot, doc, pos, weights, coords):
    count = len(weights.operands)
    segs = cls.shape[0]

    def kernel(coords_ref, *refs):
        sources, (cls_ref, cot_ref, hot_ref, doc_ref, pos_ref, out_ref, wide_out, table, staged, wide, sems) = (
            refs[:count],
            refs[count:],
        )
        weights.start(coords_ref, sources, staged, sems)
        lanes = lax.broadcasted_iota(jnp.int32, (1, LANES), 1)
        for s in range(segs):
            wide_out[s : s + 1, D : 2 * D] = cot_ref[s, 0:1, :].astype(jnp.float32)
            tag = jnp.where(lanes == 0, doc_ref[s], jnp.where(lanes == 1, pos_ref[s], 0))
            wide_out[s : s + 1, 2 * D :] = tag.astype(jnp.float32)
        weights.wait(0, set(), staged, sems)
        weights.matrix(0, staged, wide, table)
        wide_out[:, :D] = cls_ref[...] + dot_nn(hot_ref[...], table[...])
        out_ref[...] = low(wide_out[...])

    def whole(shape):
        return pl.BlockSpec(shape, lambda i: (0,) * len(shape))

    return ordered(
        kernel,
        grid=(1,),
        out_shape=jax.ShapeDtypeStruct((segs, 2 * D + LANES), jnp.bfloat16),
        in_specs=[spec_smem()] + [spec_hbm()] * count
        + [whole(cls.shape), whole((segs, BLK, D)), whole(hot.shape), spec_smem(), spec_smem()],
        out_specs=whole((segs, 2 * D + LANES)),
        scratch_shapes=[
            pltpu.VMEM((segs, 2 * D + LANES), jnp.float32),
            pltpu.VMEM((LONG_SEGS, D), jnp.bfloat16),
        ]
        + weights.scratch,
        compiler_params=kernel_params(60),
        cost_estimate=cost(3),
    )(coords, *weights.operands, cls, cot, hot, doc, pos)


def token_back(grad_one, dqkv, w_qkv, first, count, previous=None):
    n = grad_one.shape[0]

    def kernel(one_ref, dqkv_ref, wqkv_ref, *refs):
        total = one_ref[...]
        for j in range(3):
            cols = slice(j * D, (j + 1) * D)
            total = total + dot_nt(dqkv_ref[:, cols], wqkv_ref[:, cols])
        refs[-1][...] = low(total)

    return in_parts(
        kernel,
        3 * count,
        count,
        [grad_one, dqkv, w_qkv],
        [tiles(D, first), tiles(3 * D, first), fixed((D, 3 * D))],
        [jax.ShapeDtypeStruct((n, D), jnp.bfloat16)],
        [tiles(D, first)],
        [],
        previous,
    )
AXES = ("seg", "doc")


def send(geo, value, axis, step):
    return lax.ppermute(value, AXES, geo.shift(axis, step))


def along_z(geo, value):
    return [value] + [send(geo, value, Z, r) for r in range(1, geo.n_doc)]


STEPS = 4


def slab(place, rows):
    return pl.BlockSpec((pl.squeezed, rows, LANES), lambda i: (place, i, 0))


def flat_call(kernel, inputs, outs, micros=2):
    arrays, specs = [], []
    for value, places in inputs:
        rows = value.size // LANES // places
        for place in range(places):
            arrays.append(value.reshape(places, rows, LANES))
            specs.append(slab(place, rows // STEPS))
    shapes, out_specs = [], []
    for shape, places in outs:
        rows = math.prod(shape) // LANES // max(places, 1)
        shapes.append(jax.ShapeDtypeStruct((max(places, 1), rows, LANES), jnp.bfloat16))
        out_specs.append(pl.BlockSpec((max(places, 1), rows // STEPS, LANES), lambda i: (0, i, 0)))
    results = ordered(
        kernel,
        grid=(STEPS,),
        out_shape=shapes,
        in_specs=specs,
        out_specs=out_specs,
        compiler_params=kernel_params(24),
        cost_estimate=cost(micros),
    )(*arrays)
    return [value.reshape(shape) for value, (shape, _) in zip(results, outs)]


def gather_plane(geo, halves, step):
    orders = ((X, Y), (Y, X))
    inputs, outs = [], []
    for half, order in zip(halves, orders):
        came = [send(geo, half, order[step], r) for r in range(1, geo.size(order[step]))]
        inputs += [(value, 1) for value in [half] + came]
        outs.append(((1 + len(came),) + half.shape, 1 + len(came)))

    def kernel(*refs):
        sources, targets = refs[: len(inputs)], refs[len(inputs) :]
        for target, (_, places) in zip(targets, outs):
            for place in range(places):
                target[place] = sources[place][...]
            sources = sources[places:]

    return flat_call(kernel, inputs, outs)


def gather_cores(geo, halves):
    return [array for half in halves for array in (half, send(geo, half, C, 1))]


def reduce_cores(geo, arrays):
    return [[arrays[2 * half], send(geo, arrays[2 * half + 1], C, 1)] for half in range(2)]


def added(sources):
    return low(sum(source[...].astype(jnp.float32) for source in sources))


def reduce_plane(geo, groups, step):
    orders = ((Y, X), (X, Y))
    inputs, outs, jobs = [], [], []
    for halves, step in zip(groups, step):
        for half, order in zip(halves, orders):
            places = geo.size(order[step])
            inputs += [(value, places) for value in half]
            outs += [(half[0].shape[1:], 0)] * places
            jobs.append((len(half), places, order[step]))

    def kernel(*refs):
        count = sum(places for _, places in inputs)
        sources, targets = refs[:count], refs[count:]
        for terms, places, _ in jobs:
            for place in range(places):
                targets[place][0] = added(sources[place : terms * places : places])
            sources, targets = sources[terms * places :], targets[places:]

    results = flat_call(kernel, inputs, outs)
    reduced = []
    for _, places, axis in jobs:
        mine, results = results[:places], results[places:]
        reduced.append([mine[0]] + [send(geo, mine[r], axis, r) for r in range(1, places)])
    return [reduced[2 * i : 2 * i + 2] for i in range(len(groups))]


def reduce_line(geo, halves, my_z):
    nd = geo.n_doc
    inputs = [value for half in halves for value in half]
    count = inputs[0].shape[0] // nd
    rows = [half[0].shape[1] for half in halves]

    def kernel(z_ref, *refs):
        sources, targets = refs[: len(inputs)], refs[len(inputs) :]
        done = 0
        for half, n in zip(halves, rows):
            terms, sources = sources[: len(half)], sources[len(half) :]
            for r in range(nd):
                z = wrap(z_ref[0] + r, nd)
                for s in range(count):
                    total = sum(term[s * nd + z].astype(jnp.float32) for term in terms)
                    targets[r][s, done : done + n] = low(total)
            done += n

    outs = ordered(
        kernel,
        out_shape=[jax.ShapeDtypeStruct((count, geo.share, LANES), jnp.bfloat16)] * nd,
        in_specs=[spec_smem()] + [spec_vmem()] * len(inputs),
        out_specs=[spec_vmem()] * nd,
        compiler_params=kernel_params(24),
        cost_estimate=cost(2),
    )(my_z.reshape(1), *inputs)
    return [outs[0]] + [send(geo, outs[r], Z, r) for r in range(1, nd)]


def sum_line(geo, line):
    def kernel(*refs):
        refs[-1][0] = added(refs[:-1])

    return flat_call(kernel, [(part, 1) for part in line], [(line[0].shape, 0)])[0]


def sum_all(geo, line, *others):
    count = line[0].shape[0]

    def kernel(*refs):
        sources, target = refs[:-1], refs[-1]
        target[:count] = added(sources[: len(line)])
        row = count
        for source in sources[len(line) :]:
            target[row : row + source.shape[0]] = source[...]
            row += source.shape[0]

    return ordered(
        kernel,
        out_shape=jax.ShapeDtypeStruct((geo.n_seg, geo.share, LANES), jnp.bfloat16),
        in_specs=[spec_vmem()] * (len(line) + len(others)),
        out_specs=spec_vmem(),
        compiler_params=kernel_params(),
        cost_estimate=cost(2),
    )(*line, *others)


def gate(value):
    def kernel(source, target):
        target[0] = source[...]

    return flat_call(kernel, [(value, 1)], [(value.shape, 0)])[0]


def turn():
    def kernel(target):
        target[...] = jnp.zeros_like(target)

    ordered(
        kernel,
        out_shape=jax.ShapeDtypeStruct((8, LANES), jnp.float32),
        in_specs=[],
        out_specs=spec_vmem(),
        compiler_params=kernel_params(),
        cost_estimate=cost(0),
    )()
def row_rates(geo, n_tokens, n_cls):
    runs = []
    cross = list(LAYOUT)[-13:]
    row = 0
    for name, shape in LAYOUT.items():
        scale = 1.0 / math.sqrt(n_cls if name in cross else n_tokens)
        rate = 0.2
        if len(shape) == 2:
            rate = 1.0 if name == cross[0] else 0.5 / math.sqrt(shape[0])
        runs.append((row, scale, rate))
        row += math.prod(shape) // LANES
    runs.append((row, 0.0, 0.2))
    begins = [run[0] for run in runs] + [geo.chunk * geo.n_dev]
    found = []
    for n in range(geo.n_dev):
        lo, hi = n * geo.chunk, (n + 1) * geo.chunk
        found.append(
            [(max(run[0] - lo, 0), *run[1:]) for run, end in zip(runs, begins[1:]) if run[0] < hi and end > lo]
        )
    most = max(len(rows) for rows in found)
    found = [rows + [(geo.chunk, 0.0, 0.0)] * (most - len(rows)) for rows in found]
    return np.asarray(found, np.float32).transpose(0, 2, 1).copy()


def matmul(left, right):
    return jnp.dot(left, right, preferred_element_type=jnp.float32)


def column_sum(rows):
    return jnp.sum(rows.astype(jnp.float32), axis=0, keepdims=True)


def local(tokens, cotangent, seg_doc, seg_pos, master, momentum, average):
    n_seg = lax.axis_size(AXES[0])
    n_doc = lax.axis_size(AXES[1])
    geo = Geometry(n_seg, n_doc, master.shape[0])
    by = geo.by_name
    gather = Buckets(geo, [4, 4, 1], by.w_out, by.pos_table)
    buckets = Buckets(geo, [4, 4, 4, 1], by.w_out, by.w_down, by.pos_table)
    my_seg, my_doc = lax.axis_index(AXES[0]), lax.axis_index(AXES[1])
    me = my_seg * n_doc + my_doc
    coords = jnp.stack([my_seg // 4, my_seg // 2 % 2, my_seg % 2, my_doc]).astype(jnp.int32)
    table = lax.dynamic_index_in_dim(jnp.asarray(geo.block_tables()[1]), me, 0, False)
    pad_rows = ceil_to(geo.chunk + 4 * BLK, 8)
    ORDER.start()
    aligned = align_rows(geo, table, master.reshape(geo.chunk, LANES), pad_rows)
    shares = lax.all_to_all(aligned.reshape(geo.n_seg, geo.share, LANES), AXES[0], 0, 0, tiled=True)
    parts = [shares[span.start // n_doc : span.stop // n_doc] for span in gather.ranges]

    seg_count = tokens.shape[1]
    n_rows = n_seg * seg_count
    tiles_all = seg_count * SEG_LEN // TILE
    middle = max(1, tiles_all - 2)
    last = tiles_all - 1 - middle
    inputs = tokens[0].reshape(seg_count * SEG_LEN, D)
    cot_rows = cotangent[0]

    line = place_line(geo, along_z(geo, parts[0]), my_doc)
    parts_b = along_z(geo, parts[1])
    ORDER.wait_for(*parts_b[1:2])
    plane = gather_plane(geo, line, 0)
    ORDER.wait_for(*parts_b[2:3])
    turn()
    plane_b = place_line(geo, parts_b, my_doc)
    plane = gather_plane(geo, plane, 1)
    gathered = [gather_cores(geo, plane), None, None]

    def weights(*numbers):
        return Weights(geo, gather, gathered, [item_name(i) for i in numbers])

    def own(values):
        return lax.dynamic_slice_in_dim(values, my_seg * seg_count, seg_count, axis=0)

    plane_b = gather_plane(geo, plane_b, 0)
    gathered[2] = [lax.all_gather(gate(parts[2]), AXES)]
    *outs, w_qkv, vec_a = attend_first(inputs, weights(0, 1), coords)
    outs = attend_layer(inputs, w_qkv, vec_a, 1, middle, outs)
    plane_b = gather_plane(geo, plane_b, 1)
    gathered[1] = gather_cores(geo, plane_b)
    if last:
        outs = attend_layer(inputs, w_qkv, vec_a, 1 + middle, last, outs)
    packed, attended, stat = outs
    hidden_low, normal_one, active, slope, normal_two, rates, hidden_two, cls, w_out, w_up, w_down, vec = feed_layer(
        inputs, attended, weights(1, 2, 3, 4, 5, 6, 7), coords
    )

    hot = (seg_pos[0][:, None] == jnp.arange(LONG_SEGS)[None, :]).astype(jnp.bfloat16)
    mine = class_rows(cls, cot_rows, hot, seg_doc[0], seg_pos[0], weights(8), coords)
    tagged = lax.all_gather(mine, AXES[0], axis=0, tiled=True)
    rows, all_grad, all_doc, all_pos = tagged[:, :D], tagged[:, D : 2 * D], tagged[:, 2 * D], tagged[:, 2 * D + 1]
    crossed, grad_rows, line_c = cross_layer(
        rows, all_pos, all_doc, all_grad, weights(9, 10, 11, 12, 13, 14, 15, 16), coords,
        CrossPack(geo, buckets.ranges[3], n_rows), my_seg.astype(jnp.int32).reshape(1),
    )
    line_c = reduce_line(geo, [[line_c]], my_doc)

    grads = {}
    dm, du, dao, da, grad_one, sums = feed_back(
        cot_rows.reshape(-1, D), own(grad_rows).astype(jnp.float32), normal_two, slope, normal_one, rates,
        w_down, w_up, w_out, vec,
    )
    sums_c = sum_line(geo, line_c)
    grads[item_name(8)] = low(matmul(hot.T, own(grad_rows)))
    for number, row in ((3, 2), (5, 5), (7, 9)):
        grads[item_name(number)] = (sums, row)
    *arrays_d, grads[item_name(6)] = grad_bucket(
        geo, buckets, 2, grads, coords, item_name(6), active, dm, 512, keep=True
    )
    halves_d = reduce_cores(geo, arrays_d)
    grads[item_name(2)] = low(matmul(attended.T, dao))
    ORDER.wait_for(grads[item_name(2)])
    halves_d, = reduce_plane(geo, [halves_d], [0])
    arrays_b = grad_bucket(geo, buckets, 1, grads, coords, item_name(4), hidden_low, du, 256)
    halves_b = reduce_cores(geo, arrays_b)
    back = attend_back(packed, stat, da, 0, 1)
    halves_d, halves_b = reduce_plane(geo, [halves_d, halves_b], [1, 0])
    if tiles_all > 1:
        back = attend_back(packed, stat, da, 1, middle, back)
    line_d = reduce_line(geo, halves_d, my_doc)
    halves_b, = reduce_plane(geo, [halves_b], [1])
    if last:
        back = attend_back(packed, stat, da, 1 + middle, last, back)
    dqkv, qv_sums = back
    sums_d = sum_line(geo, line_d)
    line_b = reduce_line(geo, halves_b, my_doc)
    grads[item_name(1)] = (qv_sums, 0)
    arrays_a = grad_bucket(geo, buckets, 0, grads, coords, item_name(0), inputs, dqkv, 256)
    halves_a = reduce_cores(geo, arrays_a)
    halves_a, = reduce_plane(geo, [halves_a], [0])
    token_grad, = token_back(grad_one, dqkv, w_qkv, 0, tiles_all)
    sums_b = sum_line(geo, line_b)
    halves_a, = reduce_plane(geo, [halves_a], [1])
    first_row = lax.broadcasted_iota(jnp.int32, (seg_count, SEG_LEN, D), 1) == 0
    mixed_out = jnp.where(
        first_row, own(crossed)[:, None, :], hidden_two.reshape(seg_count, SEG_LEN, D)
    )
    line_a = reduce_line(geo, halves_a, my_doc)
    owned = lax.all_to_all(
        sum_all(geo, line_a, sums_b, sums_d, sums_c), AXES[0], 0, 0, tiled=True
    )
    n_cls = n_doc * n_rows
    rates = lax.dynamic_index_in_dim(jnp.asarray(row_rates(geo, n_cls * SEG_LEN, n_cls)), me, 0, False)
    begins, factors = rates[0].astype(jnp.int32), rates[1:].reshape(-1)
    state = [value.reshape(geo.chunk, LANES) for value in (master, momentum, average)]
    weight, moment, smooth, copy_low = (
        value.reshape(-1)
        for value in update_rows(geo, table, owned.reshape(-1, LANES), begins, factors, state, pad_rows)
    )
    return (
        mixed_out[None],
        token_grad.reshape(1, seg_count, SEG_LEN, D),
        weight,
        moment,
        smooth,
        copy_low,
    )


def item_name(number):
    return item_list(0)[number].name


def solution(mesh):
    layer = P(AXES[1], AXES[0], None, None)
    ids = P(AXES[1], AXES[0])
    flat = P(AXES)
    return jax.shard_map(
        local,
        mesh=mesh,
        in_specs=(layer, layer, ids, ids, flat, flat, flat),
        out_specs=(layer, layer, flat, flat, flat, flat),
        check_vma=False,
    )
```
